32 devices in a mesh: wide: 8 (over y, x, core), narrow: 4 (over z).
Axes of the slice: x: 2, y: 2, z: 4, core: 2. Of those that a mesh axis runs over, the one named last changes fastest.
Arguments:
- tokens: bfloat16 [4, 2048, 2048], P('narrow', 'wide'), may hold values from -6 to 6
- lengths: int32 [4, 4], P('narrow'), may hold values from 1 to 2045, as said below
- gain_attn: bfloat16 [2048], P(('wide', 'narrow')), may hold values from 0.25 to 1.75
- w_qkv: bfloat16 [2048, 3072], P(('wide', 'narrow')), may hold values from -0.125 to 0.125
- w_out: bfloat16 [2048, 2048], P(('wide', 'narrow')), may hold values from -1 to 1
- gain_mlp: bfloat16 [2048], P(('wide', 'narrow')), may hold values from 0.25 to 1.75
- w_gateup: bfloat16 [2048, 16384], P(('wide', 'narrow')), may hold values from -0.125 to 0.125
- w_down: bfloat16 [8192, 2048], P(('wide', 'narrow')), may hold values from -0.0625 to 0.0625
- cotangent: bfloat16 [4, 2048, 2048], P('narrow', 'wide'), may hold values from -6 to 6
Outputs:
- layer_out: bfloat16 [4, 2048, 2048], P('narrow', 'wide')
- grad_tokens: bfloat16 [4, 2048, 2048], P('narrow', 'wide')
- grad_gain_attn: float32 [2048], P(('wide', 'narrow'))
- grad_qkv: float32 [2048, 3072], P(('wide', 'narrow'))
- grad_wout: float32 [2048, 2048], P(('wide', 'narrow'))
- grad_gain_mlp: float32 [2048], P(('wide', 'narrow'))
- grad_gateup: float32 [2048, 16384], P(('wide', 'narrow'))
- grad_down: float32 [8192, 2048], P(('wide', 'narrow'))
The draws below stay inside these ranges and needn't reach their ends.
Inputs may be any that keep to these rules, and one draw needn't show every extreme that they name: `lengths`: each row sums to 2048. In each row one entry, at a place drawn per row, is larger than 1792; the others are at most 64.
All inputs are finite; a program needn't handle non-finite values.
Results may differ from the reference program's by a relative error of at most 0.015.
Values may be sent and summed in bfloat16 or wider, within the bound.
A program may use at most 512 MiB of HBM per device.

```python
import math
import jax
import jax.numpy as jnp
from jax import lax

D = 2048
FF = 8192
HEADS = 32
KV_HEADS = 8
HEAD_DIM = 64
TOK_DEV = 256
SLOTS = 4
PACKS = 4
PACK_LEN = 2048
QD = 2048
KD = 512


def draw_lengths(key, part):
    key = jax.random.fold_in(key, 7)
    short_key, longest_key = jax.random.split(key)
    short_runs = jax.random.randint(short_key, (PACKS, SLOTS), 1, TOK_DEV // 4 + 1)
    first_pack = jnp.arange(PACKS)[:, None] == 0
    short_runs = jnp.where(first_pack, 1, short_runs)
    longest = jax.random.randint(longest_key, (PACKS, 1), 0, SLOTS)
    is_longest = jnp.arange(SLOTS)[None, :] == longest
    remainder = jnp.sum(jnp.where(is_longest, 0, short_runs), -1, keepdims=True)
    return jnp.where(is_longest, PACK_LEN - remainder, short_runs).astype(jnp.int32)


def levels(stream_key, shape, shards, low, top_value):
    def one(dim, parts):
        steps = jax.random.uniform(jax.random.fold_in(jax.random.fold_in(stream_key, 6), dim), (parts,), jnp.float32, low / len(shards), top_value / len(shards))
        return jnp.repeat(jnp.exp(steps), shape[dim] // parts).reshape((-1,) + (1,) * (len(shape) - dim - 1))

    gain = one(*shards[0])
    for cut in shards[1:]:
        gain = gain * one(*cut)
    return gain


def scatter_about(own_key, extent, spread, most, shards=(), kind=jnp.bfloat16):
    values = jax.random.normal(own_key, extent, jnp.float32) * spread
    if len(shards) > 0:
        values = levels(own_key, extent, shards, -0.22, 0.18) * values
    return jnp.clip(values, min=-most, max=most).astype(kind)


def setup_inputs(seed: int = 0) -> dict:
    key_list = jax.random.split(jax.random.key(seed), 10)
    return {
        "tokens": scatter_about(key_list[0], (PACKS, PACK_LEN, D), 1.0, 6.0, ((0, 4), (1, 8))),
        "lengths": draw_lengths(jax.random.fold_in(key_list[9], 71), 0),
        "gain_attn": jnp.clip(1.0 + 0.15 * jax.random.normal(key_list[2], (D,), jnp.float32), 0.25, 1.75).astype(jnp.bfloat16),
        "w_qkv": scatter_about(key_list[3], (D, QD + 2 * KD), D ** -0.5, 0.125, ((0, 32),)),
        "w_out": scatter_about(key_list[4], (QD, D), (QD // 64) ** -0.5, 1.0, ((0, 32),)),
        "gain_mlp": jnp.clip(1.0 + 0.15 * jax.random.normal(key_list[5], (D,), jnp.float32), 0.25, 1.75).astype(jnp.bfloat16),
        "w_gateup": scatter_about(key_list[6], (D, 2 * FF), D ** -0.5, 0.125, ((0, 32),)),
        "w_down": scatter_about(key_list[7], (FF, D), FF ** -0.5, 0.0625, ((0, 32),)),
        "cotangent": scatter_about(key_list[8], (PACKS, PACK_LEN, D), 1.0, 6.0, ((0, 4), (1, 8))),
    }


EPS = 1e-05
NEGATIVE = -1e+30

@jax.custom_vjp
def low(v):
    return lax.optimization_barrier(v.astype(jnp.bfloat16)).astype(jnp.float32)

@jax.custom_vjp
def low_back(v):
    return v

def low_keep(v):
    return (low(v), None)

def low_pass(kept, grad):
    return (grad,)

def back_keep(v):
    return (v, None)

def back_low(kept, grad):
    return (low(grad),)
low.defvjp(low_keep, low_pass)
low_back.defvjp(back_keep, back_low)

def matmul(left, right):
    return jnp.dot(left, right, precision=lax.Precision.HIGHEST)

def places(lengths_row, total_rows):
    seq_ends = jnp.cumsum(lengths_row).astype(jnp.int32)
    starts = seq_ends - lengths_row
    row_index = jnp.arange(total_rows, dtype=jnp.int32)
    segments = lax.optimization_barrier(jnp.sum((row_index[:, None] >= seq_ends[None, :]).astype(jnp.int32), -1))
    slot_index = jnp.arange(lengths_row.shape[0], dtype=jnp.int32)
    owned = segments[:, None] == slot_index[None, :]
    positions = row_index - lax.optimization_barrier(jnp.sum(jnp.where(owned, starts[None, :], 0), -1))
    return (segments, positions)

def rotary(positions, half_width):
    channel = jnp.arange(half_width, dtype=jnp.float32)
    inverse_rate = jnp.power(500000.0, -channel / half_width)
    wavelength = 2.0 * math.pi / inverse_rate
    smooth = (8192.0 / wavelength - 1.0) / 3.0
    blended = (1.0 - smooth) * inverse_rate / 32.0 + smooth * inverse_rate
    frequency = jnp.where(wavelength < 2048.0, inverse_rate, jnp.where(wavelength > 8192.0, inverse_rate / 32.0, blended))
    angles = positions[:, None] * frequency[None, :]
    return (jnp.cos(angles), jnp.sin(angles))

def rotate(vector, cosine_table, sine_table):
    half_width = vector.shape[-1] // 2
    front_half = vector[..., :half_width]
    back_half = vector[..., half_width:]
    cosine_part = cosine_table[:, None, :]
    sine_part = sine_table[:, None, :]
    return jnp.concatenate([front_half * cosine_part - back_half * sine_part, back_half * cosine_part + front_half * sine_part], -1)

def attend(queries, keys_all, values_all, segments):
    pack_rows = queries.shape[0]
    block_len = min(512, pack_rows)
    n_blocks = pack_rows // block_len
    groups = HEADS // KV_HEADS
    score_scale = 1.0 / math.sqrt(HEAD_DIM)
    grouped = queries.reshape(n_blocks, block_len, KV_HEADS, groups, HEAD_DIM)
    block_starts = jnp.arange(n_blocks, dtype=jnp.int32) * block_len
    key_index = jnp.arange(pack_rows, dtype=jnp.int32)

    def one_block(pack_item):
        block_queries, block_start = pack_item
        row_index = block_start + jnp.arange(block_len, dtype=jnp.int32)
        row_segments = lax.dynamic_slice_in_dim(segments, block_start, block_len)
        scores = jnp.einsum('qkgd,pkd->kgqp', block_queries, keys_all, precision=lax.Precision.HIGHEST) * score_scale
        scores = low_back(scores)
        allowed = (row_segments[:, None] == segments[None, :]) & (key_index[None, :] <= row_index[:, None])
        scores = jnp.where(allowed, scores, NEGATIVE)
        running_top = lax.optimization_barrier(jnp.max(scores, -1, keepdims=True))
        running_sum = lax.optimization_barrier(jnp.sum(jnp.where(allowed, jnp.exp(scores - running_top), 0.0), -1, keepdims=True))
        log_total = running_top + jnp.log(running_sum)
        rounded_prob = low(jnp.where(allowed, jnp.exp(scores - log_total), 0.0))
        return jnp.einsum('kgqp,pkd->qkgd', rounded_prob, values_all, precision=lax.Precision.HIGHEST)
    results = lax.map(jax.checkpoint(one_block), (grouped, block_starts))
    return results.reshape(pack_rows, HEADS * HEAD_DIM)

def decoder_layer(inputs, gain_attn, w_qkv, w_out, gain_mlp, w_gateup, w_down, segments, cosine_table, sine_table):
    pack_rows = inputs.shape[0]
    query_width = HEADS * HEAD_DIM
    key_width = KV_HEADS * HEAD_DIM
    normed_one = low(inputs * lax.rsqrt(lax.optimization_barrier(jnp.mean(inputs * inputs, -1, keepdims=True)) + EPS) * gain_attn)
    projected = low_back(matmul(normed_one, w_qkv))
    queries = low(rotate(projected[:, :query_width].reshape(pack_rows, HEADS, HEAD_DIM), cosine_table, sine_table))
    keys_all = low(rotate(projected[:, query_width:query_width + key_width].reshape(pack_rows, KV_HEADS, HEAD_DIM), cosine_table, sine_table))
    values_all = low(projected[:, query_width + key_width:].reshape(pack_rows, KV_HEADS, HEAD_DIM))
    attended_low = low_back(low(attend(queries, keys_all, values_all, segments)))
    branch = low_back(matmul(attended_low, w_out))
    middle = inputs + branch
    normed_two = low(middle * lax.rsqrt(lax.optimization_barrier(jnp.mean(middle * middle, -1, keepdims=True)) + EPS) * gain_mlp)
    gate_up = low_back(matmul(normed_two, w_gateup))
    hidden = low(jax.nn.silu(gate_up[:, :FF]) * gate_up[:, FF:])
    return middle + matmul(hidden, w_down)

def reference(tokens, lengths, gain_attn, w_qkv, w_out, gain_mlp, w_gateup, w_down, cotangent):
    weights = tuple((array.astype(jnp.float32) for array in (gain_attn, w_qkv, w_out, gain_mlp, w_gateup, w_down)))

    def per_pack(grad_sums, pack_item):
        tokens_pack, cotangent_pack, lengths_row = pack_item
        segments, positions = places(lengths_row, PACK_LEN)
        cosine_table, sine_table = rotary(positions.astype(jnp.float32), HEAD_DIM // 2)

        def forward(inputs, *layer_weights):
            return decoder_layer(inputs, *layer_weights, segments, cosine_table, sine_table)
        result, pullback = jax.vjp(forward, tokens_pack.astype(jnp.float32), *weights)
        gradients = pullback(cotangent_pack.astype(jnp.float32))
        grad_sums = tuple((running + extra for running, extra in zip(grad_sums, gradients[1:])))
        return (grad_sums, (result.astype(jnp.bfloat16), gradients[0].astype(jnp.bfloat16)))
    empty_sums = tuple((jnp.zeros_like(array) for array in weights))
    grad_sums, (layer_out, grad_tokens) = lax.scan(per_pack, empty_sums, (tokens, cotangent, lengths))
    return (layer_out, grad_tokens, grad_sums[0], grad_sums[1], grad_sums[2], grad_sums[3], grad_sums[4], grad_sums[5])
```

```python
import functools
import math

import jax
import jax.numpy as jnp
from jax import lax
from jax.experimental import pallas as pl
from jax.experimental.pallas import tpu as pltpu
from jax.sharding import PartitionSpec as P

FF = 8192
HEADS = 32
KV_HEADS = 8
HEAD_DIM = 64
HALF = HEAD_DIM // 2
EPS = 1e-05
NEGATIVE = -1e30
SCORE_SCALE = 1.0 / math.sqrt(HEAD_DIM)
BOTH = ("wide", "narrow")
F32 = jnp.float32
BF16 = jnp.bfloat16
NN = (((1,), (0,)), ((), ()))
NT = (((1,), (1,)), ((), ()))
TN = (((0,), (0,)), ((), ()))


def dot(left, right, dims, kind=F32):
    return lax.dot_general(left, right, dims, preferred_element_type=F32).astype(kind)


def places(lengths_row, total_rows):
    seq_ends = jnp.cumsum(lengths_row)
    starts = seq_ends - lengths_row
    row_index = jnp.arange(total_rows, dtype=jnp.int32)
    segments = jnp.sum((row_index[:, None] >= seq_ends[None, :]).astype(jnp.int32), -1)
    slot_index = jnp.arange(lengths_row.shape[0], dtype=jnp.int32)
    owned = segments[:, None] == slot_index[None, :]
    first = jnp.sum(jnp.where(owned, starts[None, :], 0), -1)
    return first, row_index - first


def rotary(positions, half_width):
    channel = jnp.arange(half_width, dtype=jnp.float32)
    inverse_rate = jnp.power(500000.0, -channel / half_width)
    wavelength = 2.0 * math.pi / inverse_rate
    smooth = (8192.0 / wavelength - 1.0) / 3.0
    blended = (1.0 - smooth) * inverse_rate / 32.0 + smooth * inverse_rate
    frequency = jnp.where(
        wavelength < 2048.0,
        inverse_rate,
        jnp.where(wavelength > 8192.0, inverse_rate / 32.0, blended),
    )
    angles = frequency[:, None] * positions[None, :]
    return jnp.cos(angles), jnp.sin(angles)


def norm_back(grad_unit, unit_rows, row_scale):
    return row_scale * (grad_unit - unit_rows * jnp.mean(grad_unit * unit_rows, -1, keepdims=True))


def attend_kernel(groups, start_ref, x_ref, low_ref, full_ref, log_ref, keys, top, total, acc):
    i = pl.program_id(0)
    blocks, _, rows = x_ref.shape
    width = groups * HEAD_DIM

    @pl.when(i == 0)
    def _():
        for j in range(blocks):
            keys[j] = x_ref[j, width : width + HEAD_DIM, :].T

    top[...] = jnp.full_like(top, NEGATIVE)
    total[...] = jnp.zeros_like(total)
    acc[...] = jnp.zeros_like(acc)
    start = start_ref[0]
    query_row = i * rows + lax.broadcasted_iota(jnp.int32, (rows, rows), 1)
    key_row = lax.broadcasted_iota(jnp.int32, (rows, rows), 0)

    def step(j, carry):
        key_index = key_row + j * rows
        allowed = (key_index <= query_row) & (key_index >= start)
        key_block = keys[j]
        value_block = x_ref[j, width + HEAD_DIM :, :]
        for h in range(groups):
            own = pl.ds(h * HEAD_DIM, HEAD_DIM)
            scores = dot(key_block, x_ref[i, own, :], NN)
            scores = jnp.where(allowed, scores, NEGATIVE)
            old = top[h : h + 1, :]
            new = jnp.maximum(old, jnp.max(scores, 0, keepdims=True))
            shrink = jnp.exp(old - new)
            prob = jnp.exp(scores - new)
            top[h : h + 1, :] = new
            total[h : h + 1, :] = total[h : h + 1, :] * shrink + jnp.sum(prob, 0, keepdims=True)
            acc[own, :] = acc[own, :] * shrink + dot(value_block, prob.astype(BF16), NN)
        return carry

    lax.fori_loop(0, i + 1, step, 0)
    log_ref[0] = top[...] + jnp.log(total[...])
    for h in range(groups):
        own = pl.ds(h * HEAD_DIM, HEAD_DIM)
        result = acc[own, :] / total[h : h + 1, :]
        full_ref[0, own, :] = result
        low_ref[0, own, :] = result.astype(BF16)


def attend(x, start, groups):
    blocks, _, rows = x.shape
    width = groups * HEAD_DIM
    whole = lambda i: (0, 0, 0)
    mine = lambda i: (i, 0, 0)
    return pl.pallas_call(
        functools.partial(attend_kernel, groups),
        grid=(blocks,),
        out_shape=(
            jax.ShapeDtypeStruct((blocks, width, rows), BF16),
            jax.ShapeDtypeStruct((blocks, width, rows), F32),
            jax.ShapeDtypeStruct((blocks, groups, rows), F32),
        ),
        in_specs=[pl.BlockSpec((1, 1, rows), mine), pl.BlockSpec(x.shape, whole)],
        out_specs=(
            pl.BlockSpec((1, width, rows), mine),
            pl.BlockSpec((1, width, rows), mine),
            pl.BlockSpec((1, groups, rows), mine),
        ),
        scratch_shapes=[
            pltpu.VMEM((blocks, rows, HEAD_DIM), BF16),
            pltpu.VMEM((groups, rows), F32),
            pltpu.VMEM((groups, rows), F32),
            pltpu.VMEM((width, rows), F32),
        ],
        compiler_params=pltpu.CompilerParams(vmem_limit_bytes=32 << 20),
        cost_estimate=pl.CostEstimate(
            flops=16 * width * (blocks * rows) ** 2,
            bytes_accessed=2 * x.size * 2,
            transcendentals=groups * (blocks * rows) ** 2 // 2,
        ),
    )(start, x)


def attend_back_kernel(
    groups, start_ref, x_ref, grad_ref, full_ref, log_ref, cos_ref, sin_ref, out_ref,
    keys, values, acc, acc_keys, acc_values,
):
    i = pl.program_id(0)
    blocks, _, rows = x_ref.shape
    width = groups * HEAD_DIM

    @pl.when(i == 0)
    def _():
        for j in range(blocks):
            keys[j] = x_ref[j, width : width + HEAD_DIM, :].T
            values[j] = x_ref[j, width + HEAD_DIM :, :].T
        acc_keys[...] = jnp.zeros_like(acc_keys)
        acc_values[...] = jnp.zeros_like(acc_values)

    acc[...] = jnp.zeros_like(acc)
    start = start_ref[0]
    query_row = i * rows + lax.broadcasted_iota(jnp.int32, (rows, rows), 1)
    key_row = lax.broadcasted_iota(jnp.int32, (rows, rows), 0)
    deltas = [
        jnp.sum(
            grad_ref[0, pl.ds(h * HEAD_DIM, HEAD_DIM), :].astype(F32)
            * full_ref[0, pl.ds(h * HEAD_DIM, HEAD_DIM), :],
            0,
            keepdims=True,
        )
        for h in range(groups)
    ]

    def step(j, carry):
        key_index = key_row + j * rows
        allowed = (key_index <= query_row) & (key_index >= start)
        key_block = keys[j]
        value_block = values[j]
        key_columns = x_ref[j, width : width + HEAD_DIM, :]
        grad_keys = acc_keys[j]
        grad_values = acc_values[j]
        for h in range(groups):
            own = pl.ds(h * HEAD_DIM, HEAD_DIM)
            query = x_ref[i, own, :]
            grad = grad_ref[0, own, :]
            scores = dot(key_block, query, NN)
            scores = jnp.where(allowed, scores, NEGATIVE)
            prob = jnp.exp(scores - log_ref[0, h : h + 1, :])
            grad_prob = dot(value_block, grad, NN)
            grad_scores = (prob * (grad_prob - deltas[h])).astype(BF16)
            acc[own, :] += dot(key_columns, grad_scores, NN)
            grad_keys = grad_keys + dot(query, grad_scores, NT)
            grad_values = grad_values + dot(grad, prob.astype(BF16), NT)
        acc_keys[j] = grad_keys
        acc_values[j] = grad_values
        return carry

    lax.fori_loop(0, i + 1, step, 0)

    def turn_back(block, cos, sin):
        front, back = block[:HALF, :], block[HALF:, :]
        return (front * cos + back * sin).astype(BF16), (back * cos - front * sin).astype(BF16)

    for h in range(groups):
        at = h * HEAD_DIM
        front, back = turn_back(acc[pl.ds(at, HEAD_DIM), :] * SCORE_SCALE, cos_ref[i], sin_ref[i])
        out_ref[i, pl.ds(at, HALF), :] = front
        out_ref[i, pl.ds(at + HALF, HALF), :] = back

    @pl.when(i == blocks - 1)
    def _():
        for j in range(blocks):
            front, back = turn_back(acc_keys[j], cos_ref[j], sin_ref[j])
            out_ref[j, pl.ds(width, HALF), :] = front
            out_ref[j, pl.ds(width + HALF, HALF), :] = back
            out_ref[j, pl.ds(width + HEAD_DIM, HEAD_DIM), :] = acc_values[j].astype(BF16)


def attend_back(x, grad, full, log_total, start, cos, sin, groups):
    blocks, _, rows = x.shape
    width = groups * HEAD_DIM
    whole = lambda i: (0, 0, 0)
    mine = lambda i: (i, 0, 0)
    return pl.pallas_call(
        functools.partial(attend_back_kernel, groups),
        grid=(blocks,),
        out_shape=jax.ShapeDtypeStruct(x.shape, BF16),
        in_specs=[
            pl.BlockSpec((1, 1, rows), mine),
            pl.BlockSpec(x.shape, whole),
            pl.BlockSpec((1, width, rows), mine),
            pl.BlockSpec((1, width, rows), mine),
            pl.BlockSpec((1, groups, rows), mine),
            pl.BlockSpec(cos.shape, whole),
            pl.BlockSpec(sin.shape, whole),
        ],
        out_specs=pl.BlockSpec(x.shape, whole),
        scratch_shapes=[
            pltpu.VMEM((blocks, rows, HEAD_DIM), BF16),
            pltpu.VMEM((blocks, rows, HEAD_DIM), BF16),
            pltpu.VMEM((width, rows), F32),
            pltpu.VMEM((blocks, HEAD_DIM, rows), F32),
            pltpu.VMEM((blocks, HEAD_DIM, rows), F32),
        ],
        compiler_params=pltpu.CompilerParams(vmem_limit_bytes=40 << 20),
        cost_estimate=pl.CostEstimate(
            flops=40 * width * (blocks * rows) ** 2,
            bytes_accessed=4 * x.size * 2,
            transcendentals=groups * (blocks * rows) ** 2 // 2,
        ),
    )(start, x, grad, full, log_total, cos, sin)


def middle_kernel(step_rows, x_ref, c_ref, gate_ref, up_ref, down_ref, hidden_ref, dgate_ref, dup_ref):
    def step(t, carry):
        rows = pl.ds(pl.multiple_of(t * step_rows, step_rows), step_rows)
        x = x_ref[rows, :]
        gate = dot(x, gate_ref[...], NN)
        up = dot(x, up_ref[...], NN)
        grad = dot(c_ref[rows, :], down_ref[...], NT)
        sig = 1.0 / (1.0 + jnp.exp(-gate))
        silu = gate * sig
        hidden_ref[rows, :] = (silu * up).astype(BF16)
        dgate_ref[rows, :] = (grad * up * (sig + silu * (1.0 - sig))).astype(BF16)
        dup_ref[rows, :] = (grad * silu).astype(BF16)
        return carry

    lax.fori_loop(0, x_ref.shape[0] // step_rows, step, 0)


def middle_part(x, c, gate_up, down):
    tokens, width = x.shape
    own = down.shape[0]
    tile = min(256, own)
    tiles = own // tile
    shape = jax.ShapeDtypeStruct((tokens, own), BF16)
    out = pl.BlockSpec((tokens, tile), lambda f: (0, f))
    return pl.pallas_call(
        functools.partial(middle_kernel, 256),
        grid=(tiles,),
        out_shape=(shape, shape, shape),
        in_specs=[
            pl.BlockSpec((tokens, width), lambda f: (0, 0)),
            pl.BlockSpec((tokens, width), lambda f: (0, 0)),
            pl.BlockSpec((width, tile), lambda f: (0, f)),
            pl.BlockSpec((width, tile), lambda f: (0, f + tiles)),
            pl.BlockSpec((tile, width), lambda f: (f, 0)),
        ],
        out_specs=(out, out, out),
        compiler_params=pltpu.CompilerParams(vmem_limit_bytes=56 << 20),
        cost_estimate=pl.CostEstimate(
            flops=6 * tokens * width * own,
            bytes_accessed=2 * (2 * tokens * width + 3 * width * own + 3 * tokens * own),
            transcendentals=tokens * own,
        ),
    )(x, c, gate_up, gate_up, down)


def gather(x, axis):
    return lax.all_gather(x, axis, axis=0, tiled=True)


def scatter_sum(x, axis):
    return lax.psum_scatter(x, axis, scatter_dimension=0, tiled=True)


def exchange(x, axis):
    return lax.all_to_all(x, axis, split_axis=0, concat_axis=0, tiled=True)


def per_device(tokens, lengths, gain_attn, w_qkv, w_out, gain_mlp, w_gateup, w_down, cotangent):
    rows, width = tokens.shape[1:]
    wide, narrow = lax.axis_size("wide"), lax.axis_size("narrow")
    pack_rows = rows * wide
    query_width, key_width = HEADS * HEAD_DIM, KV_HEADS * HEAD_DIM
    groups = HEADS // wide
    copies = wide // KV_HEADS
    own_ff = FF // narrow
    first, positions = places(lengths[0], pack_rows)
    cos_all, sin_all = rotary(positions.astype(F32), HALF)
    first_row = lax.axis_index("wide") * rows
    cos = lax.dynamic_slice_in_dim(cos_all, first_row, rows, 1)
    sin = lax.dynamic_slice_in_dim(sin_all, first_row, rows, 1)
    cos_all = cos_all.reshape(HALF, wide, rows).transpose(1, 0, 2)
    sin_all = sin_all.reshape(HALF, wide, rows).transpose(1, 0, 2)
    start = first.reshape(wide, 1, rows)

    gains = jnp.stack([gain_attn, gain_mlp], -1)
    with_gains = jnp.concatenate([w_qkv, jnp.pad(gains, ((0, 0), (0, 126)))], -1)
    qkv_gained = gather(with_gains, BOTH)
    qkv_whole = qkv_gained[:, : w_qkv.shape[1]]
    gain_one = qkv_gained[:, w_qkv.shape[1]].astype(F32)
    gain_two = qkv_gained[:, w_qkv.shape[1] + 1].astype(F32)
    out_whole = gather(w_out, BOTH)
    shard = w_gateup.shape[0]
    gateup_cut = w_gateup.reshape(shard, 2, wide, narrow, -1).transpose(3, 0, 1, 2, 4)
    gateup_own = gather(
        exchange(gateup_cut.reshape(narrow, shard, 2 * own_ff), "narrow").reshape(-1, 2 * own_ff),
        "wide",
    )
    down_own = gather(w_down, "wide")
    cot_group = gather(cotangent[0], "narrow")

    inputs = tokens[0].astype(F32)
    scale_one = lax.rsqrt(jnp.mean(inputs * inputs, -1, keepdims=True) + EPS)
    unit_one = inputs * scale_one
    normed_one = (unit_one * gain_one).astype(BF16)
    projected = dot(qkv_whole, normed_one, (((0,), (1,)), ((), ())))
    turning = projected[: query_width + key_width].reshape(HEADS + KV_HEADS, 2, HALF, rows)
    front, back = turning[:, 0], turning[:, 1]
    turned = jnp.stack([front * cos - back * sin, back * cos + front * sin], 1)
    queries = (turned[:HEADS] * SCORE_SCALE).astype(BF16).reshape(wide, groups * HEAD_DIM, rows)
    keys = turned[HEADS:].astype(BF16).reshape(KV_HEADS, HEAD_DIM, rows)
    values = projected[query_width + key_width :].astype(BF16).reshape(KV_HEADS, HEAD_DIM, rows)
    keys_values = jnp.repeat(jnp.concatenate([keys, values], 1), copies, 0)
    heads = exchange(jnp.concatenate([queries, keys_values], 1), "wide")
    attended_heads, attended_full, log_total = attend(heads, start, groups)
    attended_low = exchange(attended_heads, "wide").reshape(query_width, rows)
    middle = inputs + dot(attended_low, out_whole, TN)
    scale_two = lax.rsqrt(jnp.mean(middle * middle, -1, keepdims=True) + EPS)
    unit_two = middle * scale_two
    normed_two = (unit_two * gain_two).astype(BF16)

    normed_group = gather(normed_two, "narrow")
    hidden, grad_gate, grad_up = middle_part(normed_group, cot_group, gateup_own, down_own)
    grad_gate_up = jnp.concatenate([grad_gate, grad_up], -1)
    grad_normed_two = scatter_sum(dot(grad_gate_up, gateup_own, NT, BF16), "narrow").astype(F32)
    layer_out = (middle + scatter_sum(dot(hidden, down_own, NN, BF16), "narrow")).astype(BF16)[None]
    grad_down = scatter_sum(dot(hidden, cot_group, TN, BF16), "wide").astype(F32)
    grad_gateup = scatter_sum(dot(normed_group, grad_gate_up, TN, BF16), "wide")
    grad_gateup = exchange(grad_gateup.reshape(narrow, shard, 2 * own_ff), "narrow")
    grad_gateup = (
        grad_gateup.reshape(narrow, shard, 2, wide, -1)
        .transpose(1, 2, 3, 0, 4)
        .reshape(shard, 2 * FF)
        .astype(F32)
    )

    part_gain_two = jnp.sum(grad_normed_two * unit_two, 0)
    grad_middle = cotangent[0].astype(F32) + norm_back(
        grad_normed_two * gain_two, unit_two, scale_two
    )
    grad_branch = grad_middle.astype(BF16)
    grad_wout = scatter_sum(dot(attended_low, grad_branch, NN, BF16), BOTH).astype(F32)
    grad_attended = dot(out_whole, grad_branch, NT, BF16).reshape(wide, groups * HEAD_DIM, rows)
    grad_heads = attend_back(
        heads, exchange(grad_attended, "wide"), attended_full, log_total, start, cos_all, sin_all,
        groups,
    )
    grad_heads = exchange(grad_heads, "wide")
    grad_queries = grad_heads[:, : groups * HEAD_DIM].reshape(query_width, rows)
    grad_keys_values = (
        grad_heads[:, groups * HEAD_DIM :]
        .reshape(KV_HEADS, copies, 2, HEAD_DIM, rows)
        .astype(F32)
        .sum(1)
        .astype(BF16)
    )
    grad_projected = jnp.concatenate(
        [
            grad_queries,
            grad_keys_values[:, 0].reshape(key_width, rows),
            grad_keys_values[:, 1].reshape(key_width, rows),
        ],
        0,
    )
    grad_normed_one = dot(grad_projected, qkv_whole, (((0,), (1,)), ((), ())))
    part_gain_one = jnp.sum(grad_normed_one * unit_one, 0)
    part_gains = jnp.stack([part_gain_one, part_gain_two], -1)
    part_qkv = dot(normed_one, grad_projected, (((0,), (1,)), ((), ())), BF16)
    grad_qkv = scatter_sum(part_qkv, BOTH).astype(F32)
    grad_gains = scatter_sum(part_gains, BOTH)
    grad_inputs = grad_middle + norm_back(grad_normed_one * gain_one, unit_one, scale_one)
    grad_tokens = grad_inputs.astype(BF16)[None]
    return (
        layer_out,
        grad_tokens,
        grad_gains[:, 0],
        grad_qkv,
        grad_wout,
        grad_gains[:, 1],
        grad_gateup,
        grad_down,
    )


def solution(mesh):
    rows, packs = P("narrow", "wide", None), P("narrow", None)
    weight, gain = P(BOTH, None), P(BOTH)
    return jax.shard_map(
        per_device,
        mesh=mesh,
        in_specs=(rows, packs, gain, weight, weight, gain, weight, weight, rows),
        out_specs=(rows, rows, gain, weight, weight, gain, weight, weight),
        check_vma=False,
    )
```

```python
import functools
import math

import jax
import jax.numpy as jnp
from jax import lax
from jax.experimental import pallas as pl
from jax.experimental.pallas import tpu as pltpu
from jax.sharding import PartitionSpec as P

FF = 8192
HEADS = 32
KV_HEADS = 8
HEAD_DIM = 64
HALF = HEAD_DIM // 2
EPS = 1e-05
NEGATIVE = -1e30
SCORE_SCALE = 1.0 / math.sqrt(HEAD_DIM)
BOTH = ("wide", "narrow")
F32 = jnp.float32
BF16 = jnp.bfloat16
NN = (((1,), (0,)), ((), ()))
NT = (((1,), (1,)), ((), ()))
TN = (((0,), (0,)), ((), ()))


def dot(left, right, dims, kind=F32):
    return lax.dot_general(left, right, dims, preferred_element_type=F32).astype(kind)


def places(lengths_row, total_rows):
    seq_ends = jnp.cumsum(lengths_row)
    starts = seq_ends - lengths_row
    row_index = jnp.arange(total_rows, dtype=jnp.int32)
    segments = jnp.sum((row_index[:, None] >= seq_ends[None, :]).astype(jnp.int32), -1)
    slot_index = jnp.arange(lengths_row.shape[0], dtype=jnp.int32)
    owned = segments[:, None] == slot_index[None, :]
    first = jnp.sum(jnp.where(owned, starts[None, :], 0), -1)
    return first, row_index - first


def rotary(positions, half_width):
    channel = jnp.arange(half_width, dtype=jnp.float32)
    inverse_rate = jnp.power(500000.0, -channel / half_width)
    wavelength = 2.0 * math.pi / inverse_rate
    smooth = (8192.0 / wavelength - 1.0) / 3.0
    blended = (1.0 - smooth) * inverse_rate / 32.0 + smooth * inverse_rate
    frequency = jnp.where(
        wavelength < 2048.0,
        inverse_rate,
        jnp.where(wavelength > 8192.0, inverse_rate / 32.0, blended),
    )
    angles = frequency[:, None] * positions[None, :]
    return jnp.cos(angles), jnp.sin(angles)


def norm_back(grad_unit, unit_rows, row_scale):
    return row_scale * (grad_unit - unit_rows * jnp.mean(grad_unit * unit_rows, -1, keepdims=True))


def attend_kernel(groups, start_ref, x_ref, low_ref, full_ref, log_ref, keys, top, total, acc):
    i = pl.program_id(0)
    blocks, _, rows = x_ref.shape
    width = groups * HEAD_DIM

    @pl.when(i == 0)
    def _():
        for j in range(blocks):
            keys[j] = x_ref[j, width : width + HEAD_DIM, :].T

    top[...] = jnp.full_like(top, NEGATIVE)
    total[...] = jnp.zeros_like(total)
    acc[...] = jnp.zeros_like(acc)
    start = start_ref[0]
    query_row = i * rows + lax.broadcasted_iota(jnp.int32, (rows, rows), 1)
    key_row = lax.broadcasted_iota(jnp.int32, (rows, rows), 0)

    def step(j, carry):
        key_index = key_row + j * rows
        allowed = (key_index <= query_row) & (key_index >= start)
        key_block = keys[j]
        value_block = x_ref[j, width + HEAD_DIM :, :]
        for h in range(groups):
            own = pl.ds(h * HEAD_DIM, HEAD_DIM)
            scores = dot(key_block, x_ref[i, own, :], NN)
            scores = jnp.where(allowed, scores, NEGATIVE)
            old = top[h : h + 1, :]
            new = jnp.maximum(old, jnp.max(scores, 0, keepdims=True))
            shrink = jnp.exp(old - new)
            prob = jnp.exp(scores - new)
            top[h : h + 1, :] = new
            total[h : h + 1, :] = total[h : h + 1, :] * shrink + jnp.sum(prob, 0, keepdims=True)
            acc[own, :] = acc[own, :] * shrink + dot(value_block, prob.astype(BF16), NN)
        return carry

    lax.fori_loop(0, i + 1, step, 0)
    log_ref[0] = top[...] + jnp.log(total[...])
    for h in range(groups):
        own = pl.ds(h * HEAD_DIM, HEAD_DIM)
        result = acc[own, :] / total[h : h + 1, :]
        full_ref[0, own, :] = result
        low_ref[0, own, :] = result.astype(BF16)


def attend(x, start, groups):
    blocks, _, rows = x.shape
    width = groups * HEAD_DIM
    whole = lambda i: (0, 0, 0)
    mine = lambda i: (i, 0, 0)
    return pl.pallas_call(
        functools.partial(attend_kernel, groups),
        grid=(blocks,),
        out_shape=(
            jax.ShapeDtypeStruct((blocks, width, rows), BF16),
            jax.ShapeDtypeStruct((blocks, width, rows), F32),
            jax.ShapeDtypeStruct((blocks, groups, rows), F32),
        ),
        in_specs=[pl.BlockSpec((1, 1, rows), mine), pl.BlockSpec(x.shape, whole)],
        out_specs=(
            pl.BlockSpec((1, width, rows), mine),
            pl.BlockSpec((1, width, rows), mine),
            pl.BlockSpec((1, groups, rows), mine),
        ),
        scratch_shapes=[
            pltpu.VMEM((blocks, rows, HEAD_DIM), BF16),
            pltpu.VMEM((groups, rows), F32),
            pltpu.VMEM((groups, rows), F32),
            pltpu.VMEM((width, rows), F32),
        ],
        compiler_params=pltpu.CompilerParams(vmem_limit_bytes=32 << 20),
        cost_estimate=pl.CostEstimate(
            flops=16 * width * (blocks * rows) ** 2,
            bytes_accessed=2 * x.size * 2,
            transcendentals=groups * (blocks * rows) ** 2 // 2,
        ),
    )(start, x)


def attend_back_kernel(
    groups, start_ref, x_ref, grad_ref, full_ref, log_ref, cos_ref, sin_ref, out_ref,
    keys, values, acc, acc_keys, acc_values,
):
    i = pl.program_id(0)
    blocks, _, rows = x_ref.shape
    width = groups * HEAD_DIM

    @pl.when(i == 0)
    def _():
        for j in range(blocks):
            keys[j] = x_ref[j, width : width + HEAD_DIM, :].T
            values[j] = x_ref[j, width + HEAD_DIM :, :].T
        acc_keys[...] = jnp.zeros_like(acc_keys)
        acc_values[...] = jnp.zeros_like(acc_values)

    acc[...] = jnp.zeros_like(acc)
    start = start_ref[0]
    query_row = i * rows + lax.broadcasted_iota(jnp.int32, (rows, rows), 1)
    key_row = lax.broadcasted_iota(jnp.int32, (rows, rows), 0)
    deltas = [
        jnp.sum(
            grad_ref[0, pl.ds(h * HEAD_DIM, HEAD_DIM), :].astype(F32)
            * full_ref[0, pl.ds(h * HEAD_DIM, HEAD_DIM), :],
            0,
            keepdims=True,
        )
        for h in range(groups)
    ]

    def step(j, carry):
        key_index = key_row + j * rows
        allowed = (key_index <= query_row) & (key_index >= start)
        key_block = keys[j]
        value_block = values[j]
        key_columns = x_ref[j, width : width + HEAD_DIM, :]
        grad_keys = acc_keys[j]
        grad_values = acc_values[j]
        for h in range(groups):
            own = pl.ds(h * HEAD_DIM, HEAD_DIM)
            query = x_ref[i, own, :]
            grad = grad_ref[0, own, :]
            scores = dot(key_block, query, NN)
            scores = jnp.where(allowed, scores, NEGATIVE)
            prob = jnp.exp(scores - log_ref[0, h : h + 1, :])
            grad_prob = dot(value_block, grad, NN)
            grad_scores = (prob * (grad_prob - deltas[h])).astype(BF16)
            acc[own, :] += dot(key_columns, grad_scores, NN)
            grad_keys = grad_keys + dot(query, grad_scores, NT)
            grad_values = grad_values + dot(grad, prob.astype(BF16), NT)
        acc_keys[j] = grad_keys
        acc_values[j] = grad_values
        return carry

    lax.fori_loop(0, i + 1, step, 0)

    def turn_back(block, cos, sin):
        front, back = block[:HALF, :], block[HALF:, :]
        return (front * cos + back * sin).astype(BF16), (back * cos - front * sin).astype(BF16)

    for h in range(groups):
        at = h * HEAD_DIM
        front, back = turn_back(acc[pl.ds(at, HEAD_DIM), :] * SCORE_SCALE, cos_ref[i], sin_ref[i])
        out_ref[i, pl.ds(at, HALF), :] = front
        out_ref[i, pl.ds(at + HALF, HALF), :] = back

    @pl.when(i == blocks - 1)
    def _():
        for j in range(blocks):
            front, back = turn_back(acc_keys[j], cos_ref[j], sin_ref[j])
            out_ref[j, pl.ds(width, HALF), :] = front
            out_ref[j, pl.ds(width + HALF, HALF), :] = back
            out_ref[j, pl.ds(width + HEAD_DIM, HEAD_DIM), :] = acc_values[j].astype(BF16)


def attend_back(x, grad, full, log_total, start, cos, sin, groups):
    blocks, _, rows = x.shape
    width = groups * HEAD_DIM
    whole = lambda i: (0, 0, 0)
    mine = lambda i: (i, 0, 0)
    return pl.pallas_call(
        functools.partial(attend_back_kernel, groups),
        grid=(blocks,),
        out_shape=jax.ShapeDtypeStruct(x.shape, BF16),
        in_specs=[
            pl.BlockSpec((1, 1, rows), mine),
            pl.BlockSpec(x.shape, whole),
            pl.BlockSpec((1, width, rows), mine),
            pl.BlockSpec((1, width, rows), mine),
            pl.BlockSpec((1, groups, rows), mine),
            pl.BlockSpec(cos.shape, whole),
            pl.BlockSpec(sin.shape, whole),
        ],
        out_specs=pl.BlockSpec(x.shape, whole),
        scratch_shapes=[
            pltpu.VMEM((blocks, rows, HEAD_DIM), BF16),
            pltpu.VMEM((blocks, rows, HEAD_DIM), BF16),
            pltpu.VMEM((width, rows), F32),
            pltpu.VMEM((blocks, HEAD_DIM, rows), F32),
            pltpu.VMEM((blocks, HEAD_DIM, rows), F32),
        ],
        compiler_params=pltpu.CompilerParams(vmem_limit_bytes=40 << 20),
        cost_estimate=pl.CostEstimate(
            flops=40 * width * (blocks * rows) ** 2,
            bytes_accessed=4 * x.size * 2,
            transcendentals=groups * (blocks * rows) ** 2 // 2,
        ),
    )(start, x, grad, full, log_total, cos, sin)


def gather(x, axis):
    return lax.all_gather(x, axis, axis=0, tiled=True)


def scatter_sum(x, axis):
    return lax.psum_scatter(x, axis, scatter_dimension=0, tiled=True)


def exchange(x, axis):
    return lax.all_to_all(x, axis, split_axis=0, concat_axis=0, tiled=True)


def across(x, mask):
    return lax.ppermute(x, "wide", [(i, i ^ mask) for i in range(lax.axis_size("wide"))])


def shift(x, step):
    n = lax.axis_size("narrow")
    return lax.ppermute(x, "narrow", [(i, (i + step) % n) for i in range(n)])


def pick(x, index, axis):
    return lax.dynamic_index_in_dim(x, index, axis, keepdims=False)


def plus(left, right, kind=BF16):
    return (left.astype(F32) + right.astype(F32)).astype(kind)


def shift_exchange(x):
    n, me = x.shape[0], lax.axis_index("narrow")
    out = jnp.zeros_like(x)
    out = lax.dynamic_update_index_in_dim(out, pick(x, me, 0), me, 0)
    for step in range(1, n):
        came = shift(pick(x, (me + step) % n, 0), step)
        out = lax.dynamic_update_index_in_dim(out, came, (me - step) % n, 0)
    return out


def shift_gather(x):
    n, me = lax.axis_size("narrow"), lax.axis_index("narrow")
    out = jnp.zeros((n,) + x.shape, x.dtype)
    out = lax.dynamic_update_index_in_dim(out, x, me, 0)
    for step in range(1, n):
        out = lax.dynamic_update_index_in_dim(out, shift(x, step), (me - step) % n, 0)
    return out.reshape((-1,) + x.shape[1:])


def shift_scatter_sum(x):
    n, me = lax.axis_size("narrow"), lax.axis_index("narrow")
    x = x.reshape((n, -1) + x.shape[1:])
    total = pick(x, me, 0).astype(F32)
    for step in range(1, n):
        total = total + shift(pick(x, (me + step) % n, 0), step).astype(F32)
    return total


def wide_gather(x):
    wide, me = lax.axis_size("wide"), lax.axis_index("wide")
    pieces = {0: x}
    if wide == 8:
        half = x.shape[0] // 2
        pieces[2] = across(x, 2)
        pieces[4] = across(x, 4)
        pieces[6] = jnp.concatenate(
            [across(pieces[2][:half], 4), across(pieces[4][half:], 2)], 0
        )
    else:
        for mask in range(2, wide, 2):
            pieces[mask] = across(x, mask)
    for mask in range(0, wide, 2):
        pieces[mask + 1] = across(pieces[mask], 1)
    out = jnp.zeros((wide,) + x.shape, x.dtype)
    for mask in range(wide):
        out = lax.dynamic_update_index_in_dim(out, pieces[mask], me ^ mask, 0)
    return out.reshape((-1,) + x.shape[1:])


def wide_scatter_sum(make, kind=BF16):
    wide, me = lax.axis_size("wide"), lax.axis_index("wide")
    chips = wide // 2
    core, chip = me % 2, me // 2
    came = across(make(1 - core), 1)
    held = plus(make(core), came)
    if chips == 4:
        x, y = chip % 2, chip // 2
        columns = held.shape[2]
        held = held.reshape((2, 2) + held.shape[1:])
        left, right = held[..., : columns // 2], held[..., columns // 2 :]
        left = plus(pick(left, x, 1), across(pick(left, 1 - x, 1), 2))
        right = plus(pick(right, y, 0), across(pick(right, 1 - y, 0), 4))
        left = plus(pick(left, y, 0), across(pick(left, 1 - y, 0), 4), kind)
        right = plus(pick(right, x, 0), across(pick(right, 1 - x, 0), 2), kind)
        return jnp.concatenate([left, right], -1)
    bit = 1
    while held.shape[0] > 1:
        held = held.reshape((-1, 2) + held.shape[1:])
        own = (chip // bit) % 2
        held = plus(pick(held, own, 1), across(pick(held, 1 - own, 1), 2 * bit))
        bit *= 2
    return held[0].astype(kind)


MESH = pl.DeviceIdType.MESH


def gather_kernel(
    wide, narrow, lag, qkv_ref, out_w_ref, cut_ref, qkv_all, out_all, cut_all,
    own_sem, x_send, x_recv, z_sends, z_recvs, m_sends, m_recvs, r_sends, r_recvs, c_sends, c_recvs,
):
    w, n = lax.axis_index("wide"), lax.axis_index("narrow")
    relay = wide == 8
    masks = [2, 4] if relay else list(range(2, wide, 2))
    chips = wide // 2

    def to_wide(mask):
        return {"wide": w ^ mask, "narrow": n}

    def to_narrow(other):
        return {"wide": w, "narrow": other}

    barrier = pltpu.get_barrier_semaphore()
    for mask in [1] + masks:
        pl.semaphore_signal(barrier, inc=1, device_id=to_wide(mask), device_id_type=MESH)
    for step in range(1, narrow):
        pl.semaphore_signal(
            barrier, inc=1, device_id=to_narrow(lax.rem(n + step, narrow)), device_id_type=MESH
        )
    pl.semaphore_wait(barrier, len(masks) + narrow)

    def owner_of(side, d):
        return n - d if side == 0 else n + d

    def valid(side, d):
        return n - d >= 0 if side == 0 else n + d < narrow

    def can_pass(side, d):
        if side == 0:
            return (n - (d - 1) >= 0) & (n < narrow - 1)
        return (n + (d - 1) < narrow) & (n > 0)

    def slot(side, d):
        return d - 1 + side * (narrow - 1) if d else 2 * (narrow - 1)

    def at_distance(d, action):
        if d == 0:
            action(0, 0)
            return
        for side in (0, 1):
            pl.when(valid(side, d))(functools.partial(action, side, d))

    class Flow:
        def __init__(self, index, x_ref, out_ref):
            self.x_ref, self.out_ref = x_ref, out_ref
            self.z_send, self.z_recv = z_sends.at[index], z_recvs.at[index]
            self.m_send, self.m_recv = m_sends.at[index], m_recvs.at[index]
            self.r_send, self.r_recv = r_sends.at[index], r_recvs.at[index]
            self.c_send, self.c_recv = c_sends.at[index], c_recvs.at[index]
            self.own = pltpu.make_async_copy(x_ref, self.place(w, n), own_sem.at[index])

        def place(self, owner_w, owner_n, part=None):
            depth = self.x_ref.shape[0]
            half = depth // 2
            at = (owner_w * narrow + owner_n) * depth
            if part is None:
                return self.out_ref.at[pl.ds(pl.multiple_of(at, depth), depth), :]
            return self.out_ref.at[pl.ds(pl.multiple_of(at + part * half, half), half), :]

        def z_copy(self, side, d):
            block = owner_of(side, d - 1)
            return pltpu.make_async_remote_copy(
                src_ref=self.x_ref if d == 1 else self.place(w, block),
                dst_ref=self.place(w, block),
                send_sem=self.z_send.at[side, d],
                recv_sem=self.z_recv.at[side, d],
                device_id=to_narrow(n + 1 if side == 0 else n - 1),
                device_id_type=MESH,
            )

        def z_wait(self, side, d):
            block = self.place(w, owner_of(side, d))
            pltpu.make_async_copy(block, block, self.z_recv.at[side, d]).wait()

        def m_copy(self, i, side, d):
            block = self.place(w, owner_of(side, d))
            return pltpu.make_async_remote_copy(
                src_ref=self.x_ref if d == 0 else block,
                dst_ref=block,
                send_sem=self.m_send.at[i, slot(side, d)],
                recv_sem=self.m_recv.at[i, slot(side, d)],
                device_id=to_wide(masks[i]),
                device_id_type=MESH,
            )

        def m_wait(self, i, side, d):
            block = self.place(w ^ masks[i], owner_of(side, d))
            pltpu.make_async_copy(block, block, self.m_recv.at[i, slot(side, d)]).wait()

        def r_copy(self, part, side, d):
            block = self.place(w ^ masks[part], owner_of(side, d), part)
            return pltpu.make_async_remote_copy(
                src_ref=block,
                dst_ref=block,
                send_sem=self.r_send.at[part, slot(side, d)],
                recv_sem=self.r_recv.at[part, slot(side, d)],
                device_id=to_wide(masks[1 - part]),
                device_id_type=MESH,
            )

        def r_wait(self, part, side, d):
            block = self.place(w ^ 6, owner_of(side, d), part)
            pltpu.make_async_copy(block, block, self.r_recv.at[part, slot(side, d)]).wait()

        def c_copy(self, chip, side, d):
            block = self.place(w ^ (2 * chip), owner_of(side, d))
            return pltpu.make_async_remote_copy(
                src_ref=self.x_ref if d == 0 and chip == 0 else block,
                dst_ref=block,
                send_sem=self.c_send.at[chip, slot(side, d)],
                recv_sem=self.c_recv.at[chip, slot(side, d)],
                device_id=to_wide(1),
                device_id_type=MESH,
            )

        def c_wait(self, chip, side, d):
            block = self.place((w ^ 1) ^ (2 * chip), owner_of(side, d))
            pltpu.make_async_copy(block, block, self.c_recv.at[chip, slot(side, d)]).wait()

        def send_from_here(self, side, d):
            if d > 0:
                self.z_wait(side, d)
            if 0 < d < narrow - 1:
                pl.when(can_pass(side, d + 1))(lambda: self.z_copy(side, d + 1).start())
            for i in range(len(masks)):
                self.m_copy(i, side, d).start()
            self.c_copy(0, side, d).start()

        def send_on(self, side, d):
            for i in range(len(masks)):
                self.m_wait(i, side, d)
                if relay:
                    self.r_copy(i, side, d).start()
                self.c_copy(masks[i] // 2, side, d).start()

        def send_last(self, side, d):
            self.r_wait(0, side, d)
            self.r_wait(1, side, d)
            self.c_copy(3, side, d).start()

        def step(self, t):
            if t == 0:
                self.own.start()
                for side in (0, 1):
                    pl.when(can_pass(side, 1))(lambda side=side: self.z_copy(side, 1).start())
            if 0 <= t < narrow:
                at_distance(t, self.send_from_here)
            if 0 <= t - 1 < narrow:
                at_distance(t - 1, self.send_on)
            if relay and 0 <= t - 2 < narrow:
                at_distance(t - 2, self.send_last)

        def finish(self, side, d):
            for i in range(len(masks)):
                self.m_copy(i, side, d).wait_send()
                if relay:
                    self.r_copy(i, side, d).wait_send()
            for chip in range(chips):
                self.c_copy(chip, side, d).wait_send()
                self.c_wait(chip, side, d)

        def end(self):
            self.own.wait()
            for side in (0, 1):
                for d in range(1, narrow):
                    pl.when(can_pass(side, d))(
                        lambda side=side, d=d: self.z_copy(side, d).wait_send()
                    )
            for d in range(narrow):
                at_distance(d, self.finish)

    depth = cut_ref.shape[1]

    def rows_of(owner):
        return cut_all.at[pl.ds(pl.multiple_of(owner * depth, depth), depth), :]

    def cut_copy(step):
        other = lax.rem(n + step, narrow)
        return pltpu.make_async_remote_copy(
            src_ref=cut_ref.at[other],
            dst_ref=rows_of(n),
            send_sem=x_send.at[step],
            recv_sem=x_recv.at[step],
            device_id=to_narrow(other),
            device_id_type=MESH,
        )

    def cut_wait(step):
        block = rows_of(lax.rem(n + narrow - step, narrow))
        pltpu.make_async_copy(block, block, x_recv.at[step]).wait()

    flows = [Flow(0, qkv_ref, qkv_all), Flow(1, out_w_ref, out_all)]
    own_cut = pltpu.make_async_copy(cut_ref.at[n], rows_of(n), own_sem.at[2])
    own_cut.start()
    last = narrow + 2
    for t in range(last + lag):
        if t < last:
            flows[0].step(t)
        if t == min(2, narrow - 1):
            for step in range(1, narrow):
                cut_copy(step).start()
        if t >= lag:
            flows[1].step(t - lag)
    for flow in flows:
        flow.end()
    own_cut.wait()
    for step in range(1, narrow):
        cut_copy(step).wait_send()
        cut_wait(step)


def gather_weights(qkv, out, cut):
    wide, narrow = lax.axis_size("wide"), lax.axis_size("narrow")
    slots = 2 * narrow - 1
    masks = 2 if wide == 8 else wide // 2 - 1
    dma = pltpu.SemaphoreType.DMA
    hbm = pl.BlockSpec(memory_space=pl.ANY)
    every = wide * narrow
    return pl.pallas_call(
        functools.partial(gather_kernel, wide, narrow, 3),
        out_shape=(
            jax.ShapeDtypeStruct((every * qkv.shape[0], qkv.shape[1]), BF16),
            jax.ShapeDtypeStruct((every * out.shape[0], out.shape[1]), BF16),
            jax.ShapeDtypeStruct((narrow * cut.shape[1], cut.shape[2]), BF16),
        ),
        in_specs=[hbm, hbm, hbm],
        out_specs=(hbm, hbm, hbm),
        scratch_shapes=[
            dma((3,)),
            dma((narrow,)),
            dma((narrow,)),
            dma((2, 2, narrow)),
            dma((2, 2, narrow)),
            dma((2, masks, slots)),
            dma((2, masks, slots)),
            dma((2, 2, slots)),
            dma((2, 2, slots)),
            dma((2, wide // 2, slots)),
            dma((2, wide // 2, slots)),
        ],
        compiler_params=pltpu.CompilerParams(collective_id=0, has_side_effects=True),
        cost_estimate=pl.CostEstimate(flops=0, bytes_accessed=300 << 20, transcendentals=0),
    )(qkv, out, cut)


def feed_kernel(
    narrow, x_ref, cot_ref, gate_up_ref, down_ref,
    group_ref, hidden_out, grad_out, low_out, grad_x_ref,
    gate_up, down, cot, hidden, grads, low, came,
    load_sem, x_send, x_recv, out_sem, g_send, g_recv,
):
    w, n = lax.axis_index("wide"), lax.axis_index("narrow")
    rows, width = x_ref.shape
    own = down.shape[0]
    tile = 256
    tiles = own // tile
    wtiles = width // tile

    def to_narrow(other):
        return {"wide": w, "narrow": other}

    loads = [
        pltpu.make_async_copy(gate_up_ref, gate_up, load_sem.at[0]),
        pltpu.make_async_copy(down_ref, down, load_sem.at[1]),
        pltpu.make_async_copy(cot_ref, cot, load_sem.at[2]),
        pltpu.make_async_copy(x_ref, group_ref.at[n], load_sem.at[3]),
    ]
    for load in loads:
        load.start()

    barrier = pltpu.get_barrier_semaphore()
    for step in range(1, narrow):
        pl.semaphore_signal(
            barrier, inc=1, device_id=to_narrow(lax.rem(n + step, narrow)), device_id_type=MESH
        )
    pl.semaphore_wait(barrier, narrow - 1)

    def owner_of(side, d):
        return n - d if side == 0 else n + d

    def valid(side, d):
        return n - d >= 0 if side == 0 else (n + d < narrow) & (d > 0)

    def passes(side, d):
        if side == 0:
            return (n - d >= 0) & (n < narrow - 1)
        return (n + d < narrow) & (n > 0)

    def x_copy(side, d):
        block = group_ref.at[owner_of(side, d)]
        return pltpu.make_async_remote_copy(
            src_ref=block,
            dst_ref=block,
            send_sem=x_send.at[side, d],
            recv_sem=x_recv.at[side, d + 1],
            device_id=to_narrow(n + 1 if side == 0 else n - 1),
            device_id_type=MESH,
        )

    def x_wait(side, d):
        block = group_ref.at[owner_of(side, d)]
        pltpu.make_async_copy(block, block, x_recv.at[side, d]).wait()

    def out_copies(at, block):
        return [
            pltpu.make_async_copy(hidden.at[at], hidden_out.at[block], out_sem.at[at, 0]),
            pltpu.make_async_copy(grads.at[at], grad_out.at[block], out_sem.at[at, 1]),
            pltpu.make_async_copy(low.at[at], low_out.at[block], out_sem.at[at, 2]),
        ]

    def g_copy(block):
        return pltpu.make_async_remote_copy(
            src_ref=cot.at[block],
            dst_ref=came.at[n],
            send_sem=g_send.at[block],
            recv_sem=g_recv.at[n],
            device_id=to_narrow(block),
            device_id_type=MESH,
        )

    def compute(side, d):
        block = n - d + 2 * d * side
        before = 1 + jnp.minimum(n, d - 1) + jnp.minimum(narrow - 1 - n, d - 1)
        before = jnp.where(d == 0, 0, before + jnp.where((side == 1) & (n - d >= 0), 1, 0))
        at = lax.rem(before, 2)

        @pl.when(before >= 2)
        def _():
            for copy in out_copies(at, block):
                copy.wait()

        def first(f, carry):
            columns = pl.ds(pl.multiple_of(f * tile, tile), tile)
            other = pl.ds(pl.multiple_of(own + f * tile, tile), tile)
            x = group_ref[block]
            gate = dot(x, gate_up[:, columns], NN)
            up = dot(x, gate_up[:, other], NN)
            grad = dot(cot[block], down[columns, :], NT)
            sig = 1.0 / (1.0 + jnp.exp(-gate))
            silu = gate * sig
            hidden[at, :, columns] = (silu * up).astype(BF16)
            grads[at, :, columns] = (grad * up * (sig + silu * (1.0 - sig))).astype(BF16)
            grads[at, :, other] = (grad * silu).astype(BF16)
            return carry

        lax.fori_loop(0, tiles, first, 0)

        def second(f, carry):
            columns = pl.ds(pl.multiple_of(f * tile, tile), tile)
            cot[block, :, columns] = dot(grads[at], gate_up[columns, :], NT, BF16)
            low[at, :, columns] = dot(hidden[at], down[:, columns], NN, BF16)
            return carry

        lax.fori_loop(0, wtiles, second, 0)
        for copy in out_copies(at, block):
            copy.start()
        pl.when(block != n)(lambda: g_copy(block).start())

    def distance(d, carry):
        for side in (0, 1):

            @pl.when(valid(side, d) & (d > 0))
            def _():
                x_wait(side, d)

            @pl.when(passes(side, d))
            def _():
                x_copy(side, d).start()

        @pl.when(d == 0)
        def _():
            for load in loads[:3]:
                load.wait()

        def one(side, carry):
            ok = jnp.where(side == 0, n - d, jnp.where(d > 0, narrow - 1 - n - d, -1)) >= 0
            pl.when(ok)(lambda: compute(side, d))
            return carry

        lax.fori_loop(0, 2, one, 0)
        return carry

    loads[3].wait()
    lax.fori_loop(0, narrow, distance, 0)

    for at in range(min(2, narrow)):
        for copy in out_copies(at, n):
            copy.wait()
    for side in (0, 1):
        for d in range(narrow - 1):
            pl.when(passes(side, d))(lambda side=side, d=d: x_copy(side, d).wait_send())
    for step in range(1, narrow):
        other = lax.rem(n + step, narrow)
        g_copy(other).wait_send()
        block = came.at[other]
        pltpu.make_async_copy(block, block, g_recv.at[other]).wait()

    def add(r, carry):
        part = pl.ds(pl.multiple_of(r * 16, 16), 16)
        total = cot[n, part, :].astype(F32)
        for step in range(1, narrow):
            total = total + came[lax.rem(n + step, narrow), part, :].astype(F32)
        grad_x_ref[part, :] = total
        return carry

    lax.fori_loop(0, rows // 16, add, 0)


def feed(x, cot_group, gate_up, down):
    narrow = lax.axis_size("narrow")
    rows, width = x.shape
    own = down.shape[0]
    dma = pltpu.SemaphoreType.DMA
    hbm = pl.BlockSpec(memory_space=pl.ANY)
    vmem = pl.BlockSpec(memory_space=pltpu.VMEM)
    group, hidden, grads, low, grad_x = pl.pallas_call(
        functools.partial(feed_kernel, narrow),
        out_shape=(
            jax.ShapeDtypeStruct((narrow, rows, width), BF16),
            jax.ShapeDtypeStruct((narrow, rows, own), BF16),
            jax.ShapeDtypeStruct((narrow, rows, 2 * own), BF16),
            jax.ShapeDtypeStruct((narrow, rows, width), BF16),
            jax.ShapeDtypeStruct((rows, width), F32),
        ),
        in_specs=[vmem, hbm, hbm, hbm],
        out_specs=(vmem, hbm, hbm, hbm, vmem),
        scratch_shapes=[
            pltpu.VMEM((width, 2 * own), BF16),
            pltpu.VMEM((own, width), BF16),
            pltpu.VMEM((narrow, rows, width), BF16),
            pltpu.VMEM((2, rows, own), BF16),
            pltpu.VMEM((2, rows, 2 * own), BF16),
            pltpu.VMEM((2, rows, width), BF16),
            pltpu.VMEM((narrow, rows, width), BF16),
            dma((4,)),
            dma((2, narrow + 1)),
            dma((2, narrow + 1)),
            dma((2, 3)),
            dma((narrow,)),
            dma((narrow,)),
        ],
        compiler_params=pltpu.CompilerParams(
            collective_id=1, has_side_effects=True, vmem_limit_bytes=58 << 20
        ),
        cost_estimate=pl.CostEstimate(
            flops=12 * narrow * rows * width * own, bytes_accessed=300 << 20, transcendentals=0
        ),
    )(x, cot_group.reshape(narrow, rows, width), gate_up, down)
    flat = lambda y: y.reshape((-1,) + y.shape[2:])
    return flat(group), flat(hidden), flat(grads), flat(low), grad_x


def per_device(tokens, lengths, gain_attn, w_qkv, w_out, gain_mlp, w_gateup, w_down, cotangent):
    rows, width = tokens.shape[1:]
    wide, narrow = lax.axis_size("wide"), lax.axis_size("narrow")
    pack_rows = rows * wide
    query_width, key_width = HEADS * HEAD_DIM, KV_HEADS * HEAD_DIM
    groups = HEADS // wide
    copies = wide // KV_HEADS
    own_ff = FF // narrow
    first, positions = places(lengths[0], pack_rows)
    cos_all, sin_all = rotary(positions.astype(F32), HALF)
    first_row = lax.axis_index("wide") * rows
    cos = lax.dynamic_slice_in_dim(cos_all, first_row, rows, 1)
    sin = lax.dynamic_slice_in_dim(sin_all, first_row, rows, 1)
    cos_all = cos_all.reshape(HALF, wide, rows).transpose(1, 0, 2)
    sin_all = sin_all.reshape(HALF, wide, rows).transpose(1, 0, 2)
    start = first.reshape(wide, 1, rows)

    gains = jnp.stack([gain_attn, gain_mlp], -1)
    with_gains = jnp.concatenate([w_qkv, jnp.pad(gains, ((0, 0), (0, 126)))], -1)
    shard = w_gateup.shape[0]
    gateup_cut = w_gateup.reshape(shard, 2, wide, narrow, -1).transpose(3, 0, 1, 2, 4)
    qkv_gained, out_whole, gateup_rows = gather_weights(
        with_gains, w_out, gateup_cut.reshape(narrow, shard, 2 * own_ff)
    )
    qkv_whole = qkv_gained[:, : w_qkv.shape[1]]
    gain_one = qkv_gained[:, w_qkv.shape[1]].astype(F32)
    gain_two = qkv_gained[:, w_qkv.shape[1] + 1].astype(F32)
    gateup_own = gather(gateup_rows, "wide")
    down_own = gather(w_down, "wide")
    cot_group = shift_gather(cotangent[0])

    inputs = tokens[0].astype(F32)
    scale_one = lax.rsqrt(jnp.mean(inputs * inputs, -1, keepdims=True) + EPS)
    unit_one = inputs * scale_one
    normed_one = (unit_one * gain_one).astype(BF16)
    projected = dot(qkv_whole, normed_one, (((0,), (1,)), ((), ())))
    turning = projected[: query_width + key_width].reshape(HEADS + KV_HEADS, 2, HALF, rows)
    front, back = turning[:, 0], turning[:, 1]
    turned = jnp.stack([front * cos - back * sin, back * cos + front * sin], 1)
    queries = (turned[:HEADS] * SCORE_SCALE).astype(BF16).reshape(wide, groups * HEAD_DIM, rows)
    keys = turned[HEADS:].astype(BF16).reshape(KV_HEADS, HEAD_DIM, rows)
    values = projected[query_width + key_width :].astype(BF16).reshape(KV_HEADS, HEAD_DIM, rows)
    keys_values = jnp.repeat(jnp.concatenate([keys, values], 1), copies, 0)
    heads = exchange(jnp.concatenate([queries, keys_values], 1), "wide")
    attended_heads, attended_full, log_total = attend(heads, start, groups)
    attended_low = exchange(attended_heads, "wide").reshape(query_width, rows)
    middle = inputs + dot(attended_low, out_whole, TN)
    scale_two = lax.rsqrt(jnp.mean(middle * middle, -1, keepdims=True) + EPS)
    unit_two = middle * scale_two
    normed_two = (unit_two * gain_two).astype(BF16)

    normed_group, hidden, grad_gate_up, low_part, grad_normed_two = feed(
        normed_two, cot_group, gateup_own, down_own
    )
    layer_out = (middle + scatter_sum(low_part, "narrow")).astype(BF16)[None]
    chips = wide // 2

    def of_core(left, right, dims, core):
        free = 1 - dims[0][0][0]
        size = left.shape[free] // wide
        cuts = [lax.slice_in_dim(left, w * size, (w + 1) * size, axis=free) for w in range(wide)]
        part = jnp.concatenate(
            [jnp.where(core == 0, cuts[w], cuts[w + 1]) for w in range(0, wide, 2)], free
        )
        return dot(part, right, dims, BF16).reshape(chips, size, -1)

    grad_gateup = scatter_sum(dot(normed_group, grad_gate_up, TN, BF16), "wide")
    grad_gateup = shift_exchange(grad_gateup.reshape(narrow, shard, 2 * own_ff))
    grad_down = scatter_sum(dot(hidden, cot_group, TN, BF16), "wide").astype(F32)
    grad_gateup = (
        grad_gateup.reshape(narrow, shard, 2, wide, -1)
        .transpose(1, 2, 3, 0, 4)
        .reshape(shard, 2 * FF)
        .astype(F32)
    )

    part_gain_two = jnp.sum(grad_normed_two * unit_two, 0)
    grad_middle = cotangent[0].astype(F32) + norm_back(
        grad_normed_two * gain_two, unit_two, scale_two
    )
    grad_branch = grad_middle.astype(BF16)
    grad_wout = shift_scatter_sum(
        wide_scatter_sum(lambda core: of_core(attended_low, grad_branch, NN, core))
    )
    grad_attended = dot(out_whole, grad_branch, NT, BF16).reshape(wide, groups * HEAD_DIM, rows)
    grad_heads = attend_back(
        heads, exchange(grad_attended, "wide"), attended_full, log_total, start, cos_all, sin_all,
        groups,
    )
    grad_heads = exchange(grad_heads, "wide")
    grad_queries = grad_heads[:, : groups * HEAD_DIM].reshape(query_width, rows)
    grad_keys_values = (
        grad_heads[:, groups * HEAD_DIM :]
        .reshape(KV_HEADS, copies, 2, HEAD_DIM, rows)
        .astype(F32)
        .sum(1)
        .astype(BF16)
    )
    grad_projected = jnp.concatenate(
        [
            grad_queries,
            grad_keys_values[:, 0].reshape(key_width, rows),
            grad_keys_values[:, 1].reshape(key_width, rows),
        ],
        0,
    )
    grad_normed_one = dot(grad_projected, qkv_whole, (((0,), (1,)), ((), ())))
    part_gain_one = jnp.sum(grad_normed_one * unit_one, 0)
    part_gains = jnp.stack([part_gain_one, part_gain_two], 0).reshape(2, wide, narrow, shard)
    part_gains = jnp.sum(exchange(part_gains.transpose(1, 2, 0, 3), "wide"), 0)
    grad_gains = jnp.sum(exchange(part_gains, "narrow"), 0)
    back_dims = (((0,), (1,)), ((), ()))
    grad_qkv = shift_scatter_sum(
        wide_scatter_sum(lambda core: of_core(normed_one, grad_projected, back_dims, core))
    )
    grad_inputs = grad_middle + norm_back(grad_normed_one * gain_one, unit_one, scale_one)
    grad_tokens = grad_inputs.astype(BF16)[None]
    return (
        layer_out,
        grad_tokens,
        grad_gains[0],
        grad_qkv,
        grad_wout,
        grad_gains[1],
        grad_gateup,
        grad_down,
    )


def solution(mesh):
    rows, packs = P("narrow", "wide", None), P("narrow", None)
    weight, gain = P(BOTH, None), P(BOTH)
    return jax.shard_map(
        per_device,
        mesh=mesh,
        in_specs=(rows, packs, gain, weight, weight, gain, weight, weight, rows),
        out_specs=(rows, rows, gain, weight, weight, gain, weight, weight),
        check_vma=False,
    )
```

```python
import functools
import math

import jax
import jax.numpy as jnp
from jax import lax
from jax.experimental import pallas as pl
from jax.experimental.pallas import tpu as pltpu
from jax.sharding import PartitionSpec as P

FF = 8192
HEADS = 32
KV_HEADS = 8
HEAD_DIM = 64
HALF = HEAD_DIM // 2
EPS = 1e-05
NEGATIVE = -1e30
SCORE_SCALE = 1.0 / math.sqrt(HEAD_DIM)
BOTH = ("wide", "narrow")
F32 = jnp.float32
BF16 = jnp.bfloat16
NN = (((1,), (0,)), ((), ()))
NT = (((1,), (1,)), ((), ()))
TN = (((0,), (0,)), ((), ()))


def dot(left, right, dims, kind=F32):
    return lax.dot_general(left, right, dims, preferred_element_type=F32).astype(kind)


def places(lengths_row, total_rows):
    seq_ends = jnp.cumsum(lengths_row)
    starts = seq_ends - lengths_row
    row_index = jnp.arange(total_rows, dtype=jnp.int32)
    segments = jnp.sum((row_index[:, None] >= seq_ends[None, :]).astype(jnp.int32), -1)
    slot_index = jnp.arange(lengths_row.shape[0], dtype=jnp.int32)
    owned = segments[:, None] == slot_index[None, :]
    first = jnp.sum(jnp.where(owned, starts[None, :], 0), -1)
    return first, row_index - first


def rotary(positions, half_width):
    channel = jnp.arange(half_width, dtype=jnp.float32)
    inverse_rate = jnp.power(500000.0, -channel / half_width)
    wavelength = 2.0 * math.pi / inverse_rate
    smooth = (8192.0 / wavelength - 1.0) / 3.0
    blended = (1.0 - smooth) * inverse_rate / 32.0 + smooth * inverse_rate
    frequency = jnp.where(
        wavelength < 2048.0,
        inverse_rate,
        jnp.where(wavelength > 8192.0, inverse_rate / 32.0, blended),
    )
    angles = frequency[:, None] * positions[None, :]
    return jnp.cos(angles), jnp.sin(angles)


def norm_back(grad_unit, unit_rows, row_scale):
    return row_scale * (grad_unit - unit_rows * jnp.mean(grad_unit * unit_rows, -1, keepdims=True))


MESH = pl.DeviceIdType.MESH


class Flow:
    def __init__(self, wide, narrow, x_ref, out_ref, sems):
        self.wide, self.narrow, self.x_ref, self.out_ref = wide, narrow, x_ref, out_ref
        self.w, self.n = lax.axis_index("wide"), lax.axis_index("narrow")
        (self.own_sem, self.z_send, self.z_recv, self.m_send, self.m_recv,
         self.r_send, self.r_recv, self.c_send, self.c_recv) = sems
        self.relay = wide == 8
        self.masks = [2, 4] if self.relay else list(range(2, wide, 2))
        self.last = narrow + 2

    def to_wide(self, mask):
        return {"wide": self.w ^ mask, "narrow": self.n}

    def owner_of(self, side, d):
        return self.n - d if side == 0 else self.n + d

    def valid(self, side, d):
        return self.n - d >= 0 if side == 0 else self.n + d < self.narrow

    def can_pass(self, side, d):
        if side == 0:
            return (self.n - (d - 1) >= 0) & (self.n < self.narrow - 1)
        return (self.n + (d - 1) < self.narrow) & (self.n > 0)

    def slot(self, side, d):
        return d - 1 + side * (self.narrow - 1) if d else 2 * (self.narrow - 1)

    def at_distance(self, d, action):
        if d == 0:
            action(0, 0)
            return
        for side in (0, 1):
            pl.when(self.valid(side, d))(functools.partial(action, side, d))

    def place(self, owner_w, owner_n, part=None):
        depth = self.x_ref.shape[0]
        half = depth // 2
        at = (owner_w * self.narrow + owner_n) * depth
        if part is None:
            return self.out_ref.at[pl.ds(pl.multiple_of(at, depth), depth), :]
        return self.out_ref.at[pl.ds(pl.multiple_of(at + part * half, half), half), :]

    def own_copy(self):
        return pltpu.make_async_copy(self.x_ref, self.place(self.w, self.n), self.own_sem)

    def z_copy(self, side, d):
        block = self.place(self.w, self.owner_of(side, d - 1))
        return pltpu.make_async_remote_copy(
            src_ref=self.x_ref if d == 1 else block,
            dst_ref=block,
            send_sem=self.z_send.at[side, d],
            recv_sem=self.z_recv.at[side, d],
            device_id={"wide": self.w, "narrow": self.n + 1 if side == 0 else self.n - 1},
            device_id_type=MESH,
        )

    def z_wait(self, side, d):
        block = self.place(self.w, self.owner_of(side, d))
        pltpu.make_async_copy(block, block, self.z_recv.at[side, d]).wait()

    def m_copy(self, i, side, d):
        block = self.place(self.w, self.owner_of(side, d))
        return pltpu.make_async_remote_copy(
            src_ref=self.x_ref if d == 0 else block,
            dst_ref=block,
            send_sem=self.m_send.at[i, self.slot(side, d)],
            recv_sem=self.m_recv.at[i, self.slot(side, d)],
            device_id=self.to_wide(self.masks[i]),
            device_id_type=MESH,
        )

    def m_wait(self, i, side, d):
        block = self.place(self.w ^ self.masks[i], self.owner_of(side, d))
        pltpu.make_async_copy(block, block, self.m_recv.at[i, self.slot(side, d)]).wait()

    def r_copy(self, part, side, d):
        block = self.place(self.w ^ self.masks[part], self.owner_of(side, d), part)
        return pltpu.make_async_remote_copy(
            src_ref=block,
            dst_ref=block,
            send_sem=self.r_send.at[part, self.slot(side, d)],
            recv_sem=self.r_recv.at[part, self.slot(side, d)],
            device_id=self.to_wide(self.masks[1 - part]),
            device_id_type=MESH,
        )

    def r_wait(self, part, side, d):
        block = self.place(self.w ^ 6, self.owner_of(side, d), part)
        pltpu.make_async_copy(block, block, self.r_recv.at[part, self.slot(side, d)]).wait()

    def c_copy(self, chip, side, d):
        block = self.place(self.w ^ (2 * chip), self.owner_of(side, d))
        return pltpu.make_async_remote_copy(
            src_ref=self.x_ref if d == 0 and chip == 0 else block,
            dst_ref=block,
            send_sem=self.c_send.at[chip, self.slot(side, d)],
            recv_sem=self.c_recv.at[chip, self.slot(side, d)],
            device_id=self.to_wide(1),
            device_id_type=MESH,
        )

    def c_wait(self, chip, side, d):
        block = self.place((self.w ^ 1) ^ (2 * chip), self.owner_of(side, d))
        pltpu.make_async_copy(block, block, self.c_recv.at[chip, self.slot(side, d)]).wait()

    def send_from_here(self, side, d):
        if d > 0:
            self.z_wait(side, d)
        if 0 < d < self.narrow - 1:
            pl.when(self.can_pass(side, d + 1))(lambda: self.z_copy(side, d + 1).start())
        for i in range(len(self.masks)):
            self.m_copy(i, side, d).start()
        self.c_copy(0, side, d).start()

    def send_on(self, side, d):
        for i in range(len(self.masks)):
            self.m_wait(i, side, d)
            if self.relay:
                self.r_copy(i, side, d).start()
            self.c_copy(self.masks[i] // 2, side, d).start()

    def send_last(self, side, d):
        self.r_wait(0, side, d)
        self.r_wait(1, side, d)
        self.c_copy(3, side, d).start()

    def step(self, t):
        if t == 0:
            self.own_copy().start()
            for side in (0, 1):
                pl.when(self.can_pass(side, 1))(lambda side=side: self.z_copy(side, 1).start())
        if 0 <= t < self.narrow:
            self.at_distance(t, self.send_from_here)
        if 0 <= t - 1 < self.narrow:
            self.at_distance(t - 1, self.send_on)
        if self.relay and 0 <= t - 2 < self.narrow:
            self.at_distance(t - 2, self.send_last)

    def finish(self, side, d):
        for i in range(len(self.masks)):
            self.m_copy(i, side, d).wait_send()
            if self.relay:
                self.r_copy(i, side, d).wait_send()
        for chip in range(self.wide // 2):
            self.c_copy(chip, side, d).wait_send()
            self.c_wait(chip, side, d)

    def end(self):
        self.own_copy().wait()
        for side in (0, 1):
            for d in range(1, self.narrow):
                pl.when(self.can_pass(side, d))(
                    lambda side=side, d=d: self.z_copy(side, d).wait_send()
                )
        for d in range(self.narrow):
            self.at_distance(d, self.finish)


class Line:
    def __init__(self, narrow, x_ref, out_ref, sems):
        self.narrow, self.x_ref, self.out_ref = narrow, x_ref, out_ref
        self.w, self.n = lax.axis_index("wide"), lax.axis_index("narrow")
        self.own_sem, self.send, self.recv = sems

    def owner_of(self, side, d):
        return self.n - d if side == 0 else self.n + d

    def valid(self, side, d):
        return self.n - d >= 0 if side == 0 else self.n + d < self.narrow

    def can_pass(self, side, d):
        if side == 0:
            return (self.n - (d - 1) >= 0) & (self.n < self.narrow - 1)
        return (self.n + (d - 1) < self.narrow) & (self.n > 0)

    def own_copy(self):
        return pltpu.make_async_copy(self.x_ref, self.out_ref.at[self.n], self.own_sem)

    def copy(self, side, d):
        block = self.out_ref.at[self.owner_of(side, d - 1)]
        return pltpu.make_async_remote_copy(
            src_ref=self.x_ref if d == 1 else block,
            dst_ref=block,
            send_sem=self.send.at[side, d],
            recv_sem=self.recv.at[side, d],
            device_id={"wide": self.w, "narrow": self.n + 1 if side == 0 else self.n - 1},
            device_id_type=MESH,
        )

    def pass_on(self, side, d):
        arrive(self.out_ref.at[self.owner_of(side, d)], self.recv.at[side, d])
        if d < self.narrow - 1:
            pl.when(self.can_pass(side, d + 1))(lambda: self.copy(side, d + 1).start())

    def step(self, t):
        if t == 0:
            self.own_copy().start()
        for side in (0, 1):
            if t == 0:
                pl.when(self.can_pass(side, 1))(lambda side=side: self.copy(side, 1).start())
            else:
                pl.when(self.valid(side, t))(lambda side=side: self.pass_on(side, t))

    def end(self):
        self.own_copy().wait()
        for side in (0, 1):
            for d in range(1, self.narrow):
                pl.when(self.can_pass(side, d))(lambda side=side, d=d: self.copy(side, d).wait_send())


def flow_sems(wide, narrow):
    slots = 2 * narrow - 1
    masks = 2 if wide == 8 else wide // 2 - 1
    dma = pltpu.SemaphoreType.DMA
    return [
        dma(()),
        dma((2, narrow)),
        dma((2, narrow)),
        dma((masks, slots)),
        dma((masks, slots)),
        dma((2, slots)),
        dma((2, slots)),
        dma((wide // 2, slots)),
        dma((wide // 2, slots)),
    ]


def greet(wide, narrow):
    w, n = lax.axis_index("wide"), lax.axis_index("narrow")
    barrier = pltpu.get_barrier_semaphore()
    for mask in range(1, wide):
        pl.semaphore_signal(
            barrier, inc=1, device_id={"wide": w ^ mask, "narrow": n}, device_id_type=MESH
        )
    for step in range(1, narrow):
        other = lax.rem(n + step, narrow)
        pl.semaphore_signal(
            barrier, inc=1, device_id={"wide": w, "narrow": other}, device_id_type=MESH
        )
    pl.semaphore_wait(barrier, wide + narrow - 2)


def to_owner(source, target, send_sem, recv_sem, mask):
    w, n = lax.axis_index("wide"), lax.axis_index("narrow")
    return pltpu.make_async_remote_copy(
        src_ref=source,
        dst_ref=target,
        send_sem=send_sem,
        recv_sem=recv_sem,
        device_id={"wide": w ^ mask, "narrow": n},
        device_id_type=MESH,
    )


def to_block(source, target, send_sem, recv_sem, owner):
    n = lax.axis_index("narrow")
    return pltpu.make_async_remote_copy(
        src_ref=source,
        dst_ref=target,
        send_sem=send_sem,
        recv_sem=recv_sem,
        device_id={"wide": owner, "narrow": n},
        device_id_type=MESH,
    )


def arrive(block, sem):
    pltpu.make_async_copy(block, block, sem).wait()


def attend_kernel(
    wide, narrow, groups, start_ref, mine_ref, w_ref, c_ref,
    x_ref, low_ref, full_ref, log_ref, w_all, c_all,
    keys, top, total, acc, done, own_sem, in_send, in_recv, out_send, out_recv,
    line_own, line_send, line_recv, *sems,
):
    me = lax.axis_index("wide")
    blocks, _, rows = x_ref.shape
    width = groups * HEAD_DIM
    own_in = pltpu.make_async_copy(mine_ref.at[me], x_ref.at[me], own_sem.at[0])
    own_in.start()
    greet(wide, narrow)
    for mask in range(1, wide):
        to_owner(
            mine_ref.at[me ^ mask], x_ref.at[me], in_send.at[mask], in_recv.at[me], mask
        ).start()
    flow = Flow(wide, narrow, w_ref, w_all, sems)
    line = Line(narrow, c_ref, c_all, (line_own, line_send, line_recv))
    flow.step(0)
    line.step(0)
    spread = {}
    for t in range(1, flow.last):
        spread.setdefault(min(blocks, blocks // 2 - 1 + t), []).append(functools.partial(flow.step, t))
    for t in range(1, narrow):
        spread.setdefault(min(blocks, blocks // 2 + 2 * t - 1), []).append(functools.partial(line.step, t))
    key_row = lax.broadcasted_iota(jnp.int32, (rows, rows), 0)
    column = lax.broadcasted_iota(jnp.int32, (rows, rows), 1)
    own_in.wait()

    def block(i, carry):
        pl.when(i != me)(lambda: arrive(x_ref.at[i], in_recv.at[i]))
        for at, actions in spread.items():
            if at < blocks:

                @pl.when(i == at)
                def _():
                    for action in actions:
                        action()

        keys[i] = x_ref[i, width : width + HEAD_DIM, :].T
        top[...] = jnp.full_like(top, NEGATIVE)
        total[...] = jnp.zeros_like(total)
        acc[...] = jnp.zeros_like(acc)
        start = start_ref[i]
        query_row = i * rows + column

        def step(j, carry):
            key_index = key_row + j * rows
            allowed = (key_index <= query_row) & (key_index >= start)
            key_block = keys[j]
            value_block = x_ref[j, width + HEAD_DIM :, :]
            for h in range(groups):
                own = pl.ds(h * HEAD_DIM, HEAD_DIM)
                scores = dot(key_block, x_ref[i, own, :], NN)
                scores = jnp.where(allowed, scores, NEGATIVE)
                old = top[h : h + 1, :]
                new = jnp.maximum(old, jnp.max(scores, 0, keepdims=True))
                shrink = jnp.exp(old - new)
                prob = jnp.exp(scores - new)
                top[h : h + 1, :] = new
                total[h : h + 1, :] = total[h : h + 1, :] * shrink + jnp.sum(prob, 0, keepdims=True)
                acc[own, :] = acc[own, :] * shrink + dot(value_block, prob.astype(BF16), NN)
            return carry

        lax.fori_loop(0, i + 1, step, 0)
        log_ref[i] = top[...] + jnp.log(total[...])
        for h in range(groups):
            own = pl.ds(h * HEAD_DIM, HEAD_DIM)
            result = acc[own, :] / total[h : h + 1, :]
            full_ref[i, own, :] = result
            done[i, own, :] = result.astype(BF16)

        @pl.when(i != me)
        def _():
            to_block(done.at[i], low_ref.at[me], out_send.at[i], out_recv.at[me], i).start()

        return carry

    lax.fori_loop(0, blocks, block, 0)
    low_ref[me] = done[me]
    for action in spread.get(blocks, []):
        action()
    flow.end()
    line.end()
    for mask in range(1, wide):
        to_owner(
            mine_ref.at[me ^ mask], x_ref.at[me], in_send.at[mask], in_recv.at[me], mask
        ).wait_send()
        other = me ^ mask
        arrive(low_ref.at[other], out_recv.at[other])
        arrive(done.at[other], out_send.at[other])


def attend(mine, start, w_out, cot, groups):
    wide, narrow = lax.axis_size("wide"), lax.axis_size("narrow")
    blocks, features, rows = mine.shape
    width = groups * HEAD_DIM
    dma = pltpu.SemaphoreType.DMA
    hbm = pl.BlockSpec(memory_space=pl.ANY)
    vmem = pl.BlockSpec(memory_space=pltpu.VMEM)
    return pl.pallas_call(
        functools.partial(attend_kernel, wide, narrow, groups),
        out_shape=(
            jax.ShapeDtypeStruct((blocks, features, rows), BF16),
            jax.ShapeDtypeStruct((blocks, width, rows), BF16),
            jax.ShapeDtypeStruct((blocks, width, rows), F32),
            jax.ShapeDtypeStruct((blocks, groups, rows), F32),
            jax.ShapeDtypeStruct((wide * narrow * w_out.shape[0], w_out.shape[1]), BF16),
            jax.ShapeDtypeStruct((narrow,) + cot.shape, BF16),
        ),
        in_specs=[vmem, vmem, hbm, hbm],
        out_specs=(vmem, vmem, vmem, vmem, hbm, hbm),
        scratch_shapes=[
            pltpu.VMEM((blocks, rows, HEAD_DIM), BF16),
            pltpu.VMEM((groups, rows), F32),
            pltpu.VMEM((groups, rows), F32),
            pltpu.VMEM((width, rows), F32),
            pltpu.VMEM((blocks, width, rows), BF16),
            dma((1,)),
            dma((wide,)),
            dma((wide,)),
            dma((wide,)),
            dma((wide,)),
            dma(()),
            dma((2, narrow)),
            dma((2, narrow)),
        ]
        + flow_sems(wide, narrow),
        compiler_params=pltpu.CompilerParams(
            collective_id=3, has_side_effects=True, vmem_limit_bytes=40 << 20
        ),
        cost_estimate=pl.CostEstimate(
            flops=32 * width * (blocks * rows) ** 2,
            bytes_accessed=64 << 20,
            transcendentals=groups * (blocks * rows) ** 2 // 2,
        ),
    )(start, mine, w_out, cot)


def attend_back_kernel(
    wide, narrow, groups, start_ref, x_ref, mine_ref, full_ref, log_ref, cos_ref, sin_ref, part_ref,
    out_ref, came_ref,
    keys, values, acc, acc_keys, acc_values, grad_ref, done, own_sem, in_send, in_recv,
    q_send, q_recv, k_send, k_recv, p_send, p_recv,
):
    me, n = lax.axis_index("wide"), lax.axis_index("narrow")

    def part_copy(step):
        other = lax.rem(n + step, narrow)
        return pltpu.make_async_remote_copy(
            src_ref=part_ref.at[other],
            dst_ref=came_ref.at[step],
            send_sem=p_send.at[step],
            recv_sem=p_recv.at[step],
            device_id={"wide": me, "narrow": other},
            device_id_type=MESH,
        )

    own_part = pltpu.make_async_copy(part_ref.at[n], came_ref.at[0], p_send.at[0])
    blocks, _, rows = x_ref.shape
    width = groups * HEAD_DIM
    own_in = pltpu.make_async_copy(mine_ref.at[me], grad_ref.at[me], own_sem.at[0])
    own_in.start()
    for j in range(blocks):
        keys[j] = x_ref[j, width : width + HEAD_DIM, :].T
        values[j] = x_ref[j, width + HEAD_DIM :, :].T
    acc_keys[...] = jnp.zeros_like(acc_keys)
    acc_values[...] = jnp.zeros_like(acc_values)
    greet(wide, narrow)
    for mask in range(1, wide):
        to_owner(
            mine_ref.at[me ^ mask], grad_ref.at[me], in_send.at[mask], in_recv.at[me], mask
        ).start()
    own_part.start()
    for step in range(1, narrow):
        part_copy(step).start()
    key_row = lax.broadcasted_iota(jnp.int32, (rows, rows), 0)
    column = lax.broadcasted_iota(jnp.int32, (rows, rows), 1)
    own_in.wait()
    of_queries, of_keys = pl.ds(0, width), pl.ds(width, 2 * HEAD_DIM)

    def turn_back(block, cos, sin):
        front, back = block[:HALF, :], block[HALF:, :]
        return (front * cos + back * sin).astype(BF16), (back * cos - front * sin).astype(BF16)

    def block(i, carry):
        pl.when(i != me)(lambda: arrive(grad_ref.at[i], in_recv.at[i]))
        acc[...] = jnp.zeros_like(acc)
        start = start_ref[i]
        query_row = i * rows + column
        deltas = [
            jnp.sum(
                grad_ref[i, pl.ds(h * HEAD_DIM, HEAD_DIM), :].astype(F32)
                * full_ref[i, pl.ds(h * HEAD_DIM, HEAD_DIM), :],
                0,
                keepdims=True,
            )
            for h in range(groups)
        ]

        def step(j, carry):
            key_index = key_row + j * rows
            allowed = (key_index <= query_row) & (key_index >= start)
            key_block = keys[j]
            value_block = values[j]
            key_columns = x_ref[j, width : width + HEAD_DIM, :]
            grad_keys = acc_keys[j]
            grad_values = acc_values[j]
            for h in range(groups):
                own = pl.ds(h * HEAD_DIM, HEAD_DIM)
                query = x_ref[i, own, :]
                grad = grad_ref[i, own, :]
                scores = dot(key_block, query, NN)
                scores = jnp.where(allowed, scores, NEGATIVE)
                prob = jnp.exp(scores - log_ref[i, h : h + 1, :])
                grad_prob = dot(value_block, grad, NN)
                grad_scores = (prob * (grad_prob - deltas[h])).astype(BF16)
                acc[own, :] += dot(key_columns, grad_scores, NN)
                grad_keys = grad_keys + dot(query, grad_scores, NT)
                grad_values = grad_values + dot(grad, prob.astype(BF16), NT)
            acc_keys[j] = grad_keys
            acc_values[j] = grad_values
            return carry

        lax.fori_loop(0, i + 1, step, 0)
        for h in range(groups):
            at = h * HEAD_DIM
            front, back = turn_back(
                acc[pl.ds(at, HEAD_DIM), :] * SCORE_SCALE, cos_ref[i], sin_ref[i]
            )
            done[i, pl.ds(at, HALF), :] = front
            done[i, pl.ds(at + HALF, HALF), :] = back

        @pl.when(i != me)
        def _():
            to_block(
                done.at[i, of_queries], out_ref.at[me, of_queries], q_send.at[i], q_recv.at[me], i
            ).start()

        return carry

    lax.fori_loop(0, blocks, block, 0)

    def last(j, carry):
        front, back = turn_back(acc_keys[j], cos_ref[j], sin_ref[j])
        done[j, pl.ds(width, HALF), :] = front
        done[j, pl.ds(width + HALF, HALF), :] = back
        done[j, pl.ds(width + HEAD_DIM, HEAD_DIM), :] = acc_values[j].astype(BF16)

        @pl.when(j != me)
        def _():
            to_block(
                done.at[j, of_keys], out_ref.at[me, of_keys], k_send.at[j], k_recv.at[me], j
            ).start()

        return carry

    lax.fori_loop(0, blocks, last, 0)
    out_ref[me] = done[me]
    for mask in range(1, wide):
        other = me ^ mask
        arrive(mine_ref.at[other], in_send.at[mask])
        arrive(done.at[other, of_queries], q_send.at[other])
        arrive(done.at[other, of_keys], k_send.at[other])
        arrive(out_ref.at[other, of_queries], q_recv.at[other])
        arrive(out_ref.at[other, of_keys], k_recv.at[other])
    own_part.wait()
    for step in range(1, narrow):
        part_copy(step).wait()


def attend_back(x, mine, full, log_total, start, cos, sin, part, groups):
    wide, narrow = lax.axis_size("wide"), lax.axis_size("narrow")
    blocks, features, rows = x.shape
    width = groups * HEAD_DIM
    dma = pltpu.SemaphoreType.DMA
    hbm = pl.BlockSpec(memory_space=pl.ANY)
    vmem = pl.BlockSpec(memory_space=pltpu.VMEM)
    return pl.pallas_call(
        functools.partial(attend_back_kernel, wide, narrow, groups),
        out_shape=(
            jax.ShapeDtypeStruct(x.shape, BF16),
            jax.ShapeDtypeStruct(part.shape, BF16),
        ),
        in_specs=[vmem] * 7 + [hbm],
        out_specs=(vmem, hbm),
        scratch_shapes=[
            pltpu.VMEM((blocks, rows, HEAD_DIM), BF16),
            pltpu.VMEM((blocks, rows, HEAD_DIM), BF16),
            pltpu.VMEM((width, rows), F32),
            pltpu.VMEM((blocks, HEAD_DIM, rows), F32),
            pltpu.VMEM((blocks, HEAD_DIM, rows), F32),
            pltpu.VMEM((blocks, width, rows), BF16),
            pltpu.VMEM((blocks, features, rows), BF16),
            dma((1,)),
        ]
        + [dma((wide,))] * 6
        + [dma((narrow,))] * 2,
        compiler_params=pltpu.CompilerParams(
            collective_id=4, has_side_effects=True, vmem_limit_bytes=40 << 20
        ),
        cost_estimate=pl.CostEstimate(
            flops=40 * width * (blocks * rows) ** 2,
            bytes_accessed=4 * x.size * 2,
            transcendentals=groups * (blocks * rows) ** 2 // 2,
        ),
    )(start, x, mine, full, log_total, cos, sin, part)


def gather(x, axis):
    return lax.all_gather(x, axis, axis=0, tiled=True)


def scatter_sum(x, axis):
    return lax.psum_scatter(x, axis, scatter_dimension=0, tiled=True)


def shift(x, step):
    n = lax.axis_size("narrow")
    return lax.ppermute(x, "narrow", [(i, (i + step) % n) for i in range(n)])


def pick(x, index, axis):
    return lax.dynamic_index_in_dim(x, index, axis, keepdims=False)


def gather_kernel(wide, narrow, aligned, qkv_ref, cut_ref, qkv_all, cut_all, x_send, x_recv, x_own, *sems):
    w, n = lax.axis_index("wide"), lax.axis_index("narrow")
    greet(wide, narrow)
    flow = Flow(wide, narrow, qkv_ref, qkv_all, sems)
    depth = qkv_ref.shape[0]
    piece = cut_all.shape[1] // (2 * wide)

    def rows_of(owner):
        return cut_all.at[pl.ds(pl.multiple_of(owner * depth, depth), depth), :]

    def pieces(other):
        if not aligned:
            return [(cut_ref.at[other], pl.ds(0, cut_all.shape[1]))]
        return [
            (
                cut_ref.at[:, pl.ds(pl.multiple_of((j * narrow + other) * piece, piece), piece)],
                pl.ds(j * piece, piece),
            )
            for j in range(2 * wide)
        ]

    def target(columns):
        return cut_all.at[pl.ds(pl.multiple_of(n * depth, depth), depth), columns]

    def cut_start(step):
        other = lax.rem(n + step, narrow)
        for source, columns in pieces(other):
            pltpu.make_async_remote_copy(
                src_ref=source,
                dst_ref=target(columns),
                send_sem=x_send.at[step],
                recv_sem=x_recv.at[step],
                device_id={"wide": w, "narrow": other},
                device_id_type=MESH,
            ).start()

    for t in range(flow.last):
        flow.step(t)
        if t == min(1, narrow - 1):
            for source, columns in pieces(n):
                pltpu.make_async_copy(source, target(columns), x_own).start()
            for step in range(1, narrow):
                cut_start(step)
    flow.end()
    own = rows_of(n)
    pltpu.make_async_copy(own, own, x_own).wait()
    for step in range(1, narrow):
        pltpu.make_async_copy(own, own, x_send.at[step]).wait()
        block = rows_of(lax.rem(n + narrow - step, narrow))
        pltpu.make_async_copy(block, block, x_recv.at[step]).wait()


def gather_weights(qkv, gateup):
    wide, narrow = lax.axis_size("wide"), lax.axis_size("narrow")
    dma = pltpu.SemaphoreType.DMA
    hbm = pl.BlockSpec(memory_space=pl.ANY)
    every = wide * narrow
    shard, columns = gateup.shape
    aligned = (columns // (2 * every)) % 128 == 0
    if not aligned:
        gateup = gateup.reshape(shard, 2, wide, narrow, -1).transpose(3, 0, 1, 2, 4)
        gateup = gateup.reshape(narrow, shard, columns // narrow)
    return pl.pallas_call(
        functools.partial(gather_kernel, wide, narrow, aligned),
        out_shape=(
            jax.ShapeDtypeStruct((every * qkv.shape[0], qkv.shape[1]), BF16),
            jax.ShapeDtypeStruct((narrow * shard, columns // narrow), BF16),
        ),
        in_specs=[hbm, hbm],
        out_specs=(hbm, hbm),
        scratch_shapes=[dma((narrow,)), dma((narrow,)), dma(())] + flow_sems(wide, narrow),
        compiler_params=pltpu.CompilerParams(collective_id=0, has_side_effects=True),
        cost_estimate=pl.CostEstimate(flops=0, bytes_accessed=200 << 20, transcendentals=0),
    )(qkv, gateup)


def feed_kernel(
    narrow, x_ref, cot_ref, gate_up_ref, down_ref,
    group_ref, hidden_out, grad_out, low_out, grad_x_ref,
    gate_up, down, cot, hidden, grads, low, came,
    load_sem, x_send, x_recv, out_sem, g_send, g_recv,
):
    w, n = lax.axis_index("wide"), lax.axis_index("narrow")
    rows, width = x_ref.shape
    own = down.shape[0]
    tile = 256
    tiles = own // tile
    wtiles = width // tile

    def to_narrow(other):
        return {"wide": w, "narrow": other}

    loads = [
        pltpu.make_async_copy(gate_up_ref, gate_up, load_sem.at[0]),
        pltpu.make_async_copy(down_ref, down, load_sem.at[1]),
        pltpu.make_async_copy(cot_ref, cot, load_sem.at[2]),
        pltpu.make_async_copy(x_ref, group_ref.at[n], load_sem.at[3]),
    ]
    for load in loads:
        load.start()

    barrier = pltpu.get_barrier_semaphore()
    for step in range(1, narrow):
        pl.semaphore_signal(
            barrier, inc=1, device_id=to_narrow(lax.rem(n + step, narrow)), device_id_type=MESH
        )
    pl.semaphore_wait(barrier, narrow - 1)

    def owner_of(side, d):
        return n - d if side == 0 else n + d

    def valid(side, d):
        return n - d >= 0 if side == 0 else (n + d < narrow) & (d > 0)

    def passes(side, d):
        if side == 0:
            return (n - d >= 0) & (n < narrow - 1)
        return (n + d < narrow) & (n > 0)

    def x_copy(side, d):
        block = group_ref.at[owner_of(side, d)]
        return pltpu.make_async_remote_copy(
            src_ref=block,
            dst_ref=block,
            send_sem=x_send.at[side, d],
            recv_sem=x_recv.at[side, d + 1],
            device_id=to_narrow(n + 1 if side == 0 else n - 1),
            device_id_type=MESH,
        )

    def x_wait(side, d):
        block = group_ref.at[owner_of(side, d)]
        pltpu.make_async_copy(block, block, x_recv.at[side, d]).wait()

    def out_copies(at, block):
        return [
            pltpu.make_async_copy(hidden.at[at], hidden_out.at[block], out_sem.at[at, 0]),
            pltpu.make_async_copy(grads.at[at], grad_out.at[block], out_sem.at[at, 1]),
            pltpu.make_async_copy(low.at[at], low_out.at[block], out_sem.at[at, 2]),
        ]

    def g_copy(block):
        return pltpu.make_async_remote_copy(
            src_ref=cot.at[block],
            dst_ref=came.at[n],
            send_sem=g_send.at[block],
            recv_sem=g_recv.at[n],
            device_id=to_narrow(block),
            device_id_type=MESH,
        )

    def compute(side, d):
        block = n - d + 2 * d * side
        before = 1 + jnp.minimum(n, d - 1) + jnp.minimum(narrow - 1 - n, d - 1)
        before = jnp.where(d == 0, 0, before + jnp.where((side == 1) & (n - d >= 0), 1, 0))
        at = lax.rem(before, 2)

        @pl.when(before >= 2)
        def _():
            for copy in out_copies(at, block):
                copy.wait()

        def first(f, carry):
            columns = pl.ds(pl.multiple_of(f * tile, tile), tile)
            other = pl.ds(pl.multiple_of(own + f * tile, tile), tile)
            x = group_ref[block]
            gate = dot(x, gate_up[:, columns], NN)
            up = dot(x, gate_up[:, other], NN)
            grad = dot(cot[block], down[columns, :], NT)
            sig = 1.0 / (1.0 + jnp.exp(-gate))
            silu = gate * sig
            hidden[at, :, columns] = (silu * up).astype(BF16)
            grads[at, :, columns] = (grad * up * (sig + silu * (1.0 - sig))).astype(BF16)
            grads[at, :, other] = (grad * silu).astype(BF16)
            return carry

        lax.fori_loop(0, tiles, first, 0)

        def second(f, carry):
            columns = pl.ds(pl.multiple_of(f * tile, tile), tile)
            cot[block, :, columns] = dot(grads[at], gate_up[columns, :], NT, BF16)
            low[at, :, columns] = dot(hidden[at], down[:, columns], NN, BF16)
            return carry

        lax.fori_loop(0, wtiles, second, 0)
        for copy in out_copies(at, block):
            copy.start()
        pl.when(block != n)(lambda: g_copy(block).start())

    def distance(d, carry):
        for side in (0, 1):

            @pl.when(valid(side, d) & (d > 0))
            def _():
                x_wait(side, d)

            @pl.when(passes(side, d))
            def _():
                x_copy(side, d).start()

        @pl.when(d == 0)
        def _():
            for load in loads[:3]:
                load.wait()

        def one(side, carry):
            ok = jnp.where(side == 0, n - d, jnp.where(d > 0, narrow - 1 - n - d, -1)) >= 0
            pl.when(ok)(lambda: compute(side, d))
            return carry

        lax.fori_loop(0, 2, one, 0)
        return carry

    loads[3].wait()
    lax.fori_loop(0, narrow, distance, 0)

    for at in range(min(2, narrow)):
        for copy in out_copies(at, n):
            copy.wait()
    for side in (0, 1):
        for d in range(narrow - 1):
            pl.when(passes(side, d))(lambda side=side, d=d: x_copy(side, d).wait_send())
    for step in range(1, narrow):
        other = lax.rem(n + step, narrow)
        g_copy(other).wait_send()
        block = came.at[other]
        pltpu.make_async_copy(block, block, g_recv.at[other]).wait()

    def add(r, carry):
        part = pl.ds(pl.multiple_of(r * 16, 16), 16)
        total = cot[n, part, :].astype(F32)
        for step in range(1, narrow):
            total = total + came[lax.rem(n + step, narrow), part, :].astype(F32)
        grad_x_ref[part, :] = total
        return carry

    lax.fori_loop(0, rows // 16, add, 0)


def feed(x, cot_group, gate_up, down):
    narrow = lax.axis_size("narrow")
    rows, width = x.shape
    own = down.shape[0]
    dma = pltpu.SemaphoreType.DMA
    hbm = pl.BlockSpec(memory_space=pl.ANY)
    vmem = pl.BlockSpec(memory_space=pltpu.VMEM)
    group, hidden, grads, low, grad_x = pl.pallas_call(
        functools.partial(feed_kernel, narrow),
        out_shape=(
            jax.ShapeDtypeStruct((narrow, rows, width), BF16),
            jax.ShapeDtypeStruct((narrow, rows, own), BF16),
            jax.ShapeDtypeStruct((narrow, rows, 2 * own), BF16),
            jax.ShapeDtypeStruct((narrow, rows, width), BF16),
            jax.ShapeDtypeStruct((rows, width), F32),
        ),
        in_specs=[vmem, hbm, hbm, hbm],
        out_specs=(vmem, hbm, hbm, hbm, vmem),
        scratch_shapes=[
            pltpu.VMEM((width, 2 * own), BF16),
            pltpu.VMEM((own, width), BF16),
            pltpu.VMEM((narrow, rows, width), BF16),
            pltpu.VMEM((2, rows, own), BF16),
            pltpu.VMEM((2, rows, 2 * own), BF16),
            pltpu.VMEM((2, rows, width), BF16),
            pltpu.VMEM((narrow, rows, width), BF16),
            dma((4,)),
            dma((2, narrow + 1)),
            dma((2, narrow + 1)),
            dma((2, 3)),
            dma((narrow,)),
            dma((narrow,)),
        ],
        compiler_params=pltpu.CompilerParams(
            collective_id=1, has_side_effects=True, vmem_limit_bytes=58 << 20
        ),
        cost_estimate=pl.CostEstimate(
            flops=12 * narrow * rows * width * own, bytes_accessed=300 << 20, transcendentals=0
        ),
    )(x, cot_group.reshape(narrow, rows, width), gate_up, down)
    flat = lambda y: y.reshape((-1,) + y.shape[2:])
    return flat(group), flat(hidden), flat(grads), flat(low), grad_x


def sum_kernel(
    wide, narrow, chunk, wout_ref, qkv_ref, gains_ref, *refs
):
    cut_refs, refs = refs[:narrow], refs[narrow:]
    (
        wout_out, qkv_out, cut_out, gains_out,
        held, core_in, chip_in, z_in, gain_w, gain_sum, gain_z,
        load_sem, core_send, core_recv, chip_send, chip_recv, z_send, z_recv,
        gw_send, gw_recv, gz_send, gz_recv,
    ) = refs
    w, n = lax.axis_index("wide"), lax.axis_index("narrow")
    core, chip = lax.rem(w, 2), w // 2
    chips = wide // 2
    bits = chips.bit_length() - 1
    rows = held.shape[2]
    shard = rows // narrow
    half = chunk // 2
    first_chunks = wout_ref.shape[3] // chunk
    chunks = first_chunks + qkv_ref.shape[3] // chunk
    orders = [list(range(bits)), list(range(bits))[::-1]]

    def to_wide(mask):
        return {"wide": w ^ mask, "narrow": n}

    def to_narrow(step):
        return {"wide": w, "narrow": lax.rem(n + step, narrow)}

    barrier = pltpu.get_barrier_semaphore()
    for mask in range(1, wide):
        pl.semaphore_signal(barrier, inc=1, device_id=to_wide(mask), device_id_type=MESH)
    for step in range(1, narrow):
        pl.semaphore_signal(barrier, inc=1, device_id=to_narrow(step), device_id_type=MESH)
    pl.semaphore_wait(barrier, wide - 1 + narrow - 1)

    def columns_of(q):
        return pl.ds(pl.multiple_of(q * chunk, chunk), chunk)

    def copies_from(ref, q, at):
        load = pltpu.make_async_copy(
            ref.at[:, core, :, columns_of(at)], held.at[q], load_sem.at[q]
        )
        send = pltpu.make_async_remote_copy(
            src_ref=ref.at[:, 1 - core, :, columns_of(at)],
            dst_ref=core_in.at[q],
            send_sem=core_send.at[q],
            recv_sem=core_recv.at[q],
            device_id=to_wide(1),
            device_id_type=MESH,
        )
        return load, send

    def begin(q):
        @pl.when(q < first_chunks)
        def _():
            for copy in copies_from(wout_ref, q, q):
                copy.start()

        @pl.when(q >= first_chunks)
        def _():
            for copy in copies_from(qkv_ref, q, jnp.maximum(q - first_chunks, 0)):
                copy.start()

    def add_to(target, other, size):
        def one(r, carry):
            part = pl.ds(pl.multiple_of(r * 16, 16), 16)
            target(part)[...] = (
                target(part)[...].astype(F32) + other(part)[...].astype(F32)
            ).astype(BF16)
            return carry

        lax.fori_loop(0, size // 16, one, 0)

    def tiles_of(h, stage):
        order = orders[h]
        rest = order[stage + 1 :]
        offset = sum(chips >> (i + 1) for i in range(stage))
        fixed = sum(1 << b for b in order[: stage + 1])
        result = []
        for v in range(1 << len(rest)):
            extra = sum(((v >> i) & 1) << b for i, b in enumerate(rest))
            result.append((offset + v, (chip & fixed) + extra))
        return result

    def lanes(h):
        return pl.ds(h * half, half)

    def chip_copy(q, h, stage, slot, kept):
        bit = orders[h][stage]
        return pltpu.make_async_remote_copy(
            src_ref=held.at[q, kept ^ (1 << bit), :, lanes(h)],
            dst_ref=chip_in.at[q, h, slot],
            send_sem=chip_send.at[q, h, slot],
            recv_sem=chip_recv.at[q, h, slot],
            device_id=to_wide(2 << bit),
            device_id_type=MESH,
        )

    def send_stage(q, stage):
        for h in (0, 1):
            for slot, kept in tiles_of(h, stage):
                chip_copy(q, h, stage, slot, kept).start()

    def z_copy(q, step):
        other = lax.rem(n + step, narrow)
        return pltpu.make_async_remote_copy(
            src_ref=held.at[q, chip, pl.ds(pl.multiple_of(other * shard, shard), shard), :],
            dst_ref=z_in.at[q, step],
            send_sem=z_send.at[q, step],
            recv_sem=z_recv.at[q, step],
            device_id=to_narrow(step),
            device_id_type=MESH,
        )

    def after_core(q):
        load, _ = copies_from(wout_ref, q, 0)
        load.wait()
        pltpu.make_async_copy(core_in.at[q], core_in.at[q], core_recv.at[q]).wait()
        for k in range(chips):
            add_to(
                lambda part, k=k: held.at[q, k, part, :],
                lambda part, k=k: core_in.at[q, k, part, :],
                rows,
            )
        send_stage(q, 0)

    def after_stage(q, stage):
        for h in (0, 1):
            for slot, kept in tiles_of(h, stage):
                block = chip_in.at[q, h, slot]
                pltpu.make_async_copy(block, block, chip_recv.at[q, h, slot]).wait()
                add_to(
                    lambda part, h=h, kept=kept: held.at[q, kept, part, lanes(h)],
                    lambda part, h=h, slot=slot: chip_in.at[q, h, slot, part, :],
                    rows,
                )
        if stage + 1 < bits:
            send_stage(q, stage + 1)
        else:
            for step in range(1, narrow):
                z_copy(q, step).start()

    def after_z(q):
        for step in range(1, narrow):
            block = z_in.at[q, step]
            pltpu.make_async_copy(block, block, z_recv.at[q, step]).wait()

        def total(r):
            part = pl.ds(pl.multiple_of(n * shard + r * 16, 16), 16)
            value = held[q, chip, part, :].astype(F32)
            for step in range(1, narrow):
                value = value + z_in[q, step, pl.ds(pl.multiple_of(r * 16, 16), 16), :].astype(F32)
            return value

        @pl.when(q < first_chunks)
        def _():
            def one(r, carry):
                to = pl.ds(pl.multiple_of(r * 16, 16), 16)
                wout_out[to, columns_of(jnp.minimum(q, first_chunks - 1))] = total(r)
                return carry

            lax.fori_loop(0, shard // 16, one, 0)

        @pl.when(q >= first_chunks)
        def _():
            def one(r, carry):
                to = pl.ds(pl.multiple_of(r * 16, 16), 16)
                qkv_out[to, columns_of(jnp.maximum(q - first_chunks, 0))] = total(r)
                return carry

            lax.fori_loop(0, shard // 16, one, 0)

    def gw_copy(mask):
        return pltpu.make_async_remote_copy(
            src_ref=gains_ref.at[w ^ mask],
            dst_ref=gain_w.at[mask],
            send_sem=gw_send.at[mask],
            recv_sem=gw_recv.at[mask],
            device_id=to_wide(mask),
            device_id_type=MESH,
        )

    def gz_copy(step):
        return pltpu.make_async_remote_copy(
            src_ref=gain_sum.at[lax.rem(n + step, narrow)],
            dst_ref=gain_z.at[step],
            send_sem=gz_send.at[step],
            recv_sem=gz_recv.at[step],
            device_id=to_narrow(step),
            device_id_type=MESH,
        )

    ahead = min(3, chunks)
    for q in range(ahead):
        begin(q)
    for mask in range(1, wide):
        gw_copy(mask).start()
    piece = cut_refs[0].shape[1] // (2 * wide)
    for step in range(narrow):
        if cut_out.shape[0] == narrow:
            cut_out[lax.rem(n + narrow - step, narrow)] = cut_refs[step][...].astype(F32)
            continue
        for j in range(2 * wide):
            at = (j * narrow + lax.rem(n + narrow - step, narrow)) * piece
            cut_out[:, pl.ds(pl.multiple_of(at, piece), piece)] = cut_refs[step][
                :, pl.ds(j * piece, piece)
            ].astype(F32)

    def turn(t, carry):
        pl.when(t + ahead < chunks)(lambda: begin(t + ahead))
        pl.when(t < chunks)(lambda: after_core(t))
        for stage in range(bits):
            q = t - 1 - stage
            pl.when((q >= 0) & (q < chunks))(lambda q=q, stage=stage: after_stage(q, stage))
        q = t - 1 - bits
        pl.when(q >= 0)(lambda: after_z(q))
        return carry

    lax.fori_loop(0, chunks + bits + 1, turn, 0)

    total = gains_ref[w]
    for mask in range(1, wide):
        block = gain_w.at[mask]
        pltpu.make_async_copy(block, block, gw_recv.at[mask]).wait()
        total = total + gain_w[mask]
    gain_sum[...] = total
    for step in range(1, narrow):
        gz_copy(step).start()

    total = gain_sum[n]
    for step in range(1, narrow):
        block = gain_z.at[step]
        pltpu.make_async_copy(block, block, gz_recv.at[step]).wait()
        total = total + gain_z[step]
    gains_out[...] = total

    for mask in range(1, wide):
        gw_copy(mask).wait_send()
    for step in range(1, narrow):
        gz_copy(step).wait_send()

    def drain(q, carry):
        _, send = copies_from(wout_ref, q, 0)
        send.wait_send()
        for stage in range(bits):
            for h in (0, 1):
                for slot, kept in tiles_of(h, stage):
                    chip_copy(q, h, stage, slot, kept).wait_send()
        for step in range(1, narrow):
            z_copy(q, step).wait_send()
        return carry

    lax.fori_loop(0, chunks, drain, 0)


def sum_all(wout, qkv, cuts, gains):
    wide, narrow = lax.axis_size("wide"), lax.axis_size("narrow")
    chips, _, rows, _ = wout.shape
    chunk = 512
    chunks = (wout.shape[3] + qkv.shape[3]) // chunk
    shard, cut_width = cuts[0].shape
    aligned = (cut_width // (2 * wide)) % 128 == 0
    cut_shape = (shard, narrow * cut_width) if aligned else (narrow, shard, cut_width)
    dma = pltpu.SemaphoreType.DMA
    hbm = pl.BlockSpec(memory_space=pl.ANY)
    vmem = pl.BlockSpec(memory_space=pltpu.VMEM)
    results = pl.pallas_call(
        functools.partial(sum_kernel, wide, narrow, chunk),
        out_shape=(
            jax.ShapeDtypeStruct((shard, wout.shape[3]), F32),
            jax.ShapeDtypeStruct((shard, qkv.shape[3]), F32),
            jax.ShapeDtypeStruct(cut_shape, F32),
            jax.ShapeDtypeStruct((8, 128), F32),
        ),
        in_specs=[hbm, hbm, vmem] + [vmem] * narrow,
        out_specs=(vmem, vmem, vmem, vmem),
        scratch_shapes=[
            pltpu.VMEM((chunks, chips, rows, chunk), BF16),
            pltpu.VMEM((chunks, chips, rows, chunk), BF16),
            pltpu.VMEM((chunks, 2, chips - 1, rows, chunk // 2), BF16),
            pltpu.VMEM((chunks, narrow, shard, chunk), BF16),
            pltpu.VMEM((wide, narrow, 8, 128), F32),
            pltpu.VMEM((narrow, 8, 128), F32),
            pltpu.VMEM((narrow, 8, 128), F32),
            dma((chunks,)),
            dma((chunks,)),
            dma((chunks,)),
            dma((chunks, 2, chips - 1)),
            dma((chunks, 2, chips - 1)),
            dma((chunks, narrow)),
            dma((chunks, narrow)),
            dma((wide,)),
            dma((wide,)),
            dma((narrow,)),
            dma((narrow,)),
        ],
        compiler_params=pltpu.CompilerParams(
            collective_id=2, has_side_effects=True, vmem_limit_bytes=54 << 20
        ),
        cost_estimate=pl.CostEstimate(flops=0, bytes_accessed=300 << 20, transcendentals=0),
    )(wout, qkv, gains, *cuts)
    return results, aligned


def per_device(tokens, lengths, gain_attn, w_qkv, w_out, gain_mlp, w_gateup, w_down, cotangent):
    rows, width = tokens.shape[1:]
    wide, narrow = lax.axis_size("wide"), lax.axis_size("narrow")
    pack_rows = rows * wide
    query_width, key_width = HEADS * HEAD_DIM, KV_HEADS * HEAD_DIM
    groups = HEADS // wide
    copies = wide // KV_HEADS
    own_ff = FF // narrow
    first, positions = places(lengths[0], pack_rows)
    cos_all, sin_all = rotary(positions.astype(F32), HALF)
    first_row = lax.axis_index("wide") * rows
    cos = lax.dynamic_slice_in_dim(cos_all, first_row, rows, 1)
    sin = lax.dynamic_slice_in_dim(sin_all, first_row, rows, 1)
    cos_all = cos_all.reshape(HALF, wide, rows).transpose(1, 0, 2)
    sin_all = sin_all.reshape(HALF, wide, rows).transpose(1, 0, 2)
    start = first.reshape(wide, 1, rows)

    gains = jnp.stack([gain_attn, gain_mlp], -1)
    with_gains = jnp.concatenate([w_qkv, jnp.pad(gains, ((0, 0), (0, 126)))], -1)
    shard = w_gateup.shape[0]
    qkv_gained, gateup_rows = gather_weights(with_gains, w_gateup)
    qkv_whole = qkv_gained[:, : w_qkv.shape[1]]
    gain_one = qkv_gained[:, w_qkv.shape[1]].astype(F32)
    gain_two = qkv_gained[:, w_qkv.shape[1] + 1].astype(F32)
    gateup_own = gather(gateup_rows, "wide")
    down_own = gather(w_down, "wide")

    inputs = tokens[0].astype(F32)
    scale_one = lax.rsqrt(jnp.mean(inputs * inputs, -1, keepdims=True) + EPS)
    unit_one = inputs * scale_one
    normed_one = (unit_one * gain_one).astype(BF16)
    projected = dot(qkv_whole, normed_one, (((0,), (1,)), ((), ())))
    turning = projected[: query_width + key_width].reshape(HEADS + KV_HEADS, 2, HALF, rows)
    front, back = turning[:, 0], turning[:, 1]
    turned = jnp.stack([front * cos - back * sin, back * cos + front * sin], 1)
    queries = (turned[:HEADS] * SCORE_SCALE).astype(BF16).reshape(wide, groups * HEAD_DIM, rows)
    keys = turned[HEADS:].astype(BF16).reshape(KV_HEADS, HEAD_DIM, rows)
    values = projected[query_width + key_width :].astype(BF16).reshape(KV_HEADS, HEAD_DIM, rows)
    keys_values = jnp.repeat(jnp.concatenate([keys, values], 1), copies, 0)
    heads, attended_low, attended_full, log_total, out_whole, cot_group = attend(
        jnp.concatenate([queries, keys_values], 1), start, w_out, cotangent[0], groups
    )
    cot_group = cot_group.reshape(-1, width)
    attended_low = attended_low.reshape(query_width, rows)
    middle = inputs + dot(attended_low, out_whole, TN)
    scale_two = lax.rsqrt(jnp.mean(middle * middle, -1, keepdims=True) + EPS)
    unit_two = middle * scale_two
    normed_two = (unit_two * gain_two).astype(BF16)

    normed_group, hidden, grad_gate_up, low_part, grad_normed_two = feed(
        normed_two, cot_group, gateup_own, down_own
    )
    part_gateup = dot(normed_group, grad_gate_up, TN, BF16)
    hidden, part_gateup = lax.optimization_barrier((hidden, part_gateup))
    grad_gateup = scatter_sum(part_gateup, "wide").reshape(narrow, shard, 2 * own_ff)
    grad_down = scatter_sum(dot(hidden, cot_group, TN, BF16), "wide")
    me = lax.axis_index("narrow")
    cuts = [pick(grad_gateup, me, 0)]
    for step in range(1, narrow):
        cuts.append(shift(pick(grad_gateup, (me + step) % narrow, 0), step))

    part_gain_two = jnp.sum(grad_normed_two * unit_two, 0)
    grad_middle = cotangent[0].astype(F32) + norm_back(
        grad_normed_two * gain_two, unit_two, scale_two
    )
    grad_branch = grad_middle.astype(BF16)
    grad_attended = dot(out_whole, grad_branch, NT, BF16).reshape(wide, groups * HEAD_DIM, rows)
    grad_heads, low_came = attend_back(
        heads, grad_attended, attended_full, log_total, start, cos_all, sin_all,
        low_part.reshape(narrow, rows, width), groups,
    )
    layer_out = (middle + jnp.sum(low_came.astype(F32), 0)).astype(BF16)[None]
    grad_queries = grad_heads[:, : groups * HEAD_DIM].reshape(query_width, rows)
    grad_keys_values = (
        grad_heads[:, groups * HEAD_DIM :]
        .reshape(KV_HEADS, copies, 2, HEAD_DIM, rows)
        .astype(F32)
        .sum(1)
        .astype(BF16)
    )
    grad_projected = jnp.concatenate(
        [
            grad_queries,
            grad_keys_values[:, 0].reshape(key_width, rows),
            grad_keys_values[:, 1].reshape(key_width, rows),
        ],
        0,
    )
    grad_normed_one = dot(grad_projected, qkv_whole, (((0,), (1,)), ((), ())))
    part_gain_one = jnp.sum(grad_normed_one * unit_one, 0)
    part_gains = jnp.stack([part_gain_one, part_gain_two], 0).reshape(2, wide, narrow, shard)
    part_gains = jnp.pad(
        part_gains.transpose(1, 2, 0, 3), ((0, 0), (0, 0), (0, 6), (0, 128 - shard))
    )
    cut = (wide // 2, 2, narrow * shard, -1)
    part_wout = dot(attended_low, grad_branch, NN, BF16).reshape(cut)
    part_qkv = dot(normed_one, grad_projected, (((0,), (1,)), ((), ())), BF16).reshape(cut)
    (grad_wout, grad_qkv, grad_gateup, grad_gains), done = sum_all(
        part_wout, part_qkv, cuts, part_gains
    )
    if not done:
        grad_gateup = (
            grad_gateup.reshape(narrow, shard, 2, wide, -1)
            .transpose(1, 2, 3, 0, 4)
            .reshape(shard, 2 * FF)
        )
    (grad_down, grad_wout) = lax.optimization_barrier((grad_down, grad_wout))
    grad_down = grad_down.astype(F32)
    grad_inputs = grad_middle + norm_back(grad_normed_one * gain_one, unit_one, scale_one)
    grad_tokens = grad_inputs.astype(BF16)[None]
    return (
        layer_out,
        grad_tokens,
        grad_gains[0, :shard],
        grad_qkv,
        grad_wout,
        grad_gains[1, :shard],
        grad_gateup,
        grad_down,
    )


def solution(mesh):
    rows, packs = P("narrow", "wide", None), P("narrow", None)
    weight, gain = P(BOTH, None), P(BOTH)
    return jax.shard_map(
        per_device,
        mesh=mesh,
        in_specs=(rows, packs, gain, weight, weight, gain, weight, weight, rows),
        out_specs=(rows, rows, gain, weight, weight, gain, weight, weight),
        check_vma=False,
    )
```

```python
import functools
import math

import jax
import jax.numpy as jnp
from jax import lax
from jax.experimental import pallas as pl
from jax.experimental.pallas import tpu as pltpu
from jax.sharding import PartitionSpec as P

FF = 8192
HEADS = 32
KV_HEADS = 8
HEAD_DIM = 64
HALF = HEAD_DIM // 2
EPS = 1e-05
NEGATIVE = -1e30
SCORE_SCALE = 1.0 / math.sqrt(HEAD_DIM)
BOTH = ("wide", "narrow")
F32 = jnp.float32
BF16 = jnp.bfloat16
NN = (((1,), (0,)), ((), ()))
NT = (((1,), (1,)), ((), ()))
TN = (((0,), (0,)), ((), ()))


def dot(left, right, dims, kind=F32):
    return lax.dot_general(left, right, dims, preferred_element_type=F32).astype(kind)


def places(lengths_row, total_rows):
    seq_ends = jnp.cumsum(lengths_row)
    starts = seq_ends - lengths_row
    row_index = jnp.arange(total_rows, dtype=jnp.int32)
    segments = jnp.sum((row_index[:, None] >= seq_ends[None, :]).astype(jnp.int32), -1)
    slot_index = jnp.arange(lengths_row.shape[0], dtype=jnp.int32)
    owned = segments[:, None] == slot_index[None, :]
    first = jnp.sum(jnp.where(owned, starts[None, :], 0), -1)
    return first, row_index - first


def rotary(positions, half_width):
    channel = jnp.arange(half_width, dtype=jnp.float32)
    inverse_rate = jnp.power(500000.0, -channel / half_width)
    wavelength = 2.0 * math.pi / inverse_rate
    smooth = (8192.0 / wavelength - 1.0) / 3.0
    blended = (1.0 - smooth) * inverse_rate / 32.0 + smooth * inverse_rate
    frequency = jnp.where(
        wavelength < 2048.0,
        inverse_rate,
        jnp.where(wavelength > 8192.0, inverse_rate / 32.0, blended),
    )
    angles = frequency[:, None] * positions[None, :]
    return jnp.cos(angles), jnp.sin(angles)


def norm_back(grad_unit, unit_rows, row_scale):
    return row_scale * (grad_unit - unit_rows * jnp.mean(grad_unit * unit_rows, -1, keepdims=True))


MESH = pl.DeviceIdType.MESH


class Flow:
    def __init__(self, wide, narrow, x_ref, out_ref, sems):
        self.wide, self.narrow, self.x_ref, self.out_ref = wide, narrow, x_ref, out_ref
        self.w, self.n = lax.axis_index("wide"), lax.axis_index("narrow")
        (self.own_sem, self.z_send, self.z_recv, self.m_send, self.m_recv,
         self.r_send, self.r_recv, self.c_send, self.c_recv) = sems
        self.relay = wide == 8
        self.masks = [2, 4] if self.relay else list(range(2, wide, 2))
        self.last = narrow + 2

    def to_wide(self, mask):
        return {"wide": self.w ^ mask, "narrow": self.n}

    def owner_of(self, side, d):
        return self.n - d if side == 0 else self.n + d

    def valid(self, side, d):
        return self.n - d >= 0 if side == 0 else self.n + d < self.narrow

    def can_pass(self, side, d):
        if side == 0:
            return (self.n - (d - 1) >= 0) & (self.n < self.narrow - 1)
        return (self.n + (d - 1) < self.narrow) & (self.n > 0)

    def slot(self, side, d):
        return d - 1 + side * (self.narrow - 1) if d else 2 * (self.narrow - 1)

    def at_distance(self, d, action):
        if d == 0:
            action(0, 0)
            return
        for side in (0, 1):
            pl.when(self.valid(side, d))(functools.partial(action, side, d))

    def place(self, owner_w, owner_n, part=None):
        depth = self.x_ref.shape[0]
        half = depth // 2
        at = (owner_w * self.narrow + owner_n) * depth
        if part is None:
            return self.out_ref.at[pl.ds(pl.multiple_of(at, depth), depth), :]
        return self.out_ref.at[pl.ds(pl.multiple_of(at + part * half, half), half), :]

    def own_copy(self):
        return pltpu.make_async_copy(self.x_ref, self.place(self.w, self.n), self.own_sem)

    def z_copy(self, side, d):
        block = self.place(self.w, self.owner_of(side, d - 1))
        return pltpu.make_async_remote_copy(
            src_ref=self.x_ref if d == 1 else block,
            dst_ref=block,
            send_sem=self.z_send.at[side, d],
            recv_sem=self.z_recv.at[side, d],
            device_id={"wide": self.w, "narrow": self.n + 1 if side == 0 else self.n - 1},
            device_id_type=MESH,
        )

    def z_wait(self, side, d):
        block = self.place(self.w, self.owner_of(side, d))
        pltpu.make_async_copy(block, block, self.z_recv.at[side, d]).wait()

    def m_copy(self, i, side, d):
        block = self.place(self.w, self.owner_of(side, d))
        return pltpu.make_async_remote_copy(
            src_ref=self.x_ref if d == 0 else block,
            dst_ref=block,
            send_sem=self.m_send.at[i, self.slot(side, d)],
            recv_sem=self.m_recv.at[i, self.slot(side, d)],
            device_id=self.to_wide(self.masks[i]),
            device_id_type=MESH,
        )

    def m_wait(self, i, side, d):
        block = self.place(self.w ^ self.masks[i], self.owner_of(side, d))
        pltpu.make_async_copy(block, block, self.m_recv.at[i, self.slot(side, d)]).wait()

    def r_copy(self, part, side, d):
        block = self.place(self.w ^ self.masks[part], self.owner_of(side, d), part)
        return pltpu.make_async_remote_copy(
            src_ref=block,
            dst_ref=block,
            send_sem=self.r_send.at[part, self.slot(side, d)],
            recv_sem=self.r_recv.at[part, self.slot(side, d)],
            device_id=self.to_wide(self.masks[1 - part]),
            device_id_type=MESH,
        )

    def r_wait(self, part, side, d):
        block = self.place(self.w ^ 6, self.owner_of(side, d), part)
        pltpu.make_async_copy(block, block, self.r_recv.at[part, self.slot(side, d)]).wait()

    def c_copy(self, chip, side, d):
        block = self.place(self.w ^ (2 * chip), self.owner_of(side, d))
        return pltpu.make_async_remote_copy(
            src_ref=self.x_ref if d == 0 and chip == 0 else block,
            dst_ref=block,
            send_sem=self.c_send.at[chip, self.slot(side, d)],
            recv_sem=self.c_recv.at[chip, self.slot(side, d)],
            device_id=self.to_wide(1),
            device_id_type=MESH,
        )

    def c_wait(self, chip, side, d):
        block = self.place((self.w ^ 1) ^ (2 * chip), self.owner_of(side, d))
        pltpu.make_async_copy(block, block, self.c_recv.at[chip, self.slot(side, d)]).wait()

    def send_from_here(self, side, d):
        if d > 0:
            self.z_wait(side, d)
        if 0 < d < self.narrow - 1:
            pl.when(self.can_pass(side, d + 1))(lambda: self.z_copy(side, d + 1).start())
        for i in range(len(self.masks)):
            self.m_copy(i, side, d).start()
        self.c_copy(0, side, d).start()

    def send_on(self, side, d):
        for i in range(len(self.masks)):
            self.m_wait(i, side, d)
            if self.relay:
                self.r_copy(i, side, d).start()
            self.c_copy(self.masks[i] // 2, side, d).start()

    def send_last(self, side, d):
        self.r_wait(0, side, d)
        self.r_wait(1, side, d)
        self.c_copy(3, side, d).start()

    def step(self, t):
        if t == 0:
            self.own_copy().start()
            for side in (0, 1):
                pl.when(self.can_pass(side, 1))(lambda side=side: self.z_copy(side, 1).start())
        if 0 <= t < self.narrow:
            self.at_distance(t, self.send_from_here)
        if 0 <= t - 1 < self.narrow:
            self.at_distance(t - 1, self.send_on)
        if self.relay and 0 <= t - 2 < self.narrow:
            self.at_distance(t - 2, self.send_last)

    def finish(self, side, d):
        for i in range(len(self.masks)):
            self.m_copy(i, side, d).wait_send()
            if self.relay:
                self.r_copy(i, side, d).wait_send()
        for chip in range(self.wide // 2):
            self.c_copy(chip, side, d).wait_send()
            self.c_wait(chip, side, d)

    def end(self):
        self.own_copy().wait()
        for side in (0, 1):
            for d in range(1, self.narrow):
                pl.when(self.can_pass(side, d))(
                    lambda side=side, d=d: self.z_copy(side, d).wait_send()
                )
        for d in range(self.narrow):
            self.at_distance(d, self.finish)


class Line:
    def __init__(self, narrow, x_ref, out_ref, sems):
        self.narrow, self.x_ref, self.out_ref = narrow, x_ref, out_ref
        self.w, self.n = lax.axis_index("wide"), lax.axis_index("narrow")
        self.own_sem, self.send, self.recv = sems

    def owner_of(self, side, d):
        return self.n - d if side == 0 else self.n + d

    def valid(self, side, d):
        return self.n - d >= 0 if side == 0 else self.n + d < self.narrow

    def can_pass(self, side, d):
        if side == 0:
            return (self.n - (d - 1) >= 0) & (self.n < self.narrow - 1)
        return (self.n + (d - 1) < self.narrow) & (self.n > 0)

    def own_copy(self):
        return pltpu.make_async_copy(self.x_ref, self.out_ref.at[self.n], self.own_sem)

    def copy(self, side, d):
        block = self.out_ref.at[self.owner_of(side, d - 1)]
        return pltpu.make_async_remote_copy(
            src_ref=self.x_ref if d == 1 else block,
            dst_ref=block,
            send_sem=self.send.at[side, d],
            recv_sem=self.recv.at[side, d],
            device_id={"wide": self.w, "narrow": self.n + 1 if side == 0 else self.n - 1},
            device_id_type=MESH,
        )

    def pass_on(self, side, d):
        arrive(self.out_ref.at[self.owner_of(side, d)], self.recv.at[side, d])
        if d < self.narrow - 1:
            pl.when(self.can_pass(side, d + 1))(lambda: self.copy(side, d + 1).start())

    def step(self, t):
        if t == 0:
            self.own_copy().start()
        for side in (0, 1):
            if t == 0:
                pl.when(self.can_pass(side, 1))(lambda side=side: self.copy(side, 1).start())
            else:
                pl.when(self.valid(side, t))(lambda side=side: self.pass_on(side, t))

    def end(self):
        self.own_copy().wait()
        for side in (0, 1):
            for d in range(1, self.narrow):
                pl.when(self.can_pass(side, d))(lambda side=side, d=d: self.copy(side, d).wait_send())


def flow_sems(wide, narrow):
    slots = 2 * narrow - 1
    masks = 2 if wide == 8 else wide // 2 - 1
    dma = pltpu.SemaphoreType.DMA
    return [
        dma(()),
        dma((2, narrow)),
        dma((2, narrow)),
        dma((masks, slots)),
        dma((masks, slots)),
        dma((2, slots)),
        dma((2, slots)),
        dma((wide // 2, slots)),
        dma((wide // 2, slots)),
    ]


class Reduce:
    def __init__(self, wide, narrow, source, out_ref, refs):
        self.wide, self.narrow, self.source, self.out_ref = wide, narrow, source, out_ref
        self.w, self.n = lax.axis_index("wide"), lax.axis_index("narrow")
        self.core, self.chip = lax.rem(self.w, 2), self.w // 2
        self.chips = wide // 2
        self.bits = self.chips.bit_length() - 1
        (self.held, self.core_in, self.chip_in, self.z_in, self.load_sem, self.core_send, self.core_recv,
         self.chip_send, self.chip_recv, self.z_send, self.z_recv) = refs
        self.chunks = self.held.shape[0]
        self.rows, self.chunk = self.held.shape[2:]
        self.shard = self.rows // narrow
        self.orders = [list(range(self.bits)), list(range(self.bits))[::-1]]

    def columns_of(self, q):
        return pl.ds(pl.multiple_of(q * self.chunk, self.chunk), self.chunk)

    def begin(self, q):
        pltpu.make_async_copy(
            self.source.at[:, self.core, :, self.columns_of(q)], self.held.at[q], self.load_sem.at[q]
        ).start()
        pltpu.make_async_remote_copy(
            src_ref=self.source.at[:, 1 - self.core, :, self.columns_of(q)],
            dst_ref=self.core_in.at[q],
            send_sem=self.core_send.at[q],
            recv_sem=self.core_recv.at[q],
            device_id={"wide": self.w ^ 1, "narrow": self.n},
            device_id_type=MESH,
        ).start()

    def add_to(self, target, other):
        def one(r, carry):
            part = pl.ds(pl.multiple_of(r * 16, 16), 16)
            target(part)[...] = (
                target(part)[...].astype(F32) + other(part)[...].astype(F32)
            ).astype(BF16)
            return carry

        lax.fori_loop(0, self.rows // 16, one, 0)

    def tiles_of(self, h, stage):
        order = self.orders[h]
        rest = order[stage + 1 :]
        offset = sum(self.chips >> (i + 1) for i in range(stage))
        fixed = sum(1 << b for b in order[: stage + 1])
        result = []
        for v in range(1 << len(rest)):
            extra = sum(((v >> i) & 1) << b for i, b in enumerate(rest))
            result.append((offset + v, (self.chip & fixed) + extra))
        return result

    def lanes(self, h):
        return pl.ds(h * (self.chunk // 2), self.chunk // 2)

    def chip_copy(self, q, h, stage, slot, kept):
        bit = self.orders[h][stage]
        return pltpu.make_async_remote_copy(
            src_ref=self.held.at[q, kept ^ (1 << bit), :, self.lanes(h)],
            dst_ref=self.chip_in.at[q, h, slot],
            send_sem=self.chip_send.at[q, h, slot],
            recv_sem=self.chip_recv.at[q, h, slot],
            device_id={"wide": self.w ^ (2 << bit), "narrow": self.n},
            device_id_type=MESH,
        )

    def send_stage(self, q, stage):
        for h in (0, 1):
            for slot, kept in self.tiles_of(h, stage):
                self.chip_copy(q, h, stage, slot, kept).start()

    def after_core(self, q):
        pltpu.make_async_copy(self.held.at[q], self.held.at[q], self.load_sem.at[q]).wait()
        arrive(self.core_in.at[q], self.core_recv.at[q])
        for k in range(self.chips):
            self.add_to(
                lambda part, k=k: self.held.at[q, k, part, :],
                lambda part, k=k: self.core_in.at[q, k, part, :],
            )
        self.send_stage(q, 0)

    def z_copy(self, q, step):
        other = lax.rem(self.n + step, self.narrow)
        own = pl.ds(pl.multiple_of(other * self.shard, self.shard), self.shard)
        return pltpu.make_async_remote_copy(
            src_ref=self.held.at[q, self.chip, own, :],
            dst_ref=self.z_in.at[q, step],
            send_sem=self.z_send.at[q, step],
            recv_sem=self.z_recv.at[q, step],
            device_id={"wide": self.w, "narrow": other},
            device_id_type=MESH,
        )

    def after_stage(self, q, stage):
        for h in (0, 1):
            for slot, kept in self.tiles_of(h, stage):
                arrive(self.chip_in.at[q, h, slot], self.chip_recv.at[q, h, slot])
                self.add_to(
                    lambda part, h=h, kept=kept: self.held.at[q, kept, part, self.lanes(h)],
                    lambda part, h=h, slot=slot: self.chip_in.at[q, h, slot, part, :],
                )
        if stage + 1 < self.bits:
            self.send_stage(q, stage + 1)
        else:
            for step in range(1, self.narrow):
                self.z_copy(q, step).start()

    def after_z(self, q):
        for step in range(1, self.narrow):
            arrive(self.z_in.at[q, step], self.z_recv.at[q, step])

        def one(r, carry):
            to = pl.ds(pl.multiple_of(r * 16, 16), 16)
            own = pl.ds(pl.multiple_of(self.n * self.shard + r * 16, 16), 16)
            value = self.held[q, self.chip, own, :].astype(F32)
            for step in range(1, self.narrow):
                value = value + self.z_in[q, step, to, :].astype(F32)
            self.out_ref[to, self.columns_of(q)] = value
            return carry

        lax.fori_loop(0, self.shard // 16, one, 0)

    def drain(self):
        def one(q, carry):
            arrive(self.core_in.at[q], self.core_send.at[q])
            for stage in range(self.bits):
                for h in (0, 1):
                    for slot, kept in self.tiles_of(h, stage):
                        self.chip_copy(q, h, stage, slot, kept).wait_send()
            for step in range(1, self.narrow):
                self.z_copy(q, step).wait_send()
            return carry

        lax.fori_loop(0, self.chunks, one, 0)


def reduce_scratch(wide, narrow, source, chunk):
    chips, rows, chunks = wide // 2, source.shape[2], source.shape[3] // chunk
    dma = pltpu.SemaphoreType.DMA
    return [
        pltpu.VMEM((chunks, chips, rows, chunk), BF16),
        pltpu.VMEM((chunks, chips, rows, chunk), BF16),
        pltpu.VMEM((chunks, 2, chips - 1, rows, chunk // 2), BF16),
        pltpu.VMEM((chunks, narrow, rows // narrow, chunk), BF16),
        dma((chunks,)),
        dma((chunks,)),
        dma((chunks,)),
        dma((chunks, 2, chips - 1)),
        dma((chunks, 2, chips - 1)),
        dma((chunks, narrow)),
        dma((chunks, narrow)),
    ]


def greet(wide, narrow):
    w, n = lax.axis_index("wide"), lax.axis_index("narrow")
    barrier = pltpu.get_barrier_semaphore()
    for mask in range(1, wide):
        pl.semaphore_signal(
            barrier, inc=1, device_id={"wide": w ^ mask, "narrow": n}, device_id_type=MESH
        )
    for step in range(1, narrow):
        other = lax.rem(n + step, narrow)
        pl.semaphore_signal(
            barrier, inc=1, device_id={"wide": w, "narrow": other}, device_id_type=MESH
        )
    pl.semaphore_wait(barrier, wide + narrow - 2)


def to_owner(source, target, send_sem, recv_sem, mask):
    w, n = lax.axis_index("wide"), lax.axis_index("narrow")
    return pltpu.make_async_remote_copy(
        src_ref=source,
        dst_ref=target,
        send_sem=send_sem,
        recv_sem=recv_sem,
        device_id={"wide": w ^ mask, "narrow": n},
        device_id_type=MESH,
    )


def to_block(source, target, send_sem, recv_sem, owner):
    n = lax.axis_index("narrow")
    return pltpu.make_async_remote_copy(
        src_ref=source,
        dst_ref=target,
        send_sem=send_sem,
        recv_sem=recv_sem,
        device_id={"wide": owner, "narrow": n},
        device_id_type=MESH,
    )


def arrive(block, sem):
    pltpu.make_async_copy(block, block, sem).wait()


def attend_kernel(
    wide, narrow, groups, start_ref, mine_ref, w_ref, c_ref,
    x_ref, low_ref, full_ref, log_ref, w_all, c_all,
    keys, top, total, acc, done, own_sem, in_send, in_recv, out_send, out_recv,
    line_own, line_send, line_recv, *sems,
):
    me = lax.axis_index("wide")
    blocks, _, rows = x_ref.shape
    width = groups * HEAD_DIM
    own_in = pltpu.make_async_copy(mine_ref.at[me], x_ref.at[me], own_sem.at[0])
    own_in.start()
    greet(wide, narrow)
    for mask in range(1, wide):
        to_owner(
            mine_ref.at[me ^ mask], x_ref.at[me], in_send.at[mask], in_recv.at[me], mask
        ).start()
    flow = Flow(wide, narrow, w_ref, w_all, sems)
    line = Line(narrow, c_ref, c_all, (line_own, line_send, line_recv))
    flow.step(0)
    line.step(0)
    spread = {}
    for t in range(1, flow.last):
        spread.setdefault(min(blocks, blocks // 2 - 1 + t), []).append(functools.partial(flow.step, t))
    for t in range(1, narrow):
        spread.setdefault(min(blocks, blocks // 2 + 2 * t - 1), []).append(functools.partial(line.step, t))
    key_row = lax.broadcasted_iota(jnp.int32, (rows, rows), 0)
    column = lax.broadcasted_iota(jnp.int32, (rows, rows), 1)
    own_in.wait()

    def block(i, carry):
        pl.when(i != me)(lambda: arrive(x_ref.at[i], in_recv.at[i]))
        for at, actions in spread.items():
            if at < blocks:

                @pl.when(i == at)
                def _():
                    for action in actions:
                        action()

        keys[i] = x_ref[i, width : width + HEAD_DIM, :].T
        top[...] = jnp.full_like(top, NEGATIVE)
        total[...] = jnp.zeros_like(total)
        acc[...] = jnp.zeros_like(acc)
        start = start_ref[i]
        query_row = i * rows + column

        def step(j, carry):
            key_index = key_row + j * rows
            allowed = (key_index <= query_row) & (key_index >= start)
            key_block = keys[j]
            value_block = x_ref[j, width + HEAD_DIM :, :]
            for h in range(groups):
                own = pl.ds(h * HEAD_DIM, HEAD_DIM)
                scores = dot(key_block, x_ref[i, own, :], NN)
                scores = jnp.where(allowed, scores, NEGATIVE)
                old = top[h : h + 1, :]
                new = jnp.maximum(old, jnp.max(scores, 0, keepdims=True))
                shrink = jnp.exp(old - new)
                prob = jnp.exp(scores - new)
                top[h : h + 1, :] = new
                total[h : h + 1, :] = total[h : h + 1, :] * shrink + jnp.sum(prob, 0, keepdims=True)
                acc[own, :] = acc[own, :] * shrink + dot(value_block, prob.astype(BF16), NN)
            return carry

        lax.fori_loop(0, i + 1, step, 0)
        log_ref[i] = top[...] + jnp.log(total[...])
        for h in range(groups):
            own = pl.ds(h * HEAD_DIM, HEAD_DIM)
            result = acc[own, :] / total[h : h + 1, :]
            full_ref[i, own, :] = result
            done[i, own, :] = result.astype(BF16)

        @pl.when(i != me)
        def _():
            to_block(done.at[i], low_ref.at[me], out_send.at[i], out_recv.at[me], i).start()

        return carry

    lax.fori_loop(0, blocks, block, 0)
    low_ref[me] = done[me]
    for action in spread.get(blocks, []):
        action()
    flow.end()
    line.end()
    for mask in range(1, wide):
        to_owner(
            mine_ref.at[me ^ mask], x_ref.at[me], in_send.at[mask], in_recv.at[me], mask
        ).wait_send()
        other = me ^ mask
        arrive(low_ref.at[other], out_recv.at[other])
        arrive(done.at[other], out_send.at[other])


def attend(mine, start, w_out, cot, groups):
    wide, narrow = lax.axis_size("wide"), lax.axis_size("narrow")
    blocks, features, rows = mine.shape
    width = groups * HEAD_DIM
    dma = pltpu.SemaphoreType.DMA
    hbm = pl.BlockSpec(memory_space=pl.ANY)
    vmem = pl.BlockSpec(memory_space=pltpu.VMEM)
    return pl.pallas_call(
        functools.partial(attend_kernel, wide, narrow, groups),
        out_shape=(
            jax.ShapeDtypeStruct((blocks, features, rows), BF16),
            jax.ShapeDtypeStruct((blocks, width, rows), BF16),
            jax.ShapeDtypeStruct((blocks, width, rows), F32),
            jax.ShapeDtypeStruct((blocks, groups, rows), F32),
            jax.ShapeDtypeStruct((wide * narrow * w_out.shape[0], w_out.shape[1]), BF16),
            jax.ShapeDtypeStruct((narrow,) + cot.shape, BF16),
        ),
        in_specs=[vmem, vmem, hbm, hbm],
        out_specs=(vmem, vmem, vmem, vmem, hbm, hbm),
        scratch_shapes=[
            pltpu.VMEM((blocks, rows, HEAD_DIM), BF16),
            pltpu.VMEM((groups, rows), F32),
            pltpu.VMEM((groups, rows), F32),
            pltpu.VMEM((width, rows), F32),
            pltpu.VMEM((blocks, width, rows), BF16),
            dma((1,)),
            dma((wide,)),
            dma((wide,)),
            dma((wide,)),
            dma((wide,)),
            dma(()),
            dma((2, narrow)),
            dma((2, narrow)),
        ]
        + flow_sems(wide, narrow),
        compiler_params=pltpu.CompilerParams(
            collective_id=3, has_side_effects=True, vmem_limit_bytes=40 << 20
        ),
        cost_estimate=pl.CostEstimate(
            flops=32 * width * (blocks * rows) ** 2,
            bytes_accessed=64 << 20,
            transcendentals=groups * (blocks * rows) ** 2 // 2,
        ),
    )(start, mine, w_out, cot)


def attend_back_kernel(
    wide, narrow, groups, start_ref, x_ref, mine_ref, full_ref, log_ref, cos_ref, sin_ref, part_ref,
    weight_ref, out_ref, came_ref, weight_out,
    keys, values, acc, acc_keys, acc_values, grad_ref, done, own_sem, in_send, in_recv,
    q_send, q_recv, k_send, k_recv, p_send, p_recv, *refs,
):
    reduce = Reduce(wide, narrow, weight_ref, weight_out, refs)
    me, n = lax.axis_index("wide"), lax.axis_index("narrow")

    def part_copy(step):
        other = lax.rem(n + step, narrow)
        return pltpu.make_async_remote_copy(
            src_ref=part_ref.at[other],
            dst_ref=came_ref.at[step],
            send_sem=p_send.at[step],
            recv_sem=p_recv.at[step],
            device_id={"wide": me, "narrow": other},
            device_id_type=MESH,
        )

    own_part = pltpu.make_async_copy(part_ref.at[n], came_ref.at[0], p_send.at[0])
    blocks, _, rows = x_ref.shape
    width = groups * HEAD_DIM
    own_in = pltpu.make_async_copy(mine_ref.at[me], grad_ref.at[me], own_sem.at[0])
    own_in.start()
    for j in range(blocks):
        keys[j] = x_ref[j, width : width + HEAD_DIM, :].T
        values[j] = x_ref[j, width + HEAD_DIM :, :].T
    acc_keys[...] = jnp.zeros_like(acc_keys)
    acc_values[...] = jnp.zeros_like(acc_values)
    greet(wide, narrow)
    for mask in range(1, wide):
        to_owner(
            mine_ref.at[me ^ mask], grad_ref.at[me], in_send.at[mask], in_recv.at[me], mask
        ).start()
    for q in range(reduce.chunks):
        reduce.begin(q)
    own_part.start()
    for step in range(1, narrow):
        part_copy(step).start()

    def weight_turn(c):
        chunks = reduce.chunks
        q = jnp.maximum(c - 2, 0) // 2
        ready = (c >= 2) & (lax.rem(c, 2) == 0) & (q < chunks)
        pl.when(ready)(lambda: reduce.after_core(jnp.minimum(q, chunks - 1)))
        actions = [functools.partial(reduce.after_stage, stage=stage) for stage in range(reduce.bits)]
        for index, action in enumerate(actions + [reduce.after_z]):
            since = jnp.maximum(c - (2 * chunks + 6 + 6 * index), -1)
            q = jnp.maximum(since, 0) // 5
            ready = (since >= 0) & (lax.rem(jnp.maximum(since, 0), 5) == 0) & (q < chunks)
            pl.when(ready)(functools.partial(action, jnp.minimum(q, chunks - 1)))

    turns = 2 * reduce.chunks + 6 + 6 * reduce.bits + 5 * (reduce.chunks - 1) + 1
    key_row = lax.broadcasted_iota(jnp.int32, (rows, rows), 0)
    column = lax.broadcasted_iota(jnp.int32, (rows, rows), 1)
    own_in.wait()
    of_queries, of_keys = pl.ds(0, width), pl.ds(width, 2 * HEAD_DIM)

    def turn_back(block, cos, sin):
        front, back = block[:HALF, :], block[HALF:, :]
        return (front * cos + back * sin).astype(BF16), (back * cos - front * sin).astype(BF16)

    def block(i, carry):
        pl.when(i != me)(lambda: arrive(grad_ref.at[i], in_recv.at[i]))
        acc[...] = jnp.zeros_like(acc)
        start = start_ref[i]
        query_row = i * rows + column
        deltas = [
            jnp.sum(
                grad_ref[i, pl.ds(h * HEAD_DIM, HEAD_DIM), :].astype(F32)
                * full_ref[i, pl.ds(h * HEAD_DIM, HEAD_DIM), :],
                0,
                keepdims=True,
            )
            for h in range(groups)
        ]

        def step(j, carry):
            key_index = key_row + j * rows
            allowed = (key_index <= query_row) & (key_index >= start)
            key_block = keys[j]
            value_block = values[j]
            key_columns = x_ref[j, width : width + HEAD_DIM, :]
            grad_keys = acc_keys[j]
            grad_values = acc_values[j]
            for h in range(groups):
                own = pl.ds(h * HEAD_DIM, HEAD_DIM)
                query = x_ref[i, own, :]
                grad = grad_ref[i, own, :]
                scores = dot(key_block, query, NN)
                scores = jnp.where(allowed, scores, NEGATIVE)
                prob = jnp.exp(scores - log_ref[i, h : h + 1, :])
                grad_prob = dot(value_block, grad, NN)
                grad_scores = (prob * (grad_prob - deltas[h])).astype(BF16)
                acc[own, :] += dot(key_columns, grad_scores, NN)
                grad_keys = grad_keys + dot(query, grad_scores, NT)
                grad_values = grad_values + dot(grad, prob.astype(BF16), NT)
            acc_keys[j] = grad_keys
            acc_values[j] = grad_values
            weight_turn(i * (i + 1) // 2 + j)
            return carry

        lax.fori_loop(0, i + 1, step, 0)
        for h in range(groups):
            at = h * HEAD_DIM
            front, back = turn_back(
                acc[pl.ds(at, HEAD_DIM), :] * SCORE_SCALE, cos_ref[i], sin_ref[i]
            )
            done[i, pl.ds(at, HALF), :] = front
            done[i, pl.ds(at + HALF, HALF), :] = back

        @pl.when(i != me)
        def _():
            to_block(
                done.at[i, of_queries], out_ref.at[me, of_queries], q_send.at[i], q_recv.at[me], i
            ).start()

        return carry

    lax.fori_loop(0, blocks, block, 0)

    def last(j, carry):
        front, back = turn_back(acc_keys[j], cos_ref[j], sin_ref[j])
        done[j, pl.ds(width, HALF), :] = front
        done[j, pl.ds(width + HALF, HALF), :] = back
        done[j, pl.ds(width + HEAD_DIM, HEAD_DIM), :] = acc_values[j].astype(BF16)

        @pl.when(j != me)
        def _():
            to_block(
                done.at[j, of_keys], out_ref.at[me, of_keys], k_send.at[j], k_recv.at[me], j
            ).start()

        return carry

    lax.fori_loop(0, blocks, last, 0)
    out_ref[me] = done[me]

    def left(c, carry):
        weight_turn(c)
        return carry

    lax.fori_loop(blocks * (blocks + 1) // 2, max(turns, blocks * (blocks + 1) // 2), left, 0)

    reduce.drain()
    for mask in range(1, wide):
        other = me ^ mask
        arrive(mine_ref.at[other], in_send.at[mask])
        arrive(done.at[other, of_queries], q_send.at[other])
        arrive(done.at[other, of_keys], k_send.at[other])
        arrive(out_ref.at[other, of_queries], q_recv.at[other])
        arrive(out_ref.at[other, of_keys], k_recv.at[other])
    own_part.wait()
    for step in range(1, narrow):
        part_copy(step).wait()


def attend_back(x, mine, full, log_total, start, cos, sin, part, weight, groups):
    wide, narrow = lax.axis_size("wide"), lax.axis_size("narrow")
    blocks, features, rows = x.shape
    width = groups * HEAD_DIM
    dma = pltpu.SemaphoreType.DMA
    hbm = pl.BlockSpec(memory_space=pl.ANY)
    vmem = pl.BlockSpec(memory_space=pltpu.VMEM)
    return pl.pallas_call(
        functools.partial(attend_back_kernel, wide, narrow, groups),
        out_shape=(
            jax.ShapeDtypeStruct(x.shape, BF16),
            jax.ShapeDtypeStruct(part.shape, BF16),
            jax.ShapeDtypeStruct((weight.shape[2] // narrow, weight.shape[3]), F32),
        ),
        in_specs=[vmem] * 7 + [hbm, hbm],
        out_specs=(vmem, hbm, vmem),
        scratch_shapes=[
            pltpu.VMEM((blocks, rows, HEAD_DIM), BF16),
            pltpu.VMEM((blocks, rows, HEAD_DIM), BF16),
            pltpu.VMEM((width, rows), F32),
            pltpu.VMEM((blocks, HEAD_DIM, rows), F32),
            pltpu.VMEM((blocks, HEAD_DIM, rows), F32),
            pltpu.VMEM((blocks, width, rows), BF16),
            pltpu.VMEM((blocks, features, rows), BF16),
            dma((1,)),
        ]
        + [dma((wide,))] * 6
        + [dma((narrow,))] * 2
        + reduce_scratch(wide, narrow, weight, 512),
        compiler_params=pltpu.CompilerParams(
            collective_id=4, has_side_effects=True, vmem_limit_bytes=50 << 20
        ),
        cost_estimate=pl.CostEstimate(
            flops=40 * width * (blocks * rows) ** 2,
            bytes_accessed=4 * x.size * 2,
            transcendentals=groups * (blocks * rows) ** 2 // 2,
        ),
    )(start, x, mine, full, log_total, cos, sin, part, weight)


def gather(x, axis):
    return lax.all_gather(x, axis, axis=0, tiled=True)


def scatter_sum(x, axis):
    return lax.psum_scatter(x, axis, scatter_dimension=0, tiled=True)


def gather_kernel(wide, narrow, aligned, qkv_ref, cut_ref, qkv_all, cut_all, x_send, x_recv, x_own, *sems):
    w, n = lax.axis_index("wide"), lax.axis_index("narrow")
    greet(wide, narrow)
    flow = Flow(wide, narrow, qkv_ref, qkv_all, sems)
    depth = qkv_ref.shape[0]
    piece = cut_all.shape[1] // (2 * wide)

    def rows_of(owner):
        return cut_all.at[pl.ds(pl.multiple_of(owner * depth, depth), depth), :]

    def pieces(other):
        if not aligned:
            return [(cut_ref.at[other], pl.ds(0, cut_all.shape[1]))]
        return [
            (
                cut_ref.at[:, pl.ds(pl.multiple_of((j * narrow + other) * piece, piece), piece)],
                pl.ds(j * piece, piece),
            )
            for j in range(2 * wide)
        ]

    def target(columns):
        return cut_all.at[pl.ds(pl.multiple_of(n * depth, depth), depth), columns]

    def cut_start(step):
        other = lax.rem(n + step, narrow)
        for source, columns in pieces(other):
            pltpu.make_async_remote_copy(
                src_ref=source,
                dst_ref=target(columns),
                send_sem=x_send.at[step],
                recv_sem=x_recv.at[step],
                device_id={"wide": w, "narrow": other},
                device_id_type=MESH,
            ).start()

    for t in range(flow.last):
        flow.step(t)
        if t == min(1, narrow - 1):
            for source, columns in pieces(n):
                pltpu.make_async_copy(source, target(columns), x_own).start()
            for step in range(1, narrow):
                cut_start(step)
    flow.end()
    own = rows_of(n)
    pltpu.make_async_copy(own, own, x_own).wait()
    for step in range(1, narrow):
        pltpu.make_async_copy(own, own, x_send.at[step]).wait()
        block = rows_of(lax.rem(n + narrow - step, narrow))
        pltpu.make_async_copy(block, block, x_recv.at[step]).wait()


def gather_weights(qkv, gateup):
    wide, narrow = lax.axis_size("wide"), lax.axis_size("narrow")
    dma = pltpu.SemaphoreType.DMA
    hbm = pl.BlockSpec(memory_space=pl.ANY)
    every = wide * narrow
    shard, columns = gateup.shape
    aligned = (columns // (2 * every)) % 128 == 0
    if not aligned:
        gateup = gateup.reshape(shard, 2, wide, narrow, -1).transpose(3, 0, 1, 2, 4)
        gateup = gateup.reshape(narrow, shard, columns // narrow)
    return pl.pallas_call(
        functools.partial(gather_kernel, wide, narrow, aligned),
        out_shape=(
            jax.ShapeDtypeStruct((every * qkv.shape[0], qkv.shape[1]), BF16),
            jax.ShapeDtypeStruct((narrow * shard, columns // narrow), BF16),
        ),
        in_specs=[hbm, hbm],
        out_specs=(hbm, hbm),
        scratch_shapes=[dma((narrow,)), dma((narrow,)), dma(())] + flow_sems(wide, narrow),
        compiler_params=pltpu.CompilerParams(collective_id=0, has_side_effects=True),
        cost_estimate=pl.CostEstimate(flops=0, bytes_accessed=200 << 20, transcendentals=0),
    )(qkv, gateup)


def feed_kernel(
    narrow, x_ref, cot_ref, gate_up_ref, down_ref,
    low_out, grad_x_ref, part_gate_up, part_down,
    group_ref, gate_up, down, cot, hidden, grads, low, came,
    load_sem, x_send, x_recv, out_sem, g_send, g_recv,
):
    w, n = lax.axis_index("wide"), lax.axis_index("narrow")
    rows, width = x_ref.shape
    own = down.shape[0]
    tile = 256
    tiles = own // tile
    wtiles = width // tile

    def to_narrow(other):
        return {"wide": w, "narrow": other}

    loads = [
        pltpu.make_async_copy(gate_up_ref, gate_up, load_sem.at[0]),
        pltpu.make_async_copy(down_ref, down, load_sem.at[1]),
        pltpu.make_async_copy(cot_ref, cot, load_sem.at[2]),
        pltpu.make_async_copy(x_ref, group_ref.at[n], load_sem.at[3]),
    ]
    for load in loads:
        load.start()

    barrier = pltpu.get_barrier_semaphore()
    for step in range(1, narrow):
        pl.semaphore_signal(
            barrier, inc=1, device_id=to_narrow(lax.rem(n + step, narrow)), device_id_type=MESH
        )
    pl.semaphore_wait(barrier, narrow - 1)

    def owner_of(side, d):
        return n - d if side == 0 else n + d

    def valid(side, d):
        return n - d >= 0 if side == 0 else (n + d < narrow) & (d > 0)

    def passes(side, d):
        if side == 0:
            return (n - d >= 0) & (n < narrow - 1)
        return (n + d < narrow) & (n > 0)

    def x_copy(side, d):
        block = group_ref.at[owner_of(side, d)]
        return pltpu.make_async_remote_copy(
            src_ref=block,
            dst_ref=block,
            send_sem=x_send.at[side, d],
            recv_sem=x_recv.at[side, d + 1],
            device_id=to_narrow(n + 1 if side == 0 else n - 1),
            device_id_type=MESH,
        )

    def x_wait(side, d):
        block = group_ref.at[owner_of(side, d)]
        pltpu.make_async_copy(block, block, x_recv.at[side, d]).wait()

    def out_copy(at, block):
        return pltpu.make_async_copy(low.at[at], low_out.at[block], out_sem.at[at])

    def g_copy(block):
        return pltpu.make_async_remote_copy(
            src_ref=cot.at[block],
            dst_ref=came.at[n],
            send_sem=g_send.at[block],
            recv_sem=g_recv.at[n],
            device_id=to_narrow(block),
            device_id_type=MESH,
        )

    def compute(side, d):
        block = n - d + 2 * d * side
        before = 1 + jnp.minimum(n, d - 1) + jnp.minimum(narrow - 1 - n, d - 1)
        before = jnp.where(d == 0, 0, before + jnp.where((side == 1) & (n - d >= 0), 1, 0))
        at = lax.rem(before, 2)

        pl.when(before >= 2)(lambda: out_copy(at, block).wait())

        def first(f, carry):
            columns = pl.ds(pl.multiple_of(f * tile, tile), tile)
            other = pl.ds(pl.multiple_of(own + f * tile, tile), tile)
            x = group_ref[block]
            gate = dot(x, gate_up[:, columns], NN)
            up = dot(x, gate_up[:, other], NN)
            grad = dot(cot[block], down[columns, :], NT)
            sig = 1.0 / (1.0 + jnp.exp(-gate))
            silu = gate * sig
            hidden[block, :, columns] = (silu * up).astype(BF16)
            grads[block, :, columns] = (grad * up * (sig + silu * (1.0 - sig))).astype(BF16)
            grads[block, :, other] = (grad * silu).astype(BF16)
            return carry

        lax.fori_loop(0, tiles, first, 0)

        def second(f, carry):
            columns = pl.ds(pl.multiple_of(f * tile, tile), tile)
            cot[block, :, columns] = dot(grads[block], gate_up[columns, :], NT, BF16)
            low[at, :, columns] = dot(hidden[block], down[:, columns], NN, BF16)
            return carry

        lax.fori_loop(0, wtiles, second, 0)
        out_copy(at, block).start()
        pl.when(block != n)(lambda: g_copy(block).start())

    def distance(d, carry):
        for side in (0, 1):

            @pl.when(valid(side, d) & (d > 0))
            def _():
                x_wait(side, d)

            @pl.when(passes(side, d))
            def _():
                x_copy(side, d).start()

        @pl.when(d == 0)
        def _():
            for load in loads[:3]:
                load.wait()

        def one(side, carry):
            ok = jnp.where(side == 0, n - d, jnp.where(d > 0, narrow - 1 - n - d, -1)) >= 0
            pl.when(ok)(lambda: compute(side, d))
            return carry

        lax.fori_loop(0, 2, one, 0)
        return carry

    loads[3].wait()
    lax.fori_loop(0, narrow, distance, 0)

    tokens = narrow * rows
    again = [
        pltpu.make_async_copy(
            cot_ref.at[o], gate_up.at[pl.ds(o * rows, rows), pl.ds(0, width)], load_sem.at[4 + o]
        )
        for o in range(narrow)
    ]
    for load in again:
        load.start()
    for at in range(2):
        out_copy(at, n).wait()

    def flipped(ref, columns):
        return jnp.concatenate([ref[o, :, columns].T for o in range(narrow)], 1)

    def weight_tile(t, left, right, at_row, out_ref, first):
        at = lax.rem(t, 2)
        copy = pltpu.make_async_copy(low.at[at], out_ref, out_sem.at[at])
        pl.when(t >= 2)(lambda: copy.wait())
        turned = flipped(left, pl.ds(pl.multiple_of(at_row, tile), tile))

        def one(c, carry):
            columns = pl.ds(pl.multiple_of(c * 512, 512), 512)
            source = pl.ds(pl.multiple_of(first + c * 512, 512), 512)
            low[at, :, columns] = dot(turned, right(source), NN, BF16)
            return carry

        lax.fori_loop(0, width // 512, one, 0)
        copy.start()

    halves = 2 * own // width

    def gate_up_tile(t, carry):
        row, half = t // halves * tile, lax.rem(t, halves) * width
        row, half = pl.multiple_of(row, tile), pl.multiple_of(half, width)
        weight_tile(
            t, group_ref, lambda source: grads[:, :, source].reshape(tokens, 512), row,
            part_gate_up.at[pl.ds(row, tile), pl.ds(half, width)], half,
        )
        return carry

    def down_tile(t, carry):
        row = pl.multiple_of(t * tile, tile)
        weight_tile(
            t + 2, hidden, lambda source: gate_up[pl.ds(0, tokens), source], row,
            part_down.at[pl.ds(row, tile), :], 0,
        )
        return carry

    lax.fori_loop(0, wtiles * halves, gate_up_tile, 0)
    for load in again:
        load.wait()
    lax.fori_loop(0, tiles, down_tile, 0)
    for at in range(2):
        out_copy(at, n).wait()
    for side in (0, 1):
        for d in range(narrow - 1):
            pl.when(passes(side, d))(lambda side=side, d=d: x_copy(side, d).wait_send())
    for step in range(1, narrow):
        other = lax.rem(n + step, narrow)
        g_copy(other).wait_send()
        block = came.at[other]
        pltpu.make_async_copy(block, block, g_recv.at[other]).wait()

    def add(r, carry):
        part = pl.ds(pl.multiple_of(r * 16, 16), 16)
        total = cot[n, part, :].astype(F32)
        for step in range(1, narrow):
            total = total + came[lax.rem(n + step, narrow), part, :].astype(F32)
        grad_x_ref[part, :] = total
        return carry

    lax.fori_loop(0, rows // 16, add, 0)


def feed(x, cot_group, gate_up, down):
    narrow = lax.axis_size("narrow")
    rows, width = x.shape
    own = down.shape[0]
    dma = pltpu.SemaphoreType.DMA
    hbm = pl.BlockSpec(memory_space=pl.ANY)
    vmem = pl.BlockSpec(memory_space=pltpu.VMEM)
    return pl.pallas_call(
        functools.partial(feed_kernel, narrow),
        out_shape=(
            jax.ShapeDtypeStruct((narrow, rows, width), BF16),
            jax.ShapeDtypeStruct((rows, width), F32),
            jax.ShapeDtypeStruct((width, 2 * own), BF16),
            jax.ShapeDtypeStruct((own, width), BF16),
        ),
        in_specs=[vmem, hbm, hbm, hbm],
        out_specs=(hbm, vmem, hbm, hbm),
        scratch_shapes=[
            pltpu.VMEM((narrow, rows, width), BF16),
            pltpu.VMEM((width, 2 * own), BF16),
            pltpu.VMEM((own, width), BF16),
            pltpu.VMEM((narrow, rows, width), BF16),
            pltpu.VMEM((narrow, rows, own), BF16),
            pltpu.VMEM((narrow, rows, 2 * own), BF16),
            pltpu.VMEM((2, rows, width), BF16),
            pltpu.VMEM((narrow, rows, width), BF16),
            dma((4 + narrow,)),
            dma((2, narrow + 1)),
            dma((2, narrow + 1)),
            dma((2,)),
            dma((narrow,)),
            dma((narrow,)),
        ],
        compiler_params=pltpu.CompilerParams(
            collective_id=1, has_side_effects=True, vmem_limit_bytes=58 << 20
        ),
        cost_estimate=pl.CostEstimate(
            flops=12 * narrow * rows * width * own, bytes_accessed=300 << 20, transcendentals=0
        ),
    )(x, cot_group.reshape(narrow, rows, width), gate_up, down)


def sum_kernel(
    wide, narrow, qkv_ref, cut_ref, gains_ref, qkv_out, cut_out, gains_out,
    cut_in, gain_w, gain_sum, gain_z, own_sem, cut_send, cut_recv, gw_send, gw_recv, gz_send, gz_recv, *refs,
):
    reduce = Reduce(wide, narrow, qkv_ref, qkv_out, refs)
    w, n = reduce.w, reduce.n
    chunks, bits = reduce.chunks, reduce.bits
    greet(wide, narrow)

    def to_wide(mask):
        return {"wide": w ^ mask, "narrow": n}

    def to_narrow(step):
        return {"wide": w, "narrow": lax.rem(n + step, narrow)}

    own_cut = pltpu.make_async_copy(cut_ref.at[n], cut_in.at[n], own_sem)

    def cut_copy(step):
        return pltpu.make_async_remote_copy(
            src_ref=cut_ref.at[lax.rem(n + step, narrow)],
            dst_ref=cut_in.at[n],
            send_sem=cut_send.at[step],
            recv_sem=cut_recv.at[step],
            device_id=to_narrow(step),
            device_id_type=MESH,
        )

    def gw_copy(mask):
        return pltpu.make_async_remote_copy(
            src_ref=gains_ref.at[w ^ mask],
            dst_ref=gain_w.at[mask],
            send_sem=gw_send.at[mask],
            recv_sem=gw_recv.at[mask],
            device_id=to_wide(mask),
            device_id_type=MESH,
        )

    def gz_copy(step):
        return pltpu.make_async_remote_copy(
            src_ref=gain_sum.at[lax.rem(n + step, narrow)],
            dst_ref=gain_z.at[step],
            send_sem=gz_send.at[step],
            recv_sem=gz_recv.at[step],
            device_id=to_narrow(step),
            device_id_type=MESH,
        )

    ahead = min(4, chunks)
    for q in range(ahead):
        reduce.begin(q)
    own_cut.start()
    for step in range(1, narrow):
        cut_copy(step).start()
    for mask in range(1, wide):
        gw_copy(mask).start()

    def turn(t, carry):
        pl.when(t + ahead < chunks)(lambda: reduce.begin(t + ahead))
        pl.when(t < chunks)(lambda: reduce.after_core(t))
        for stage in range(bits):
            q = t - 1 - stage
            pl.when((q >= 0) & (q < chunks))(functools.partial(reduce.after_stage, q, stage))
        q = t - 1 - bits
        pl.when(q >= 0)(lambda: reduce.after_z(q))
        return carry

    lax.fori_loop(0, chunks + bits + 1, turn, 0)

    total = gains_ref[w]
    for mask in range(1, wide):
        block = gain_w.at[mask]
        pltpu.make_async_copy(block, block, gw_recv.at[mask]).wait()
        total = total + gain_w[mask]
    gain_sum[...] = total
    for step in range(1, narrow):
        gz_copy(step).start()

    own_cut.wait()
    for step in range(1, narrow):
        other = lax.rem(n + narrow - step, narrow)
        arrive(cut_in.at[other], cut_recv.at[step])
    piece = cut_in.shape[2] // (2 * wide)
    if cut_out.shape[0] == narrow:
        for other in range(narrow):
            cut_out[other] = cut_in[other].astype(F32)
    else:
        for j in range(2 * wide):
            for other in range(narrow):
                cut_out[:, pl.ds((j * narrow + other) * piece, piece)] = cut_in[
                    other, :, pl.ds(j * piece, piece)
                ].astype(F32)

    total = gain_sum[n]
    for step in range(1, narrow):
        block = gain_z.at[step]
        pltpu.make_async_copy(block, block, gz_recv.at[step]).wait()
        total = total + gain_z[step]
    gains_out[...] = total

    for mask in range(1, wide):
        gw_copy(mask).wait_send()
    for step in range(1, narrow):
        gz_copy(step).wait_send()
        cut_copy(step).wait_send()
    reduce.drain()


def sum_all(qkv, cut, gains):
    wide, narrow = lax.axis_size("wide"), lax.axis_size("narrow")
    shard, cut_width = cut.shape[1:]
    aligned = (cut_width // (2 * wide)) % 128 == 0
    cut_shape = (shard, narrow * cut_width) if aligned else cut.shape
    dma = pltpu.SemaphoreType.DMA
    hbm = pl.BlockSpec(memory_space=pl.ANY)
    vmem = pl.BlockSpec(memory_space=pltpu.VMEM)
    results = pl.pallas_call(
        functools.partial(sum_kernel, wide, narrow),
        out_shape=(
            jax.ShapeDtypeStruct((shard, qkv.shape[3]), F32),
            jax.ShapeDtypeStruct(cut_shape, F32),
            jax.ShapeDtypeStruct((8, 128), F32),
        ),
        in_specs=[hbm, hbm, vmem],
        out_specs=(vmem, vmem, vmem),
        scratch_shapes=[
            pltpu.VMEM(cut.shape, BF16),
            pltpu.VMEM((wide, narrow, 8, 128), F32),
            pltpu.VMEM((narrow, 8, 128), F32),
            pltpu.VMEM((narrow, 8, 128), F32),
            dma(()),
            dma((narrow,)),
            dma((narrow,)),
            dma((wide,)),
            dma((wide,)),
            dma((narrow,)),
            dma((narrow,)),
        ]
        + reduce_scratch(wide, narrow, qkv, 256),
        compiler_params=pltpu.CompilerParams(
            collective_id=2, has_side_effects=True, vmem_limit_bytes=54 << 20
        ),
        cost_estimate=pl.CostEstimate(flops=0, bytes_accessed=300 << 20, transcendentals=0),
    )(qkv, cut, gains)
    return results, aligned


def per_device(tokens, lengths, gain_attn, w_qkv, w_out, gain_mlp, w_gateup, w_down, cotangent):
    rows, width = tokens.shape[1:]
    wide, narrow = lax.axis_size("wide"), lax.axis_size("narrow")
    pack_rows = rows * wide
    query_width, key_width = HEADS * HEAD_DIM, KV_HEADS * HEAD_DIM
    groups = HEADS // wide
    copies = wide // KV_HEADS
    own_ff = FF // narrow
    first, positions = places(lengths[0], pack_rows)
    cos_all, sin_all = rotary(positions.astype(F32), HALF)
    first_row = lax.axis_index("wide") * rows
    cos = lax.dynamic_slice_in_dim(cos_all, first_row, rows, 1)
    sin = lax.dynamic_slice_in_dim(sin_all, first_row, rows, 1)
    cos_all = cos_all.reshape(HALF, wide, rows).transpose(1, 0, 2)
    sin_all = sin_all.reshape(HALF, wide, rows).transpose(1, 0, 2)
    start = first.reshape(wide, 1, rows)

    gains = jnp.stack([gain_attn, gain_mlp], -1)
    with_gains = jnp.concatenate([w_qkv, jnp.pad(gains, ((0, 0), (0, 126)))], -1)
    shard = w_gateup.shape[0]
    qkv_gained, gateup_rows = gather_weights(with_gains, w_gateup)
    qkv_whole = qkv_gained[:, : w_qkv.shape[1]]
    gain_one = qkv_gained[:, w_qkv.shape[1]].astype(F32)
    gain_two = qkv_gained[:, w_qkv.shape[1] + 1].astype(F32)
    gateup_own = gather(gateup_rows, "wide")
    down_own = gather(w_down, "wide")

    inputs = tokens[0].astype(F32)
    scale_one = lax.rsqrt(jnp.mean(inputs * inputs, -1, keepdims=True) + EPS)
    unit_one = inputs * scale_one
    normed_one = (unit_one * gain_one).astype(BF16)
    projected = dot(qkv_whole, normed_one, (((0,), (1,)), ((), ())))
    turning = projected[: query_width + key_width].reshape(HEADS + KV_HEADS, 2, HALF, rows)
    front, back = turning[:, 0], turning[:, 1]
    turned = jnp.stack([front * cos - back * sin, back * cos + front * sin], 1)
    queries = (turned[:HEADS] * SCORE_SCALE).astype(BF16).reshape(wide, groups * HEAD_DIM, rows)
    keys = turned[HEADS:].astype(BF16).reshape(KV_HEADS, HEAD_DIM, rows)
    values = projected[query_width + key_width :].astype(BF16).reshape(KV_HEADS, HEAD_DIM, rows)
    keys_values = jnp.repeat(jnp.concatenate([keys, values], 1), copies, 0)
    heads, attended_low, attended_full, log_total, out_whole, cot_group = attend(
        jnp.concatenate([queries, keys_values], 1), start, w_out, cotangent[0], groups
    )
    cot_group = cot_group.reshape(-1, width)
    attended_low = attended_low.reshape(query_width, rows)
    middle = inputs + dot(attended_low, out_whole, TN)
    scale_two = lax.rsqrt(jnp.mean(middle * middle, -1, keepdims=True) + EPS)
    unit_two = middle * scale_two
    normed_two = (unit_two * gain_two).astype(BF16)

    low_part, grad_normed_two, part_gateup, part_down = feed(
        normed_two, cot_group, gateup_own, down_own
    )
    grad_gateup = scatter_sum(part_gateup, "wide").reshape(narrow, shard, 2 * own_ff)
    grad_down = scatter_sum(part_down, "wide")
    part_gain_two = jnp.sum(grad_normed_two * unit_two, 0)
    grad_middle = cotangent[0].astype(F32) + norm_back(
        grad_normed_two * gain_two, unit_two, scale_two
    )
    grad_branch = grad_middle.astype(BF16)
    grad_attended = dot(out_whole, grad_branch, NT, BF16).reshape(wide, groups * HEAD_DIM, rows)
    cut = (wide // 2, 2, narrow * shard, -1)
    part_wout = dot(attended_low, grad_branch, NN, BF16).reshape(cut)
    grad_heads, low_came, grad_wout = attend_back(
        heads, grad_attended, attended_full, log_total, start, cos_all, sin_all, low_part, part_wout,
        groups,
    )
    layer_out = (middle + jnp.sum(low_came.astype(F32), 0)).astype(BF16)[None]
    grad_queries = grad_heads[:, : groups * HEAD_DIM].reshape(query_width, rows)
    grad_keys_values = (
        grad_heads[:, groups * HEAD_DIM :]
        .reshape(KV_HEADS, copies, 2, HEAD_DIM, rows)
        .astype(F32)
        .sum(1)
        .astype(BF16)
    )
    grad_projected = jnp.concatenate(
        [
            grad_queries,
            grad_keys_values[:, 0].reshape(key_width, rows),
            grad_keys_values[:, 1].reshape(key_width, rows),
        ],
        0,
    )
    grad_normed_one = dot(grad_projected, qkv_whole, (((0,), (1,)), ((), ())))
    part_gain_one = jnp.sum(grad_normed_one * unit_one, 0)
    part_gains = jnp.stack([part_gain_one, part_gain_two], 0).reshape(2, wide, narrow, shard)
    part_gains = jnp.pad(
        part_gains.transpose(1, 2, 0, 3), ((0, 0), (0, 0), (0, 6), (0, 128 - shard))
    )
    part_qkv = dot(normed_one, grad_projected, (((0,), (1,)), ((), ())), BF16).reshape(cut)
    (grad_qkv, grad_gateup, grad_gains), done = sum_all(part_qkv, grad_gateup, part_gains)
    if not done:
        grad_gateup = (
            grad_gateup.reshape(narrow, shard, 2, wide, -1)
            .transpose(1, 2, 3, 0, 4)
            .reshape(shard, 2 * FF)
        )
    grad_down, grad_gains = lax.optimization_barrier((grad_down, grad_gains))
    grad_down = grad_down.astype(F32)
    grad_inputs = grad_middle + norm_back(grad_normed_one * gain_one, unit_one, scale_one)
    grad_tokens = grad_inputs.astype(BF16)[None]
    return (
        layer_out,
        grad_tokens,
        grad_gains[0, :shard],
        grad_qkv,
        grad_wout,
        grad_gains[1, :shard],
        grad_gateup,
        grad_down,
    )


def solution(mesh):
    rows, packs = P("narrow", "wide", None), P("narrow", None)
    weight, gain = P(BOTH, None), P(BOTH)
    return jax.shard_map(
        per_device,
        mesh=mesh,
        in_specs=(rows, packs, gain, weight, weight, gain, weight, weight, rows),
        out_specs=(rows, rows, gain, weight, weight, gain, weight, weight),
        check_vma=False,
    )
```

```python
import functools
import math

import jax
import jax.numpy as jnp
from jax import lax
from jax.experimental import pallas as pl
from jax.experimental.pallas import tpu as pltpu
from jax.sharding import PartitionSpec as P

FF = 8192
HEADS = 32
KV_HEADS = 8
HEAD_DIM = 64
HALF = HEAD_DIM // 2
EPS = 1e-05
NEGATIVE = -1e30
SCORE_SCALE = 1.0 / math.sqrt(HEAD_DIM)
BOTH = ("wide", "narrow")
F32 = jnp.float32
BF16 = jnp.bfloat16
NN = (((1,), (0,)), ((), ()))
NT = (((1,), (1,)), ((), ()))
TN = (((0,), (0,)), ((), ()))


def dot(left, right, dims, kind=F32):
    return lax.dot_general(left, right, dims, preferred_element_type=F32).astype(kind)


def places(lengths_row, total_rows):
    seq_ends = jnp.cumsum(lengths_row)
    starts = seq_ends - lengths_row
    row_index = jnp.arange(total_rows, dtype=jnp.int32)
    segments = jnp.sum((row_index[:, None] >= seq_ends[None, :]).astype(jnp.int32), -1)
    slot_index = jnp.arange(lengths_row.shape[0], dtype=jnp.int32)
    owned = segments[:, None] == slot_index[None, :]
    first = jnp.sum(jnp.where(owned, starts[None, :], 0), -1)
    return first, row_index - first


def rotary(positions, half_width):
    channel = jnp.arange(half_width, dtype=jnp.float32)
    inverse_rate = jnp.power(500000.0, -channel / half_width)
    wavelength = 2.0 * math.pi / inverse_rate
    smooth = (8192.0 / wavelength - 1.0) / 3.0
    blended = (1.0 - smooth) * inverse_rate / 32.0 + smooth * inverse_rate
    frequency = jnp.where(
        wavelength < 2048.0,
        inverse_rate,
        jnp.where(wavelength > 8192.0, inverse_rate / 32.0, blended),
    )
    angles = frequency[:, None] * positions[None, :]
    return jnp.cos(angles), jnp.sin(angles)


def norm_back(grad_unit, unit_rows, row_scale):
    return row_scale * (grad_unit - unit_rows * jnp.mean(grad_unit * unit_rows, -1, keepdims=True))


MESH = pl.DeviceIdType.MESH


class Flow:
    def __init__(self, wide, narrow, x_ref, out_ref, sems):
        self.wide, self.narrow, self.x_ref, self.out_ref = wide, narrow, x_ref, out_ref
        self.w, self.n = lax.axis_index("wide"), lax.axis_index("narrow")
        (self.own_sem, self.z_send, self.z_recv, self.m_send, self.m_recv,
         self.r_send, self.r_recv, self.c_send, self.c_recv) = sems
        self.relay = wide == 8
        self.masks = [2, 4] if self.relay else list(range(2, wide, 2))
        self.last = narrow + 2

    def to_wide(self, mask):
        return {"wide": self.w ^ mask, "narrow": self.n}

    def owner_of(self, side, d):
        return self.n - d if side == 0 else self.n + d

    def valid(self, side, d):
        return self.n - d >= 0 if side == 0 else self.n + d < self.narrow

    def can_pass(self, side, d):
        if side == 0:
            return (self.n - (d - 1) >= 0) & (self.n < self.narrow - 1)
        return (self.n + (d - 1) < self.narrow) & (self.n > 0)

    def slot(self, side, d):
        return d - 1 + side * (self.narrow - 1) if d else 2 * (self.narrow - 1)

    def at_distance(self, d, action):
        if d == 0:
            action(0, 0)
            return
        for side in (0, 1):
            pl.when(self.valid(side, d))(functools.partial(action, side, d))

    def place(self, owner_w, owner_n, part=None):
        depth = self.x_ref.shape[0]
        half = depth // 2
        at = (owner_w * self.narrow + owner_n) * depth
        if part is None:
            return self.out_ref.at[pl.ds(pl.multiple_of(at, depth), depth), :]
        return self.out_ref.at[pl.ds(pl.multiple_of(at + part * half, half), half), :]

    def own_copy(self):
        return pltpu.make_async_copy(self.x_ref, self.place(self.w, self.n), self.own_sem)

    def z_copy(self, side, d):
        block = self.place(self.w, self.owner_of(side, d - 1))
        return pltpu.make_async_remote_copy(
            src_ref=self.x_ref if d == 1 else block,
            dst_ref=block,
            send_sem=self.z_send.at[side, d],
            recv_sem=self.z_recv.at[side, d],
            device_id={"wide": self.w, "narrow": self.n + 1 if side == 0 else self.n - 1},
            device_id_type=MESH,
        )

    def z_wait(self, side, d):
        block = self.place(self.w, self.owner_of(side, d))
        pltpu.make_async_copy(block, block, self.z_recv.at[side, d]).wait()

    def m_copy(self, i, side, d):
        block = self.place(self.w, self.owner_of(side, d))
        return pltpu.make_async_remote_copy(
            src_ref=self.x_ref if d == 0 else block,
            dst_ref=block,
            send_sem=self.m_send.at[i, self.slot(side, d)],
            recv_sem=self.m_recv.at[i, self.slot(side, d)],
            device_id=self.to_wide(self.masks[i]),
            device_id_type=MESH,
        )

    def m_wait(self, i, side, d):
        block = self.place(self.w ^ self.masks[i], self.owner_of(side, d))
        pltpu.make_async_copy(block, block, self.m_recv.at[i, self.slot(side, d)]).wait()

    def r_copy(self, part, side, d):
        block = self.place(self.w ^ self.masks[part], self.owner_of(side, d), part)
        return pltpu.make_async_remote_copy(
            src_ref=block,
            dst_ref=block,
            send_sem=self.r_send.at[part, self.slot(side, d)],
            recv_sem=self.r_recv.at[part, self.slot(side, d)],
            device_id=self.to_wide(self.masks[1 - part]),
            device_id_type=MESH,
        )

    def r_wait(self, part, side, d):
        block = self.place(self.w ^ 6, self.owner_of(side, d), part)
        pltpu.make_async_copy(block, block, self.r_recv.at[part, self.slot(side, d)]).wait()

    def c_copy(self, chip, side, d):
        block = self.place(self.w ^ (2 * chip), self.owner_of(side, d))
        return pltpu.make_async_remote_copy(
            src_ref=self.x_ref if d == 0 and chip == 0 else block,
            dst_ref=block,
            send_sem=self.c_send.at[chip, self.slot(side, d)],
            recv_sem=self.c_recv.at[chip, self.slot(side, d)],
            device_id=self.to_wide(1),
            device_id_type=MESH,
        )

    def c_wait(self, chip, side, d):
        block = self.place((self.w ^ 1) ^ (2 * chip), self.owner_of(side, d))
        pltpu.make_async_copy(block, block, self.c_recv.at[chip, self.slot(side, d)]).wait()

    def send_from_here(self, side, d):
        if d > 0:
            self.z_wait(side, d)
        if 0 < d < self.narrow - 1:
            pl.when(self.can_pass(side, d + 1))(lambda: self.z_copy(side, d + 1).start())
        for i in range(len(self.masks)):
            self.m_copy(i, side, d).start()
        self.c_copy(0, side, d).start()

    def send_on(self, side, d):
        for i in range(len(self.masks)):
            self.m_wait(i, side, d)
            if self.relay:
                self.r_copy(i, side, d).start()
            self.c_copy(self.masks[i] // 2, side, d).start()

    def send_last(self, side, d):
        self.r_wait(0, side, d)
        self.r_wait(1, side, d)
        self.c_copy(3, side, d).start()

    def step(self, t):
        if t == 0:
            self.own_copy().start()
            for side in (0, 1):
                pl.when(self.can_pass(side, 1))(lambda side=side: self.z_copy(side, 1).start())
        if 0 <= t < self.narrow:
            self.at_distance(t, self.send_from_here)
        if 0 <= t - 1 < self.narrow:
            self.at_distance(t - 1, self.send_on)
        if self.relay and 0 <= t - 2 < self.narrow:
            self.at_distance(t - 2, self.send_last)

    def finish(self, side, d):
        for i in range(len(self.masks)):
            self.m_copy(i, side, d).wait_send()
            if self.relay:
                self.r_copy(i, side, d).wait_send()
        for chip in range(self.wide // 2):
            self.c_copy(chip, side, d).wait_send()
            self.c_wait(chip, side, d)

    def end(self):
        self.own_copy().wait()
        for side in (0, 1):
            for d in range(1, self.narrow):
                pl.when(self.can_pass(side, d))(
                    lambda side=side, d=d: self.z_copy(side, d).wait_send()
                )
        for d in range(self.narrow):
            self.at_distance(d, self.finish)


class Line:
    def __init__(self, narrow, x_ref, out_ref, sems):
        self.narrow, self.x_ref, self.out_ref = narrow, x_ref, out_ref
        self.w, self.n = lax.axis_index("wide"), lax.axis_index("narrow")
        self.own_sem, self.send, self.recv = sems

    def owner_of(self, side, d):
        return self.n - d if side == 0 else self.n + d

    def valid(self, side, d):
        return self.n - d >= 0 if side == 0 else self.n + d < self.narrow

    def can_pass(self, side, d):
        if side == 0:
            return (self.n - (d - 1) >= 0) & (self.n < self.narrow - 1)
        return (self.n + (d - 1) < self.narrow) & (self.n > 0)

    def own_copy(self):
        return pltpu.make_async_copy(self.x_ref, self.out_ref.at[self.n], self.own_sem)

    def copy(self, side, d):
        block = self.out_ref.at[self.owner_of(side, d - 1)]
        return pltpu.make_async_remote_copy(
            src_ref=self.x_ref if d == 1 else block,
            dst_ref=block,
            send_sem=self.send.at[side, d],
            recv_sem=self.recv.at[side, d],
            device_id={"wide": self.w, "narrow": self.n + 1 if side == 0 else self.n - 1},
            device_id_type=MESH,
        )

    def pass_on(self, side, d):
        arrive(self.out_ref.at[self.owner_of(side, d)], self.recv.at[side, d])
        if d < self.narrow - 1:
            pl.when(self.can_pass(side, d + 1))(lambda: self.copy(side, d + 1).start())

    def step(self, t):
        if t == 0:
            self.own_copy().start()
        for side in (0, 1):
            if t == 0:
                pl.when(self.can_pass(side, 1))(lambda side=side: self.copy(side, 1).start())
            else:
                pl.when(self.valid(side, t))(lambda side=side: self.pass_on(side, t))

    def end(self):
        self.own_copy().wait()
        for side in (0, 1):
            for d in range(1, self.narrow):
                pl.when(self.can_pass(side, d))(lambda side=side, d=d: self.copy(side, d).wait_send())


def flow_sems(wide, narrow):
    slots = 2 * narrow - 1
    masks = 2 if wide == 8 else wide // 2 - 1
    dma = pltpu.SemaphoreType.DMA
    return [
        dma(()),
        dma((2, narrow)),
        dma((2, narrow)),
        dma((masks, slots)),
        dma((masks, slots)),
        dma((2, slots)),
        dma((2, slots)),
        dma((wide // 2, slots)),
        dma((wide // 2, slots)),
    ]


class Reduce:
    def __init__(self, wide, narrow, source, out_ref, refs):
        self.wide, self.narrow, self.source, self.out_ref = wide, narrow, source, out_ref
        self.w, self.n = lax.axis_index("wide"), lax.axis_index("narrow")
        self.core, self.chip = lax.rem(self.w, 2), self.w // 2
        self.chips = wide // 2
        self.bits = self.chips.bit_length() - 1
        (self.held, self.core_in, self.chip_in, self.z_in, self.load_sem, self.core_send, self.core_recv,
         self.chip_send, self.chip_recv, self.z_send, self.z_recv) = refs
        self.chunks = self.held.shape[0]
        self.rows, self.chunk = self.held.shape[2:]
        self.shard = self.rows // narrow
        self.orders = [list(range(self.bits)), list(range(self.bits))[::-1]]

    def columns_of(self, q):
        return pl.ds(pl.multiple_of(q * self.chunk, self.chunk), self.chunk)

    def begin(self, q):
        pltpu.make_async_copy(
            self.source.at[:, self.core, :, self.columns_of(q)], self.held.at[q], self.load_sem.at[q]
        ).start()
        pltpu.make_async_remote_copy(
            src_ref=self.source.at[:, 1 - self.core, :, self.columns_of(q)],
            dst_ref=self.core_in.at[q],
            send_sem=self.core_send.at[q],
            recv_sem=self.core_recv.at[q],
            device_id={"wide": self.w ^ 1, "narrow": self.n},
            device_id_type=MESH,
        ).start()

    def add_to(self, target, other):
        def one(r, carry):
            part = pl.ds(pl.multiple_of(r * 16, 16), 16)
            target(part)[...] = (
                target(part)[...].astype(F32) + other(part)[...].astype(F32)
            ).astype(BF16)
            return carry

        lax.fori_loop(0, self.rows // 16, one, 0)

    def tiles_of(self, h, stage):
        order = self.orders[h]
        rest = order[stage + 1 :]
        offset = sum(self.chips >> (i + 1) for i in range(stage))
        fixed = sum(1 << b for b in order[: stage + 1])
        result = []
        for v in range(1 << len(rest)):
            extra = sum(((v >> i) & 1) << b for i, b in enumerate(rest))
            result.append((offset + v, (self.chip & fixed) + extra))
        return result

    def lanes(self, h):
        return pl.ds(h * (self.chunk // 2), self.chunk // 2)

    def chip_copy(self, q, h, stage, slot, kept):
        bit = self.orders[h][stage]
        return pltpu.make_async_remote_copy(
            src_ref=self.held.at[q, kept ^ (1 << bit), :, self.lanes(h)],
            dst_ref=self.chip_in.at[q, h, slot],
            send_sem=self.chip_send.at[q, h, slot],
            recv_sem=self.chip_recv.at[q, h, slot],
            device_id={"wide": self.w ^ (2 << bit), "narrow": self.n},
            device_id_type=MESH,
        )

    def send_stage(self, q, stage):
        for h in (0, 1):
            for slot, kept in self.tiles_of(h, stage):
                self.chip_copy(q, h, stage, slot, kept).start()

    def after_core(self, q):
        pltpu.make_async_copy(self.held.at[q], self.held.at[q], self.load_sem.at[q]).wait()
        arrive(self.core_in.at[q], self.core_recv.at[q])
        for k in range(self.chips):
            self.add_to(
                lambda part, k=k: self.held.at[q, k, part, :],
                lambda part, k=k: self.core_in.at[q, k, part, :],
            )
        self.send_stage(q, 0)

    def z_copy(self, q, step):
        other = lax.rem(self.n + step, self.narrow)
        own = pl.ds(pl.multiple_of(other * self.shard, self.shard), self.shard)
        return pltpu.make_async_remote_copy(
            src_ref=self.held.at[q, self.chip, own, :],
            dst_ref=self.z_in.at[q, step],
            send_sem=self.z_send.at[q, step],
            recv_sem=self.z_recv.at[q, step],
            device_id={"wide": self.w, "narrow": other},
            device_id_type=MESH,
        )

    def after_stage(self, q, stage):
        for h in (0, 1):
            for slot, kept in self.tiles_of(h, stage):
                arrive(self.chip_in.at[q, h, slot], self.chip_recv.at[q, h, slot])
                self.add_to(
                    lambda part, h=h, kept=kept: self.held.at[q, kept, part, self.lanes(h)],
                    lambda part, h=h, slot=slot: self.chip_in.at[q, h, slot, part, :],
                )
        if stage + 1 < self.bits:
            self.send_stage(q, stage + 1)
        else:
            for step in range(1, self.narrow):
                self.z_copy(q, step).start()

    def after_z(self, q):
        for step in range(1, self.narrow):
            arrive(self.z_in.at[q, step], self.z_recv.at[q, step])

        def one(r, carry):
            to = pl.ds(pl.multiple_of(r * 16, 16), 16)
            own = pl.ds(pl.multiple_of(self.n * self.shard + r * 16, 16), 16)
            value = self.held[q, self.chip, own, :].astype(F32)
            for step in range(1, self.narrow):
                value = value + self.z_in[q, step, to, :].astype(F32)
            self.out_ref[to, self.columns_of(q)] = value
            return carry

        lax.fori_loop(0, self.shard // 16, one, 0)

    def after_all(self):
        def one(q, carry):
            self.after_z(q)
            return carry

        lax.fori_loop(0, self.chunks, one, 0)

    def drain(self):
        def one(q, carry):
            arrive(self.core_in.at[q], self.core_send.at[q])
            for stage in range(self.bits):
                for h in (0, 1):
                    for slot, kept in self.tiles_of(h, stage):
                        self.chip_copy(q, h, stage, slot, kept).wait_send()
            for step in range(1, self.narrow):
                self.z_copy(q, step).wait_send()
            return carry

        lax.fori_loop(0, self.chunks, one, 0)


def reduce_scratch(wide, narrow, source, chunk):
    chips, rows, chunks = wide // 2, source.shape[2], source.shape[3] // chunk
    dma = pltpu.SemaphoreType.DMA
    return [
        pltpu.VMEM((chunks, chips, rows, chunk), BF16),
        pltpu.VMEM((chunks, chips, rows, chunk), BF16),
        pltpu.VMEM((chunks, 2, chips - 1, rows, chunk // 2), BF16),
        pltpu.VMEM((chunks, narrow, rows // narrow, chunk), BF16),
        dma((chunks,)),
        dma((chunks,)),
        dma((chunks,)),
        dma((chunks, 2, chips - 1)),
        dma((chunks, 2, chips - 1)),
        dma((chunks, narrow)),
        dma((chunks, narrow)),
    ]


def greet(wide, narrow):
    w, n = lax.axis_index("wide"), lax.axis_index("narrow")
    barrier = pltpu.get_barrier_semaphore()
    for mask in range(1, wide):
        pl.semaphore_signal(
            barrier, inc=1, device_id={"wide": w ^ mask, "narrow": n}, device_id_type=MESH
        )
    for step in range(1, narrow):
        other = lax.rem(n + step, narrow)
        pl.semaphore_signal(
            barrier, inc=1, device_id={"wide": w, "narrow": other}, device_id_type=MESH
        )
    pl.semaphore_wait(barrier, wide + narrow - 2)


def to_owner(source, target, send_sem, recv_sem, mask):
    w, n = lax.axis_index("wide"), lax.axis_index("narrow")
    return pltpu.make_async_remote_copy(
        src_ref=source,
        dst_ref=target,
        send_sem=send_sem,
        recv_sem=recv_sem,
        device_id={"wide": w ^ mask, "narrow": n},
        device_id_type=MESH,
    )


def to_block(source, target, send_sem, recv_sem, owner):
    n = lax.axis_index("narrow")
    return pltpu.make_async_remote_copy(
        src_ref=source,
        dst_ref=target,
        send_sem=send_sem,
        recv_sem=recv_sem,
        device_id={"wide": owner, "narrow": n},
        device_id_type=MESH,
    )


def arrive(block, sem):
    pltpu.make_async_copy(block, block, sem).wait()


def attend_kernel(
    wide, narrow, groups, start_ref, mine_ref, w_ref, c_ref,
    x_ref, low_ref, full_ref, log_ref, w_all, c_all,
    keys, top, total, acc, done, own_sem, in_send, in_recv, out_send, out_recv,
    line_own, line_send, line_recv, *sems,
):
    me = lax.axis_index("wide")
    blocks, _, rows = x_ref.shape
    width = groups * HEAD_DIM
    own_in = pltpu.make_async_copy(mine_ref.at[me], x_ref.at[me], own_sem.at[0])
    own_in.start()
    greet(wide, narrow)
    for mask in range(1, wide):
        to_owner(
            mine_ref.at[me ^ mask], x_ref.at[me], in_send.at[mask], in_recv.at[me], mask
        ).start()
    flow = Flow(wide, narrow, w_ref, w_all, sems)
    line = Line(narrow, c_ref, c_all, (line_own, line_send, line_recv))
    flow.step(0)
    line.step(0)
    spread = {}
    for t in range(1, flow.last):
        spread.setdefault(min(blocks, blocks // 2 - 1 + t), []).append(functools.partial(flow.step, t))
    for t in range(1, narrow):
        spread.setdefault(min(blocks, blocks // 2 + 2 * t - 1), []).append(functools.partial(line.step, t))
    key_row = lax.broadcasted_iota(jnp.int32, (rows, rows), 0)
    column = lax.broadcasted_iota(jnp.int32, (rows, rows), 1)
    own_in.wait()

    def block(i, carry):
        pl.when(i != me)(lambda: arrive(x_ref.at[i], in_recv.at[i]))
        for at, actions in spread.items():
            if at < blocks:

                @pl.when(i == at)
                def _():
                    for action in actions:
                        action()

        keys[i] = x_ref[i, width : width + HEAD_DIM, :].T
        top[...] = jnp.full_like(top, NEGATIVE)
        total[...] = jnp.zeros_like(total)
        acc[...] = jnp.zeros_like(acc)
        start = start_ref[i]
        query_row = i * rows + column

        def step(j, carry):
            key_index = key_row + j * rows
            allowed = (key_index <= query_row) & (key_index >= start)
            key_block = keys[j]
            value_block = x_ref[j, width + HEAD_DIM :, :]
            for h in range(groups):
                own = pl.ds(h * HEAD_DIM, HEAD_DIM)
                scores = dot(key_block, x_ref[i, own, :], NN)
                scores = jnp.where(allowed, scores, NEGATIVE)
                old = top[h : h + 1, :]
                new = jnp.maximum(old, jnp.max(scores, 0, keepdims=True))
                shrink = jnp.exp(old - new)
                prob = jnp.exp(scores - new)
                top[h : h + 1, :] = new
                total[h : h + 1, :] = total[h : h + 1, :] * shrink + jnp.sum(prob, 0, keepdims=True)
                acc[own, :] = acc[own, :] * shrink + dot(value_block, prob.astype(BF16), NN)
            return carry

        lax.fori_loop(0, i + 1, step, 0)
        log_ref[i] = top[...] + jnp.log(total[...])
        for h in range(groups):
            own = pl.ds(h * HEAD_DIM, HEAD_DIM)
            result = acc[own, :] / total[h : h + 1, :]
            full_ref[i, own, :] = result
            done[i, own, :] = result.astype(BF16)

        @pl.when(i != me)
        def _():
            to_block(done.at[i], low_ref.at[me], out_send.at[i], out_recv.at[me], i).start()

        return carry

    lax.fori_loop(0, blocks, block, 0)
    low_ref[me] = done[me]
    for action in spread.get(blocks, []):
        action()
    flow.end()
    line.end()
    for mask in range(1, wide):
        to_owner(
            mine_ref.at[me ^ mask], x_ref.at[me], in_send.at[mask], in_recv.at[me], mask
        ).wait_send()
        other = me ^ mask
        arrive(low_ref.at[other], out_recv.at[other])
        arrive(done.at[other], out_send.at[other])


def attend(mine, start, w_out, cot, groups):
    wide, narrow = lax.axis_size("wide"), lax.axis_size("narrow")
    blocks, features, rows = mine.shape
    width = groups * HEAD_DIM
    dma = pltpu.SemaphoreType.DMA
    hbm = pl.BlockSpec(memory_space=pl.ANY)
    vmem = pl.BlockSpec(memory_space=pltpu.VMEM)
    return pl.pallas_call(
        functools.partial(attend_kernel, wide, narrow, groups),
        out_shape=(
            jax.ShapeDtypeStruct((blocks, features, rows), BF16),
            jax.ShapeDtypeStruct((blocks, width, rows), BF16),
            jax.ShapeDtypeStruct((blocks, width, rows), F32),
            jax.ShapeDtypeStruct((blocks, groups, rows), F32),
            jax.ShapeDtypeStruct((wide * narrow * w_out.shape[0], w_out.shape[1]), BF16),
            jax.ShapeDtypeStruct((narrow,) + cot.shape, BF16),
        ),
        in_specs=[vmem, vmem, hbm, hbm],
        out_specs=(vmem, vmem, vmem, vmem, hbm, hbm),
        scratch_shapes=[
            pltpu.VMEM((blocks, rows, HEAD_DIM), BF16),
            pltpu.VMEM((groups, rows), F32),
            pltpu.VMEM((groups, rows), F32),
            pltpu.VMEM((width, rows), F32),
            pltpu.VMEM((blocks, width, rows), BF16),
            dma((1,)),
            dma((wide,)),
            dma((wide,)),
            dma((wide,)),
            dma((wide,)),
            dma(()),
            dma((2, narrow)),
            dma((2, narrow)),
        ]
        + flow_sems(wide, narrow),
        compiler_params=pltpu.CompilerParams(
            collective_id=3, has_side_effects=True, vmem_limit_bytes=40 << 20
        ),
        cost_estimate=pl.CostEstimate(
            flops=32 * width * (blocks * rows) ** 2,
            bytes_accessed=64 << 20,
            transcendentals=groups * (blocks * rows) ** 2 // 2,
        ),
    )(start, mine, w_out, cot)


def attend_back_kernel(
    wide, narrow, groups, start_ref, x_ref, mine_ref, full_ref, log_ref, cos_ref, sin_ref, part_ref,
    weight_ref, out_ref, came_ref, weight_out,
    keys, values, acc, acc_keys, acc_values, grad_ref, done, own_sem, in_send, in_recv,
    q_send, q_recv, k_send, k_recv, p_send, p_recv, *refs,
):
    reduce = Reduce(wide, narrow, weight_ref, weight_out, refs)
    me, n = lax.axis_index("wide"), lax.axis_index("narrow")

    def part_copy(step):
        other = lax.rem(n + step, narrow)
        return pltpu.make_async_remote_copy(
            src_ref=part_ref.at[other],
            dst_ref=came_ref.at[step],
            send_sem=p_send.at[step],
            recv_sem=p_recv.at[step],
            device_id={"wide": me, "narrow": other},
            device_id_type=MESH,
        )

    own_part = pltpu.make_async_copy(part_ref.at[n], came_ref.at[0], p_send.at[0])
    blocks, _, rows = x_ref.shape
    width = groups * HEAD_DIM
    own_in = pltpu.make_async_copy(mine_ref.at[me], grad_ref.at[me], own_sem.at[0])
    own_in.start()
    for j in range(blocks):
        keys[j] = x_ref[j, width : width + HEAD_DIM, :].T
        values[j] = x_ref[j, width + HEAD_DIM :, :].T
    acc_keys[...] = jnp.zeros_like(acc_keys)
    acc_values[...] = jnp.zeros_like(acc_values)
    greet(wide, narrow)
    for mask in range(1, wide):
        to_owner(
            mine_ref.at[me ^ mask], grad_ref.at[me], in_send.at[mask], in_recv.at[me], mask
        ).start()
    for q in range(reduce.chunks):
        reduce.begin(q)
    own_part.start()
    for step in range(1, narrow):
        part_copy(step).start()

    def weight_turn(c):
        chunks = reduce.chunks
        q = jnp.maximum(c - 2, 0) // 2
        ready = (c >= 2) & (lax.rem(c, 2) == 0) & (q < chunks)
        pl.when(ready)(lambda: reduce.after_core(jnp.minimum(q, chunks - 1)))
        actions = [functools.partial(reduce.after_stage, stage=stage) for stage in range(reduce.bits)]
        for index, action in enumerate(actions):
            since = jnp.maximum(c - (2 * chunks + 6 + 6 * index), -1)
            q = jnp.maximum(since, 0) // 5
            ready = (since >= 0) & (lax.rem(jnp.maximum(since, 0), 5) == 0) & (q < chunks)
            pl.when(ready)(functools.partial(action, jnp.minimum(q, chunks - 1)))

    turns = 2 * reduce.chunks + 6 + 6 * (reduce.bits - 1) + 5 * (reduce.chunks - 1) + 1
    key_row = lax.broadcasted_iota(jnp.int32, (rows, rows), 0)
    column = lax.broadcasted_iota(jnp.int32, (rows, rows), 1)
    own_in.wait()
    of_queries, of_keys = pl.ds(0, width), pl.ds(width, 2 * HEAD_DIM)

    def turn_back(block, cos, sin):
        front, back = block[:HALF, :], block[HALF:, :]
        return (front * cos + back * sin).astype(BF16), (back * cos - front * sin).astype(BF16)

    def block(i, carry):
        pl.when(i != me)(lambda: arrive(grad_ref.at[i], in_recv.at[i]))
        acc[...] = jnp.zeros_like(acc)
        start = start_ref[i]
        query_row = i * rows + column
        deltas = [
            jnp.sum(
                grad_ref[i, pl.ds(h * HEAD_DIM, HEAD_DIM), :].astype(F32)
                * full_ref[i, pl.ds(h * HEAD_DIM, HEAD_DIM), :],
                0,
                keepdims=True,
            )
            for h in range(groups)
        ]

        def step(j, carry):
            key_index = key_row + j * rows
            allowed = (key_index <= query_row) & (key_index >= start)
            key_block = keys[j]
            value_block = values[j]
            key_columns = x_ref[j, width : width + HEAD_DIM, :]
            grad_keys = acc_keys[j]
            grad_values = acc_values[j]
            for h in range(groups):
                own = pl.ds(h * HEAD_DIM, HEAD_DIM)
                query = x_ref[i, own, :]
                grad = grad_ref[i, own, :]
                scores = dot(key_block, query, NN)
                scores = jnp.where(allowed, scores, NEGATIVE)
                prob = jnp.exp(scores - log_ref[i, h : h + 1, :])
                grad_prob = dot(value_block, grad, NN)
                grad_scores = (prob * (grad_prob - deltas[h])).astype(BF16)
                acc[own, :] += dot(key_columns, grad_scores, NN)
                grad_keys = grad_keys + dot(query, grad_scores, NT)
                grad_values = grad_values + dot(grad, prob.astype(BF16), NT)
            acc_keys[j] = grad_keys
            acc_values[j] = grad_values
            weight_turn(i * (i + 1) // 2 + j)
            return carry

        lax.fori_loop(0, i + 1, step, 0)
        for h in range(groups):
            at = h * HEAD_DIM
            front, back = turn_back(
                acc[pl.ds(at, HEAD_DIM), :] * SCORE_SCALE, cos_ref[i], sin_ref[i]
            )
            done[i, pl.ds(at, HALF), :] = front
            done[i, pl.ds(at + HALF, HALF), :] = back

        @pl.when(i != me)
        def _():
            to_block(
                done.at[i, of_queries], out_ref.at[me, of_queries], q_send.at[i], q_recv.at[me], i
            ).start()

        return carry

    lax.fori_loop(0, blocks, block, 0)

    def last(j, carry):
        front, back = turn_back(acc_keys[j], cos_ref[j], sin_ref[j])
        done[j, pl.ds(width, HALF), :] = front
        done[j, pl.ds(width + HALF, HALF), :] = back
        done[j, pl.ds(width + HEAD_DIM, HEAD_DIM), :] = acc_values[j].astype(BF16)

        @pl.when(j != me)
        def _():
            to_block(
                done.at[j, of_keys], out_ref.at[me, of_keys], k_send.at[j], k_recv.at[me], j
            ).start()

        return carry

    lax.fori_loop(0, blocks, last, 0)
    out_ref[me] = done[me]

    def left(c, carry):
        weight_turn(c)
        return carry

    lax.fori_loop(blocks * (blocks + 1) // 2, max(turns, blocks * (blocks + 1) // 2), left, 0)

    reduce.after_all()
    reduce.drain()
    for mask in range(1, wide):
        other = me ^ mask
        arrive(mine_ref.at[other], in_send.at[mask])
        arrive(done.at[other, of_queries], q_send.at[other])
        arrive(done.at[other, of_keys], k_send.at[other])
        arrive(out_ref.at[other, of_queries], q_recv.at[other])
        arrive(out_ref.at[other, of_keys], k_recv.at[other])
    own_part.wait()
    for step in range(1, narrow):
        part_copy(step).wait()


def attend_back(x, mine, full, log_total, start, cos, sin, part, weight, groups):
    wide, narrow = lax.axis_size("wide"), lax.axis_size("narrow")
    blocks, features, rows = x.shape
    width = groups * HEAD_DIM
    dma = pltpu.SemaphoreType.DMA
    hbm = pl.BlockSpec(memory_space=pl.ANY)
    vmem = pl.BlockSpec(memory_space=pltpu.VMEM)
    return pl.pallas_call(
        functools.partial(attend_back_kernel, wide, narrow, groups),
        out_shape=(
            jax.ShapeDtypeStruct(x.shape, BF16),
            jax.ShapeDtypeStruct(part.shape, BF16),
            jax.ShapeDtypeStruct((weight.shape[2] // narrow, weight.shape[3]), F32),
        ),
        in_specs=[vmem] * 7 + [hbm, hbm],
        out_specs=(vmem, hbm, vmem),
        scratch_shapes=[
            pltpu.VMEM((blocks, rows, HEAD_DIM), BF16),
            pltpu.VMEM((blocks, rows, HEAD_DIM), BF16),
            pltpu.VMEM((width, rows), F32),
            pltpu.VMEM((blocks, HEAD_DIM, rows), F32),
            pltpu.VMEM((blocks, HEAD_DIM, rows), F32),
            pltpu.VMEM((blocks, width, rows), BF16),
            pltpu.VMEM((blocks, features, rows), BF16),
            dma((1,)),
        ]
        + [dma((wide,))] * 6
        + [dma((narrow,))] * 2
        + reduce_scratch(wide, narrow, weight, 512),
        compiler_params=pltpu.CompilerParams(
            collective_id=4, has_side_effects=True, vmem_limit_bytes=50 << 20
        ),
        cost_estimate=pl.CostEstimate(
            flops=40 * width * (blocks * rows) ** 2,
            bytes_accessed=4 * x.size * 2,
            transcendentals=groups * (blocks * rows) ** 2 // 2,
        ),
    )(start, x, mine, full, log_total, cos, sin, part, weight)


def gather(x, axis):
    return lax.all_gather(x, axis, axis=0, tiled=True)


def scatter_sum(x, axis):
    return lax.psum_scatter(x, axis, scatter_dimension=0, tiled=True)


def gather_kernel(wide, narrow, aligned, qkv_ref, cut_ref, qkv_all, cut_all, x_send, x_recv, x_own, *sems):
    w, n = lax.axis_index("wide"), lax.axis_index("narrow")
    greet(wide, narrow)
    flow = Flow(wide, narrow, qkv_ref, qkv_all, sems)
    depth = qkv_ref.shape[0]
    piece = cut_all.shape[1] // (2 * wide)

    def rows_of(owner):
        return cut_all.at[pl.ds(pl.multiple_of(owner * depth, depth), depth), :]

    def pieces(other):
        if not aligned:
            return [(cut_ref.at[other], pl.ds(0, cut_all.shape[1]))]
        return [
            (
                cut_ref.at[:, pl.ds(pl.multiple_of((j * narrow + other) * piece, piece), piece)],
                pl.ds(j * piece, piece),
            )
            for j in range(2 * wide)
        ]

    def target(columns):
        return cut_all.at[pl.ds(pl.multiple_of(n * depth, depth), depth), columns]

    def cut_start(step):
        other = lax.rem(n + step, narrow)
        for source, columns in pieces(other):
            pltpu.make_async_remote_copy(
                src_ref=source,
                dst_ref=target(columns),
                send_sem=x_send.at[step],
                recv_sem=x_recv.at[step],
                device_id={"wide": w, "narrow": other},
                device_id_type=MESH,
            ).start()

    for t in range(flow.last):
        flow.step(t)
        if t == min(1, narrow - 1):
            for source, columns in pieces(n):
                pltpu.make_async_copy(source, target(columns), x_own).start()
            for step in range(1, narrow):
                cut_start(step)
    flow.end()
    own = rows_of(n)
    pltpu.make_async_copy(own, own, x_own).wait()
    for step in range(1, narrow):
        pltpu.make_async_copy(own, own, x_send.at[step]).wait()
        block = rows_of(lax.rem(n + narrow - step, narrow))
        pltpu.make_async_copy(block, block, x_recv.at[step]).wait()


def gather_weights(qkv, gateup):
    wide, narrow = lax.axis_size("wide"), lax.axis_size("narrow")
    dma = pltpu.SemaphoreType.DMA
    hbm = pl.BlockSpec(memory_space=pl.ANY)
    every = wide * narrow
    shard, columns = gateup.shape
    aligned = (columns // (2 * every)) % 128 == 0
    if not aligned:
        gateup = gateup.reshape(shard, 2, wide, narrow, -1).transpose(3, 0, 1, 2, 4)
        gateup = gateup.reshape(narrow, shard, columns // narrow)
    return pl.pallas_call(
        functools.partial(gather_kernel, wide, narrow, aligned),
        out_shape=(
            jax.ShapeDtypeStruct((every * qkv.shape[0], qkv.shape[1]), BF16),
            jax.ShapeDtypeStruct((narrow * shard, columns // narrow), BF16),
        ),
        in_specs=[hbm, hbm],
        out_specs=(hbm, hbm),
        scratch_shapes=[dma((narrow,)), dma((narrow,)), dma(())] + flow_sems(wide, narrow),
        compiler_params=pltpu.CompilerParams(collective_id=0, has_side_effects=True),
        cost_estimate=pl.CostEstimate(flops=0, bytes_accessed=200 << 20, transcendentals=0),
    )(qkv, gateup)


def feed_kernel(
    narrow, x_ref, cot_ref, gate_up_ref, down_ref,
    low_out, grad_x_ref, part_gate_up, part_down,
    group_ref, gate_up, down, cot, hidden, grads, low, came,
    load_sem, x_send, x_recv, out_sem, g_send, g_recv,
):
    w, n = lax.axis_index("wide"), lax.axis_index("narrow")
    rows, width = x_ref.shape
    own = down.shape[0]
    tile = 256
    tiles = own // tile
    wtiles = width // tile

    def to_narrow(other):
        return {"wide": w, "narrow": other}

    loads = [
        pltpu.make_async_copy(gate_up_ref, gate_up, load_sem.at[0]),
        pltpu.make_async_copy(down_ref, down, load_sem.at[1]),
        pltpu.make_async_copy(cot_ref, cot, load_sem.at[2]),
        pltpu.make_async_copy(x_ref, group_ref.at[n], load_sem.at[3]),
    ]
    for load in loads:
        load.start()

    barrier = pltpu.get_barrier_semaphore()
    for step in range(1, narrow):
        pl.semaphore_signal(
            barrier, inc=1, device_id=to_narrow(lax.rem(n + step, narrow)), device_id_type=MESH
        )
    pl.semaphore_wait(barrier, narrow - 1)

    def owner_of(side, d):
        return n - d if side == 0 else n + d

    def valid(side, d):
        return n - d >= 0 if side == 0 else (n + d < narrow) & (d > 0)

    def passes(side, d):
        if side == 0:
            return (n - d >= 0) & (n < narrow - 1)
        return (n + d < narrow) & (n > 0)

    def x_copy(side, d):
        block = group_ref.at[owner_of(side, d)]
        return pltpu.make_async_remote_copy(
            src_ref=block,
            dst_ref=block,
            send_sem=x_send.at[side, d],
            recv_sem=x_recv.at[side, d + 1],
            device_id=to_narrow(n + 1 if side == 0 else n - 1),
            device_id_type=MESH,
        )

    def x_wait(side, d):
        block = group_ref.at[owner_of(side, d)]
        pltpu.make_async_copy(block, block, x_recv.at[side, d]).wait()

    def out_copy(at, block):
        return pltpu.make_async_copy(low.at[at], low_out.at[block], out_sem.at[at])

    def g_copy(block):
        return pltpu.make_async_remote_copy(
            src_ref=cot.at[block],
            dst_ref=came.at[n],
            send_sem=g_send.at[block],
            recv_sem=g_recv.at[n],
            device_id=to_narrow(block),
            device_id_type=MESH,
        )

    def compute(side, d):
        block = n - d + 2 * d * side
        before = 1 + jnp.minimum(n, d - 1) + jnp.minimum(narrow - 1 - n, d - 1)
        before = jnp.where(d == 0, 0, before + jnp.where((side == 1) & (n - d >= 0), 1, 0))
        at = lax.rem(before, 2)

        pl.when(before >= 2)(lambda: out_copy(at, block).wait())

        def first(f, carry):
            columns = pl.ds(pl.multiple_of(f * tile, tile), tile)
            other = pl.ds(pl.multiple_of(own + f * tile, tile), tile)
            x = group_ref[block]
            gate = dot(x, gate_up[:, columns], NN)
            up = dot(x, gate_up[:, other], NN)
            grad = dot(cot[block], down[columns, :], NT)
            sig = 1.0 / (1.0 + jnp.exp(-gate))
            silu = gate * sig
            hidden[block, :, columns] = (silu * up).astype(BF16)
            grads[block, :, columns] = (grad * up * (sig + silu * (1.0 - sig))).astype(BF16)
            grads[block, :, other] = (grad * silu).astype(BF16)
            return carry

        lax.fori_loop(0, tiles, first, 0)

        def second(f, carry):
            columns = pl.ds(pl.multiple_of(f * tile, tile), tile)
            cot[block, :, columns] = dot(grads[block], gate_up[columns, :], NT, BF16)
            low[at, :, columns] = dot(hidden[block], down[:, columns], NN, BF16)
            return carry

        lax.fori_loop(0, wtiles, second, 0)
        out_copy(at, block).start()
        pl.when(block != n)(lambda: g_copy(block).start())

    def distance(d, carry):
        for side in (0, 1):

            @pl.when(passes(side, d + 1))
            def _():
                x_wait(side, d + 1)
                x_copy(side, d + 1).start()

            @pl.when(valid(side, d) & (d > 0) & jnp.logical_not(passes(side, d)))
            def _():
                x_wait(side, d)

        @pl.when(d == 0)
        def _():
            for load in loads[:3]:
                load.wait()

        def one(side, carry):
            ok = jnp.where(side == 0, n - d, jnp.where(d > 0, narrow - 1 - n - d, -1)) >= 0
            pl.when(ok)(lambda: compute(side, d))
            return carry

        lax.fori_loop(0, 2, one, 0)
        return carry

    loads[3].wait()
    for side in (0, 1):
        pl.when(passes(side, 0))(lambda side=side: x_copy(side, 0).start())
    lax.fori_loop(0, narrow, distance, 0)

    tokens = narrow * rows
    again = [
        pltpu.make_async_copy(
            cot_ref.at[o], gate_up.at[pl.ds(o * rows, rows), pl.ds(0, width)], load_sem.at[4 + o]
        )
        for o in range(narrow)
    ]
    for load in again:
        load.start()
    for at in range(2):
        out_copy(at, n).wait()

    def flipped(ref, columns):
        return jnp.concatenate([ref[o, :, columns].T for o in range(narrow)], 1)

    def weight_tile(t, left, right, at_row, out_ref, first):
        at = lax.rem(t, 2)
        copy = pltpu.make_async_copy(low.at[at], out_ref, out_sem.at[at])
        pl.when(t >= 2)(lambda: copy.wait())
        turned = flipped(left, pl.ds(pl.multiple_of(at_row, tile), tile))

        def one(c, carry):
            columns = pl.ds(pl.multiple_of(c * 512, 512), 512)
            source = pl.ds(pl.multiple_of(first + c * 512, 512), 512)
            low[at, :, columns] = dot(turned, right(source), NN, BF16)
            return carry

        lax.fori_loop(0, width // 512, one, 0)
        copy.start()

    halves = 2 * own // width

    def gate_up_tile(t, carry):
        row, half = t // halves * tile, lax.rem(t, halves) * width
        row, half = pl.multiple_of(row, tile), pl.multiple_of(half, width)
        weight_tile(
            t, group_ref, lambda source: grads[:, :, source].reshape(tokens, 512), row,
            part_gate_up.at[pl.ds(row, tile), pl.ds(half, width)], half,
        )
        return carry

    def down_tile(t, carry):
        row = pl.multiple_of(t * tile, tile)
        weight_tile(
            t + 2, hidden, lambda source: gate_up[pl.ds(0, tokens), source], row,
            part_down.at[pl.ds(row, tile), :], 0,
        )
        return carry

    lax.fori_loop(0, wtiles * halves, gate_up_tile, 0)
    for load in again:
        load.wait()
    lax.fori_loop(0, tiles, down_tile, 0)
    for at in range(2):
        out_copy(at, n).wait()
    for side in (0, 1):
        for d in range(narrow - 1):
            pl.when(passes(side, d))(lambda side=side, d=d: x_copy(side, d).wait_send())
    for step in range(1, narrow):
        other = lax.rem(n + step, narrow)
        g_copy(other).wait_send()
        block = came.at[other]
        pltpu.make_async_copy(block, block, g_recv.at[other]).wait()

    def add(r, carry):
        part = pl.ds(pl.multiple_of(r * 16, 16), 16)
        total = cot[n, part, :].astype(F32)
        for step in range(1, narrow):
            total = total + came[lax.rem(n + step, narrow), part, :].astype(F32)
        grad_x_ref[part, :] = total
        return carry

    lax.fori_loop(0, rows // 16, add, 0)


def feed(x, cot_group, gate_up, down):
    narrow = lax.axis_size("narrow")
    rows, width = x.shape
    own = down.shape[0]
    dma = pltpu.SemaphoreType.DMA
    hbm = pl.BlockSpec(memory_space=pl.ANY)
    vmem = pl.BlockSpec(memory_space=pltpu.VMEM)
    return pl.pallas_call(
        functools.partial(feed_kernel, narrow),
        out_shape=(
            jax.ShapeDtypeStruct((narrow, rows, width), BF16),
            jax.ShapeDtypeStruct((rows, width), F32),
            jax.ShapeDtypeStruct((width, 2 * own), BF16),
            jax.ShapeDtypeStruct((own, width), BF16),
        ),
        in_specs=[vmem, hbm, hbm, hbm],
        out_specs=(hbm, vmem, hbm, hbm),
        scratch_shapes=[
            pltpu.VMEM((narrow, rows, width), BF16),
            pltpu.VMEM((width, 2 * own), BF16),
            pltpu.VMEM((own, width), BF16),
            pltpu.VMEM((narrow, rows, width), BF16),
            pltpu.VMEM((narrow, rows, own), BF16),
            pltpu.VMEM((narrow, rows, 2 * own), BF16),
            pltpu.VMEM((2, rows, width), BF16),
            pltpu.VMEM((narrow, rows, width), BF16),
            dma((4 + narrow,)),
            dma((2, narrow + 1)),
            dma((2, narrow + 1)),
            dma((2,)),
            dma((narrow,)),
            dma((narrow,)),
        ],
        compiler_params=pltpu.CompilerParams(
            collective_id=1, has_side_effects=True, vmem_limit_bytes=58 << 20
        ),
        cost_estimate=pl.CostEstimate(
            flops=12 * narrow * rows * width * own, bytes_accessed=300 << 20, transcendentals=0
        ),
    )(x, cot_group.reshape(narrow, rows, width), gate_up, down)


def sum_kernel(
    wide, narrow, qkv_ref, cut_ref, gains_ref, qkv_out, cut_out, gains_out,
    cut_in, gain_w, gain_sum, gain_z, own_sem, cut_send, cut_recv, gw_send, gw_recv, gz_send, gz_recv, *refs,
):
    reduce = Reduce(wide, narrow, qkv_ref, qkv_out, refs)
    w, n = reduce.w, reduce.n
    chunks, bits = reduce.chunks, reduce.bits
    greet(wide, narrow)

    def to_wide(mask):
        return {"wide": w ^ mask, "narrow": n}

    def to_narrow(step):
        return {"wide": w, "narrow": lax.rem(n + step, narrow)}

    own_cut = pltpu.make_async_copy(cut_ref.at[n], cut_in.at[n], own_sem)

    def cut_copy(step):
        return pltpu.make_async_remote_copy(
            src_ref=cut_ref.at[lax.rem(n + step, narrow)],
            dst_ref=cut_in.at[n],
            send_sem=cut_send.at[step],
            recv_sem=cut_recv.at[step],
            device_id=to_narrow(step),
            device_id_type=MESH,
        )

    def gw_copy(mask):
        return pltpu.make_async_remote_copy(
            src_ref=gains_ref.at[w ^ mask],
            dst_ref=gain_w.at[mask],
            send_sem=gw_send.at[mask],
            recv_sem=gw_recv.at[mask],
            device_id=to_wide(mask),
            device_id_type=MESH,
        )

    def gz_copy(step):
        return pltpu.make_async_remote_copy(
            src_ref=gain_sum.at[lax.rem(n + step, narrow)],
            dst_ref=gain_z.at[step],
            send_sem=gz_send.at[step],
            recv_sem=gz_recv.at[step],
            device_id=to_narrow(step),
            device_id_type=MESH,
        )

    ahead = min(4, chunks)
    for q in range(ahead):
        reduce.begin(q)
    own_cut.start()
    for step in range(1, narrow):
        cut_copy(step).start()
    for mask in range(1, wide):
        gw_copy(mask).start()

    def turn(t, carry):
        pl.when(t + ahead < chunks)(lambda: reduce.begin(t + ahead))
        pl.when(t < chunks)(lambda: reduce.after_core(t))
        for stage in range(bits):
            q = t - 1 - stage
            pl.when((q >= 0) & (q < chunks))(functools.partial(reduce.after_stage, q, stage))
        return carry

    lax.fori_loop(0, chunks + bits, turn, 0)

    total = gains_ref[w]
    for mask in range(1, wide):
        block = gain_w.at[mask]
        pltpu.make_async_copy(block, block, gw_recv.at[mask]).wait()
        total = total + gain_w[mask]
    gain_sum[...] = total
    for step in range(1, narrow):
        gz_copy(step).start()

    reduce.after_all()
    own_cut.wait()
    for step in range(1, narrow):
        other = lax.rem(n + narrow - step, narrow)
        arrive(cut_in.at[other], cut_recv.at[step])
    piece = cut_in.shape[2] // (2 * wide)
    if cut_out.shape[0] == narrow:
        for other in range(narrow):
            cut_out[other] = cut_in[other].astype(F32)
    else:
        for j in range(2 * wide):
            for other in range(narrow):
                cut_out[:, pl.ds((j * narrow + other) * piece, piece)] = cut_in[
                    other, :, pl.ds(j * piece, piece)
                ].astype(F32)

    total = gain_sum[n]
    for step in range(1, narrow):
        block = gain_z.at[step]
        pltpu.make_async_copy(block, block, gz_recv.at[step]).wait()
        total = total + gain_z[step]
    gains_out[...] = total

    for mask in range(1, wide):
        gw_copy(mask).wait_send()
    for step in range(1, narrow):
        gz_copy(step).wait_send()
        cut_copy(step).wait_send()
    reduce.drain()


def sum_all(qkv, cut, gains):
    wide, narrow = lax.axis_size("wide"), lax.axis_size("narrow")
    shard, cut_width = cut.shape[1:]
    aligned = (cut_width // (2 * wide)) % 128 == 0
    cut_shape = (shard, narrow * cut_width) if aligned else cut.shape
    dma = pltpu.SemaphoreType.DMA
    hbm = pl.BlockSpec(memory_space=pl.ANY)
    vmem = pl.BlockSpec(memory_space=pltpu.VMEM)
    results = pl.pallas_call(
        functools.partial(sum_kernel, wide, narrow),
        out_shape=(
            jax.ShapeDtypeStruct((shard, qkv.shape[3]), F32),
            jax.ShapeDtypeStruct(cut_shape, F32),
            jax.ShapeDtypeStruct((8, 128), F32),
        ),
        in_specs=[hbm, hbm, vmem],
        out_specs=(vmem, vmem, vmem),
        scratch_shapes=[
            pltpu.VMEM(cut.shape, BF16),
            pltpu.VMEM((wide, narrow, 8, 128), F32),
            pltpu.VMEM((narrow, 8, 128), F32),
            pltpu.VMEM((narrow, 8, 128), F32),
            dma(()),
            dma((narrow,)),
            dma((narrow,)),
            dma((wide,)),
            dma((wide,)),
            dma((narrow,)),
            dma((narrow,)),
        ]
        + reduce_scratch(wide, narrow, qkv, 256),
        compiler_params=pltpu.CompilerParams(
            collective_id=2, has_side_effects=True, vmem_limit_bytes=54 << 20
        ),
        cost_estimate=pl.CostEstimate(flops=0, bytes_accessed=300 << 20, transcendentals=0),
    )(qkv, cut, gains)
    return results, aligned


def per_device(tokens, lengths, gain_attn, w_qkv, w_out, gain_mlp, w_gateup, w_down, cotangent):
    rows, width = tokens.shape[1:]
    wide, narrow = lax.axis_size("wide"), lax.axis_size("narrow")
    pack_rows = rows * wide
    query_width, key_width = HEADS * HEAD_DIM, KV_HEADS * HEAD_DIM
    groups = HEADS // wide
    copies = wide // KV_HEADS
    own_ff = FF // narrow
    first, positions = places(lengths[0], pack_rows)
    cos_all, sin_all = rotary(positions.astype(F32), HALF)
    first_row = lax.axis_index("wide") * rows
    cos = lax.dynamic_slice_in_dim(cos_all, first_row, rows, 1)
    sin = lax.dynamic_slice_in_dim(sin_all, first_row, rows, 1)
    cos_all = cos_all.reshape(HALF, wide, rows).transpose(1, 0, 2)
    sin_all = sin_all.reshape(HALF, wide, rows).transpose(1, 0, 2)
    start = first.reshape(wide, 1, rows)

    gains = jnp.stack([gain_attn, gain_mlp], -1)
    with_gains = jnp.concatenate([w_qkv, jnp.pad(gains, ((0, 0), (0, 126)))], -1)
    shard = w_gateup.shape[0]
    qkv_gained, gateup_rows = gather_weights(with_gains, w_gateup)
    qkv_whole = qkv_gained[:, : w_qkv.shape[1]]
    gain_one = qkv_gained[:, w_qkv.shape[1]].astype(F32)
    gain_two = qkv_gained[:, w_qkv.shape[1] + 1].astype(F32)
    gateup_own = gather(gateup_rows, "wide")
    down_own = gather(w_down, "wide")

    inputs = tokens[0].astype(F32)
    scale_one = lax.rsqrt(jnp.mean(inputs * inputs, -1, keepdims=True) + EPS)
    unit_one = inputs * scale_one
    normed_one = (unit_one * gain_one).astype(BF16)
    projected = dot(qkv_whole, normed_one, (((0,), (1,)), ((), ())))
    turning = projected[: query_width + key_width].reshape(HEADS + KV_HEADS, 2, HALF, rows)
    front, back = turning[:, 0], turning[:, 1]
    turned = jnp.stack([front * cos - back * sin, back * cos + front * sin], 1)
    queries = (turned[:HEADS] * SCORE_SCALE).astype(BF16).reshape(wide, groups * HEAD_DIM, rows)
    keys = turned[HEADS:].astype(BF16).reshape(KV_HEADS, HEAD_DIM, rows)
    values = projected[query_width + key_width :].astype(BF16).reshape(KV_HEADS, HEAD_DIM, rows)
    keys_values = jnp.repeat(jnp.concatenate([keys, values], 1), copies, 0)
    heads, attended_low, attended_full, log_total, out_whole, cot_group = attend(
        jnp.concatenate([queries, keys_values], 1), start, w_out, cotangent[0], groups
    )
    cot_group = cot_group.reshape(-1, width)
    attended_low = attended_low.reshape(query_width, rows)
    middle = inputs + dot(attended_low, out_whole, TN)
    scale_two = lax.rsqrt(jnp.mean(middle * middle, -1, keepdims=True) + EPS)
    unit_two = middle * scale_two
    normed_two = (unit_two * gain_two).astype(BF16)

    low_part, grad_normed_two, part_gateup, part_down = feed(
        normed_two, cot_group, gateup_own, down_own
    )
    grad_gateup = scatter_sum(part_gateup, "wide").reshape(narrow, shard, 2 * own_ff)
    grad_down = scatter_sum(part_down, "wide")
    part_gain_two = jnp.sum(grad_normed_two * unit_two, 0)
    grad_middle = cotangent[0].astype(F32) + norm_back(
        grad_normed_two * gain_two, unit_two, scale_two
    )
    grad_branch = grad_middle.astype(BF16)
    grad_attended = dot(out_whole, grad_branch, NT, BF16).reshape(wide, groups * HEAD_DIM, rows)
    cut = (wide // 2, 2, narrow * shard, -1)
    part_wout = dot(attended_low, grad_branch, NN, BF16).reshape(cut)
    grad_heads, low_came, grad_wout = attend_back(
        heads, grad_attended, attended_full, log_total, start, cos_all, sin_all, low_part, part_wout,
        groups,
    )
    layer_out = (middle + jnp.sum(low_came.astype(F32), 0)).astype(BF16)[None]
    grad_queries = grad_heads[:, : groups * HEAD_DIM].reshape(query_width, rows)
    grad_keys_values = (
        grad_heads[:, groups * HEAD_DIM :]
        .reshape(KV_HEADS, copies, 2, HEAD_DIM, rows)
        .astype(F32)
        .sum(1)
        .astype(BF16)
    )
    grad_projected = jnp.concatenate(
        [
            grad_queries,
            grad_keys_values[:, 0].reshape(key_width, rows),
            grad_keys_values[:, 1].reshape(key_width, rows),
        ],
        0,
    )
    grad_normed_one = dot(grad_projected, qkv_whole, (((0,), (1,)), ((), ())))
    part_gain_one = jnp.sum(grad_normed_one * unit_one, 0)
    part_gains = jnp.stack([part_gain_one, part_gain_two], 0).reshape(2, wide, narrow, shard)
    part_gains = jnp.pad(
        part_gains.transpose(1, 2, 0, 3), ((0, 0), (0, 0), (0, 6), (0, 128 - shard))
    )
    part_qkv = dot(normed_one, grad_projected, (((0,), (1,)), ((), ())), BF16).reshape(cut)
    (grad_qkv, grad_gateup, grad_gains), done = sum_all(part_qkv, grad_gateup, part_gains)
    if not done:
        grad_gateup = (
            grad_gateup.reshape(narrow, shard, 2, wide, -1)
            .transpose(1, 2, 3, 0, 4)
            .reshape(shard, 2 * FF)
        )
    grad_down, grad_gains = lax.optimization_barrier((grad_down, grad_gains))
    grad_down = grad_down.astype(F32)
    grad_inputs = grad_middle + norm_back(grad_normed_one * gain_one, unit_one, scale_one)
    grad_tokens = grad_inputs.astype(BF16)[None]
    return (
        layer_out,
        grad_tokens,
        grad_gains[0, :shard],
        grad_qkv,
        grad_wout,
        grad_gains[1, :shard],
        grad_gateup,
        grad_down,
    )


def solution(mesh):
    rows, packs = P("narrow", "wide", None), P("narrow", None)
    weight, gain = P(BOTH, None), P(BOTH)
    return jax.shard_map(
        per_device,
        mesh=mesh,
        in_specs=(rows, packs, gain, weight, weight, gain, weight, weight, rows),
        out_specs=(rows, rows, gain, weight, weight, gain, weight, weight),
        check_vma=False,
    )
```

```python
import functools
import math

import jax
import jax.numpy as jnp
from jax import lax
from jax.experimental import pallas as pl
from jax.experimental.pallas import tpu as pltpu
from jax.sharding import PartitionSpec as P

FF = 8192
HEADS = 32
KV_HEADS = 8
HEAD_DIM = 64
HALF = HEAD_DIM // 2
EPS = 1e-05
NEGATIVE = -1e30
SCORE_SCALE = 1.0 / math.sqrt(HEAD_DIM)
BOTH = ("wide", "narrow")
F32 = jnp.float32
BF16 = jnp.bfloat16
NN = (((1,), (0,)), ((), ()))
NT = (((1,), (1,)), ((), ()))
TN = (((0,), (0,)), ((), ()))


def dot(left, right, dims, kind=F32):
    return lax.dot_general(left, right, dims, preferred_element_type=F32).astype(kind)


def places(lengths_row, total_rows):
    seq_ends = jnp.cumsum(lengths_row)
    starts = seq_ends - lengths_row
    row_index = jnp.arange(total_rows, dtype=jnp.int32)
    segments = jnp.sum((row_index[:, None] >= seq_ends[None, :]).astype(jnp.int32), -1)
    slot_index = jnp.arange(lengths_row.shape[0], dtype=jnp.int32)
    owned = segments[:, None] == slot_index[None, :]
    first = jnp.sum(jnp.where(owned, starts[None, :], 0), -1)
    return first, row_index - first


def rotary(positions, half_width):
    channel = jnp.arange(half_width, dtype=jnp.float32)
    inverse_rate = jnp.power(500000.0, -channel / half_width)
    wavelength = 2.0 * math.pi / inverse_rate
    smooth = (8192.0 / wavelength - 1.0) / 3.0
    blended = (1.0 - smooth) * inverse_rate / 32.0 + smooth * inverse_rate
    frequency = jnp.where(
        wavelength < 2048.0,
        inverse_rate,
        jnp.where(wavelength > 8192.0, inverse_rate / 32.0, blended),
    )
    angles = frequency[:, None] * positions[None, :]
    return jnp.cos(angles), jnp.sin(angles)


def norm_back(grad_unit, unit_rows, row_scale):
    return row_scale * (grad_unit - unit_rows * jnp.mean(grad_unit * unit_rows, -1, keepdims=True))


MESH = pl.DeviceIdType.MESH


class Flow:
    def __init__(self, wide, narrow, x_ref, out_ref, sems):
        self.wide, self.narrow, self.x_ref, self.out_ref = wide, narrow, x_ref, out_ref
        self.w, self.n = lax.axis_index("wide"), lax.axis_index("narrow")
        (self.own_sem, self.z_send, self.z_recv, self.m_send, self.m_recv,
         self.r_send, self.r_recv, self.c_send, self.c_recv) = sems
        self.relay = wide == 8
        self.masks = [2, 4] if self.relay else list(range(2, wide, 2))
        self.last = narrow + 2

    def to_wide(self, mask):
        return {"wide": self.w ^ mask, "narrow": self.n}

    def owner_of(self, side, d):
        return self.n - d if side == 0 else self.n + d

    def valid(self, side, d):
        return self.n - d >= 0 if side == 0 else self.n + d < self.narrow

    def can_pass(self, side, d):
        if side == 0:
            return (self.n - (d - 1) >= 0) & (self.n < self.narrow - 1)
        return (self.n + (d - 1) < self.narrow) & (self.n > 0)

    def slot(self, side, d):
        return d - 1 + side * (self.narrow - 1) if d else 2 * (self.narrow - 1)

    def at_distance(self, d, action):
        if d == 0:
            action(0, 0)
            return
        for side in (0, 1):
            pl.when(self.valid(side, d))(functools.partial(action, side, d))

    def place(self, owner_w, owner_n, part=None):
        depth = self.x_ref.shape[0]
        half = depth // 2
        at = (owner_w * self.narrow + owner_n) * depth
        if part is None:
            return self.out_ref.at[pl.ds(pl.multiple_of(at, depth), depth), :]
        return self.out_ref.at[pl.ds(pl.multiple_of(at + part * half, half), half), :]

    def own_copy(self):
        return pltpu.make_async_copy(self.x_ref, self.place(self.w, self.n), self.own_sem)

    def z_copy(self, side, d):
        block = self.place(self.w, self.owner_of(side, d - 1))
        return pltpu.make_async_remote_copy(
            src_ref=self.x_ref if d == 1 else block,
            dst_ref=block,
            send_sem=self.z_send.at[side, d],
            recv_sem=self.z_recv.at[side, d],
            device_id={"wide": self.w, "narrow": self.n + 1 if side == 0 else self.n - 1},
            device_id_type=MESH,
        )

    def z_wait(self, side, d):
        block = self.place(self.w, self.owner_of(side, d))
        pltpu.make_async_copy(block, block, self.z_recv.at[side, d]).wait()

    def m_copy(self, i, side, d):
        block = self.place(self.w, self.owner_of(side, d))
        return pltpu.make_async_remote_copy(
            src_ref=self.x_ref if d == 0 else block,
            dst_ref=block,
            send_sem=self.m_send.at[i, self.slot(side, d)],
            recv_sem=self.m_recv.at[i, self.slot(side, d)],
            device_id=self.to_wide(self.masks[i]),
            device_id_type=MESH,
        )

    def m_wait(self, i, side, d):
        block = self.place(self.w ^ self.masks[i], self.owner_of(side, d))
        pltpu.make_async_copy(block, block, self.m_recv.at[i, self.slot(side, d)]).wait()

    def r_copy(self, part, side, d):
        block = self.place(self.w ^ self.masks[part], self.owner_of(side, d), part)
        return pltpu.make_async_remote_copy(
            src_ref=block,
            dst_ref=block,
            send_sem=self.r_send.at[part, self.slot(side, d)],
            recv_sem=self.r_recv.at[part, self.slot(side, d)],
            device_id=self.to_wide(self.masks[1 - part]),
            device_id_type=MESH,
        )

    def r_wait(self, part, side, d):
        block = self.place(self.w ^ 6, self.owner_of(side, d), part)
        pltpu.make_async_copy(block, block, self.r_recv.at[part, self.slot(side, d)]).wait()

    def c_copy(self, chip, side, d):
        block = self.place(self.w ^ (2 * chip), self.owner_of(side, d))
        return pltpu.make_async_remote_copy(
            src_ref=self.x_ref if d == 0 and chip == 0 else block,
            dst_ref=block,
            send_sem=self.c_send.at[chip, self.slot(side, d)],
            recv_sem=self.c_recv.at[chip, self.slot(side, d)],
            device_id=self.to_wide(1),
            device_id_type=MESH,
        )

    def c_wait(self, chip, side, d):
        block = self.place((self.w ^ 1) ^ (2 * chip), self.owner_of(side, d))
        pltpu.make_async_copy(block, block, self.c_recv.at[chip, self.slot(side, d)]).wait()

    def send_from_here(self, side, d):
        if d > 0:
            self.z_wait(side, d)
        if 0 < d < self.narrow - 1:
            pl.when(self.can_pass(side, d + 1))(lambda: self.z_copy(side, d + 1).start())
        for i in range(len(self.masks)):
            self.m_copy(i, side, d).start()
        self.c_copy(0, side, d).start()

    def send_on(self, side, d):
        for i in range(len(self.masks)):
            self.m_wait(i, side, d)
            if self.relay:
                self.r_copy(i, side, d).start()
            self.c_copy(self.masks[i] // 2, side, d).start()

    def send_last(self, side, d):
        self.r_wait(0, side, d)
        self.r_wait(1, side, d)
        self.c_copy(3, side, d).start()

    def step(self, t):
        if t == 0:
            self.own_copy().start()
            for side in (0, 1):
                pl.when(self.can_pass(side, 1))(lambda side=side: self.z_copy(side, 1).start())
        if 0 <= t < self.narrow:
            self.at_distance(t, self.send_from_here)
        if 0 <= t - 1 < self.narrow:
            self.at_distance(t - 1, self.send_on)
        if self.relay and 0 <= t - 2 < self.narrow:
            self.at_distance(t - 2, self.send_last)

    def finish(self, side, d):
        for i in range(len(self.masks)):
            self.m_copy(i, side, d).wait_send()
            if self.relay:
                self.r_copy(i, side, d).wait_send()
        for chip in range(self.wide // 2):
            self.c_copy(chip, side, d).wait_send()
            self.c_wait(chip, side, d)

    def end(self):
        self.own_copy().wait()
        for side in (0, 1):
            for d in range(1, self.narrow):
                pl.when(self.can_pass(side, d))(
                    lambda side=side, d=d: self.z_copy(side, d).wait_send()
                )
        for d in range(self.narrow):
            self.at_distance(d, self.finish)


class Line:
    def __init__(self, narrow, x_ref, out_ref, sems):
        self.narrow, self.x_ref, self.out_ref = narrow, x_ref, out_ref
        self.w, self.n = lax.axis_index("wide"), lax.axis_index("narrow")
        self.own_sem, self.send, self.recv = sems

    def owner_of(self, side, d):
        return self.n - d if side == 0 else self.n + d

    def valid(self, side, d):
        return self.n - d >= 0 if side == 0 else self.n + d < self.narrow

    def can_pass(self, side, d):
        if side == 0:
            return (self.n - (d - 1) >= 0) & (self.n < self.narrow - 1)
        return (self.n + (d - 1) < self.narrow) & (self.n > 0)

    def own_copy(self):
        return pltpu.make_async_copy(self.x_ref, self.out_ref.at[self.n], self.own_sem)

    def copy(self, side, d):
        block = self.out_ref.at[self.owner_of(side, d - 1)]
        return pltpu.make_async_remote_copy(
            src_ref=self.x_ref if d == 1 else block,
            dst_ref=block,
            send_sem=self.send.at[side, d],
            recv_sem=self.recv.at[side, d],
            device_id={"wide": self.w, "narrow": self.n + 1 if side == 0 else self.n - 1},
            device_id_type=MESH,
        )

    def pass_on(self, side, d):
        arrive(self.out_ref.at[self.owner_of(side, d)], self.recv.at[side, d])
        if d < self.narrow - 1:
            pl.when(self.can_pass(side, d + 1))(lambda: self.copy(side, d + 1).start())

    def step(self, t):
        if t == 0:
            self.own_copy().start()
        for side in (0, 1):
            if t == 0:
                pl.when(self.can_pass(side, 1))(lambda side=side: self.copy(side, 1).start())
            else:
                pl.when(self.valid(side, t))(lambda side=side: self.pass_on(side, t))

    def end(self):
        self.own_copy().wait()
        for side in (0, 1):
            for d in range(1, self.narrow):
                pl.when(self.can_pass(side, d))(lambda side=side, d=d: self.copy(side, d).wait_send())


def flow_sems(wide, narrow):
    slots = 2 * narrow - 1
    masks = 2 if wide == 8 else wide // 2 - 1
    dma = pltpu.SemaphoreType.DMA
    return [
        dma(()),
        dma((2, narrow)),
        dma((2, narrow)),
        dma((masks, slots)),
        dma((masks, slots)),
        dma((2, slots)),
        dma((2, slots)),
        dma((wide // 2, slots)),
        dma((wide // 2, slots)),
    ]


class Reduce:
    def __init__(self, wide, narrow, left, right, dims, out_ref, refs):
        self.wide, self.narrow, self.left, self.right, self.dims = wide, narrow, left, right, dims
        self.out_ref = out_ref
        self.w, self.n = lax.axis_index("wide"), lax.axis_index("narrow")
        self.core, self.chip = lax.rem(self.w, 2), self.w // 2
        self.chips = wide // 2
        self.bits = self.chips.bit_length() - 1
        (self.turned, self.held, self.away, self.core_in, self.chip_in, self.z_in, self.core_send, self.core_recv,
         self.chip_send, self.chip_recv, self.z_send, self.z_recv) = refs
        self.chunks = self.held.shape[0]
        self.rows, self.chunk = self.held.shape[2:]
        self.shard = self.rows // narrow
        self.orders = [list(range(self.bits)), list(range(self.bits))[::-1]]

    def columns_of(self, q):
        return pl.ds(pl.multiple_of(q * self.chunk, self.chunk), self.chunk)

    def arrange(self):
        for k in range(self.chips):
            for core in (0, 1):
                at = (2 * k + core) * self.rows
                if self.dims == NT:
                    tile = self.left[:, at : at + self.rows].T
                else:
                    tile = self.left[at : at + self.rows, :]
                self.turned[core, k * self.rows : (k + 1) * self.rows, :] = tile

    def begin(self, q):
        columns = self.columns_of(q)
        right = self.right[columns, :] if self.dims == NT else self.right[:, columns]
        shape = self.held.shape[1:]
        self.away[q] = dot(self.turned[1 - self.core], right, self.dims, BF16).reshape(shape)
        self.held[q] = dot(self.turned[self.core], right, self.dims, BF16).reshape(shape)
        pltpu.make_async_remote_copy(
            src_ref=self.away.at[q],
            dst_ref=self.core_in.at[q],
            send_sem=self.core_send.at[q],
            recv_sem=self.core_recv.at[q],
            device_id={"wide": self.w ^ 1, "narrow": self.n},
            device_id_type=MESH,
        ).start()

    def add_to(self, target, other):
        def one(r, carry):
            part = pl.ds(pl.multiple_of(r * 16, 16), 16)
            target(part)[...] = (
                target(part)[...].astype(F32) + other(part)[...].astype(F32)
            ).astype(BF16)
            return carry

        lax.fori_loop(0, self.rows // 16, one, 0)

    def tiles_of(self, h, stage):
        order = self.orders[h]
        rest = order[stage + 1 :]
        offset = sum(self.chips >> (i + 1) for i in range(stage))
        fixed = sum(1 << b for b in order[: stage + 1])
        result = []
        for v in range(1 << len(rest)):
            extra = sum(((v >> i) & 1) << b for i, b in enumerate(rest))
            result.append((offset + v, (self.chip & fixed) + extra))
        return result

    def lanes(self, h):
        return pl.ds(h * (self.chunk // 2), self.chunk // 2)

    def chip_copy(self, q, h, stage, slot, kept):
        bit = self.orders[h][stage]
        return pltpu.make_async_remote_copy(
            src_ref=self.held.at[q, kept ^ (1 << bit), :, self.lanes(h)],
            dst_ref=self.chip_in.at[q, h, slot],
            send_sem=self.chip_send.at[q, h, slot],
            recv_sem=self.chip_recv.at[q, h, slot],
            device_id={"wide": self.w ^ (2 << bit), "narrow": self.n},
            device_id_type=MESH,
        )

    def send_stage(self, q, stage):
        for h in (0, 1):
            for slot, kept in self.tiles_of(h, stage):
                self.chip_copy(q, h, stage, slot, kept).start()

    def after_core(self, q):
        arrive(self.core_in.at[q], self.core_recv.at[q])
        for k in range(self.chips):
            self.add_to(
                lambda part, k=k: self.held.at[q, k, part, :],
                lambda part, k=k: self.core_in.at[q, k, part, :],
            )
        self.send_stage(q, 0)

    def z_copy(self, q, step):
        other = lax.rem(self.n + step, self.narrow)
        own = pl.ds(pl.multiple_of(other * self.shard, self.shard), self.shard)
        return pltpu.make_async_remote_copy(
            src_ref=self.held.at[q, self.chip, own, :],
            dst_ref=self.z_in.at[q, step],
            send_sem=self.z_send.at[q, step],
            recv_sem=self.z_recv.at[q, step],
            device_id={"wide": self.w, "narrow": other},
            device_id_type=MESH,
        )

    def after_stage(self, q, stage):
        for h in (0, 1):
            for slot, kept in self.tiles_of(h, stage):
                arrive(self.chip_in.at[q, h, slot], self.chip_recv.at[q, h, slot])
                self.add_to(
                    lambda part, h=h, kept=kept: self.held.at[q, kept, part, self.lanes(h)],
                    lambda part, h=h, slot=slot: self.chip_in.at[q, h, slot, part, :],
                )
        if stage + 1 < self.bits:
            self.send_stage(q, stage + 1)
        else:
            for step in range(1, self.narrow):
                self.z_copy(q, step).start()

    def after_z(self, q):
        for step in range(1, self.narrow):
            arrive(self.z_in.at[q, step], self.z_recv.at[q, step])

        def one(r, carry):
            to = pl.ds(pl.multiple_of(r * 16, 16), 16)
            own = pl.ds(pl.multiple_of(self.n * self.shard + r * 16, 16), 16)
            value = self.held[q, self.chip, own, :].astype(F32)
            for step in range(1, self.narrow):
                value = value + self.z_in[q, step, to, :].astype(F32)
            self.out_ref[to, self.columns_of(q)] = value
            return carry

        lax.fori_loop(0, self.shard // 16, one, 0)

    def after_all(self):
        def one(q, carry):
            self.after_z(q)
            return carry

        lax.fori_loop(0, self.chunks, one, 0)

    def drain(self):
        def one(q, carry):
            arrive(self.core_in.at[q], self.core_send.at[q])
            for stage in range(self.bits):
                for h in (0, 1):
                    for slot, kept in self.tiles_of(h, stage):
                        self.chip_copy(q, h, stage, slot, kept).wait_send()
            for step in range(1, self.narrow):
                self.z_copy(q, step).wait_send()
            return carry

        lax.fori_loop(0, self.chunks, one, 0)


def reduce_scratch(wide, narrow, rows, tokens, columns, chunk):
    chips, rows, chunks = wide // 2, rows // wide, columns // chunk
    dma = pltpu.SemaphoreType.DMA
    return [
        pltpu.VMEM((2, chips * rows, tokens), BF16),
        pltpu.VMEM((chunks, chips, rows, chunk), BF16),
        pltpu.VMEM((chunks, chips, rows, chunk), BF16),
        pltpu.VMEM((chunks, chips, rows, chunk), BF16),
        pltpu.VMEM((chunks, 2, chips - 1, rows, chunk // 2), BF16),
        pltpu.VMEM((chunks, narrow, rows // narrow, chunk), BF16),
        dma((chunks,)),
        dma((chunks,)),
        dma((chunks, 2, chips - 1)),
        dma((chunks, 2, chips - 1)),
        dma((chunks, narrow)),
        dma((chunks, narrow)),
    ]


def greet(wide, narrow):
    w, n = lax.axis_index("wide"), lax.axis_index("narrow")
    barrier = pltpu.get_barrier_semaphore()
    for mask in range(1, wide):
        pl.semaphore_signal(
            barrier, inc=1, device_id={"wide": w ^ mask, "narrow": n}, device_id_type=MESH
        )
    for step in range(1, narrow):
        other = lax.rem(n + step, narrow)
        pl.semaphore_signal(
            barrier, inc=1, device_id={"wide": w, "narrow": other}, device_id_type=MESH
        )
    pl.semaphore_wait(barrier, wide + narrow - 2)


def to_owner(source, target, send_sem, recv_sem, mask):
    w, n = lax.axis_index("wide"), lax.axis_index("narrow")
    return pltpu.make_async_remote_copy(
        src_ref=source,
        dst_ref=target,
        send_sem=send_sem,
        recv_sem=recv_sem,
        device_id={"wide": w ^ mask, "narrow": n},
        device_id_type=MESH,
    )


def to_block(source, target, send_sem, recv_sem, owner):
    n = lax.axis_index("narrow")
    return pltpu.make_async_remote_copy(
        src_ref=source,
        dst_ref=target,
        send_sem=send_sem,
        recv_sem=recv_sem,
        device_id={"wide": owner, "narrow": n},
        device_id_type=MESH,
    )


def arrive(block, sem):
    pltpu.make_async_copy(block, block, sem).wait()


def attend_kernel(
    wide, narrow, groups, start_ref, mine_ref, w_ref, c_ref,
    x_ref, low_ref, full_ref, log_ref, w_all, c_all,
    keys, top, total, acc, done, own_sem, in_send, in_recv, out_send, out_recv,
    line_own, line_send, line_recv, *sems,
):
    me = lax.axis_index("wide")
    blocks, _, rows = x_ref.shape
    width = groups * HEAD_DIM
    own_in = pltpu.make_async_copy(mine_ref.at[me], x_ref.at[me], own_sem.at[0])
    own_in.start()
    greet(wide, narrow)
    for mask in range(1, wide):
        to_owner(
            mine_ref.at[me ^ mask], x_ref.at[me], in_send.at[mask], in_recv.at[me], mask
        ).start()
    flow = Flow(wide, narrow, w_ref, w_all, sems)
    line = Line(narrow, c_ref, c_all, (line_own, line_send, line_recv))
    flow.step(0)
    line.step(0)
    spread = {}
    for t in range(1, flow.last):
        spread.setdefault(min(blocks, blocks // 2 - 1 + t), []).append(functools.partial(flow.step, t))
    for t in range(1, narrow):
        spread.setdefault(min(blocks, blocks // 2 + 2 * t - 1), []).append(functools.partial(line.step, t))
    key_row = lax.broadcasted_iota(jnp.int32, (rows, rows), 0)
    column = lax.broadcasted_iota(jnp.int32, (rows, rows), 1)
    own_in.wait()

    def block(i, carry):
        pl.when(i != me)(lambda: arrive(x_ref.at[i], in_recv.at[i]))
        for at, actions in spread.items():
            if at < blocks:

                @pl.when(i == at)
                def _():
                    for action in actions:
                        action()

        keys[i] = x_ref[i, width : width + HEAD_DIM, :].T
        top[...] = jnp.full_like(top, NEGATIVE)
        total[...] = jnp.zeros_like(total)
        acc[...] = jnp.zeros_like(acc)
        start = start_ref[i]
        query_row = i * rows + column

        def step(j, carry):
            key_index = key_row + j * rows
            allowed = (key_index <= query_row) & (key_index >= start)
            key_block = keys[j]
            value_block = x_ref[j, width + HEAD_DIM :, :]
            for h in range(groups):
                own = pl.ds(h * HEAD_DIM, HEAD_DIM)
                scores = dot(key_block, x_ref[i, own, :], NN)
                scores = jnp.where(allowed, scores, NEGATIVE)
                old = top[h : h + 1, :]
                new = jnp.maximum(old, jnp.max(scores, 0, keepdims=True))
                shrink = jnp.exp(old - new)
                prob = jnp.exp(scores - new)
                top[h : h + 1, :] = new
                total[h : h + 1, :] = total[h : h + 1, :] * shrink + jnp.sum(prob, 0, keepdims=True)
                acc[own, :] = acc[own, :] * shrink + dot(value_block, prob.astype(BF16), NN)
            return carry

        lax.fori_loop(0, i + 1, step, 0)
        log_ref[i] = top[...] + jnp.log(total[...])
        for h in range(groups):
            own = pl.ds(h * HEAD_DIM, HEAD_DIM)
            result = acc[own, :] / total[h : h + 1, :]
            full_ref[i, own, :] = result
            done[i, own, :] = result.astype(BF16)

        @pl.when(i != me)
        def _():
            to_block(done.at[i], low_ref.at[me], out_send.at[i], out_recv.at[me], i).start()

        return carry

    lax.fori_loop(0, blocks, block, 0)
    low_ref[me] = done[me]
    for action in spread.get(blocks, []):
        action()
    flow.end()
    line.end()
    for mask in range(1, wide):
        to_owner(
            mine_ref.at[me ^ mask], x_ref.at[me], in_send.at[mask], in_recv.at[me], mask
        ).wait_send()
        other = me ^ mask
        arrive(low_ref.at[other], out_recv.at[other])
        arrive(done.at[other], out_send.at[other])


def attend(mine, start, w_out, cot, groups):
    wide, narrow = lax.axis_size("wide"), lax.axis_size("narrow")
    blocks, features, rows = mine.shape
    width = groups * HEAD_DIM
    dma = pltpu.SemaphoreType.DMA
    hbm = pl.BlockSpec(memory_space=pl.ANY)
    vmem = pl.BlockSpec(memory_space=pltpu.VMEM)
    return pl.pallas_call(
        functools.partial(attend_kernel, wide, narrow, groups),
        out_shape=(
            jax.ShapeDtypeStruct((blocks, features, rows), BF16),
            jax.ShapeDtypeStruct((blocks, width, rows), BF16),
            jax.ShapeDtypeStruct((blocks, width, rows), F32),
            jax.ShapeDtypeStruct((blocks, groups, rows), F32),
            jax.ShapeDtypeStruct((wide * narrow * w_out.shape[0], w_out.shape[1]), BF16),
            jax.ShapeDtypeStruct((narrow,) + cot.shape, BF16),
        ),
        in_specs=[vmem, vmem, hbm, hbm],
        out_specs=(vmem, vmem, vmem, vmem, hbm, hbm),
        scratch_shapes=[
            pltpu.VMEM((blocks, rows, HEAD_DIM), BF16),
            pltpu.VMEM((groups, rows), F32),
            pltpu.VMEM((groups, rows), F32),
            pltpu.VMEM((width, rows), F32),
            pltpu.VMEM((blocks, width, rows), BF16),
            dma((1,)),
            dma((wide,)),
            dma((wide,)),
            dma((wide,)),
            dma((wide,)),
            dma(()),
            dma((2, narrow)),
            dma((2, narrow)),
        ]
        + flow_sems(wide, narrow),
        compiler_params=pltpu.CompilerParams(
            collective_id=3, has_side_effects=True, vmem_limit_bytes=40 << 20
        ),
        cost_estimate=pl.CostEstimate(
            flops=32 * width * (blocks * rows) ** 2,
            bytes_accessed=64 << 20,
            transcendentals=groups * (blocks * rows) ** 2 // 2,
        ),
    )(start, mine, w_out, cot)


def attend_back_kernel(
    wide, narrow, groups, start_ref, x_ref, mine_ref, full_ref, log_ref, cos_ref, sin_ref, part_ref,
    left_ref, right_ref, out_ref, came_ref, weight_out,
    keys, values, acc, acc_keys, acc_values, grad_ref, done, own_sem, in_send, in_recv,
    q_send, q_recv, k_send, k_recv, p_send, p_recv, *refs,
):
    reduce = Reduce(wide, narrow, left_ref, right_ref, NN, weight_out, refs)
    me, n = lax.axis_index("wide"), lax.axis_index("narrow")

    def part_copy(step):
        other = lax.rem(n + step, narrow)
        return pltpu.make_async_remote_copy(
            src_ref=part_ref.at[other],
            dst_ref=came_ref.at[step],
            send_sem=p_send.at[step],
            recv_sem=p_recv.at[step],
            device_id={"wide": me, "narrow": other},
            device_id_type=MESH,
        )

    own_part = pltpu.make_async_copy(part_ref.at[n], came_ref.at[0], p_send.at[0])
    blocks, _, rows = x_ref.shape
    width = groups * HEAD_DIM
    own_in = pltpu.make_async_copy(mine_ref.at[me], grad_ref.at[me], own_sem.at[0])
    own_in.start()
    for j in range(blocks):
        keys[j] = x_ref[j, width : width + HEAD_DIM, :].T
        values[j] = x_ref[j, width + HEAD_DIM :, :].T
    acc_keys[...] = jnp.zeros_like(acc_keys)
    acc_values[...] = jnp.zeros_like(acc_values)
    greet(wide, narrow)
    for mask in range(1, wide):
        to_owner(
            mine_ref.at[me ^ mask], grad_ref.at[me], in_send.at[mask], in_recv.at[me], mask
        ).start()
    reduce.arrange()
    lax.fori_loop(0, reduce.chunks, lambda q, carry: (reduce.begin(q), carry)[1], 0)
    own_part.start()
    for step in range(1, narrow):
        part_copy(step).start()

    def weight_turn(c):
        chunks = reduce.chunks
        q = jnp.maximum(c - 2, 0) // 2
        ready = (c >= 2) & (lax.rem(c, 2) == 0) & (q < chunks)
        pl.when(ready)(lambda: reduce.after_core(jnp.minimum(q, chunks - 1)))
        actions = [functools.partial(reduce.after_stage, stage=stage) for stage in range(reduce.bits)]
        for index, action in enumerate(actions):
            since = jnp.maximum(c - (2 * chunks + 6 + 6 * index), -1)
            q = jnp.maximum(since, 0) // 5
            ready = (since >= 0) & (lax.rem(jnp.maximum(since, 0), 5) == 0) & (q < chunks)
            pl.when(ready)(functools.partial(action, jnp.minimum(q, chunks - 1)))

    turns = 2 * reduce.chunks + 6 + 6 * (reduce.bits - 1) + 5 * (reduce.chunks - 1) + 1
    key_row = lax.broadcasted_iota(jnp.int32, (rows, rows), 0)
    column = lax.broadcasted_iota(jnp.int32, (rows, rows), 1)
    own_in.wait()
    of_queries, of_keys = pl.ds(0, width), pl.ds(width, 2 * HEAD_DIM)

    def turn_back(block, cos, sin):
        front, back = block[:HALF, :], block[HALF:, :]
        return (front * cos + back * sin).astype(BF16), (back * cos - front * sin).astype(BF16)

    def block(i, carry):
        pl.when(i != me)(lambda: arrive(grad_ref.at[i], in_recv.at[i]))
        acc[...] = jnp.zeros_like(acc)
        start = start_ref[i]
        query_row = i * rows + column
        deltas = [
            jnp.sum(
                grad_ref[i, pl.ds(h * HEAD_DIM, HEAD_DIM), :].astype(F32)
                * full_ref[i, pl.ds(h * HEAD_DIM, HEAD_DIM), :],
                0,
                keepdims=True,
            )
            for h in range(groups)
        ]

        def step(j, carry):
            key_index = key_row + j * rows
            allowed = (key_index <= query_row) & (key_index >= start)
            key_block = keys[j]
            value_block = values[j]
            key_columns = x_ref[j, width : width + HEAD_DIM, :]
            grad_keys = acc_keys[j]
            grad_values = acc_values[j]
            for h in range(groups):
                own = pl.ds(h * HEAD_DIM, HEAD_DIM)
                query = x_ref[i, own, :]
                grad = grad_ref[i, own, :]
                scores = dot(key_block, query, NN)
                scores = jnp.where(allowed, scores, NEGATIVE)
                prob = jnp.exp(scores - log_ref[i, h : h + 1, :])
                grad_prob = dot(value_block, grad, NN)
                grad_scores = (prob * (grad_prob - deltas[h])).astype(BF16)
                acc[own, :] += dot(key_columns, grad_scores, NN)
                grad_keys = grad_keys + dot(query, grad_scores, NT)
                grad_values = grad_values + dot(grad, prob.astype(BF16), NT)
            acc_keys[j] = grad_keys
            acc_values[j] = grad_values
            weight_turn(i * (i + 1) // 2 + j)
            return carry

        lax.fori_loop(0, i + 1, step, 0)
        for h in range(groups):
            at = h * HEAD_DIM
            front, back = turn_back(
                acc[pl.ds(at, HEAD_DIM), :] * SCORE_SCALE, cos_ref[i], sin_ref[i]
            )
            done[i, pl.ds(at, HALF), :] = front
            done[i, pl.ds(at + HALF, HALF), :] = back

        @pl.when(i != me)
        def _():
            to_block(
                done.at[i, of_queries], out_ref.at[me, of_queries], q_send.at[i], q_recv.at[me], i
            ).start()

        return carry

    lax.fori_loop(0, blocks, block, 0)

    def last(j, carry):
        front, back = turn_back(acc_keys[j], cos_ref[j], sin_ref[j])
        done[j, pl.ds(width, HALF), :] = front
        done[j, pl.ds(width + HALF, HALF), :] = back
        done[j, pl.ds(width + HEAD_DIM, HEAD_DIM), :] = acc_values[j].astype(BF16)

        @pl.when(j != me)
        def _():
            to_block(
                done.at[j, of_keys], out_ref.at[me, of_keys], k_send.at[j], k_recv.at[me], j
            ).start()

        return carry

    lax.fori_loop(0, blocks, last, 0)
    out_ref[me] = done[me]

    def left(c, carry):
        weight_turn(c)
        return carry

    lax.fori_loop(blocks * (blocks + 1) // 2, max(turns, blocks * (blocks + 1) // 2), left, 0)

    reduce.after_all()
    reduce.drain()
    for mask in range(1, wide):
        other = me ^ mask
        arrive(mine_ref.at[other], in_send.at[mask])
        arrive(done.at[other, of_queries], q_send.at[other])
        arrive(done.at[other, of_keys], k_send.at[other])
        arrive(out_ref.at[other, of_queries], q_recv.at[other])
        arrive(out_ref.at[other, of_keys], k_recv.at[other])
    own_part.wait()
    for step in range(1, narrow):
        part_copy(step).wait()


def attend_back(x, mine, full, log_total, start, cos, sin, part, left, right, groups):
    wide, narrow = lax.axis_size("wide"), lax.axis_size("narrow")
    blocks, features, rows = x.shape
    width = groups * HEAD_DIM
    dma = pltpu.SemaphoreType.DMA
    hbm = pl.BlockSpec(memory_space=pl.ANY)
    vmem = pl.BlockSpec(memory_space=pltpu.VMEM)
    return pl.pallas_call(
        functools.partial(attend_back_kernel, wide, narrow, groups),
        out_shape=(
            jax.ShapeDtypeStruct(x.shape, BF16),
            jax.ShapeDtypeStruct(part.shape, BF16),
            jax.ShapeDtypeStruct((left.shape[0] // (wide * narrow), right.shape[1]), F32),
        ),
        in_specs=[vmem] * 7 + [hbm, vmem, vmem],
        out_specs=(vmem, hbm, vmem),
        scratch_shapes=[
            pltpu.VMEM((blocks, rows, HEAD_DIM), BF16),
            pltpu.VMEM((blocks, rows, HEAD_DIM), BF16),
            pltpu.VMEM((width, rows), F32),
            pltpu.VMEM((blocks, HEAD_DIM, rows), F32),
            pltpu.VMEM((blocks, HEAD_DIM, rows), F32),
            pltpu.VMEM((blocks, width, rows), BF16),
            pltpu.VMEM((blocks, features, rows), BF16),
            dma((1,)),
        ]
        + [dma((wide,))] * 6
        + [dma((narrow,))] * 2
        + reduce_scratch(wide, narrow, left.shape[0], left.shape[1], right.shape[1], 512),
        compiler_params=pltpu.CompilerParams(
            collective_id=4, has_side_effects=True, vmem_limit_bytes=50 << 20
        ),
        cost_estimate=pl.CostEstimate(
            flops=40 * width * (blocks * rows) ** 2,
            bytes_accessed=4 * x.size * 2,
            transcendentals=groups * (blocks * rows) ** 2 // 2,
        ),
    )(start, x, mine, full, log_total, cos, sin, part, left, right)


def gather(x, axis):
    return lax.all_gather(x, axis, axis=0, tiled=True)


def scatter_sum(x, axis):
    return lax.psum_scatter(x, axis, scatter_dimension=0, tiled=True)


def gather_kernel(wide, narrow, aligned, qkv_ref, cut_ref, qkv_all, cut_all, x_send, x_recv, x_own, *sems):
    w, n = lax.axis_index("wide"), lax.axis_index("narrow")
    greet(wide, narrow)
    flow = Flow(wide, narrow, qkv_ref, qkv_all, sems)
    depth = qkv_ref.shape[0]
    piece = cut_all.shape[1] // (2 * wide)

    def rows_of(owner):
        return cut_all.at[pl.ds(pl.multiple_of(owner * depth, depth), depth), :]

    def pieces(other):
        if not aligned:
            return [(cut_ref.at[other], pl.ds(0, cut_all.shape[1]))]
        return [
            (
                cut_ref.at[:, pl.ds(pl.multiple_of((j * narrow + other) * piece, piece), piece)],
                pl.ds(j * piece, piece),
            )
            for j in range(2 * wide)
        ]

    def target(columns):
        return cut_all.at[pl.ds(pl.multiple_of(n * depth, depth), depth), columns]

    def cut_start(step):
        other = lax.rem(n + step, narrow)
        for source, columns in pieces(other):
            pltpu.make_async_remote_copy(
                src_ref=source,
                dst_ref=target(columns),
                send_sem=x_send.at[step],
                recv_sem=x_recv.at[step],
                device_id={"wide": w, "narrow": other},
                device_id_type=MESH,
            ).start()

    for t in range(flow.last):
        flow.step(t)
        if t == min(1, narrow - 1):
            for source, columns in pieces(n):
                pltpu.make_async_copy(source, target(columns), x_own).start()
            for step in range(1, narrow):
                cut_start(step)
    flow.end()
    own = rows_of(n)
    pltpu.make_async_copy(own, own, x_own).wait()
    for step in range(1, narrow):
        pltpu.make_async_copy(own, own, x_send.at[step]).wait()
        block = rows_of(lax.rem(n + narrow - step, narrow))
        pltpu.make_async_copy(block, block, x_recv.at[step]).wait()


def gather_weights(qkv, gateup):
    wide, narrow = lax.axis_size("wide"), lax.axis_size("narrow")
    dma = pltpu.SemaphoreType.DMA
    hbm = pl.BlockSpec(memory_space=pl.ANY)
    every = wide * narrow
    shard, columns = gateup.shape
    aligned = (columns // (2 * every)) % 128 == 0
    if not aligned:
        gateup = gateup.reshape(shard, 2, wide, narrow, -1).transpose(3, 0, 1, 2, 4)
        gateup = gateup.reshape(narrow, shard, columns // narrow)
    return pl.pallas_call(
        functools.partial(gather_kernel, wide, narrow, aligned),
        out_shape=(
            jax.ShapeDtypeStruct((every * qkv.shape[0], qkv.shape[1]), BF16),
            jax.ShapeDtypeStruct((narrow * shard, columns // narrow), BF16),
        ),
        in_specs=[hbm, hbm],
        out_specs=(hbm, hbm),
        scratch_shapes=[dma((narrow,)), dma((narrow,)), dma(())] + flow_sems(wide, narrow),
        compiler_params=pltpu.CompilerParams(collective_id=0, has_side_effects=True),
        cost_estimate=pl.CostEstimate(flops=0, bytes_accessed=200 << 20, transcendentals=0),
    )(qkv, gateup)


def feed_kernel(
    narrow, x_ref, cot_ref, gate_up_ref, down_ref,
    low_out, grad_x_ref, part_gate_up, part_down,
    group_ref, gate_up, down, cot, hidden, grads, low, came,
    load_sem, x_send, x_recv, out_sem, g_send, g_recv,
):
    w, n = lax.axis_index("wide"), lax.axis_index("narrow")
    rows, width = x_ref.shape
    own = down.shape[0]
    tile = 256
    tiles = own // tile
    wtiles = width // tile

    def to_narrow(other):
        return {"wide": w, "narrow": other}

    loads = [
        pltpu.make_async_copy(gate_up_ref, gate_up, load_sem.at[0]),
        pltpu.make_async_copy(down_ref, down, load_sem.at[1]),
        pltpu.make_async_copy(cot_ref, cot, load_sem.at[2]),
        pltpu.make_async_copy(x_ref, group_ref.at[n], load_sem.at[3]),
    ]
    for load in loads:
        load.start()

    barrier = pltpu.get_barrier_semaphore()
    for step in range(1, narrow):
        pl.semaphore_signal(
            barrier, inc=1, device_id=to_narrow(lax.rem(n + step, narrow)), device_id_type=MESH
        )
    pl.semaphore_wait(barrier, narrow - 1)

    def owner_of(side, d):
        return n - d if side == 0 else n + d

    def valid(side, d):
        return n - d >= 0 if side == 0 else (n + d < narrow) & (d > 0)

    def passes(side, d):
        if side == 0:
            return (n - d >= 0) & (n < narrow - 1)
        return (n + d < narrow) & (n > 0)

    def x_copy(side, d):
        block = group_ref.at[owner_of(side, d)]
        return pltpu.make_async_remote_copy(
            src_ref=block,
            dst_ref=block,
            send_sem=x_send.at[side, d],
            recv_sem=x_recv.at[side, d + 1],
            device_id=to_narrow(n + 1 if side == 0 else n - 1),
            device_id_type=MESH,
        )

    def x_wait(side, d):
        block = group_ref.at[owner_of(side, d)]
        pltpu.make_async_copy(block, block, x_recv.at[side, d]).wait()

    def out_copy(at, block):
        return pltpu.make_async_copy(low.at[at], low_out.at[block], out_sem.at[at])

    def g_copy(block):
        return pltpu.make_async_remote_copy(
            src_ref=cot.at[block],
            dst_ref=came.at[n],
            send_sem=g_send.at[block],
            recv_sem=g_recv.at[n],
            device_id=to_narrow(block),
            device_id_type=MESH,
        )

    def compute(side, d):
        block = n - d + 2 * d * side
        before = 1 + jnp.minimum(n, d - 1) + jnp.minimum(narrow - 1 - n, d - 1)
        before = jnp.where(d == 0, 0, before + jnp.where((side == 1) & (n - d >= 0), 1, 0))
        at = lax.rem(before, 2)

        pl.when(before >= 2)(lambda: out_copy(at, block).wait())

        def first(f, carry):
            columns = pl.ds(pl.multiple_of(f * tile, tile), tile)
            other = pl.ds(pl.multiple_of(own + f * tile, tile), tile)
            x = group_ref[block]
            gate = dot(x, gate_up[:, columns], NN)
            up = dot(x, gate_up[:, other], NN)
            grad = dot(cot[block], down[columns, :], NT)
            sig = 1.0 / (1.0 + jnp.exp(-gate))
            silu = gate * sig
            hidden[block, :, columns] = (silu * up).astype(BF16)
            grads[block, :, columns] = (grad * up * (sig + silu * (1.0 - sig))).astype(BF16)
            grads[block, :, other] = (grad * silu).astype(BF16)
            return carry

        lax.fori_loop(0, tiles, first, 0)

        def second(f, carry):
            columns = pl.ds(pl.multiple_of(f * tile, tile), tile)
            cot[block, :, columns] = dot(grads[block], gate_up[columns, :], NT, BF16)
            low[at, :, columns] = dot(hidden[block], down[:, columns], NN, BF16)
            return carry

        lax.fori_loop(0, wtiles, second, 0)
        out_copy(at, block).start()
        pl.when(block != n)(lambda: g_copy(block).start())

    def distance(d, carry):
        for side in (0, 1):

            @pl.when(passes(side, d + 1))
            def _():
                x_wait(side, d + 1)
                x_copy(side, d + 1).start()

            @pl.when(valid(side, d) & (d > 0) & jnp.logical_not(passes(side, d)))
            def _():
                x_wait(side, d)

        @pl.when(d == 0)
        def _():
            for load in loads[:3]:
                load.wait()

        def one(side, carry):
            ok = jnp.where(side == 0, n - d, jnp.where(d > 0, narrow - 1 - n - d, -1)) >= 0
            pl.when(ok)(lambda: compute(side, d))
            return carry

        lax.fori_loop(0, 2, one, 0)
        return carry

    loads[3].wait()
    for side in (0, 1):
        pl.when(passes(side, 0))(lambda side=side: x_copy(side, 0).start())
    lax.fori_loop(0, narrow, distance, 0)

    tokens = narrow * rows
    again = [
        pltpu.make_async_copy(
            cot_ref.at[o], gate_up.at[pl.ds(o * rows, rows), pl.ds(0, width)], load_sem.at[4 + o]
        )
        for o in range(narrow)
    ]
    for load in again:
        load.start()
    for at in range(2):
        out_copy(at, n).wait()

    def flipped(ref, columns):
        return jnp.concatenate([ref[o, :, columns].T for o in range(narrow)], 1)

    def weight_tile(t, left, right, at_row, out_ref, first):
        at = lax.rem(t, 2)
        copy = pltpu.make_async_copy(low.at[at], out_ref, out_sem.at[at])
        pl.when(t >= 2)(lambda: copy.wait())
        turned = flipped(left, pl.ds(pl.multiple_of(at_row, tile), tile))

        def one(c, carry):
            columns = pl.ds(pl.multiple_of(c * 512, 512), 512)
            source = pl.ds(pl.multiple_of(first + c * 512, 512), 512)
            low[at, :, columns] = dot(turned, right(source), NN, BF16)
            return carry

        lax.fori_loop(0, width // 512, one, 0)
        copy.start()

    halves = 2 * own // width

    def gate_up_tile(t, carry):
        row, half = t // halves * tile, lax.rem(t, halves) * width
        row, half = pl.multiple_of(row, tile), pl.multiple_of(half, width)
        weight_tile(
            t, group_ref, lambda source: grads[:, :, source].reshape(tokens, 512), row,
            part_gate_up.at[pl.ds(row, tile), pl.ds(half, width)], half,
        )
        return carry

    def down_tile(t, carry):
        row = pl.multiple_of(t * tile, tile)
        weight_tile(
            t + 2, hidden, lambda source: gate_up[pl.ds(0, tokens), source], row,
            part_down.at[pl.ds(row, tile), :], 0,
        )
        return carry

    lax.fori_loop(0, wtiles * halves, gate_up_tile, 0)
    for load in again:
        load.wait()
    lax.fori_loop(0, tiles, down_tile, 0)
    for at in range(2):
        out_copy(at, n).wait()
    for side in (0, 1):
        for d in range(narrow - 1):
            pl.when(passes(side, d))(lambda side=side, d=d: x_copy(side, d).wait_send())
    for step in range(1, narrow):
        other = lax.rem(n + step, narrow)
        g_copy(other).wait_send()
        block = came.at[other]
        pltpu.make_async_copy(block, block, g_recv.at[other]).wait()

    def add(r, carry):
        part = pl.ds(pl.multiple_of(r * 16, 16), 16)
        total = cot[n, part, :].astype(F32)
        for step in range(1, narrow):
            total = total + came[lax.rem(n + step, narrow), part, :].astype(F32)
        grad_x_ref[part, :] = total
        return carry

    lax.fori_loop(0, rows // 16, add, 0)


def feed(x, cot_group, gate_up, down):
    narrow = lax.axis_size("narrow")
    rows, width = x.shape
    own = down.shape[0]
    dma = pltpu.SemaphoreType.DMA
    hbm = pl.BlockSpec(memory_space=pl.ANY)
    vmem = pl.BlockSpec(memory_space=pltpu.VMEM)
    return pl.pallas_call(
        functools.partial(feed_kernel, narrow),
        out_shape=(
            jax.ShapeDtypeStruct((narrow, rows, width), BF16),
            jax.ShapeDtypeStruct((rows, width), F32),
            jax.ShapeDtypeStruct((width, 2 * own), BF16),
            jax.ShapeDtypeStruct((own, width), BF16),
        ),
        in_specs=[vmem, hbm, hbm, hbm],
        out_specs=(hbm, vmem, hbm, hbm),
        scratch_shapes=[
            pltpu.VMEM((narrow, rows, width), BF16),
            pltpu.VMEM((width, 2 * own), BF16),
            pltpu.VMEM((own, width), BF16),
            pltpu.VMEM((narrow, rows, width), BF16),
            pltpu.VMEM((narrow, rows, own), BF16),
            pltpu.VMEM((narrow, rows, 2 * own), BF16),
            pltpu.VMEM((2, rows, width), BF16),
            pltpu.VMEM((narrow, rows, width), BF16),
            dma((4 + narrow,)),
            dma((2, narrow + 1)),
            dma((2, narrow + 1)),
            dma((2,)),
            dma((narrow,)),
            dma((narrow,)),
        ],
        compiler_params=pltpu.CompilerParams(
            collective_id=1, has_side_effects=True, vmem_limit_bytes=58 << 20
        ),
        cost_estimate=pl.CostEstimate(
            flops=12 * narrow * rows * width * own, bytes_accessed=300 << 20, transcendentals=0
        ),
    )(x, cot_group.reshape(narrow, rows, width), gate_up, down)


def sum_kernel(
    wide, narrow, left_ref, right_ref, cut_ref, gains_ref, qkv_out, cut_out, gains_out,
    cut_in, gain_w, gain_sum, gain_z, own_sem, cut_send, cut_recv, gw_send, gw_recv, gz_send, gz_recv, *refs,
):
    reduce = Reduce(wide, narrow, left_ref, right_ref, NT, qkv_out, refs)
    w, n = reduce.w, reduce.n
    chunks, bits = reduce.chunks, reduce.bits
    reduce.arrange()
    greet(wide, narrow)

    def to_wide(mask):
        return {"wide": w ^ mask, "narrow": n}

    def to_narrow(step):
        return {"wide": w, "narrow": lax.rem(n + step, narrow)}

    own_cut = pltpu.make_async_copy(cut_ref.at[n], cut_in.at[n], own_sem)

    def cut_copy(step):
        return pltpu.make_async_remote_copy(
            src_ref=cut_ref.at[lax.rem(n + step, narrow)],
            dst_ref=cut_in.at[n],
            send_sem=cut_send.at[step],
            recv_sem=cut_recv.at[step],
            device_id=to_narrow(step),
            device_id_type=MESH,
        )

    def gw_copy(mask):
        return pltpu.make_async_remote_copy(
            src_ref=gains_ref.at[w ^ mask],
            dst_ref=gain_w.at[mask],
            send_sem=gw_send.at[mask],
            recv_sem=gw_recv.at[mask],
            device_id=to_wide(mask),
            device_id_type=MESH,
        )

    def gz_copy(step):
        return pltpu.make_async_remote_copy(
            src_ref=gain_sum.at[lax.rem(n + step, narrow)],
            dst_ref=gain_z.at[step],
            send_sem=gz_send.at[step],
            recv_sem=gz_recv.at[step],
            device_id=to_narrow(step),
            device_id_type=MESH,
        )

    ahead = min(4, chunks)
    lax.fori_loop(0, ahead, lambda q, carry: (reduce.begin(q), carry)[1], 0)
    own_cut.start()
    for step in range(1, narrow):
        cut_copy(step).start()
    for mask in range(1, wide):
        gw_copy(mask).start()

    def turn(t, carry):
        pl.when(t + ahead < chunks)(lambda: reduce.begin(t + ahead))
        pl.when(t < chunks)(lambda: reduce.after_core(t))
        for stage in range(bits):
            q = t - 1 - stage
            pl.when((q >= 0) & (q < chunks))(functools.partial(reduce.after_stage, q, stage))
        return carry

    lax.fori_loop(0, chunks + bits, turn, 0)

    total = gains_ref[w]
    for mask in range(1, wide):
        block = gain_w.at[mask]
        pltpu.make_async_copy(block, block, gw_recv.at[mask]).wait()
        total = total + gain_w[mask]
    gain_sum[...] = total
    for step in range(1, narrow):
        gz_copy(step).start()

    reduce.after_all()
    own_cut.wait()
    for step in range(1, narrow):
        other = lax.rem(n + narrow - step, narrow)
        arrive(cut_in.at[other], cut_recv.at[step])
    piece = cut_in.shape[2] // (2 * wide)
    if cut_out.shape[0] == narrow:
        for other in range(narrow):
            cut_out[other] = cut_in[other].astype(F32)
    else:
        for j in range(2 * wide):
            for other in range(narrow):
                cut_out[:, pl.ds((j * narrow + other) * piece, piece)] = cut_in[
                    other, :, pl.ds(j * piece, piece)
                ].astype(F32)

    total = gain_sum[n]
    for step in range(1, narrow):
        block = gain_z.at[step]
        pltpu.make_async_copy(block, block, gz_recv.at[step]).wait()
        total = total + gain_z[step]
    gains_out[...] = total

    for mask in range(1, wide):
        gw_copy(mask).wait_send()
    for step in range(1, narrow):
        gz_copy(step).wait_send()
        cut_copy(step).wait_send()
    reduce.drain()


def sum_all(left, right, cut, gains):
    wide, narrow = lax.axis_size("wide"), lax.axis_size("narrow")
    shard, cut_width = cut.shape[1:]
    aligned = (cut_width // (2 * wide)) % 128 == 0
    cut_shape = (shard, narrow * cut_width) if aligned else cut.shape
    dma = pltpu.SemaphoreType.DMA
    hbm = pl.BlockSpec(memory_space=pl.ANY)
    vmem = pl.BlockSpec(memory_space=pltpu.VMEM)
    results = pl.pallas_call(
        functools.partial(sum_kernel, wide, narrow),
        out_shape=(
            jax.ShapeDtypeStruct((shard, right.shape[0]), F32),
            jax.ShapeDtypeStruct(cut_shape, F32),
            jax.ShapeDtypeStruct((8, 128), F32),
        ),
        in_specs=[vmem, vmem, hbm, vmem],
        out_specs=(vmem, vmem, vmem),
        scratch_shapes=[
            pltpu.VMEM(cut.shape, BF16),
            pltpu.VMEM((wide, narrow, 8, 128), F32),
            pltpu.VMEM((narrow, 8, 128), F32),
            pltpu.VMEM((narrow, 8, 128), F32),
            dma(()),
            dma((narrow,)),
            dma((narrow,)),
            dma((wide,)),
            dma((wide,)),
            dma((narrow,)),
            dma((narrow,)),
        ]
        + reduce_scratch(wide, narrow, left.shape[1], left.shape[0], right.shape[0], 256),
        compiler_params=pltpu.CompilerParams(
            collective_id=2, has_side_effects=True, vmem_limit_bytes=54 << 20
        ),
        cost_estimate=pl.CostEstimate(flops=0, bytes_accessed=300 << 20, transcendentals=0),
    )(left, right, cut, gains)
    return results, aligned


def per_device(tokens, lengths, gain_attn, w_qkv, w_out, gain_mlp, w_gateup, w_down, cotangent):
    rows, width = tokens.shape[1:]
    wide, narrow = lax.axis_size("wide"), lax.axis_size("narrow")
    pack_rows = rows * wide
    query_width, key_width = HEADS * HEAD_DIM, KV_HEADS * HEAD_DIM
    groups = HEADS // wide
    copies = wide // KV_HEADS
    own_ff = FF // narrow
    first, positions = places(lengths[0], pack_rows)
    cos_all, sin_all = rotary(positions.astype(F32), HALF)
    first_row = lax.axis_index("wide") * rows
    cos = lax.dynamic_slice_in_dim(cos_all, first_row, rows, 1)
    sin = lax.dynamic_slice_in_dim(sin_all, first_row, rows, 1)
    cos_all = cos_all.reshape(HALF, wide, rows).transpose(1, 0, 2)
    sin_all = sin_all.reshape(HALF, wide, rows).transpose(1, 0, 2)
    start = first.reshape(wide, 1, rows)

    gains = jnp.stack([gain_attn, gain_mlp], -1)
    with_gains = jnp.concatenate([w_qkv, jnp.pad(gains, ((0, 0), (0, 126)))], -1)
    shard = w_gateup.shape[0]
    qkv_gained, gateup_rows = gather_weights(with_gains, w_gateup)
    qkv_whole = qkv_gained[:, : w_qkv.shape[1]]
    gain_one = qkv_gained[:, w_qkv.shape[1]].astype(F32)
    gain_two = qkv_gained[:, w_qkv.shape[1] + 1].astype(F32)
    gateup_own = gather(gateup_rows, "wide")
    down_own = gather(w_down, "wide")

    inputs = tokens[0].astype(F32)
    scale_one = lax.rsqrt(jnp.mean(inputs * inputs, -1, keepdims=True) + EPS)
    unit_one = inputs * scale_one
    normed_one = (unit_one * gain_one).astype(BF16)
    projected = dot(qkv_whole, normed_one, (((0,), (1,)), ((), ())))
    turning = projected[: query_width + key_width].reshape(HEADS + KV_HEADS, 2, HALF, rows)
    front, back = turning[:, 0], turning[:, 1]
    turned = jnp.stack([front * cos - back * sin, back * cos + front * sin], 1)
    queries = (turned[:HEADS] * SCORE_SCALE).astype(BF16).reshape(wide, groups * HEAD_DIM, rows)
    keys = turned[HEADS:].astype(BF16).reshape(KV_HEADS, HEAD_DIM, rows)
    values = projected[query_width + key_width :].astype(BF16).reshape(KV_HEADS, HEAD_DIM, rows)
    keys_values = jnp.repeat(jnp.concatenate([keys, values], 1), copies, 0)
    heads, attended_low, attended_full, log_total, out_whole, cot_group = attend(
        jnp.concatenate([queries, keys_values], 1), start, w_out, cotangent[0], groups
    )
    cot_group = cot_group.reshape(-1, width)
    attended_low = attended_low.reshape(query_width, rows)
    middle = inputs + dot(attended_low, out_whole, TN)
    scale_two = lax.rsqrt(jnp.mean(middle * middle, -1, keepdims=True) + EPS)
    unit_two = middle * scale_two
    normed_two = (unit_two * gain_two).astype(BF16)

    low_part, grad_normed_two, part_gateup, part_down = feed(
        normed_two, cot_group, gateup_own, down_own
    )
    grad_gateup = scatter_sum(part_gateup, "wide").reshape(narrow, shard, 2 * own_ff)
    grad_down = scatter_sum(part_down, "wide")
    part_gain_two = jnp.sum(grad_normed_two * unit_two, 0)
    grad_middle = cotangent[0].astype(F32) + norm_back(
        grad_normed_two * gain_two, unit_two, scale_two
    )
    grad_branch = grad_middle.astype(BF16)
    grad_attended = dot(out_whole, grad_branch, NT, BF16).reshape(wide, groups * HEAD_DIM, rows)
    grad_heads, low_came, grad_wout = attend_back(
        heads, grad_attended, attended_full, log_total, start, cos_all, sin_all, low_part,
        attended_low, grad_branch, groups,
    )
    layer_out = (middle + jnp.sum(low_came.astype(F32), 0)).astype(BF16)[None]
    grad_queries = grad_heads[:, : groups * HEAD_DIM].reshape(query_width, rows)
    grad_keys_values = (
        grad_heads[:, groups * HEAD_DIM :]
        .reshape(KV_HEADS, copies, 2, HEAD_DIM, rows)
        .astype(F32)
        .sum(1)
        .astype(BF16)
    )
    grad_projected = jnp.concatenate(
        [
            grad_queries,
            grad_keys_values[:, 0].reshape(key_width, rows),
            grad_keys_values[:, 1].reshape(key_width, rows),
        ],
        0,
    )
    grad_normed_one = dot(grad_projected, qkv_whole, (((0,), (1,)), ((), ())))
    part_gain_one = jnp.sum(grad_normed_one * unit_one, 0)
    part_gains = jnp.stack([part_gain_one, part_gain_two], 0).reshape(2, wide, narrow, shard)
    part_gains = jnp.pad(
        part_gains.transpose(1, 2, 0, 3), ((0, 0), (0, 0), (0, 6), (0, 128 - shard))
    )
    (grad_qkv, grad_gateup, grad_gains), done = sum_all(
        normed_one, grad_projected, grad_gateup, part_gains
    )
    if not done:
        grad_gateup = (
            grad_gateup.reshape(narrow, shard, 2, wide, -1)
            .transpose(1, 2, 3, 0, 4)
            .reshape(shard, 2 * FF)
        )
    grad_down, grad_gains = lax.optimization_barrier((grad_down, grad_gains))
    grad_down = grad_down.astype(F32)
    grad_inputs = grad_middle + norm_back(grad_normed_one * gain_one, unit_one, scale_one)
    grad_tokens = grad_inputs.astype(BF16)[None]
    return (
        layer_out,
        grad_tokens,
        grad_gains[0, :shard],
        grad_qkv,
        grad_wout,
        grad_gains[1, :shard],
        grad_gateup,
        grad_down,
    )


def solution(mesh):
    rows, packs = P("narrow", "wide", None), P("narrow", None)
    weight, gain = P(BOTH, None), P(BOTH)
    return jax.shard_map(
        per_device,
        mesh=mesh,
        in_specs=(rows, packs, gain, weight, weight, gain, weight, weight, rows),
        out_specs=(rows, rows, gain, weight, weight, gain, weight, weight),
        check_vma=False,
    )
```

```python
import functools
import math

import jax
import jax.numpy as jnp
from jax import lax
from jax.experimental import pallas as pl
from jax.experimental.pallas import tpu as pltpu
from jax.sharding import PartitionSpec as P

FF = 8192
HEADS = 32
KV_HEADS = 8
HEAD_DIM = 64
HALF = HEAD_DIM // 2
EPS = 1e-05
NEGATIVE = -1e30
SCORE_SCALE = 1.0 / math.sqrt(HEAD_DIM)
BOTH = ("wide", "narrow")
F32 = jnp.float32
BF16 = jnp.bfloat16
NN = (((1,), (0,)), ((), ()))
NT = (((1,), (1,)), ((), ()))
TN = (((0,), (0,)), ((), ()))


def dot(left, right, dims, kind=F32):
    return lax.dot_general(left, right, dims, preferred_element_type=F32).astype(kind)


def places(lengths_row, total_rows):
    seq_ends = jnp.cumsum(lengths_row)
    starts = seq_ends - lengths_row
    row_index = jnp.arange(total_rows, dtype=jnp.int32)
    segments = jnp.sum((row_index[:, None] >= seq_ends[None, :]).astype(jnp.int32), -1)
    slot_index = jnp.arange(lengths_row.shape[0], dtype=jnp.int32)
    owned = segments[:, None] == slot_index[None, :]
    first = jnp.sum(jnp.where(owned, starts[None, :], 0), -1)
    return first, row_index - first


def rotary(positions, half_width):
    channel = jnp.arange(half_width, dtype=jnp.float32)
    inverse_rate = jnp.power(500000.0, -channel / half_width)
    wavelength = 2.0 * math.pi / inverse_rate
    smooth = (8192.0 / wavelength - 1.0) / 3.0
    blended = (1.0 - smooth) * inverse_rate / 32.0 + smooth * inverse_rate
    frequency = jnp.where(
        wavelength < 2048.0,
        inverse_rate,
        jnp.where(wavelength > 8192.0, inverse_rate / 32.0, blended),
    )
    angles = frequency[:, None] * positions[None, :]
    return jnp.cos(angles), jnp.sin(angles)


def norm_back(grad_unit, unit_rows, row_scale):
    return row_scale * (grad_unit - unit_rows * jnp.mean(grad_unit * unit_rows, -1, keepdims=True))


MESH = pl.DeviceIdType.MESH


class Flow:
    def __init__(self, wide, narrow, x_ref, out_ref, sems):
        self.wide, self.narrow, self.x_ref, self.out_ref = wide, narrow, x_ref, out_ref
        self.w, self.n = lax.axis_index("wide"), lax.axis_index("narrow")
        (self.own_sem, self.z_send, self.z_recv, self.m_send, self.m_recv,
         self.r_send, self.r_recv, self.c_send, self.c_recv) = sems
        self.relay = wide == 8
        self.masks = [2, 4] if self.relay else list(range(2, wide, 2))
        self.last = narrow + 2

    def to_wide(self, mask):
        return {"wide": self.w ^ mask, "narrow": self.n}

    def owner_of(self, side, d):
        return self.n - d if side == 0 else self.n + d

    def valid(self, side, d):
        return self.n - d >= 0 if side == 0 else self.n + d < self.narrow

    def can_pass(self, side, d):
        if side == 0:
            return (self.n - (d - 1) >= 0) & (self.n < self.narrow - 1)
        return (self.n + (d - 1) < self.narrow) & (self.n > 0)

    def slot(self, side, d):
        return d - 1 + side * (self.narrow - 1) if d else 2 * (self.narrow - 1)

    def at_distance(self, d, action):
        if d == 0:
            action(0, 0)
            return
        for side in (0, 1):
            pl.when(self.valid(side, d))(functools.partial(action, side, d))

    def place(self, owner_w, owner_n, part=None):
        depth = self.x_ref.shape[0]
        half = depth // 2
        at = (owner_w * self.narrow + owner_n) * depth
        if part is None:
            return self.out_ref.at[pl.ds(pl.multiple_of(at, depth), depth), :]
        return self.out_ref.at[pl.ds(pl.multiple_of(at + part * half, half), half), :]

    def own_copy(self):
        return pltpu.make_async_copy(self.x_ref, self.place(self.w, self.n), self.own_sem)

    def z_copy(self, side, d):
        block = self.place(self.w, self.owner_of(side, d - 1))
        return pltpu.make_async_remote_copy(
            src_ref=self.x_ref if d == 1 else block,
            dst_ref=block,
            send_sem=self.z_send.at[side, d],
            recv_sem=self.z_recv.at[side, d],
            device_id={"wide": self.w, "narrow": self.n + 1 if side == 0 else self.n - 1},
            device_id_type=MESH,
        )

    def z_wait(self, side, d):
        block = self.place(self.w, self.owner_of(side, d))
        pltpu.make_async_copy(block, block, self.z_recv.at[side, d]).wait()

    def m_copy(self, i, side, d):
        block = self.place(self.w, self.owner_of(side, d))
        return pltpu.make_async_remote_copy(
            src_ref=self.x_ref if d == 0 else block,
            dst_ref=block,
            send_sem=self.m_send.at[i, self.slot(side, d)],
            recv_sem=self.m_recv.at[i, self.slot(side, d)],
            device_id=self.to_wide(self.masks[i]),
            device_id_type=MESH,
        )

    def m_wait(self, i, side, d):
        block = self.place(self.w ^ self.masks[i], self.owner_of(side, d))
        pltpu.make_async_copy(block, block, self.m_recv.at[i, self.slot(side, d)]).wait()

    def r_copy(self, part, side, d):
        block = self.place(self.w ^ self.masks[part], self.owner_of(side, d), part)
        return pltpu.make_async_remote_copy(
            src_ref=block,
            dst_ref=block,
            send_sem=self.r_send.at[part, self.slot(side, d)],
            recv_sem=self.r_recv.at[part, self.slot(side, d)],
            device_id=self.to_wide(self.masks[1 - part]),
            device_id_type=MESH,
        )

    def r_wait(self, part, side, d):
        block = self.place(self.w ^ 6, self.owner_of(side, d), part)
        pltpu.make_async_copy(block, block, self.r_recv.at[part, self.slot(side, d)]).wait()

    def c_copy(self, chip, side, d):
        block = self.place(self.w ^ (2 * chip), self.owner_of(side, d))
        return pltpu.make_async_remote_copy(
            src_ref=self.x_ref if d == 0 and chip == 0 else block,
            dst_ref=block,
            send_sem=self.c_send.at[chip, self.slot(side, d)],
            recv_sem=self.c_recv.at[chip, self.slot(side, d)],
            device_id=self.to_wide(1),
            device_id_type=MESH,
        )

    def c_wait(self, chip, side, d):
        block = self.place((self.w ^ 1) ^ (2 * chip), self.owner_of(side, d))
        pltpu.make_async_copy(block, block, self.c_recv.at[chip, self.slot(side, d)]).wait()

    def send_from_here(self, side, d):
        if d > 0:
            self.z_wait(side, d)
        if 0 < d < self.narrow - 1:
            pl.when(self.can_pass(side, d + 1))(lambda: self.z_copy(side, d + 1).start())
        for i in range(len(self.masks)):
            self.m_copy(i, side, d).start()
        self.c_copy(0, side, d).start()

    def send_on(self, side, d):
        for i in range(len(self.masks)):
            self.m_wait(i, side, d)
            if self.relay:
                self.r_copy(i, side, d).start()
            self.c_copy(self.masks[i] // 2, side, d).start()

    def send_last(self, side, d):
        self.r_wait(0, side, d)
        self.r_wait(1, side, d)
        self.c_copy(3, side, d).start()

    def step(self, t):
        if t == 0:
            self.own_copy().start()
            for side in (0, 1):
                pl.when(self.can_pass(side, 1))(lambda side=side: self.z_copy(side, 1).start())
        if 0 <= t < self.narrow:
            self.at_distance(t, self.send_from_here)
        if 0 <= t - 1 < self.narrow:
            self.at_distance(t - 1, self.send_on)
        if self.relay and 0 <= t - 2 < self.narrow:
            self.at_distance(t - 2, self.send_last)

    def finish(self, side, d):
        for i in range(len(self.masks)):
            self.m_copy(i, side, d).wait_send()
            if self.relay:
                self.r_copy(i, side, d).wait_send()
        for chip in range(self.wide // 2):
            self.c_copy(chip, side, d).wait_send()
            self.c_wait(chip, side, d)

    def end(self):
        self.own_copy().wait()
        for side in (0, 1):
            for d in range(1, self.narrow):
                pl.when(self.can_pass(side, d))(
                    lambda side=side, d=d: self.z_copy(side, d).wait_send()
                )
        for d in range(self.narrow):
            self.at_distance(d, self.finish)


class Line:
    def __init__(self, narrow, x_ref, out_ref, sems):
        self.narrow, self.x_ref, self.out_ref = narrow, x_ref, out_ref
        self.w, self.n = lax.axis_index("wide"), lax.axis_index("narrow")
        self.own_sem, self.send, self.recv = sems

    def owner_of(self, side, d):
        return self.n - d if side == 0 else self.n + d

    def valid(self, side, d):
        return self.n - d >= 0 if side == 0 else self.n + d < self.narrow

    def can_pass(self, side, d):
        if side == 0:
            return (self.n - (d - 1) >= 0) & (self.n < self.narrow - 1)
        return (self.n + (d - 1) < self.narrow) & (self.n > 0)

    def own_copy(self):
        return pltpu.make_async_copy(self.x_ref, self.out_ref.at[self.n], self.own_sem)

    def copy(self, side, d):
        block = self.out_ref.at[self.owner_of(side, d - 1)]
        return pltpu.make_async_remote_copy(
            src_ref=self.x_ref if d == 1 else block,
            dst_ref=block,
            send_sem=self.send.at[side, d],
            recv_sem=self.recv.at[side, d],
            device_id={"wide": self.w, "narrow": self.n + 1 if side == 0 else self.n - 1},
            device_id_type=MESH,
        )

    def pass_on(self, side, d):
        arrive(self.out_ref.at[self.owner_of(side, d)], self.recv.at[side, d])
        if d < self.narrow - 1:
            pl.when(self.can_pass(side, d + 1))(lambda: self.copy(side, d + 1).start())

    def step(self, t):
        if t == 0:
            self.own_copy().start()
        for side in (0, 1):
            if t == 0:
                pl.when(self.can_pass(side, 1))(lambda side=side: self.copy(side, 1).start())
            else:
                pl.when(self.valid(side, t))(lambda side=side: self.pass_on(side, t))

    def end(self):
        self.own_copy().wait()
        for side in (0, 1):
            for d in range(1, self.narrow):
                pl.when(self.can_pass(side, d))(lambda side=side, d=d: self.copy(side, d).wait_send())


def flow_sems(wide, narrow):
    slots = 2 * narrow - 1
    masks = 2 if wide == 8 else wide // 2 - 1
    dma = pltpu.SemaphoreType.DMA
    return [
        dma(()),
        dma((2, narrow)),
        dma((2, narrow)),
        dma((masks, slots)),
        dma((masks, slots)),
        dma((2, slots)),
        dma((2, slots)),
        dma((wide // 2, slots)),
        dma((wide // 2, slots)),
    ]


class Reduce:
    def __init__(self, wide, narrow, left, right, dims, out_ref, refs):
        self.wide, self.narrow, self.left, self.right, self.dims = wide, narrow, left, right, dims
        self.out_ref = out_ref
        self.w, self.n = lax.axis_index("wide"), lax.axis_index("narrow")
        self.core, self.chip = lax.rem(self.w, 2), self.w // 2
        self.chips = wide // 2
        self.bits = self.chips.bit_length() - 1
        (self.turned, self.held, self.away, self.core_in, self.chip_in, self.z_in, self.core_send, self.core_recv,
         self.chip_send, self.chip_recv, self.z_send, self.z_recv) = refs
        self.chunks = self.held.shape[0]
        self.rows, self.chunk = self.held.shape[2:]
        self.shard = self.rows // narrow
        self.orders = [list(range(self.bits)), list(range(self.bits))[::-1]]

    def columns_of(self, q):
        return pl.ds(pl.multiple_of(q * self.chunk, self.chunk), self.chunk)

    def arrange(self):
        for k in range(self.chips):
            for core in (0, 1):
                at = (2 * k + core) * self.rows
                if self.dims == NT:
                    tile = self.left[:, at : at + self.rows].T
                else:
                    tile = self.left[at : at + self.rows, :]
                self.turned[core, k * self.rows : (k + 1) * self.rows, :] = tile

    def begin(self, q):
        columns = self.columns_of(q)
        right = self.right[columns, :] if self.dims == NT else self.right[:, columns]
        shape = self.held.shape[1:]
        self.away[q] = dot(self.turned[1 - self.core], right, self.dims, BF16).reshape(shape)
        self.held[q] = dot(self.turned[self.core], right, self.dims, BF16).reshape(shape)
        pltpu.make_async_remote_copy(
            src_ref=self.away.at[q],
            dst_ref=self.core_in.at[q],
            send_sem=self.core_send.at[q],
            recv_sem=self.core_recv.at[q],
            device_id={"wide": self.w ^ 1, "narrow": self.n},
            device_id_type=MESH,
        ).start()

    def add_to(self, target, other):
        def one(r, carry):
            part = pl.ds(pl.multiple_of(r * 16, 16), 16)
            target(part)[...] = (
                target(part)[...].astype(F32) + other(part)[...].astype(F32)
            ).astype(BF16)
            return carry

        lax.fori_loop(0, self.rows // 16, one, 0)

    def tiles_of(self, h, stage):
        order = self.orders[h]
        rest = order[stage + 1 :]
        offset = sum(self.chips >> (i + 1) for i in range(stage))
        fixed = sum(1 << b for b in order[: stage + 1])
        result = []
        for v in range(1 << len(rest)):
            extra = sum(((v >> i) & 1) << b for i, b in enumerate(rest))
            result.append((offset + v, (self.chip & fixed) + extra))
        return result

    def lanes(self, h):
        return pl.ds(h * (self.chunk // 2), self.chunk // 2)

    def chip_copy(self, q, h, stage, slot, kept):
        bit = self.orders[h][stage]
        return pltpu.make_async_remote_copy(
            src_ref=self.held.at[q, kept ^ (1 << bit), :, self.lanes(h)],
            dst_ref=self.chip_in.at[q, h, slot],
            send_sem=self.chip_send.at[q, h, slot],
            recv_sem=self.chip_recv.at[q, h, slot],
            device_id={"wide": self.w ^ (2 << bit), "narrow": self.n},
            device_id_type=MESH,
        )

    def send_stage(self, q, stage):
        for h in (0, 1):
            for slot, kept in self.tiles_of(h, stage):
                self.chip_copy(q, h, stage, slot, kept).start()

    def after_core(self, q):
        arrive(self.core_in.at[q], self.core_recv.at[q])
        for k in range(self.chips):
            self.add_to(
                lambda part, k=k: self.held.at[q, k, part, :],
                lambda part, k=k: self.core_in.at[q, k, part, :],
            )
        self.send_stage(q, 0)

    def z_copy(self, q, step):
        other = lax.rem(self.n + step, self.narrow)
        own = pl.ds(pl.multiple_of(other * self.shard, self.shard), self.shard)
        return pltpu.make_async_remote_copy(
            src_ref=self.held.at[q, self.chip, own, :],
            dst_ref=self.z_in.at[q, step],
            send_sem=self.z_send.at[q, step],
            recv_sem=self.z_recv.at[q, step],
            device_id={"wide": self.w, "narrow": other},
            device_id_type=MESH,
        )

    def after_stage(self, q, stage):
        for h in (0, 1):
            for slot, kept in self.tiles_of(h, stage):
                arrive(self.chip_in.at[q, h, slot], self.chip_recv.at[q, h, slot])
                self.add_to(
                    lambda part, h=h, kept=kept: self.held.at[q, kept, part, self.lanes(h)],
                    lambda part, h=h, slot=slot: self.chip_in.at[q, h, slot, part, :],
                )
        if stage + 1 < self.bits:
            self.send_stage(q, stage + 1)
        else:
            for step in range(1, self.narrow):
                self.z_copy(q, step).start()

    def after_z(self, q):
        for step in range(1, self.narrow):
            arrive(self.z_in.at[q, step], self.z_recv.at[q, step])

        def one(r, carry):
            to = pl.ds(pl.multiple_of(r * 16, 16), 16)
            own = pl.ds(pl.multiple_of(self.n * self.shard + r * 16, 16), 16)
            value = self.held[q, self.chip, own, :].astype(F32)
            for step in range(1, self.narrow):
                value = value + self.z_in[q, step, to, :].astype(F32)
            self.out_ref[to, self.columns_of(q)] = value
            return carry

        lax.fori_loop(0, self.shard // 16, one, 0)

    def after_all(self):
        def one(q, carry):
            self.after_z(q)
            return carry

        lax.fori_loop(0, self.chunks, one, 0)

    def drain(self):
        def one(q, carry):
            arrive(self.core_in.at[q], self.core_send.at[q])
            for stage in range(self.bits):
                for h in (0, 1):
                    for slot, kept in self.tiles_of(h, stage):
                        self.chip_copy(q, h, stage, slot, kept).wait_send()
            for step in range(1, self.narrow):
                self.z_copy(q, step).wait_send()
            return carry

        lax.fori_loop(0, self.chunks, one, 0)


def reduce_scratch(wide, narrow, rows, tokens, columns, chunk):
    chips, rows, chunks = wide // 2, rows // wide, columns // chunk
    dma = pltpu.SemaphoreType.DMA
    return [
        pltpu.VMEM((2, chips * rows, tokens), BF16),
        pltpu.VMEM((chunks, chips, rows, chunk), BF16),
        pltpu.VMEM((chunks, chips, rows, chunk), BF16),
        pltpu.VMEM((chunks, chips, rows, chunk), BF16),
        pltpu.VMEM((chunks, 2, chips - 1, rows, chunk // 2), BF16),
        pltpu.VMEM((chunks, narrow, rows // narrow, chunk), BF16),
        dma((chunks,)),
        dma((chunks,)),
        dma((chunks, 2, chips - 1)),
        dma((chunks, 2, chips - 1)),
        dma((chunks, narrow)),
        dma((chunks, narrow)),
    ]


def greet(wide, narrow):
    w, n = lax.axis_index("wide"), lax.axis_index("narrow")
    barrier = pltpu.get_barrier_semaphore()
    for mask in range(1, wide):
        pl.semaphore_signal(
            barrier, inc=1, device_id={"wide": w ^ mask, "narrow": n}, device_id_type=MESH
        )
    for step in range(1, narrow):
        other = lax.rem(n + step, narrow)
        pl.semaphore_signal(
            barrier, inc=1, device_id={"wide": w, "narrow": other}, device_id_type=MESH
        )
    pl.semaphore_wait(barrier, wide + narrow - 2)


def to_owner(source, target, send_sem, recv_sem, mask):
    w, n = lax.axis_index("wide"), lax.axis_index("narrow")
    return pltpu.make_async_remote_copy(
        src_ref=source,
        dst_ref=target,
        send_sem=send_sem,
        recv_sem=recv_sem,
        device_id={"wide": w ^ mask, "narrow": n},
        device_id_type=MESH,
    )


def to_block(source, target, send_sem, recv_sem, owner):
    n = lax.axis_index("narrow")
    return pltpu.make_async_remote_copy(
        src_ref=source,
        dst_ref=target,
        send_sem=send_sem,
        recv_sem=recv_sem,
        device_id={"wide": owner, "narrow": n},
        device_id_type=MESH,
    )


def arrive(block, sem):
    pltpu.make_async_copy(block, block, sem).wait()


def attend_kernel(
    wide, narrow, groups, start_ref, mine_ref, w_ref, c_ref,
    x_ref, low_ref, full_ref, log_ref, w_all, c_all,
    keys, top, total, acc, done, own_sem, in_send, in_recv, out_send, out_recv,
    line_own, line_send, line_recv, *sems,
):
    me = lax.axis_index("wide")
    blocks, _, rows = x_ref.shape
    width = groups * HEAD_DIM
    own_in = pltpu.make_async_copy(mine_ref.at[me], x_ref.at[me], own_sem.at[0])
    own_in.start()
    greet(wide, narrow)
    for mask in range(1, wide):
        to_owner(
            mine_ref.at[me ^ mask], x_ref.at[me], in_send.at[mask], in_recv.at[me], mask
        ).start()
    flow = Flow(wide, narrow, w_ref, w_all, sems)
    line = Line(narrow, c_ref, c_all, (line_own, line_send, line_recv))
    flow.step(0)
    line.step(0)
    spread = {}
    for t in range(1, flow.last):
        spread.setdefault(min(blocks, blocks // 2 - 1 + t), []).append(functools.partial(flow.step, t))
    for t in range(1, narrow):
        spread.setdefault(min(blocks, blocks // 2 + 2 * t - 1), []).append(functools.partial(line.step, t))
    key_row = lax.broadcasted_iota(jnp.int32, (rows, rows), 0)
    column = lax.broadcasted_iota(jnp.int32, (rows, rows), 1)
    own_in.wait()

    def block(i, carry):
        pl.when(i != me)(lambda: arrive(x_ref.at[i], in_recv.at[i]))
        for at, actions in spread.items():
            if at < blocks:

                @pl.when(i == at)
                def _():
                    for action in actions:
                        action()

        keys[i] = x_ref[i, width : width + HEAD_DIM, :].T
        top[...] = jnp.full_like(top, NEGATIVE)
        total[...] = jnp.zeros_like(total)
        acc[...] = jnp.zeros_like(acc)
        start = start_ref[i]
        query_row = i * rows + column

        def step(j, carry):
            key_index = key_row + j * rows
            allowed = (key_index <= query_row) & (key_index >= start)
            key_block = keys[j]
            value_block = x_ref[j, width + HEAD_DIM :, :]
            for h in range(groups):
                own = pl.ds(h * HEAD_DIM, HEAD_DIM)
                scores = dot(key_block, x_ref[i, own, :], NN)
                scores = jnp.where(allowed, scores, NEGATIVE)
                old = top[h : h + 1, :]
                new = jnp.maximum(old, jnp.max(scores, 0, keepdims=True))
                shrink = jnp.exp(old - new)
                prob = jnp.exp(scores - new)
                top[h : h + 1, :] = new
                total[h : h + 1, :] = total[h : h + 1, :] * shrink + jnp.sum(prob, 0, keepdims=True)
                acc[own, :] = acc[own, :] * shrink + dot(value_block, prob.astype(BF16), NN)
            return carry

        lax.fori_loop(0, i + 1, step, 0)
        log_ref[i] = top[...] + jnp.log(total[...])
        for h in range(groups):
            own = pl.ds(h * HEAD_DIM, HEAD_DIM)
            result = acc[own, :] / total[h : h + 1, :]
            full_ref[i, own, :] = result
            done[i, own, :] = result.astype(BF16)

        @pl.when(i != me)
        def _():
            to_block(done.at[i], low_ref.at[me], out_send.at[i], out_recv.at[me], i).start()

        return carry

    lax.fori_loop(0, blocks, block, 0)
    low_ref[me] = done[me]
    for action in spread.get(blocks, []):
        action()
    flow.end()
    line.end()
    for mask in range(1, wide):
        to_owner(
            mine_ref.at[me ^ mask], x_ref.at[me], in_send.at[mask], in_recv.at[me], mask
        ).wait_send()
        other = me ^ mask
        arrive(low_ref.at[other], out_recv.at[other])
        arrive(done.at[other], out_send.at[other])


def attend(mine, start, w_out, cot, groups):
    wide, narrow = lax.axis_size("wide"), lax.axis_size("narrow")
    blocks, features, rows = mine.shape
    width = groups * HEAD_DIM
    dma = pltpu.SemaphoreType.DMA
    hbm = pl.BlockSpec(memory_space=pl.ANY)
    vmem = pl.BlockSpec(memory_space=pltpu.VMEM)
    return pl.pallas_call(
        functools.partial(attend_kernel, wide, narrow, groups),
        out_shape=(
            jax.ShapeDtypeStruct((blocks, features, rows), BF16),
            jax.ShapeDtypeStruct((blocks, width, rows), BF16),
            jax.ShapeDtypeStruct((blocks, width, rows), F32),
            jax.ShapeDtypeStruct((blocks, groups, rows), F32),
            jax.ShapeDtypeStruct((wide * narrow * w_out.shape[0], w_out.shape[1]), BF16),
            jax.ShapeDtypeStruct((narrow,) + cot.shape, BF16),
        ),
        in_specs=[vmem, vmem, hbm, hbm],
        out_specs=(vmem, vmem, vmem, vmem, hbm, hbm),
        scratch_shapes=[
            pltpu.VMEM((blocks, rows, HEAD_DIM), BF16),
            pltpu.VMEM((groups, rows), F32),
            pltpu.VMEM((groups, rows), F32),
            pltpu.VMEM((width, rows), F32),
            pltpu.VMEM((blocks, width, rows), BF16),
            dma((1,)),
            dma((wide,)),
            dma((wide,)),
            dma((wide,)),
            dma((wide,)),
            dma(()),
            dma((2, narrow)),
            dma((2, narrow)),
        ]
        + flow_sems(wide, narrow),
        compiler_params=pltpu.CompilerParams(
            collective_id=3, has_side_effects=True, vmem_limit_bytes=40 << 20
        ),
        cost_estimate=pl.CostEstimate(
            flops=32 * width * (blocks * rows) ** 2,
            bytes_accessed=64 << 20,
            transcendentals=groups * (blocks * rows) ** 2 // 2,
        ),
    )(start, mine, w_out, cot)


def attend_back_kernel(
    wide, narrow, groups, start_ref, x_ref, mine_ref, full_ref, log_ref, cos_ref, sin_ref, part_ref,
    left_ref, right_ref, out_ref, came_ref, weight_out,
    keys, values, acc, acc_keys, acc_values, grad_ref, done, own_sem, in_send, in_recv,
    q_send, q_recv, k_send, k_recv, p_send, p_recv, *refs,
):
    reduce = Reduce(wide, narrow, left_ref, right_ref, NN, weight_out, refs)
    me, n = lax.axis_index("wide"), lax.axis_index("narrow")

    def part_copy(step):
        other = lax.rem(n + step, narrow)
        return pltpu.make_async_remote_copy(
            src_ref=part_ref.at[other],
            dst_ref=came_ref.at[step],
            send_sem=p_send.at[step],
            recv_sem=p_recv.at[step],
            device_id={"wide": me, "narrow": other},
            device_id_type=MESH,
        )

    own_part = pltpu.make_async_copy(part_ref.at[n], came_ref.at[0], p_send.at[0])
    blocks, _, rows = x_ref.shape
    width = groups * HEAD_DIM
    own_in = pltpu.make_async_copy(mine_ref.at[me], grad_ref.at[me], own_sem.at[0])
    own_in.start()
    for j in range(blocks):
        keys[j] = x_ref[j, width : width + HEAD_DIM, :].T
        values[j] = x_ref[j, width + HEAD_DIM :, :].T
    acc_keys[...] = jnp.zeros_like(acc_keys)
    acc_values[...] = jnp.zeros_like(acc_values)
    greet(wide, narrow)
    for mask in range(1, wide):
        to_owner(
            mine_ref.at[me ^ mask], grad_ref.at[me], in_send.at[mask], in_recv.at[me], mask
        ).start()
    reduce.arrange()
    lax.fori_loop(0, reduce.chunks, lambda q, carry: (reduce.begin(q), carry)[1], 0)
    own_part.start()
    for step in range(1, narrow):
        part_copy(step).start()

    def weight_turn(c):
        chunks = reduce.chunks
        q = jnp.maximum(c - 2, 0) // 2
        ready = (c >= 2) & (lax.rem(c, 2) == 0) & (q < chunks)
        pl.when(ready)(lambda: reduce.after_core(jnp.minimum(q, chunks - 1)))
        actions = [functools.partial(reduce.after_stage, stage=stage) for stage in range(reduce.bits)]
        for index, action in enumerate(actions):
            since = jnp.maximum(c - (2 * chunks + 6 + 6 * index), -1)
            q = jnp.maximum(since, 0) // 5
            ready = (since >= 0) & (lax.rem(jnp.maximum(since, 0), 5) == 0) & (q < chunks)
            pl.when(ready)(functools.partial(action, jnp.minimum(q, chunks - 1)))

    turns = 2 * reduce.chunks + 6 + 6 * (reduce.bits - 1) + 5 * (reduce.chunks - 1) + 1
    key_row = lax.broadcasted_iota(jnp.int32, (rows, rows), 0)
    column = lax.broadcasted_iota(jnp.int32, (rows, rows), 1)
    own_in.wait()
    of_queries, of_keys = pl.ds(0, width), pl.ds(width, 2 * HEAD_DIM)

    def turn_back(block, cos, sin):
        front, back = block[:HALF, :], block[HALF:, :]
        return (front * cos + back * sin).astype(BF16), (back * cos - front * sin).astype(BF16)

    def block(i, carry):
        pl.when(i != me)(lambda: arrive(grad_ref.at[i], in_recv.at[i]))
        acc[...] = jnp.zeros_like(acc)
        start = start_ref[i]
        query_row = i * rows + column
        deltas = [
            jnp.sum(
                grad_ref[i, pl.ds(h * HEAD_DIM, HEAD_DIM), :].astype(F32)
                * full_ref[i, pl.ds(h * HEAD_DIM, HEAD_DIM), :],
                0,
                keepdims=True,
            )
            for h in range(groups)
        ]

        def step(j, carry):
            key_index = key_row + j * rows
            allowed = (key_index <= query_row) & (key_index >= start)
            key_block = keys[j]
            value_block = values[j]
            key_columns = x_ref[j, width : width + HEAD_DIM, :]
            grad_keys = acc_keys[j]
            grad_values = acc_values[j]
            for h in range(groups):
                own = pl.ds(h * HEAD_DIM, HEAD_DIM)
                query = x_ref[i, own, :]
                grad = grad_ref[i, own, :]
                scores = dot(key_block, query, NN)
                scores = jnp.where(allowed, scores, NEGATIVE)
                prob = jnp.exp(scores - log_ref[i, h : h + 1, :])
                grad_prob = dot(value_block, grad, NN)
                grad_scores = (prob * (grad_prob - deltas[h])).astype(BF16)
                acc[own, :] += dot(key_columns, grad_scores, NN)
                grad_keys = grad_keys + dot(query, grad_scores, NT)
                grad_values = grad_values + dot(grad, prob.astype(BF16), NT)
            acc_keys[j] = grad_keys
            acc_values[j] = grad_values
            weight_turn(i * (i + 1) // 2 + j)
            return carry

        lax.fori_loop(0, i + 1, step, 0)
        for h in range(groups):
            at = h * HEAD_DIM
            front, back = turn_back(
                acc[pl.ds(at, HEAD_DIM), :] * SCORE_SCALE, cos_ref[i], sin_ref[i]
            )
            done[i, pl.ds(at, HALF), :] = front
            done[i, pl.ds(at + HALF, HALF), :] = back

        @pl.when(i != me)
        def _():
            to_block(
                done.at[i, of_queries], out_ref.at[me, of_queries], q_send.at[i], q_recv.at[me], i
            ).start()

        return carry

    lax.fori_loop(0, blocks, block, 0)

    def last(j, carry):
        front, back = turn_back(acc_keys[j], cos_ref[j], sin_ref[j])
        done[j, pl.ds(width, HALF), :] = front
        done[j, pl.ds(width + HALF, HALF), :] = back
        done[j, pl.ds(width + HEAD_DIM, HEAD_DIM), :] = acc_values[j].astype(BF16)

        @pl.when(j != me)
        def _():
            to_block(
                done.at[j, of_keys], out_ref.at[me, of_keys], k_send.at[j], k_recv.at[me], j
            ).start()

        return carry

    lax.fori_loop(0, blocks, last, 0)
    out_ref[me] = done[me]

    def left(c, carry):
        weight_turn(c)
        return carry

    lax.fori_loop(blocks * (blocks + 1) // 2, max(turns, blocks * (blocks + 1) // 2), left, 0)

    reduce.after_all()
    reduce.drain()
    for mask in range(1, wide):
        other = me ^ mask
        arrive(mine_ref.at[other], in_send.at[mask])
        arrive(done.at[other, of_queries], q_send.at[other])
        arrive(done.at[other, of_keys], k_send.at[other])
        arrive(out_ref.at[other, of_queries], q_recv.at[other])
        arrive(out_ref.at[other, of_keys], k_recv.at[other])
    own_part.wait()
    for step in range(1, narrow):
        part_copy(step).wait()


def attend_back(x, mine, full, log_total, start, cos, sin, part, left, right, groups):
    wide, narrow = lax.axis_size("wide"), lax.axis_size("narrow")
    blocks, features, rows = x.shape
    width = groups * HEAD_DIM
    dma = pltpu.SemaphoreType.DMA
    hbm = pl.BlockSpec(memory_space=pl.ANY)
    vmem = pl.BlockSpec(memory_space=pltpu.VMEM)
    return pl.pallas_call(
        functools.partial(attend_back_kernel, wide, narrow, groups),
        out_shape=(
            jax.ShapeDtypeStruct(x.shape, BF16),
            jax.ShapeDtypeStruct(part.shape, BF16),
            jax.ShapeDtypeStruct((left.shape[0] // (wide * narrow), right.shape[1]), F32),
        ),
        in_specs=[vmem] * 7 + [hbm, vmem, vmem],
        out_specs=(vmem, hbm, vmem),
        scratch_shapes=[
            pltpu.VMEM((blocks, rows, HEAD_DIM), BF16),
            pltpu.VMEM((blocks, rows, HEAD_DIM), BF16),
            pltpu.VMEM((width, rows), F32),
            pltpu.VMEM((blocks, HEAD_DIM, rows), F32),
            pltpu.VMEM((blocks, HEAD_DIM, rows), F32),
            pltpu.VMEM((blocks, width, rows), BF16),
            pltpu.VMEM((blocks, features, rows), BF16),
            dma((1,)),
        ]
        + [dma((wide,))] * 6
        + [dma((narrow,))] * 2
        + reduce_scratch(wide, narrow, left.shape[0], left.shape[1], right.shape[1], 512),
        compiler_params=pltpu.CompilerParams(
            collective_id=4, has_side_effects=True, vmem_limit_bytes=50 << 20
        ),
        cost_estimate=pl.CostEstimate(
            flops=40 * width * (blocks * rows) ** 2,
            bytes_accessed=4 * x.size * 2,
            transcendentals=groups * (blocks * rows) ** 2 // 2,
        ),
    )(start, x, mine, full, log_total, cos, sin, part, left, right)


def gather(x, axis):
    return lax.all_gather(x, axis, axis=0, tiled=True)


def scatter_sum(x, axis):
    return lax.psum_scatter(x, axis, scatter_dimension=0, tiled=True)


def gather_kernel(wide, narrow, aligned, qkv_ref, cut_ref, qkv_all, cut_all, x_send, x_recv, x_own, *sems):
    w, n = lax.axis_index("wide"), lax.axis_index("narrow")
    greet(wide, narrow)
    flow = Flow(wide, narrow, qkv_ref, qkv_all, sems)
    depth = qkv_ref.shape[0]
    piece = cut_all.shape[1] // (2 * wide)

    def rows_of(owner):
        return cut_all.at[pl.ds(pl.multiple_of(owner * depth, depth), depth), :]

    def pieces(other):
        if not aligned:
            return [(cut_ref.at[other], pl.ds(0, cut_all.shape[1]))]
        return [
            (
                cut_ref.at[:, pl.ds(pl.multiple_of((j * narrow + other) * piece, piece), piece)],
                pl.ds(j * piece, piece),
            )
            for j in range(2 * wide)
        ]

    def target(columns):
        return cut_all.at[pl.ds(pl.multiple_of(n * depth, depth), depth), columns]

    def cut_start(step):
        other = lax.rem(n + step, narrow)
        for source, columns in pieces(other):
            pltpu.make_async_remote_copy(
                src_ref=source,
                dst_ref=target(columns),
                send_sem=x_send.at[step],
                recv_sem=x_recv.at[step],
                device_id={"wide": w, "narrow": other},
                device_id_type=MESH,
            ).start()

    for t in range(flow.last):
        flow.step(t)
        if t == min(1, narrow - 1):
            for source, columns in pieces(n):
                pltpu.make_async_copy(source, target(columns), x_own).start()
            for step in range(1, narrow):
                cut_start(step)
    flow.end()
    own = rows_of(n)
    pltpu.make_async_copy(own, own, x_own).wait()
    for step in range(1, narrow):
        pltpu.make_async_copy(own, own, x_send.at[step]).wait()
        block = rows_of(lax.rem(n + narrow - step, narrow))
        pltpu.make_async_copy(block, block, x_recv.at[step]).wait()


def gather_weights(qkv, gateup):
    wide, narrow = lax.axis_size("wide"), lax.axis_size("narrow")
    dma = pltpu.SemaphoreType.DMA
    hbm = pl.BlockSpec(memory_space=pl.ANY)
    every = wide * narrow
    shard, columns = gateup.shape
    aligned = (columns // (2 * every)) % 128 == 0
    if not aligned:
        gateup = gateup.reshape(shard, 2, wide, narrow, -1).transpose(3, 0, 1, 2, 4)
        gateup = gateup.reshape(narrow, shard, columns // narrow)
    return pl.pallas_call(
        functools.partial(gather_kernel, wide, narrow, aligned),
        out_shape=(
            jax.ShapeDtypeStruct((every * qkv.shape[0], qkv.shape[1]), BF16),
            jax.ShapeDtypeStruct((narrow * shard, columns // narrow), BF16),
        ),
        in_specs=[hbm, hbm],
        out_specs=(hbm, hbm),
        scratch_shapes=[dma((narrow,)), dma((narrow,)), dma(())] + flow_sems(wide, narrow),
        compiler_params=pltpu.CompilerParams(collective_id=0, has_side_effects=True),
        cost_estimate=pl.CostEstimate(flops=0, bytes_accessed=200 << 20, transcendentals=0),
    )(qkv, gateup)


def feed_kernel(
    narrow, x_ref, cot_ref, gate_up_ref, down_ref,
    low_out, grad_x_ref, part_gate_up, part_down,
    group_ref, gate_up, down, cot, hidden, grads, low, came,
    load_sem, x_send, x_recv, out_sem, g_send, g_recv,
):
    w, n = lax.axis_index("wide"), lax.axis_index("narrow")
    rows, width = x_ref.shape
    own = down.shape[0]
    tile = 256
    tiles = own // tile
    wtiles = width // tile

    def to_narrow(other):
        return {"wide": w, "narrow": other}

    loads = [
        pltpu.make_async_copy(gate_up_ref, gate_up, load_sem.at[0]),
        pltpu.make_async_copy(down_ref, down, load_sem.at[1]),
        pltpu.make_async_copy(cot_ref, cot, load_sem.at[2]),
        pltpu.make_async_copy(x_ref, group_ref.at[n], load_sem.at[3]),
    ]
    for load in loads:
        load.start()

    barrier = pltpu.get_barrier_semaphore()
    for step in range(1, narrow):
        pl.semaphore_signal(
            barrier, inc=1, device_id=to_narrow(lax.rem(n + step, narrow)), device_id_type=MESH
        )
    pl.semaphore_wait(barrier, narrow - 1)

    def owner_of(side, d):
        return n - d if side == 0 else n + d

    def valid(side, d):
        return n - d >= 0 if side == 0 else (n + d < narrow) & (d > 0)

    def passes(side, d):
        if side == 0:
            return (n - d >= 0) & (n < narrow - 1)
        return (n + d < narrow) & (n > 0)

    def x_copy(side, d):
        block = group_ref.at[owner_of(side, d)]
        return pltpu.make_async_remote_copy(
            src_ref=block,
            dst_ref=block,
            send_sem=x_send.at[side, d],
            recv_sem=x_recv.at[side, d + 1],
            device_id=to_narrow(n + 1 if side == 0 else n - 1),
            device_id_type=MESH,
        )

    def x_wait(side, d):
        block = group_ref.at[owner_of(side, d)]
        pltpu.make_async_copy(block, block, x_recv.at[side, d]).wait()

    def out_copy(at, block):
        return pltpu.make_async_copy(low.at[at], low_out.at[block], out_sem.at[at])

    def g_copy(block, half):
        columns = pl.ds(half * (width // 2), width // 2)
        return pltpu.make_async_remote_copy(
            src_ref=cot.at[block, :, columns],
            dst_ref=came.at[n, :, columns],
            send_sem=g_send.at[block, half],
            recv_sem=g_recv.at[n, half],
            device_id=to_narrow(block),
            device_id_type=MESH,
        )

    def compute(side, d):
        block = n - d + 2 * d * side
        before = 1 + jnp.minimum(n, d - 1) + jnp.minimum(narrow - 1 - n, d - 1)
        before = jnp.where(d == 0, 0, before + jnp.where((side == 1) & (n - d >= 0), 1, 0))
        at = lax.rem(before, 2)

        pl.when(before >= 2)(lambda: out_copy(at, block).wait())

        def first(f, carry):
            columns = pl.ds(pl.multiple_of(f * tile, tile), tile)
            other = pl.ds(pl.multiple_of(own + f * tile, tile), tile)
            x = group_ref[block]
            gate = dot(x, gate_up[:, columns], NN)
            up = dot(x, gate_up[:, other], NN)
            grad = dot(cot[block], down[columns, :], NT)
            sig = 1.0 / (1.0 + jnp.exp(-gate))
            silu = gate * sig
            hidden[block, :, columns] = (silu * up).astype(BF16)
            grads[block, :, columns] = (grad * up * (sig + silu * (1.0 - sig))).astype(BF16)
            grads[block, :, other] = (grad * silu).astype(BF16)
            return carry

        lax.fori_loop(0, tiles, first, 0)

        def second(f, carry):
            columns = pl.ds(pl.multiple_of(f * tile, tile), tile)
            cot[block, :, columns] = dot(grads[block], gate_up[columns, :], NT, BF16)
            low[at, :, columns] = dot(hidden[block], down[:, columns], NN, BF16)
            return carry

        for half in (0, 1):
            lax.fori_loop(half * (wtiles // 2), (half + 1) * (wtiles // 2), second, 0)
            pl.when(block != n)(lambda half=half: g_copy(block, half).start())
        out_copy(at, block).start()

    def distance(d, carry):
        for side in (0, 1):

            @pl.when(passes(side, d + 1))
            def _():
                x_wait(side, d + 1)
                x_copy(side, d + 1).start()

            @pl.when(valid(side, d) & (d > 0) & jnp.logical_not(passes(side, d)))
            def _():
                x_wait(side, d)

        @pl.when(d == 0)
        def _():
            for load in loads[:3]:
                load.wait()

        def one(side, carry):
            ok = jnp.where(side == 0, n - d, jnp.where(d > 0, narrow - 1 - n - d, -1)) >= 0
            pl.when(ok)(lambda: compute(side, d))
            return carry

        lax.fori_loop(0, 2, one, 0)
        return carry

    loads[3].wait()
    for side in (0, 1):
        pl.when(passes(side, 0))(lambda side=side: x_copy(side, 0).start())
    lax.fori_loop(0, narrow, distance, 0)

    tokens = narrow * rows
    again = [
        pltpu.make_async_copy(
            cot_ref.at[o], gate_up.at[pl.ds(o * rows, rows), pl.ds(0, width)], load_sem.at[4 + o]
        )
        for o in range(narrow)
    ]
    for load in again:
        load.start()
    for at in range(2):
        out_copy(at, n).wait()

    def flipped(ref, columns):
        return jnp.concatenate([ref[o, :, columns].T for o in range(narrow)], 1)

    def weight_tile(t, left, right, at_row, out_ref, first):
        at = lax.rem(t, 2)
        copy = pltpu.make_async_copy(low.at[at], out_ref, out_sem.at[at])
        pl.when(t >= 2)(lambda: copy.wait())
        turned = flipped(left, pl.ds(pl.multiple_of(at_row, tile), tile))

        def one(c, carry):
            columns = pl.ds(pl.multiple_of(c * 512, 512), 512)
            source = pl.ds(pl.multiple_of(first + c * 512, 512), 512)
            low[at, :, columns] = dot(turned, right(source), NN, BF16)
            return carry

        lax.fori_loop(0, width // 512, one, 0)
        copy.start()

    halves = 2 * own // width

    def gate_up_tile(t, carry):
        row, half = t // halves * tile, lax.rem(t, halves) * width
        row, half = pl.multiple_of(row, tile), pl.multiple_of(half, width)
        weight_tile(
            t, group_ref, lambda source: grads[:, :, source].reshape(tokens, 512), row,
            part_gate_up.at[pl.ds(row, tile), pl.ds(half, width)], half,
        )
        return carry

    def down_tile(t, carry):
        row = pl.multiple_of(t * tile, tile)
        weight_tile(
            t + 2, hidden, lambda source: gate_up[pl.ds(0, tokens), source], row,
            part_down.at[pl.ds(row, tile), :], 0,
        )
        return carry

    lax.fori_loop(0, wtiles * halves, gate_up_tile, 0)
    for load in again:
        load.wait()
    lax.fori_loop(0, tiles, down_tile, 0)
    for at in range(2):
        out_copy(at, n).wait()
    for side in (0, 1):
        for d in range(narrow - 1):
            pl.when(passes(side, d))(lambda side=side, d=d: x_copy(side, d).wait_send())
    for step in range(1, narrow):
        other = lax.rem(n + step, narrow)
        for half in (0, 1):
            g_copy(other, half).wait_send()
            arrive(came.at[other, :, pl.ds(half * (width // 2), width // 2)], g_recv.at[other, half])

    def add(r, carry):
        part = pl.ds(pl.multiple_of(r * 16, 16), 16)
        total = cot[n, part, :].astype(F32)
        for step in range(1, narrow):
            total = total + came[lax.rem(n + step, narrow), part, :].astype(F32)
        grad_x_ref[part, :] = total
        return carry

    lax.fori_loop(0, rows // 16, add, 0)


def feed(x, cot_group, gate_up, down):
    narrow = lax.axis_size("narrow")
    rows, width = x.shape
    own = down.shape[0]
    dma = pltpu.SemaphoreType.DMA
    hbm = pl.BlockSpec(memory_space=pl.ANY)
    vmem = pl.BlockSpec(memory_space=pltpu.VMEM)
    return pl.pallas_call(
        functools.partial(feed_kernel, narrow),
        out_shape=(
            jax.ShapeDtypeStruct((narrow, rows, width), BF16),
            jax.ShapeDtypeStruct((rows, width), F32),
            jax.ShapeDtypeStruct((width, 2 * own), BF16),
            jax.ShapeDtypeStruct((own, width), BF16),
        ),
        in_specs=[vmem, hbm, hbm, hbm],
        out_specs=(hbm, vmem, hbm, hbm),
        scratch_shapes=[
            pltpu.VMEM((narrow, rows, width), BF16),
            pltpu.VMEM((width, 2 * own), BF16),
            pltpu.VMEM((own, width), BF16),
            pltpu.VMEM((narrow, rows, width), BF16),
            pltpu.VMEM((narrow, rows, own), BF16),
            pltpu.VMEM((narrow, rows, 2 * own), BF16),
            pltpu.VMEM((2, rows, width), BF16),
            pltpu.VMEM((narrow, rows, width), BF16),
            dma((4 + narrow,)),
            dma((2, narrow + 1)),
            dma((2, narrow + 1)),
            dma((2,)),
            dma((narrow, 2)),
            dma((narrow, 2)),
        ],
        compiler_params=pltpu.CompilerParams(
            collective_id=1, has_side_effects=True, vmem_limit_bytes=58 << 20
        ),
        cost_estimate=pl.CostEstimate(
            flops=12 * narrow * rows * width * own, bytes_accessed=300 << 20, transcendentals=0
        ),
    )(x, cot_group.reshape(narrow, rows, width), gate_up, down)


def sum_kernel(
    wide, narrow, left_ref, right_ref, cut_ref, gains_ref, qkv_out, cut_out, gains_out,
    cut_in, gain_w, gain_sum, gain_z, own_sem, cut_send, cut_recv, gw_send, gw_recv, gz_send, gz_recv, *refs,
):
    reduce = Reduce(wide, narrow, left_ref, right_ref, NT, qkv_out, refs)
    w, n = reduce.w, reduce.n
    chunks, bits = reduce.chunks, reduce.bits
    reduce.arrange()
    greet(wide, narrow)

    def to_wide(mask):
        return {"wide": w ^ mask, "narrow": n}

    def to_narrow(step):
        return {"wide": w, "narrow": lax.rem(n + step, narrow)}

    own_cut = pltpu.make_async_copy(cut_ref.at[n], cut_in.at[n], own_sem)

    def cut_copy(step):
        return pltpu.make_async_remote_copy(
            src_ref=cut_ref.at[lax.rem(n + step, narrow)],
            dst_ref=cut_in.at[n],
            send_sem=cut_send.at[step],
            recv_sem=cut_recv.at[step],
            device_id=to_narrow(step),
            device_id_type=MESH,
        )

    def gw_copy(mask):
        return pltpu.make_async_remote_copy(
            src_ref=gains_ref.at[w ^ mask],
            dst_ref=gain_w.at[mask],
            send_sem=gw_send.at[mask],
            recv_sem=gw_recv.at[mask],
            device_id=to_wide(mask),
            device_id_type=MESH,
        )

    def gz_copy(step):
        return pltpu.make_async_remote_copy(
            src_ref=gain_sum.at[lax.rem(n + step, narrow)],
            dst_ref=gain_z.at[step],
            send_sem=gz_send.at[step],
            recv_sem=gz_recv.at[step],
            device_id=to_narrow(step),
            device_id_type=MESH,
        )

    ahead = min(4, chunks)
    lax.fori_loop(0, ahead, lambda q, carry: (reduce.begin(q), carry)[1], 0)
    own_cut.start()
    for step in range(1, narrow):
        cut_copy(step).start()
    for mask in range(1, wide):
        gw_copy(mask).start()

    def turn(t, carry):
        pl.when(t + ahead < chunks)(lambda: reduce.begin(t + ahead))
        pl.when(t < chunks)(lambda: reduce.after_core(t))
        for stage in range(bits):
            q = t - 1 - stage
            pl.when((q >= 0) & (q < chunks))(functools.partial(reduce.after_stage, q, stage))
        return carry

    lax.fori_loop(0, chunks + bits, turn, 0)

    total = gains_ref[w]
    for mask in range(1, wide):
        block = gain_w.at[mask]
        pltpu.make_async_copy(block, block, gw_recv.at[mask]).wait()
        total = total + gain_w[mask]
    gain_sum[...] = total
    for step in range(1, narrow):
        gz_copy(step).start()

    reduce.after_all()
    own_cut.wait()
    for step in range(1, narrow):
        other = lax.rem(n + narrow - step, narrow)
        arrive(cut_in.at[other], cut_recv.at[step])
    piece = cut_in.shape[2] // (2 * wide)
    if cut_out.shape[0] == narrow:
        for other in range(narrow):
            cut_out[other] = cut_in[other].astype(F32)
    else:
        for j in range(2 * wide):
            for other in range(narrow):
                cut_out[:, pl.ds((j * narrow + other) * piece, piece)] = cut_in[
                    other, :, pl.ds(j * piece, piece)
                ].astype(F32)

    total = gain_sum[n]
    for step in range(1, narrow):
        block = gain_z.at[step]
        pltpu.make_async_copy(block, block, gz_recv.at[step]).wait()
        total = total + gain_z[step]
    gains_out[...] = total

    for mask in range(1, wide):
        gw_copy(mask).wait_send()
    for step in range(1, narrow):
        gz_copy(step).wait_send()
        cut_copy(step).wait_send()
    reduce.drain()


def sum_all(left, right, cut, gains):
    wide, narrow = lax.axis_size("wide"), lax.axis_size("narrow")
    shard, cut_width = cut.shape[1:]
    aligned = (cut_width // (2 * wide)) % 128 == 0
    cut_shape = (shard, narrow * cut_width) if aligned else cut.shape
    dma = pltpu.SemaphoreType.DMA
    hbm = pl.BlockSpec(memory_space=pl.ANY)
    vmem = pl.BlockSpec(memory_space=pltpu.VMEM)
    results = pl.pallas_call(
        functools.partial(sum_kernel, wide, narrow),
        out_shape=(
            jax.ShapeDtypeStruct((shard, right.shape[0]), F32),
            jax.ShapeDtypeStruct(cut_shape, F32),
            jax.ShapeDtypeStruct((8, 128), F32),
        ),
        in_specs=[vmem, vmem, hbm, vmem],
        out_specs=(vmem, vmem, vmem),
        scratch_shapes=[
            pltpu.VMEM(cut.shape, BF16),
            pltpu.VMEM((wide, narrow, 8, 128), F32),
            pltpu.VMEM((narrow, 8, 128), F32),
            pltpu.VMEM((narrow, 8, 128), F32),
            dma(()),
            dma((narrow,)),
            dma((narrow,)),
            dma((wide,)),
            dma((wide,)),
            dma((narrow,)),
            dma((narrow,)),
        ]
        + reduce_scratch(wide, narrow, left.shape[1], left.shape[0], right.shape[0], 256),
        compiler_params=pltpu.CompilerParams(
            collective_id=2, has_side_effects=True, vmem_limit_bytes=54 << 20
        ),
        cost_estimate=pl.CostEstimate(flops=0, bytes_accessed=300 << 20, transcendentals=0),
    )(left, right, cut, gains)
    return results, aligned


def per_device(tokens, lengths, gain_attn, w_qkv, w_out, gain_mlp, w_gateup, w_down, cotangent):
    rows, width = tokens.shape[1:]
    wide, narrow = lax.axis_size("wide"), lax.axis_size("narrow")
    pack_rows = rows * wide
    query_width, key_width = HEADS * HEAD_DIM, KV_HEADS * HEAD_DIM
    groups = HEADS // wide
    copies = wide // KV_HEADS
    own_ff = FF // narrow
    first, positions = places(lengths[0], pack_rows)
    cos_all, sin_all = rotary(positions.astype(F32), HALF)
    first_row = lax.axis_index("wide") * rows
    cos = lax.dynamic_slice_in_dim(cos_all, first_row, rows, 1)
    sin = lax.dynamic_slice_in_dim(sin_all, first_row, rows, 1)
    cos_all = cos_all.reshape(HALF, wide, rows).transpose(1, 0, 2)
    sin_all = sin_all.reshape(HALF, wide, rows).transpose(1, 0, 2)
    start = first.reshape(wide, 1, rows)

    gains = jnp.stack([gain_attn, gain_mlp], -1)
    with_gains = jnp.concatenate([w_qkv, jnp.pad(gains, ((0, 0), (0, 126)))], -1)
    shard = w_gateup.shape[0]
    qkv_gained, gateup_rows = gather_weights(with_gains, w_gateup)
    qkv_whole = qkv_gained[:, : w_qkv.shape[1]]
    gain_one = qkv_gained[:, w_qkv.shape[1]].astype(F32)
    gain_two = qkv_gained[:, w_qkv.shape[1] + 1].astype(F32)
    gateup_own = gather(gateup_rows, "wide")
    down_own = gather(w_down, "wide")

    inputs = tokens[0].astype(F32)
    scale_one = lax.rsqrt(jnp.mean(inputs * inputs, -1, keepdims=True) + EPS)
    unit_one = inputs * scale_one
    normed_one = (unit_one * gain_one).astype(BF16)
    projected = dot(qkv_whole, normed_one, (((0,), (1,)), ((), ())))
    turning = projected[: query_width + key_width].reshape(HEADS + KV_HEADS, 2, HALF, rows)
    front, back = turning[:, 0], turning[:, 1]
    turned = jnp.stack([front * cos - back * sin, back * cos + front * sin], 1)
    queries = (turned[:HEADS] * SCORE_SCALE).astype(BF16).reshape(wide, groups * HEAD_DIM, rows)
    keys = turned[HEADS:].astype(BF16).reshape(KV_HEADS, HEAD_DIM, rows)
    values = projected[query_width + key_width :].astype(BF16).reshape(KV_HEADS, HEAD_DIM, rows)
    keys_values = jnp.repeat(jnp.concatenate([keys, values], 1), copies, 0)
    heads, attended_low, attended_full, log_total, out_whole, cot_group = attend(
        jnp.concatenate([queries, keys_values], 1), start, w_out, cotangent[0], groups
    )
    cot_group = cot_group.reshape(-1, width)
    attended_low = attended_low.reshape(query_width, rows)
    middle = inputs + dot(attended_low, out_whole, TN)
    scale_two = lax.rsqrt(jnp.mean(middle * middle, -1, keepdims=True) + EPS)
    unit_two = middle * scale_two
    normed_two = (unit_two * gain_two).astype(BF16)

    low_part, grad_normed_two, part_gateup, part_down = feed(
        normed_two, cot_group, gateup_own, down_own
    )
    grad_gateup = scatter_sum(part_gateup, "wide").reshape(narrow, shard, 2 * own_ff)
    grad_down = scatter_sum(part_down, "wide")
    part_gain_two = jnp.sum(grad_normed_two * unit_two, 0)
    grad_middle = cotangent[0].astype(F32) + norm_back(
        grad_normed_two * gain_two, unit_two, scale_two
    )
    grad_branch = grad_middle.astype(BF16)
    grad_attended = dot(out_whole, grad_branch, NT, BF16).reshape(wide, groups * HEAD_DIM, rows)
    grad_heads, low_came, grad_wout = attend_back(
        heads, grad_attended, attended_full, log_total, start, cos_all, sin_all, low_part,
        attended_low, grad_branch, groups,
    )
    layer_out = (middle + jnp.sum(low_came.astype(F32), 0)).astype(BF16)[None]
    grad_queries = grad_heads[:, : groups * HEAD_DIM].reshape(query_width, rows)
    grad_keys_values = (
        grad_heads[:, groups * HEAD_DIM :]
        .reshape(KV_HEADS, copies, 2, HEAD_DIM, rows)
        .astype(F32)
        .sum(1)
        .astype(BF16)
    )
    grad_projected = jnp.concatenate(
        [
            grad_queries,
            grad_keys_values[:, 0].reshape(key_width, rows),
            grad_keys_values[:, 1].reshape(key_width, rows),
        ],
        0,
    )
    grad_normed_one = dot(grad_projected, qkv_whole, (((0,), (1,)), ((), ())))
    part_gain_one = jnp.sum(grad_normed_one * unit_one, 0)
    part_gains = jnp.stack([part_gain_one, part_gain_two], 0).reshape(2, wide, narrow, shard)
    part_gains = jnp.pad(
        part_gains.transpose(1, 2, 0, 3), ((0, 0), (0, 0), (0, 6), (0, 128 - shard))
    )
    (grad_qkv, grad_gateup, grad_gains), done = sum_all(
        normed_one, grad_projected, grad_gateup, part_gains
    )
    if not done:
        grad_gateup = (
            grad_gateup.reshape(narrow, shard, 2, wide, -1)
            .transpose(1, 2, 3, 0, 4)
            .reshape(shard, 2 * FF)
        )
    grad_down, grad_gains = lax.optimization_barrier((grad_down, grad_gains))
    grad_down = grad_down.astype(F32)
    grad_inputs = grad_middle + norm_back(grad_normed_one * gain_one, unit_one, scale_one)
    grad_tokens = grad_inputs.astype(BF16)[None]
    return (
        layer_out,
        grad_tokens,
        grad_gains[0, :shard],
        grad_qkv,
        grad_wout,
        grad_gains[1, :shard],
        grad_gateup,
        grad_down,
    )


def solution(mesh):
    rows, packs = P("narrow", "wide", None), P("narrow", None)
    weight, gain = P(BOTH, None), P(BOTH)
    return jax.shard_map(
        per_device,
        mesh=mesh,
        in_specs=(rows, packs, gain, weight, weight, gain, weight, weight, rows),
        out_specs=(rows, rows, gain, weight, weight, gain, weight, weight),
        check_vma=False,
    )
```

```python
import functools
import math

import jax
import jax.numpy as jnp
from jax import lax
from jax.experimental import pallas as pl
from jax.experimental.pallas import tpu as pltpu
from jax.sharding import PartitionSpec as P

FF = 8192
HEADS = 32
KV_HEADS = 8
HEAD_DIM = 64
HALF = HEAD_DIM // 2
EPS = 1e-05
NEGATIVE = -1e30
SCORE_SCALE = 1.0 / math.sqrt(HEAD_DIM)
BOTH = ("wide", "narrow")
F32 = jnp.float32
BF16 = jnp.bfloat16
NN = (((1,), (0,)), ((), ()))
NT = (((1,), (1,)), ((), ()))
TN = (((0,), (0,)), ((), ()))


def dot(left, right, dims, kind=F32):
    return lax.dot_general(left, right, dims, preferred_element_type=F32).astype(kind)


def places(lengths_row, total_rows):
    seq_ends = jnp.cumsum(lengths_row)
    starts = seq_ends - lengths_row
    row_index = jnp.arange(total_rows, dtype=jnp.int32)
    segments = jnp.sum((row_index[:, None] >= seq_ends[None, :]).astype(jnp.int32), -1)
    slot_index = jnp.arange(lengths_row.shape[0], dtype=jnp.int32)
    owned = segments[:, None] == slot_index[None, :]
    first = jnp.sum(jnp.where(owned, starts[None, :], 0), -1)
    return first, row_index - first


def rotary(positions, half_width):
    channel = jnp.arange(half_width, dtype=jnp.float32)
    inverse_rate = jnp.power(500000.0, -channel / half_width)
    wavelength = 2.0 * math.pi / inverse_rate
    smooth = (8192.0 / wavelength - 1.0) / 3.0
    blended = (1.0 - smooth) * inverse_rate / 32.0 + smooth * inverse_rate
    frequency = jnp.where(
        wavelength < 2048.0,
        inverse_rate,
        jnp.where(wavelength > 8192.0, inverse_rate / 32.0, blended),
    )
    angles = frequency[:, None] * positions[None, :]
    return jnp.cos(angles), jnp.sin(angles)


def norm_back(grad_unit, unit_rows, row_scale):
    return row_scale * (grad_unit - unit_rows * jnp.mean(grad_unit * unit_rows, -1, keepdims=True))


MESH = pl.DeviceIdType.MESH


class Flow:
    def __init__(self, wide, narrow, x_ref, out_ref, sems):
        self.wide, self.narrow, self.x_ref, self.out_ref = wide, narrow, x_ref, out_ref
        self.w, self.n = lax.axis_index("wide"), lax.axis_index("narrow")
        (self.own_sem, self.z_send, self.z_recv, self.m_send, self.m_recv,
         self.r_send, self.r_recv, self.c_send, self.c_recv) = sems
        self.relay = wide == 8
        self.masks = [2, 4] if self.relay else list(range(2, wide, 2))
        self.last = narrow + 2

    def to_wide(self, mask):
        return {"wide": self.w ^ mask, "narrow": self.n}

    def owner_of(self, side, d):
        return self.n - d if side == 0 else self.n + d

    def valid(self, side, d):
        return self.n - d >= 0 if side == 0 else self.n + d < self.narrow

    def can_pass(self, side, d):
        if side == 0:
            return (self.n - (d - 1) >= 0) & (self.n < self.narrow - 1)
        return (self.n + (d - 1) < self.narrow) & (self.n > 0)

    def slot(self, side, d):
        return d - 1 + side * (self.narrow - 1) if d else 2 * (self.narrow - 1)

    def at_distance(self, d, action):
        if d == 0:
            action(0, 0)
            return
        for side in (0, 1):
            pl.when(self.valid(side, d))(functools.partial(action, side, d))

    def place(self, owner_w, owner_n, part=None):
        depth = self.x_ref.shape[0]
        half = depth // 2
        at = (owner_w * self.narrow + owner_n) * depth
        if part is None:
            return self.out_ref.at[pl.ds(pl.multiple_of(at, depth), depth), :]
        return self.out_ref.at[pl.ds(pl.multiple_of(at + part * half, half), half), :]

    def own_copy(self):
        return pltpu.make_async_copy(self.x_ref, self.place(self.w, self.n), self.own_sem)

    def z_copy(self, side, d):
        block = self.place(self.w, self.owner_of(side, d - 1))
        return pltpu.make_async_remote_copy(
            src_ref=self.x_ref if d == 1 else block,
            dst_ref=block,
            send_sem=self.z_send.at[side, d],
            recv_sem=self.z_recv.at[side, d],
            device_id={"wide": self.w, "narrow": self.n + 1 if side == 0 else self.n - 1},
            device_id_type=MESH,
        )

    def z_wait(self, side, d):
        block = self.place(self.w, self.owner_of(side, d))
        pltpu.make_async_copy(block, block, self.z_recv.at[side, d]).wait()

    def m_copy(self, i, side, d):
        block = self.place(self.w, self.owner_of(side, d))
        return pltpu.make_async_remote_copy(
            src_ref=self.x_ref if d == 0 else block,
            dst_ref=block,
            send_sem=self.m_send.at[i, self.slot(side, d)],
            recv_sem=self.m_recv.at[i, self.slot(side, d)],
            device_id=self.to_wide(self.masks[i]),
            device_id_type=MESH,
        )

    def m_wait(self, i, side, d):
        block = self.place(self.w ^ self.masks[i], self.owner_of(side, d))
        pltpu.make_async_copy(block, block, self.m_recv.at[i, self.slot(side, d)]).wait()

    def r_copy(self, part, side, d):
        block = self.place(self.w ^ self.masks[part], self.owner_of(side, d), part)
        return pltpu.make_async_remote_copy(
            src_ref=block,
            dst_ref=block,
            send_sem=self.r_send.at[part, self.slot(side, d)],
            recv_sem=self.r_recv.at[part, self.slot(side, d)],
            device_id=self.to_wide(self.masks[1 - part]),
            device_id_type=MESH,
        )

    def r_wait(self, part, side, d):
        block = self.place(self.w ^ 6, self.owner_of(side, d), part)
        pltpu.make_async_copy(block, block, self.r_recv.at[part, self.slot(side, d)]).wait()

    def c_copy(self, chip, side, d):
        block = self.place(self.w ^ (2 * chip), self.owner_of(side, d))
        return pltpu.make_async_remote_copy(
            src_ref=self.x_ref if d == 0 and chip == 0 else block,
            dst_ref=block,
            send_sem=self.c_send.at[chip, self.slot(side, d)],
            recv_sem=self.c_recv.at[chip, self.slot(side, d)],
            device_id=self.to_wide(1),
            device_id_type=MESH,
        )

    def c_wait(self, chip, side, d):
        block = self.place((self.w ^ 1) ^ (2 * chip), self.owner_of(side, d))
        pltpu.make_async_copy(block, block, self.c_recv.at[chip, self.slot(side, d)]).wait()

    def send_from_here(self, side, d):
        if d > 0:
            self.z_wait(side, d)
        if 0 < d < self.narrow - 1:
            pl.when(self.can_pass(side, d + 1))(lambda: self.z_copy(side, d + 1).start())
        for i in range(len(self.masks)):
            self.m_copy(i, side, d).start()
        self.c_copy(0, side, d).start()

    def send_on(self, side, d):
        for i in range(len(self.masks)):
            self.m_wait(i, side, d)
            if self.relay:
                self.r_copy(i, side, d).start()
            self.c_copy(self.masks[i] // 2, side, d).start()

    def send_last(self, side, d):
        self.r_wait(0, side, d)
        self.r_wait(1, side, d)
        self.c_copy(3, side, d).start()

    def step(self, t):
        if t == 0:
            self.own_copy().start()
            for side in (0, 1):
                pl.when(self.can_pass(side, 1))(lambda side=side: self.z_copy(side, 1).start())
        if 0 <= t < self.narrow:
            self.at_distance(t, self.send_from_here)
        if 0 <= t - 1 < self.narrow:
            self.at_distance(t - 1, self.send_on)
        if self.relay and 0 <= t - 2 < self.narrow:
            self.at_distance(t - 2, self.send_last)

    def finish(self, side, d):
        for i in range(len(self.masks)):
            self.m_copy(i, side, d).wait_send()
            if self.relay:
                self.r_copy(i, side, d).wait_send()
        for chip in range(self.wide // 2):
            self.c_copy(chip, side, d).wait_send()
            self.c_wait(chip, side, d)

    def end(self):
        self.own_copy().wait()
        for side in (0, 1):
            for d in range(1, self.narrow):
                pl.when(self.can_pass(side, d))(
                    lambda side=side, d=d: self.z_copy(side, d).wait_send()
                )
        for d in range(self.narrow):
            self.at_distance(d, self.finish)


class Line:
    def __init__(self, narrow, x_ref, out_ref, sems):
        self.narrow, self.x_ref, self.out_ref = narrow, x_ref, out_ref
        self.w, self.n = lax.axis_index("wide"), lax.axis_index("narrow")
        self.own_sem, self.send, self.recv = sems

    def owner_of(self, side, d):
        return self.n - d if side == 0 else self.n + d

    def valid(self, side, d):
        return self.n - d >= 0 if side == 0 else self.n + d < self.narrow

    def can_pass(self, side, d):
        if side == 0:
            return (self.n - (d - 1) >= 0) & (self.n < self.narrow - 1)
        return (self.n + (d - 1) < self.narrow) & (self.n > 0)

    def own_copy(self):
        return pltpu.make_async_copy(self.x_ref, self.out_ref.at[self.n], self.own_sem)

    def copy(self, side, d):
        block = self.out_ref.at[self.owner_of(side, d - 1)]
        return pltpu.make_async_remote_copy(
            src_ref=self.x_ref if d == 1 else block,
            dst_ref=block,
            send_sem=self.send.at[side, d],
            recv_sem=self.recv.at[side, d],
            device_id={"wide": self.w, "narrow": self.n + 1 if side == 0 else self.n - 1},
            device_id_type=MESH,
        )

    def pass_on(self, side, d):
        arrive(self.out_ref.at[self.owner_of(side, d)], self.recv.at[side, d])
        if d < self.narrow - 1:
            pl.when(self.can_pass(side, d + 1))(lambda: self.copy(side, d + 1).start())

    def step(self, t):
        if t == 0:
            self.own_copy().start()
        for side in (0, 1):
            if t == 0:
                pl.when(self.can_pass(side, 1))(lambda side=side: self.copy(side, 1).start())
            else:
                pl.when(self.valid(side, t))(lambda side=side: self.pass_on(side, t))

    def end(self):
        self.own_copy().wait()
        for side in (0, 1):
            for d in range(1, self.narrow):
                pl.when(self.can_pass(side, d))(lambda side=side, d=d: self.copy(side, d).wait_send())


def flow_sems(wide, narrow):
    slots = 2 * narrow - 1
    masks = 2 if wide == 8 else wide // 2 - 1
    dma = pltpu.SemaphoreType.DMA
    return [
        dma(()),
        dma((2, narrow)),
        dma((2, narrow)),
        dma((masks, slots)),
        dma((masks, slots)),
        dma((2, slots)),
        dma((2, slots)),
        dma((wide // 2, slots)),
        dma((wide // 2, slots)),
    ]


class Reduce:
    def __init__(self, wide, narrow, left, right, dims, out_ref, refs):
        self.wide, self.narrow, self.left, self.right, self.dims = wide, narrow, left, right, dims
        self.out_ref = out_ref
        self.w, self.n = lax.axis_index("wide"), lax.axis_index("narrow")
        self.core, self.chip = lax.rem(self.w, 2), self.w // 2
        self.chips = wide // 2
        self.bits = self.chips.bit_length() - 1
        (self.turned, self.held, self.away, self.core_in, self.chip_in, self.z_in, self.core_send, self.core_recv,
         self.chip_send, self.chip_recv, self.z_send, self.z_recv) = refs
        self.chunks = self.held.shape[0]
        self.rows, self.chunk = self.held.shape[2:]
        self.shard = self.rows // narrow
        self.orders = [list(range(self.bits)), list(range(self.bits))[::-1]]

    def columns_of(self, q):
        return pl.ds(pl.multiple_of(q * self.chunk, self.chunk), self.chunk)

    def arrange(self):
        for k in range(self.chips):
            for core in (0, 1):
                at = (2 * k + core) * self.rows
                if self.dims == NT:
                    tile = self.left[:, at : at + self.rows].T
                else:
                    tile = self.left[at : at + self.rows, :]
                self.turned[core, k * self.rows : (k + 1) * self.rows, :] = tile

    def begin(self, q):
        columns = self.columns_of(q)
        right = self.right[columns, :] if self.dims == NT else self.right[:, columns]
        shape = self.held.shape[1:]
        self.away[q] = dot(self.turned[1 - self.core], right, self.dims, BF16).reshape(shape)
        self.held[q] = dot(self.turned[self.core], right, self.dims, BF16).reshape(shape)
        pltpu.make_async_remote_copy(
            src_ref=self.away.at[q],
            dst_ref=self.core_in.at[q],
            send_sem=self.core_send.at[q],
            recv_sem=self.core_recv.at[q],
            device_id={"wide": self.w ^ 1, "narrow": self.n},
            device_id_type=MESH,
        ).start()

    def add_to(self, target, other):
        def one(r, carry):
            part = pl.ds(pl.multiple_of(r * 16, 16), 16)
            target(part)[...] = (
                target(part)[...].astype(F32) + other(part)[...].astype(F32)
            ).astype(BF16)
            return carry

        lax.fori_loop(0, self.rows // 16, one, 0)

    def tiles_of(self, h, stage):
        order = self.orders[h]
        rest = order[stage + 1 :]
        offset = sum(self.chips >> (i + 1) for i in range(stage))
        fixed = sum(1 << b for b in order[: stage + 1])
        result = []
        for v in range(1 << len(rest)):
            extra = sum(((v >> i) & 1) << b for i, b in enumerate(rest))
            result.append((offset + v, (self.chip & fixed) + extra))
        return result

    def lanes(self, h):
        return pl.ds(h * (self.chunk // 2), self.chunk // 2)

    def chip_copy(self, q, h, stage, slot, kept):
        bit = self.orders[h][stage]
        return pltpu.make_async_remote_copy(
            src_ref=self.held.at[q, kept ^ (1 << bit), :, self.lanes(h)],
            dst_ref=self.chip_in.at[q, h, slot],
            send_sem=self.chip_send.at[q, h, slot],
            recv_sem=self.chip_recv.at[q, h, slot],
            device_id={"wide": self.w ^ (2 << bit), "narrow": self.n},
            device_id_type=MESH,
        )

    def send_stage(self, q, stage):
        for h in (0, 1):
            for slot, kept in self.tiles_of(h, stage):
                self.chip_copy(q, h, stage, slot, kept).start()

    def after_core(self, q):
        arrive(self.core_in.at[q], self.core_recv.at[q])
        for k in range(self.chips):
            self.add_to(
                lambda part, k=k: self.held.at[q, k, part, :],
                lambda part, k=k: self.core_in.at[q, k, part, :],
            )
        self.send_stage(q, 0)

    def z_copy(self, q, step):
        other = lax.rem(self.n + step, self.narrow)
        own = pl.ds(pl.multiple_of(other * self.shard, self.shard), self.shard)
        return pltpu.make_async_remote_copy(
            src_ref=self.held.at[q, self.chip, own, :],
            dst_ref=self.z_in.at[q, step],
            send_sem=self.z_send.at[q, step],
            recv_sem=self.z_recv.at[q, step],
            device_id={"wide": self.w, "narrow": other},
            device_id_type=MESH,
        )

    def after_stage(self, q, stage):
        for h in (0, 1):
            for slot, kept in self.tiles_of(h, stage):
                arrive(self.chip_in.at[q, h, slot], self.chip_recv.at[q, h, slot])
                self.add_to(
                    lambda part, h=h, kept=kept: self.held.at[q, kept, part, self.lanes(h)],
                    lambda part, h=h, slot=slot: self.chip_in.at[q, h, slot, part, :],
                )
        if stage + 1 < self.bits:
            self.send_stage(q, stage + 1)
        else:
            for step in range(1, self.narrow):
                self.z_copy(q, step).start()

    def after_z(self, q):
        for step in range(1, self.narrow):
            arrive(self.z_in.at[q, step], self.z_recv.at[q, step])

        def one(r, carry):
            to = pl.ds(pl.multiple_of(r * 16, 16), 16)
            own = pl.ds(pl.multiple_of(self.n * self.shard + r * 16, 16), 16)
            value = self.held[q, self.chip, own, :].astype(F32)
            for step in range(1, self.narrow):
                value = value + self.z_in[q, step, to, :].astype(F32)
            self.out_ref[to, self.columns_of(q)] = value
            return carry

        lax.fori_loop(0, self.shard // 16, one, 0)

    def after_all(self):
        def one(q, carry):
            self.after_z(q)
            return carry

        lax.fori_loop(0, self.chunks, one, 0)

    def drain(self):
        def one(q, carry):
            arrive(self.core_in.at[q], self.core_send.at[q])
            for stage in range(self.bits):
                for h in (0, 1):
                    for slot, kept in self.tiles_of(h, stage):
                        self.chip_copy(q, h, stage, slot, kept).wait_send()
            for step in range(1, self.narrow):
                self.z_copy(q, step).wait_send()
            return carry

        lax.fori_loop(0, self.chunks, one, 0)


def reduce_scratch(wide, narrow, rows, tokens, columns, chunk):
    chips, rows, chunks = wide // 2, rows // wide, columns // chunk
    dma = pltpu.SemaphoreType.DMA
    return [
        pltpu.VMEM((2, chips * rows, tokens), BF16),
        pltpu.VMEM((chunks, chips, rows, chunk), BF16),
        pltpu.VMEM((chunks, chips, rows, chunk), BF16),
        pltpu.VMEM((chunks, chips, rows, chunk), BF16),
        pltpu.VMEM((chunks, 2, chips - 1, rows, chunk // 2), BF16),
        pltpu.VMEM((chunks, narrow, rows // narrow, chunk), BF16),
        dma((chunks,)),
        dma((chunks,)),
        dma((chunks, 2, chips - 1)),
        dma((chunks, 2, chips - 1)),
        dma((chunks, narrow)),
        dma((chunks, narrow)),
    ]


def greet(wide, narrow):
    w, n = lax.axis_index("wide"), lax.axis_index("narrow")
    barrier = pltpu.get_barrier_semaphore()
    for mask in range(1, wide):
        pl.semaphore_signal(
            barrier, inc=1, device_id={"wide": w ^ mask, "narrow": n}, device_id_type=MESH
        )
    for step in range(1, narrow):
        other = lax.rem(n + step, narrow)
        pl.semaphore_signal(
            barrier, inc=1, device_id={"wide": w, "narrow": other}, device_id_type=MESH
        )
    pl.semaphore_wait(barrier, wide + narrow - 2)


def to_owner(source, target, send_sem, recv_sem, mask):
    w, n = lax.axis_index("wide"), lax.axis_index("narrow")
    return pltpu.make_async_remote_copy(
        src_ref=source,
        dst_ref=target,
        send_sem=send_sem,
        recv_sem=recv_sem,
        device_id={"wide": w ^ mask, "narrow": n},
        device_id_type=MESH,
    )


def to_block(source, target, send_sem, recv_sem, owner):
    n = lax.axis_index("narrow")
    return pltpu.make_async_remote_copy(
        src_ref=source,
        dst_ref=target,
        send_sem=send_sem,
        recv_sem=recv_sem,
        device_id={"wide": owner, "narrow": n},
        device_id_type=MESH,
    )


def arrive(block, sem):
    pltpu.make_async_copy(block, block, sem).wait()


def attend_kernel(
    wide, narrow, groups, start_ref, mine_ref, w_ref, c_ref,
    x_ref, low_ref, full_ref, log_ref, w_all, c_all,
    keys, top, total, acc, done, own_sem, in_send, in_recv, out_send, out_recv,
    line_own, line_send, line_recv, *sems,
):
    me = lax.axis_index("wide")
    blocks, _, rows = x_ref.shape
    width = groups * HEAD_DIM
    own_in = pltpu.make_async_copy(mine_ref.at[me], x_ref.at[me], own_sem.at[0])
    own_in.start()
    greet(wide, narrow)
    for mask in range(1, wide):
        to_owner(
            mine_ref.at[me ^ mask], x_ref.at[me], in_send.at[mask], in_recv.at[me], mask
        ).start()
    flow = Flow(wide, narrow, w_ref, w_all, sems)
    line = Line(narrow, c_ref, c_all, (line_own, line_send, line_recv))
    flow.step(0)
    line.step(0)
    spread = {}
    for t in range(1, flow.last):
        spread.setdefault(min(blocks, blocks // 2 - 1 + t), []).append(functools.partial(flow.step, t))
    for t in range(1, narrow):
        spread.setdefault(min(blocks, blocks // 2 + 2 * t - 1), []).append(functools.partial(line.step, t))
    key_row = lax.broadcasted_iota(jnp.int32, (rows, rows), 0)
    column = lax.broadcasted_iota(jnp.int32, (rows, rows), 1)
    own_in.wait()

    def block(i, carry):
        pl.when(i != me)(lambda: arrive(x_ref.at[i], in_recv.at[i]))
        for at, actions in spread.items():
            if at < blocks:

                @pl.when(i == at)
                def _():
                    for action in actions:
                        action()

        keys[i] = x_ref[i, width : width + HEAD_DIM, :].T
        top[...] = jnp.full_like(top, NEGATIVE)
        total[...] = jnp.zeros_like(total)
        acc[...] = jnp.zeros_like(acc)
        start = start_ref[i]
        query_row = i * rows + column

        def step(j, carry):
            key_index = key_row + j * rows
            allowed = (key_index <= query_row) & (key_index >= start)
            key_block = keys[j]
            value_block = x_ref[j, width + HEAD_DIM :, :]
            for h in range(groups):
                own = pl.ds(h * HEAD_DIM, HEAD_DIM)
                scores = dot(key_block, x_ref[i, own, :], NN)
                scores = jnp.where(allowed, scores, NEGATIVE)
                old = top[h : h + 1, :]
                new = jnp.maximum(old, jnp.max(scores, 0, keepdims=True))
                shrink = jnp.exp(old - new)
                prob = jnp.exp(scores - new)
                top[h : h + 1, :] = new
                total[h : h + 1, :] = total[h : h + 1, :] * shrink + jnp.sum(prob, 0, keepdims=True)
                acc[own, :] = acc[own, :] * shrink + dot(value_block, prob.astype(BF16), NN)
            return carry

        lax.fori_loop(0, i + 1, step, 0)
        log_ref[i] = top[...] + jnp.log(total[...])
        for h in range(groups):
            own = pl.ds(h * HEAD_DIM, HEAD_DIM)
            result = acc[own, :] / total[h : h + 1, :]
            full_ref[i, own, :] = result
            done[i, own, :] = result.astype(BF16)

        @pl.when(i != me)
        def _():
            to_block(done.at[i], low_ref.at[me], out_send.at[i], out_recv.at[me], i).start()

        return carry

    lax.fori_loop(0, blocks, block, 0)
    low_ref[me] = done[me]
    for action in spread.get(blocks, []):
        action()
    flow.end()
    line.end()
    for mask in range(1, wide):
        to_owner(
            mine_ref.at[me ^ mask], x_ref.at[me], in_send.at[mask], in_recv.at[me], mask
        ).wait_send()
        other = me ^ mask
        arrive(low_ref.at[other], out_recv.at[other])
        arrive(done.at[other], out_send.at[other])


def attend(mine, start, w_out, cot, groups):
    wide, narrow = lax.axis_size("wide"), lax.axis_size("narrow")
    blocks, features, rows = mine.shape
    width = groups * HEAD_DIM
    dma = pltpu.SemaphoreType.DMA
    hbm = pl.BlockSpec(memory_space=pl.ANY)
    vmem = pl.BlockSpec(memory_space=pltpu.VMEM)
    return pl.pallas_call(
        functools.partial(attend_kernel, wide, narrow, groups),
        out_shape=(
            jax.ShapeDtypeStruct((blocks, features, rows), BF16),
            jax.ShapeDtypeStruct((blocks, width, rows), BF16),
            jax.ShapeDtypeStruct((blocks, width, rows), F32),
            jax.ShapeDtypeStruct((blocks, groups, rows), F32),
            jax.ShapeDtypeStruct((wide * narrow * w_out.shape[0], w_out.shape[1]), BF16),
            jax.ShapeDtypeStruct((narrow,) + cot.shape, BF16),
        ),
        in_specs=[vmem, vmem, hbm, hbm],
        out_specs=(vmem, vmem, vmem, vmem, hbm, hbm),
        scratch_shapes=[
            pltpu.VMEM((blocks, rows, HEAD_DIM), BF16),
            pltpu.VMEM((groups, rows), F32),
            pltpu.VMEM((groups, rows), F32),
            pltpu.VMEM((width, rows), F32),
            pltpu.VMEM((blocks, width, rows), BF16),
            dma((1,)),
            dma((wide,)),
            dma((wide,)),
            dma((wide,)),
            dma((wide,)),
            dma(()),
            dma((2, narrow)),
            dma((2, narrow)),
        ]
        + flow_sems(wide, narrow),
        compiler_params=pltpu.CompilerParams(
            collective_id=3, has_side_effects=True, vmem_limit_bytes=40 << 20
        ),
        cost_estimate=pl.CostEstimate(
            flops=32 * width * (blocks * rows) ** 2,
            bytes_accessed=64 << 20,
            transcendentals=groups * (blocks * rows) ** 2 // 2,
        ),
    )(start, mine, w_out, cot)


def attend_back_kernel(
    wide, narrow, groups, start_ref, x_ref, mine_ref, full_ref, log_ref, cos_ref, sin_ref, part_ref,
    left_ref, right_ref, out_ref, came_ref, weight_out,
    keys, values, acc, acc_keys, acc_values, grad_ref, done, own_sem, in_send, in_recv,
    q_send, q_recv, k_send, k_recv, p_send, p_recv, *refs,
):
    reduce = Reduce(wide, narrow, left_ref, right_ref, NN, weight_out, refs)
    me, n = lax.axis_index("wide"), lax.axis_index("narrow")

    def part_copy(step):
        other = lax.rem(n + step, narrow)
        return pltpu.make_async_remote_copy(
            src_ref=part_ref.at[other],
            dst_ref=came_ref.at[step],
            send_sem=p_send.at[step],
            recv_sem=p_recv.at[step],
            device_id={"wide": me, "narrow": other},
            device_id_type=MESH,
        )

    own_part = pltpu.make_async_copy(part_ref.at[n], came_ref.at[0], p_send.at[0])
    blocks, _, rows = x_ref.shape
    width = groups * HEAD_DIM
    own_in = pltpu.make_async_copy(mine_ref.at[me], grad_ref.at[me], own_sem.at[0])
    own_in.start()
    for j in range(blocks):
        keys[j] = x_ref[j, width : width + HEAD_DIM, :].T
        values[j] = x_ref[j, width + HEAD_DIM :, :].T
    acc_keys[...] = jnp.zeros_like(acc_keys)
    acc_values[...] = jnp.zeros_like(acc_values)
    greet(wide, narrow)
    for mask in range(1, wide):
        to_owner(
            mine_ref.at[me ^ mask], grad_ref.at[me], in_send.at[mask], in_recv.at[me], mask
        ).start()
    reduce.arrange()
    lax.fori_loop(0, reduce.chunks, lambda q, carry: (reduce.begin(q), carry)[1], 0)
    own_part.start()
    for step in range(1, narrow):
        part_copy(step).start()

    def weight_turn(c):
        chunks = reduce.chunks
        q = jnp.maximum(c - 2, 0) // 2
        ready = (c >= 2) & (lax.rem(c, 2) == 0) & (q < chunks)
        pl.when(ready)(lambda: reduce.after_core(jnp.minimum(q, chunks - 1)))
        actions = [functools.partial(reduce.after_stage, stage=stage) for stage in range(reduce.bits)]
        for index, action in enumerate(actions):
            since = jnp.maximum(c - (2 * chunks + 6 + 6 * index), -1)
            q = jnp.maximum(since, 0) // 5
            ready = (since >= 0) & (lax.rem(jnp.maximum(since, 0), 5) == 0) & (q < chunks)
            pl.when(ready)(functools.partial(action, jnp.minimum(q, chunks - 1)))

    turns = 2 * reduce.chunks + 6 + 6 * (reduce.bits - 1) + 5 * (reduce.chunks - 1) + 1
    key_row = lax.broadcasted_iota(jnp.int32, (rows, rows), 0)
    column = lax.broadcasted_iota(jnp.int32, (rows, rows), 1)
    own_in.wait()
    of_queries, of_keys = pl.ds(0, width), pl.ds(width, 2 * HEAD_DIM)

    def turn_back(block, cos, sin):
        front, back = block[:HALF, :], block[HALF:, :]
        return (front * cos + back * sin).astype(BF16), (back * cos - front * sin).astype(BF16)

    def block(i, carry):
        pl.when(i != me)(lambda: arrive(grad_ref.at[i], in_recv.at[i]))
        acc[...] = jnp.zeros_like(acc)
        start = start_ref[i]
        query_row = i * rows + column
        deltas = [
            jnp.sum(
                grad_ref[i, pl.ds(h * HEAD_DIM, HEAD_DIM), :].astype(F32)
                * full_ref[i, pl.ds(h * HEAD_DIM, HEAD_DIM), :],
                0,
                keepdims=True,
            )
            for h in range(groups)
        ]

        def step(j, carry):
            key_index = key_row + j * rows
            allowed = (key_index <= query_row) & (key_index >= start)
            key_block = keys[j]
            value_block = values[j]
            key_columns = x_ref[j, width : width + HEAD_DIM, :]
            grad_keys = acc_keys[j]
            grad_values = acc_values[j]
            for h in range(groups):
                own = pl.ds(h * HEAD_DIM, HEAD_DIM)
                query = x_ref[i, own, :]
                grad = grad_ref[i, own, :]
                scores = dot(key_block, query, NN)
                scores = jnp.where(allowed, scores, NEGATIVE)
                prob = jnp.exp(scores - log_ref[i, h : h + 1, :])
                grad_prob = dot(value_block, grad, NN)
                grad_scores = (prob * (grad_prob - deltas[h])).astype(BF16)
                acc[own, :] += dot(key_columns, grad_scores, NN)
                grad_keys = grad_keys + dot(query, grad_scores, NT)
                grad_values = grad_values + dot(grad, prob.astype(BF16), NT)
            acc_keys[j] = grad_keys
            acc_values[j] = grad_values
            weight_turn(i * (i + 1) // 2 + j)
            return carry

        lax.fori_loop(0, i + 1, step, 0)
        for h in range(groups):
            at = h * HEAD_DIM
            front, back = turn_back(
                acc[pl.ds(at, HEAD_DIM), :] * SCORE_SCALE, cos_ref[i], sin_ref[i]
            )
            done[i, pl.ds(at, HALF), :] = front
            done[i, pl.ds(at + HALF, HALF), :] = back

        @pl.when(i != me)
        def _():
            to_block(
                done.at[i, of_queries], out_ref.at[me, of_queries], q_send.at[i], q_recv.at[me], i
            ).start()

        return carry

    lax.fori_loop(0, blocks, block, 0)

    def last(j, carry):
        front, back = turn_back(acc_keys[j], cos_ref[j], sin_ref[j])
        done[j, pl.ds(width, HALF), :] = front
        done[j, pl.ds(width + HALF, HALF), :] = back
        done[j, pl.ds(width + HEAD_DIM, HEAD_DIM), :] = acc_values[j].astype(BF16)

        @pl.when(j != me)
        def _():
            to_block(
                done.at[j, of_keys], out_ref.at[me, of_keys], k_send.at[j], k_recv.at[me], j
            ).start()

        return carry

    lax.fori_loop(0, blocks, last, 0)
    out_ref[me] = done[me]

    def left(c, carry):
        weight_turn(c)
        return carry

    lax.fori_loop(blocks * (blocks + 1) // 2, max(turns, blocks * (blocks + 1) // 2), left, 0)

    reduce.after_all()
    reduce.drain()
    for mask in range(1, wide):
        other = me ^ mask
        arrive(mine_ref.at[other], in_send.at[mask])
        arrive(done.at[other, of_queries], q_send.at[other])
        arrive(done.at[other, of_keys], k_send.at[other])
        arrive(out_ref.at[other, of_queries], q_recv.at[other])
        arrive(out_ref.at[other, of_keys], k_recv.at[other])
    own_part.wait()
    for step in range(1, narrow):
        part_copy(step).wait()


def attend_back(x, mine, full, log_total, start, cos, sin, part, left, right, groups):
    wide, narrow = lax.axis_size("wide"), lax.axis_size("narrow")
    blocks, features, rows = x.shape
    width = groups * HEAD_DIM
    dma = pltpu.SemaphoreType.DMA
    hbm = pl.BlockSpec(memory_space=pl.ANY)
    vmem = pl.BlockSpec(memory_space=pltpu.VMEM)
    return pl.pallas_call(
        functools.partial(attend_back_kernel, wide, narrow, groups),
        out_shape=(
            jax.ShapeDtypeStruct(x.shape, BF16),
            jax.ShapeDtypeStruct(part.shape, BF16),
            jax.ShapeDtypeStruct((left.shape[0] // (wide * narrow), right.shape[1]), F32),
        ),
        in_specs=[vmem] * 7 + [hbm, vmem, vmem],
        out_specs=(vmem, hbm, vmem),
        scratch_shapes=[
            pltpu.VMEM((blocks, rows, HEAD_DIM), BF16),
            pltpu.VMEM((blocks, rows, HEAD_DIM), BF16),
            pltpu.VMEM((width, rows), F32),
            pltpu.VMEM((blocks, HEAD_DIM, rows), F32),
            pltpu.VMEM((blocks, HEAD_DIM, rows), F32),
            pltpu.VMEM((blocks, width, rows), BF16),
            pltpu.VMEM((blocks, features, rows), BF16),
            dma((1,)),
        ]
        + [dma((wide,))] * 6
        + [dma((narrow,))] * 2
        + reduce_scratch(wide, narrow, left.shape[0], left.shape[1], right.shape[1], 512),
        compiler_params=pltpu.CompilerParams(
            collective_id=4, has_side_effects=True, vmem_limit_bytes=50 << 20
        ),
        cost_estimate=pl.CostEstimate(
            flops=40 * width * (blocks * rows) ** 2,
            bytes_accessed=4 * x.size * 2,
            transcendentals=groups * (blocks * rows) ** 2 // 2,
        ),
    )(start, x, mine, full, log_total, cos, sin, part, left, right)


def gather(x, axis):
    return lax.all_gather(x, axis, axis=0, tiled=True)


def scatter_sum(x, axis):
    return lax.psum_scatter(x, axis, scatter_dimension=0, tiled=True)


def gather_kernel(wide, narrow, aligned, qkv_ref, cut_ref, qkv_all, cut_all, x_send, x_recv, x_own, *sems):
    w, n = lax.axis_index("wide"), lax.axis_index("narrow")
    greet(wide, narrow)
    flow = Flow(wide, narrow, qkv_ref, qkv_all, sems)
    depth = qkv_ref.shape[0]
    piece = cut_all.shape[1] // (2 * wide)

    def rows_of(owner):
        return cut_all.at[pl.ds(pl.multiple_of(owner * depth, depth), depth), :]

    def pieces(other):
        if not aligned:
            return [(cut_ref.at[other], pl.ds(0, cut_all.shape[1]))]
        return [
            (
                cut_ref.at[:, pl.ds(pl.multiple_of((j * narrow + other) * piece, piece), piece)],
                pl.ds(j * piece, piece),
            )
            for j in range(2 * wide)
        ]

    def target(columns):
        return cut_all.at[pl.ds(pl.multiple_of(n * depth, depth), depth), columns]

    def cut_start(step):
        other = lax.rem(n + step, narrow)
        for source, columns in pieces(other):
            pltpu.make_async_remote_copy(
                src_ref=source,
                dst_ref=target(columns),
                send_sem=x_send.at[step],
                recv_sem=x_recv.at[step],
                device_id={"wide": w, "narrow": other},
                device_id_type=MESH,
            ).start()

    for t in range(flow.last):
        flow.step(t)
        if t == min(2, narrow - 1):
            for source, columns in pieces(n):
                pltpu.make_async_copy(source, target(columns), x_own).start()
            for step in range(1, narrow):
                cut_start(step)
    flow.end()
    own = rows_of(n)
    pltpu.make_async_copy(own, own, x_own).wait()
    for step in range(1, narrow):
        pltpu.make_async_copy(own, own, x_send.at[step]).wait()
        block = rows_of(lax.rem(n + narrow - step, narrow))
        pltpu.make_async_copy(block, block, x_recv.at[step]).wait()


def gather_weights(qkv, gateup):
    wide, narrow = lax.axis_size("wide"), lax.axis_size("narrow")
    dma = pltpu.SemaphoreType.DMA
    hbm = pl.BlockSpec(memory_space=pl.ANY)
    every = wide * narrow
    shard, columns = gateup.shape
    aligned = (columns // (2 * every)) % 128 == 0
    if not aligned:
        gateup = gateup.reshape(shard, 2, wide, narrow, -1).transpose(3, 0, 1, 2, 4)
        gateup = gateup.reshape(narrow, shard, columns // narrow)
    return pl.pallas_call(
        functools.partial(gather_kernel, wide, narrow, aligned),
        out_shape=(
            jax.ShapeDtypeStruct((every * qkv.shape[0], qkv.shape[1]), BF16),
            jax.ShapeDtypeStruct((narrow * shard, columns // narrow), BF16),
        ),
        in_specs=[hbm, hbm],
        out_specs=(hbm, hbm),
        scratch_shapes=[dma((narrow,)), dma((narrow,)), dma(())] + flow_sems(wide, narrow),
        compiler_params=pltpu.CompilerParams(collective_id=0, has_side_effects=True),
        cost_estimate=pl.CostEstimate(flops=0, bytes_accessed=200 << 20, transcendentals=0),
    )(qkv, gateup)


def feed_kernel(
    narrow, x_ref, cot_ref, gate_up_ref, down_ref,
    low_out, grad_x_ref, part_gate_up, part_down,
    group_ref, gate_up, down, cot, hidden, grads, low, came,
    load_sem, x_send, x_recv, out_sem, g_send, g_recv,
):
    w, n = lax.axis_index("wide"), lax.axis_index("narrow")
    rows, width = x_ref.shape
    own = down.shape[0]
    tile = 256
    tiles = own // tile
    wtiles = width // tile

    def to_narrow(other):
        return {"wide": w, "narrow": other}

    loads = [
        pltpu.make_async_copy(gate_up_ref, gate_up, load_sem.at[0]),
        pltpu.make_async_copy(down_ref, down, load_sem.at[1]),
        pltpu.make_async_copy(cot_ref, cot, load_sem.at[2]),
        pltpu.make_async_copy(x_ref, group_ref.at[n], load_sem.at[3]),
    ]
    for load in loads:
        load.start()

    barrier = pltpu.get_barrier_semaphore()
    for step in range(1, narrow):
        pl.semaphore_signal(
            barrier, inc=1, device_id=to_narrow(lax.rem(n + step, narrow)), device_id_type=MESH
        )
    pl.semaphore_wait(barrier, narrow - 1)

    def owner_of(side, d):
        return n - d if side == 0 else n + d

    def valid(side, d):
        return n - d >= 0 if side == 0 else (n + d < narrow) & (d > 0)

    def passes(side, d):
        if side == 0:
            return (n - d >= 0) & (n < narrow - 1)
        return (n + d < narrow) & (n > 0)

    def x_copy(side, d):
        block = group_ref.at[owner_of(side, d)]
        return pltpu.make_async_remote_copy(
            src_ref=block,
            dst_ref=block,
            send_sem=x_send.at[side, d],
            recv_sem=x_recv.at[side, d + 1],
            device_id=to_narrow(n + 1 if side == 0 else n - 1),
            device_id_type=MESH,
        )

    def x_wait(side, d):
        block = group_ref.at[owner_of(side, d)]
        pltpu.make_async_copy(block, block, x_recv.at[side, d]).wait()

    def out_copy(at, block):
        return pltpu.make_async_copy(low.at[at], low_out.at[block], out_sem.at[at])

    def g_copy(block, half):
        columns = pl.ds(half * (width // 2), width // 2)
        return pltpu.make_async_remote_copy(
            src_ref=cot.at[block, :, columns],
            dst_ref=came.at[n, :, columns],
            send_sem=g_send.at[block, half],
            recv_sem=g_recv.at[n, half],
            device_id=to_narrow(block),
            device_id_type=MESH,
        )

    def compute(side, d):
        block = n - d + 2 * d * side
        before = 1 + jnp.minimum(n, d - 1) + jnp.minimum(narrow - 1 - n, d - 1)
        before = jnp.where(d == 0, 0, before + jnp.where((side == 1) & (n - d >= 0), 1, 0))
        at = lax.rem(before, 2)

        pl.when(before >= 2)(lambda: out_copy(at, block).wait())

        def first(f, carry):
            columns = pl.ds(pl.multiple_of(f * tile, tile), tile)
            other = pl.ds(pl.multiple_of(own + f * tile, tile), tile)
            x = group_ref[block]
            gate = dot(x, gate_up[:, columns], NN)
            up = dot(x, gate_up[:, other], NN)
            grad = dot(cot[block], down[columns, :], NT)
            sig = 1.0 / (1.0 + jnp.exp(-gate))
            silu = gate * sig
            hidden[block, :, columns] = (silu * up).astype(BF16)
            grads[block, :, columns] = (grad * up * (sig + silu * (1.0 - sig))).astype(BF16)
            grads[block, :, other] = (grad * silu).astype(BF16)
            return carry

        lax.fori_loop(0, tiles, first, 0)

        def second(f, carry):
            columns = pl.ds(pl.multiple_of(f * tile, tile), tile)
            cot[block, :, columns] = dot(grads[block], gate_up[columns, :], NT, BF16)
            low[at, :, columns] = dot(hidden[block], down[:, columns], NN, BF16)
            return carry

        for half in (0, 1):
            lax.fori_loop(half * (wtiles // 2), (half + 1) * (wtiles // 2), second, 0)
            pl.when(block != n)(lambda half=half: g_copy(block, half).start())
        out_copy(at, block).start()

    def distance(d, carry):
        for side in (0, 1):

            @pl.when(passes(side, d + 1))
            def _():
                x_wait(side, d + 1)
                x_copy(side, d + 1).start()

            @pl.when(valid(side, d) & (d > 0) & jnp.logical_not(passes(side, d)))
            def _():
                x_wait(side, d)

        @pl.when(d == 0)
        def _():
            for load in loads[:3]:
                load.wait()

        def one(side, carry):
            ok = jnp.where(side == 0, n - d, jnp.where(d > 0, narrow - 1 - n - d, -1)) >= 0
            pl.when(ok)(lambda: compute(side, d))
            return carry

        lax.fori_loop(0, 2, one, 0)
        return carry

    loads[3].wait()
    for side in (0, 1):
        pl.when(passes(side, 0))(lambda side=side: x_copy(side, 0).start())
    lax.fori_loop(0, narrow, distance, 0)

    tokens = narrow * rows
    again = [
        pltpu.make_async_copy(
            cot_ref.at[o], gate_up.at[pl.ds(o * rows, rows), pl.ds(0, width)], load_sem.at[4 + o]
        )
        for o in range(narrow)
    ]
    for load in again:
        load.start()
    for at in range(2):
        out_copy(at, n).wait()

    def flipped(ref, columns):
        return jnp.concatenate([ref[o, :, columns].T for o in range(narrow)], 1)

    def weight_tile(t, left, right, at_row, out_ref, first):
        at = lax.rem(t, 2)
        copy = pltpu.make_async_copy(low.at[at], out_ref, out_sem.at[at])
        pl.when(t >= 2)(lambda: copy.wait())
        turned = flipped(left, pl.ds(pl.multiple_of(at_row, tile), tile))

        def one(c, carry):
            columns = pl.ds(pl.multiple_of(c * 512, 512), 512)
            source = pl.ds(pl.multiple_of(first + c * 512, 512), 512)
            low[at, :, columns] = dot(turned, right(source), NN, BF16)
            return carry

        lax.fori_loop(0, width // 512, one, 0)
        copy.start()

    halves = 2 * own // width

    def gate_up_tile(t, carry):
        row, half = t // halves * tile, lax.rem(t, halves) * width
        row, half = pl.multiple_of(row, tile), pl.multiple_of(half, width)
        weight_tile(
            t, group_ref, lambda source: grads[:, :, source].reshape(tokens, 512), row,
            part_gate_up.at[pl.ds(row, tile), pl.ds(half, width)], half,
        )
        return carry

    def down_tile(t, carry):
        row = pl.multiple_of(t * tile, tile)
        weight_tile(
            t + 2, hidden, lambda source: gate_up[pl.ds(0, tokens), source], row,
            part_down.at[pl.ds(row, tile), :], 0,
        )
        return carry

    lax.fori_loop(0, wtiles * halves, gate_up_tile, 0)
    for load in again:
        load.wait()
    lax.fori_loop(0, tiles, down_tile, 0)
    for at in range(2):
        out_copy(at, n).wait()
    for side in (0, 1):
        for d in range(narrow - 1):
            pl.when(passes(side, d))(lambda side=side, d=d: x_copy(side, d).wait_send())
    for step in range(1, narrow):
        other = lax.rem(n + step, narrow)
        for half in (0, 1):
            g_copy(other, half).wait_send()
            arrive(came.at[other, :, pl.ds(half * (width // 2), width // 2)], g_recv.at[other, half])

    def add(r, carry):
        part = pl.ds(pl.multiple_of(r * 16, 16), 16)
        total = cot[n, part, :].astype(F32)
        for step in range(1, narrow):
            total = total + came[lax.rem(n + step, narrow), part, :].astype(F32)
        grad_x_ref[part, :] = total
        return carry

    lax.fori_loop(0, rows // 16, add, 0)


def feed(x, cot_group, gate_up, down):
    narrow = lax.axis_size("narrow")
    rows, width = x.shape
    own = down.shape[0]
    dma = pltpu.SemaphoreType.DMA
    hbm = pl.BlockSpec(memory_space=pl.ANY)
    vmem = pl.BlockSpec(memory_space=pltpu.VMEM)
    return pl.pallas_call(
        functools.partial(feed_kernel, narrow),
        out_shape=(
            jax.ShapeDtypeStruct((narrow, rows, width), BF16),
            jax.ShapeDtypeStruct((rows, width), F32),
            jax.ShapeDtypeStruct((width, 2 * own), BF16),
            jax.ShapeDtypeStruct((own, width), BF16),
        ),
        in_specs=[vmem, hbm, hbm, hbm],
        out_specs=(hbm, vmem, hbm, hbm),
        scratch_shapes=[
            pltpu.VMEM((narrow, rows, width), BF16),
            pltpu.VMEM((width, 2 * own), BF16),
            pltpu.VMEM((own, width), BF16),
            pltpu.VMEM((narrow, rows, width), BF16),
            pltpu.VMEM((narrow, rows, own), BF16),
            pltpu.VMEM((narrow, rows, 2 * own), BF16),
            pltpu.VMEM((2, rows, width), BF16),
            pltpu.VMEM((narrow, rows, width), BF16),
            dma((4 + narrow,)),
            dma((2, narrow + 1)),
            dma((2, narrow + 1)),
            dma((2,)),
            dma((narrow, 2)),
            dma((narrow, 2)),
        ],
        compiler_params=pltpu.CompilerParams(
            collective_id=1, has_side_effects=True, vmem_limit_bytes=58 << 20
        ),
        cost_estimate=pl.CostEstimate(
            flops=12 * narrow * rows * width * own, bytes_accessed=300 << 20, transcendentals=0
        ),
    )(x, cot_group.reshape(narrow, rows, width), gate_up, down)


def sum_kernel(
    wide, narrow, left_ref, right_ref, cut_ref, gains_ref, qkv_out, cut_out, gains_out,
    cut_in, gain_w, gain_sum, gain_z, own_sem, cut_send, cut_recv, gw_send, gw_recv, gz_send, gz_recv, *refs,
):
    reduce = Reduce(wide, narrow, left_ref, right_ref, NT, qkv_out, refs)
    w, n = reduce.w, reduce.n
    chunks, bits = reduce.chunks, reduce.bits
    reduce.arrange()
    greet(wide, narrow)

    def to_wide(mask):
        return {"wide": w ^ mask, "narrow": n}

    def to_narrow(step):
        return {"wide": w, "narrow": lax.rem(n + step, narrow)}

    own_cut = pltpu.make_async_copy(cut_ref.at[n], cut_in.at[n], own_sem)

    def cut_copy(step):
        return pltpu.make_async_remote_copy(
            src_ref=cut_ref.at[lax.rem(n + step, narrow)],
            dst_ref=cut_in.at[n],
            send_sem=cut_send.at[step],
            recv_sem=cut_recv.at[step],
            device_id=to_narrow(step),
            device_id_type=MESH,
        )

    def gw_copy(mask):
        return pltpu.make_async_remote_copy(
            src_ref=gains_ref.at[w ^ mask],
            dst_ref=gain_w.at[mask],
            send_sem=gw_send.at[mask],
            recv_sem=gw_recv.at[mask],
            device_id=to_wide(mask),
            device_id_type=MESH,
        )

    def gz_copy(step):
        return pltpu.make_async_remote_copy(
            src_ref=gain_sum.at[lax.rem(n + step, narrow)],
            dst_ref=gain_z.at[step],
            send_sem=gz_send.at[step],
            recv_sem=gz_recv.at[step],
            device_id=to_narrow(step),
            device_id_type=MESH,
        )

    ahead = min(4, chunks)
    lax.fori_loop(0, ahead, lambda q, carry: (reduce.begin(q), carry)[1], 0)
    own_cut.start()
    for step in range(1, narrow):
        cut_copy(step).start()
    for mask in range(1, wide):
        gw_copy(mask).start()

    def turn(t, carry):
        pl.when(t + ahead < chunks)(lambda: reduce.begin(t + ahead))
        pl.when(t < chunks)(lambda: reduce.after_core(t))
        for stage in range(bits):
            q = t - 1 - stage
            pl.when((q >= 0) & (q < chunks))(functools.partial(reduce.after_stage, q, stage))
        return carry

    lax.fori_loop(0, chunks + bits, turn, 0)

    total = gains_ref[w]
    for mask in range(1, wide):
        block = gain_w.at[mask]
        pltpu.make_async_copy(block, block, gw_recv.at[mask]).wait()
        total = total + gain_w[mask]
    gain_sum[...] = total
    for step in range(1, narrow):
        gz_copy(step).start()

    reduce.after_all()
    own_cut.wait()
    for step in range(1, narrow):
        other = lax.rem(n + narrow - step, narrow)
        arrive(cut_in.at[other], cut_recv.at[step])
    piece = cut_in.shape[2] // (2 * wide)
    if cut_out.shape[0] == narrow:
        for other in range(narrow):
            cut_out[other] = cut_in[other].astype(F32)
    else:
        for j in range(2 * wide):
            for other in range(narrow):
                cut_out[:, pl.ds((j * narrow + other) * piece, piece)] = cut_in[
                    other, :, pl.ds(j * piece, piece)
                ].astype(F32)

    total = gain_sum[n]
    for step in range(1, narrow):
        block = gain_z.at[step]
        pltpu.make_async_copy(block, block, gz_recv.at[step]).wait()
        total = total + gain_z[step]
    gains_out[...] = total

    for mask in range(1, wide):
        gw_copy(mask).wait_send()
    for step in range(1, narrow):
        gz_copy(step).wait_send()
        cut_copy(step).wait_send()
    reduce.drain()


def sum_all(left, right, cut, gains):
    wide, narrow = lax.axis_size("wide"), lax.axis_size("narrow")
    shard, cut_width = cut.shape[1:]
    aligned = (cut_width // (2 * wide)) % 128 == 0
    cut_shape = (shard, narrow * cut_width) if aligned else cut.shape
    dma = pltpu.SemaphoreType.DMA
    hbm = pl.BlockSpec(memory_space=pl.ANY)
    vmem = pl.BlockSpec(memory_space=pltpu.VMEM)
    results = pl.pallas_call(
        functools.partial(sum_kernel, wide, narrow),
        out_shape=(
            jax.ShapeDtypeStruct((shard, right.shape[0]), F32),
            jax.ShapeDtypeStruct(cut_shape, F32),
            jax.ShapeDtypeStruct((8, 128), F32),
        ),
        in_specs=[vmem, vmem, hbm, vmem],
        out_specs=(vmem, vmem, vmem),
        scratch_shapes=[
            pltpu.VMEM(cut.shape, BF16),
            pltpu.VMEM((wide, narrow, 8, 128), F32),
            pltpu.VMEM((narrow, 8, 128), F32),
            pltpu.VMEM((narrow, 8, 128), F32),
            dma(()),
            dma((narrow,)),
            dma((narrow,)),
            dma((wide,)),
            dma((wide,)),
            dma((narrow,)),
            dma((narrow,)),
        ]
        + reduce_scratch(wide, narrow, left.shape[1], left.shape[0], right.shape[0], 256),
        compiler_params=pltpu.CompilerParams(
            collective_id=2, has_side_effects=True, vmem_limit_bytes=54 << 20
        ),
        cost_estimate=pl.CostEstimate(flops=0, bytes_accessed=300 << 20, transcendentals=0),
    )(left, right, cut, gains)
    return results, aligned


def per_device(tokens, lengths, gain_attn, w_qkv, w_out, gain_mlp, w_gateup, w_down, cotangent):
    rows, width = tokens.shape[1:]
    wide, narrow = lax.axis_size("wide"), lax.axis_size("narrow")
    pack_rows = rows * wide
    query_width, key_width = HEADS * HEAD_DIM, KV_HEADS * HEAD_DIM
    groups = HEADS // wide
    copies = wide // KV_HEADS
    own_ff = FF // narrow
    first, positions = places(lengths[0], pack_rows)
    cos_all, sin_all = rotary(positions.astype(F32), HALF)
    first_row = lax.axis_index("wide") * rows
    cos = lax.dynamic_slice_in_dim(cos_all, first_row, rows, 1)
    sin = lax.dynamic_slice_in_dim(sin_all, first_row, rows, 1)
    cos_all = cos_all.reshape(HALF, wide, rows).transpose(1, 0, 2)
    sin_all = sin_all.reshape(HALF, wide, rows).transpose(1, 0, 2)
    start = first.reshape(wide, 1, rows)

    gains = jnp.stack([gain_attn, gain_mlp], -1)
    with_gains = jnp.concatenate([w_qkv, jnp.pad(gains, ((0, 0), (0, 126)))], -1)
    shard = w_gateup.shape[0]
    qkv_gained, gateup_rows = gather_weights(with_gains, w_gateup)
    qkv_whole = qkv_gained[:, : w_qkv.shape[1]]
    gain_one = qkv_gained[:, w_qkv.shape[1]].astype(F32)
    gain_two = qkv_gained[:, w_qkv.shape[1] + 1].astype(F32)
    gateup_own = gather(gateup_rows, "wide")
    down_own = gather(w_down, "wide")

    inputs = tokens[0].astype(F32)
    scale_one = lax.rsqrt(jnp.mean(inputs * inputs, -1, keepdims=True) + EPS)
    unit_one = inputs * scale_one
    normed_one = (unit_one * gain_one).astype(BF16)
    projected = dot(qkv_whole, normed_one, (((0,), (1,)), ((), ())))
    turning = projected[: query_width + key_width].reshape(HEADS + KV_HEADS, 2, HALF, rows)
    front, back = turning[:, 0], turning[:, 1]
    turned = jnp.stack([front * cos - back * sin, back * cos + front * sin], 1)
    queries = (turned[:HEADS] * SCORE_SCALE).astype(BF16).reshape(wide, groups * HEAD_DIM, rows)
    keys = turned[HEADS:].astype(BF16).reshape(KV_HEADS, HEAD_DIM, rows)
    values = projected[query_width + key_width :].astype(BF16).reshape(KV_HEADS, HEAD_DIM, rows)
    keys_values = jnp.repeat(jnp.concatenate([keys, values], 1), copies, 0)
    heads, attended_low, attended_full, log_total, out_whole, cot_group = attend(
        jnp.concatenate([queries, keys_values], 1), start, w_out, cotangent[0], groups
    )
    cot_group = cot_group.reshape(-1, width)
    attended_low = attended_low.reshape(query_width, rows)
    middle = inputs + dot(attended_low, out_whole, TN)
    scale_two = lax.rsqrt(jnp.mean(middle * middle, -1, keepdims=True) + EPS)
    unit_two = middle * scale_two
    normed_two = (unit_two * gain_two).astype(BF16)

    low_part, grad_normed_two, part_gateup, part_down = feed(
        normed_two, cot_group, gateup_own, down_own
    )
    grad_gateup = scatter_sum(part_gateup, "wide").reshape(narrow, shard, 2 * own_ff)
    grad_down = scatter_sum(part_down, "wide")
    part_gain_two = jnp.sum(grad_normed_two * unit_two, 0)
    grad_middle = cotangent[0].astype(F32) + norm_back(
        grad_normed_two * gain_two, unit_two, scale_two
    )
    grad_branch = grad_middle.astype(BF16)
    grad_attended = dot(out_whole, grad_branch, NT, BF16).reshape(wide, groups * HEAD_DIM, rows)
    grad_heads, low_came, grad_wout = attend_back(
        heads, grad_attended, attended_full, log_total, start, cos_all, sin_all, low_part,
        attended_low, grad_branch, groups,
    )
    layer_out = (middle + jnp.sum(low_came.astype(F32), 0)).astype(BF16)[None]
    grad_queries = grad_heads[:, : groups * HEAD_DIM].reshape(query_width, rows)
    grad_keys_values = (
        grad_heads[:, groups * HEAD_DIM :]
        .reshape(KV_HEADS, copies, 2, HEAD_DIM, rows)
        .astype(F32)
        .sum(1)
        .astype(BF16)
    )
    grad_projected = jnp.concatenate(
        [
            grad_queries,
            grad_keys_values[:, 0].reshape(key_width, rows),
            grad_keys_values[:, 1].reshape(key_width, rows),
        ],
        0,
    )
    grad_normed_one = dot(grad_projected, qkv_whole, (((0,), (1,)), ((), ())))
    part_gain_one = jnp.sum(grad_normed_one * unit_one, 0)
    part_gains = jnp.stack([part_gain_one, part_gain_two], 0).reshape(2, wide, narrow, shard)
    part_gains = jnp.pad(
        part_gains.transpose(1, 2, 0, 3), ((0, 0), (0, 0), (0, 6), (0, 128 - shard))
    )
    (grad_qkv, grad_gateup, grad_gains), done = sum_all(
        normed_one, grad_projected, grad_gateup, part_gains
    )
    if not done:
        grad_gateup = (
            grad_gateup.reshape(narrow, shard, 2, wide, -1)
            .transpose(1, 2, 3, 0, 4)
            .reshape(shard, 2 * FF)
        )
    grad_down, grad_gains = lax.optimization_barrier((grad_down, grad_gains))
    grad_down = grad_down.astype(F32)
    grad_inputs = grad_middle + norm_back(grad_normed_one * gain_one, unit_one, scale_one)
    grad_tokens = grad_inputs.astype(BF16)[None]
    return (
        layer_out,
        grad_tokens,
        grad_gains[0, :shard],
        grad_qkv,
        grad_wout,
        grad_gains[1, :shard],
        grad_gateup,
        grad_down,
    )


def solution(mesh):
    rows, packs = P("narrow", "wide", None), P("narrow", None)
    weight, gain = P(BOTH, None), P(BOTH)
    return jax.shard_map(
        per_device,
        mesh=mesh,
        in_specs=(rows, packs, gain, weight, weight, gain, weight, weight, rows),
        out_specs=(rows, rows, gain, weight, weight, gain, weight, weight),
        check_vma=False,
    )
```

```python
import functools
import math

import jax
import jax.numpy as jnp
from jax import lax
from jax.experimental import pallas as pl
from jax.experimental.pallas import tpu as pltpu
from jax.sharding import PartitionSpec as P

FF = 8192
HEADS = 32
KV_HEADS = 8
HEAD_DIM = 64
HALF = HEAD_DIM // 2
EPS = 1e-05
NEGATIVE = -1e30
SCORE_SCALE = 1.0 / math.sqrt(HEAD_DIM)
BOTH = ("wide", "narrow")
F32 = jnp.float32
BF16 = jnp.bfloat16
NN = (((1,), (0,)), ((), ()))
NT = (((1,), (1,)), ((), ()))
TN = (((0,), (0,)), ((), ()))


def dot(left, right, dims, kind=F32):
    return lax.dot_general(left, right, dims, preferred_element_type=F32).astype(kind)


def places(lengths_row, total_rows):
    seq_ends = jnp.cumsum(lengths_row)
    starts = seq_ends - lengths_row
    row_index = jnp.arange(total_rows, dtype=jnp.int32)
    segments = jnp.sum((row_index[:, None] >= seq_ends[None, :]).astype(jnp.int32), -1)
    slot_index = jnp.arange(lengths_row.shape[0], dtype=jnp.int32)
    owned = segments[:, None] == slot_index[None, :]
    first = jnp.sum(jnp.where(owned, starts[None, :], 0), -1)
    return first, row_index - first


def rotary(positions, half_width):
    channel = jnp.arange(half_width, dtype=jnp.float32)
    inverse_rate = jnp.power(500000.0, -channel / half_width)
    wavelength = 2.0 * math.pi / inverse_rate
    smooth = (8192.0 / wavelength - 1.0) / 3.0
    blended = (1.0 - smooth) * inverse_rate / 32.0 + smooth * inverse_rate
    frequency = jnp.where(
        wavelength < 2048.0,
        inverse_rate,
        jnp.where(wavelength > 8192.0, inverse_rate / 32.0, blended),
    )
    angles = frequency[:, None] * positions[None, :]
    return jnp.cos(angles), jnp.sin(angles)


def norm_back(grad_unit, unit_rows, row_scale):
    return row_scale * (grad_unit - unit_rows * jnp.mean(grad_unit * unit_rows, -1, keepdims=True))


MESH = pl.DeviceIdType.MESH


class Flow:
    def __init__(self, wide, narrow, x_ref, out_ref, sems):
        self.wide, self.narrow, self.x_ref, self.out_ref = wide, narrow, x_ref, out_ref
        self.w, self.n = lax.axis_index("wide"), lax.axis_index("narrow")
        (self.own_sem, self.z_send, self.z_recv, self.m_send, self.m_recv,
         self.r_send, self.r_recv, self.c_send, self.c_recv) = sems
        self.relay = wide == 8
        self.masks = [2, 4] if self.relay else list(range(2, wide, 2))
        self.last = narrow + 2

    def to_wide(self, mask):
        return {"wide": self.w ^ mask, "narrow": self.n}

    def owner_of(self, side, d):
        return self.n - d if side == 0 else self.n + d

    def valid(self, side, d):
        return self.n - d >= 0 if side == 0 else self.n + d < self.narrow

    def can_pass(self, side, d):
        if side == 0:
            return (self.n - (d - 1) >= 0) & (self.n < self.narrow - 1)
        return (self.n + (d - 1) < self.narrow) & (self.n > 0)

    def slot(self, side, d):
        return d - 1 + side * (self.narrow - 1) if d else 2 * (self.narrow - 1)

    def at_distance(self, d, action):
        if d == 0:
            action(0, 0)
            return
        for side in (0, 1):
            pl.when(self.valid(side, d))(functools.partial(action, side, d))

    def place(self, owner_w, owner_n, part=None):
        depth = self.x_ref.shape[0]
        half = depth // 2
        at = (owner_w * self.narrow + owner_n) * depth
        if part is None:
            return self.out_ref.at[pl.ds(pl.multiple_of(at, depth), depth), :]
        return self.out_ref.at[pl.ds(pl.multiple_of(at + part * half, half), half), :]

    def own_copy(self):
        return pltpu.make_async_copy(self.x_ref, self.place(self.w, self.n), self.own_sem)

    def z_copy(self, side, d):
        block = self.place(self.w, self.owner_of(side, d - 1))
        return pltpu.make_async_remote_copy(
            src_ref=self.x_ref if d == 1 else block,
            dst_ref=block,
            send_sem=self.z_send.at[side, d],
            recv_sem=self.z_recv.at[side, d],
            device_id={"wide": self.w, "narrow": self.n + 1 if side == 0 else self.n - 1},
            device_id_type=MESH,
        )

    def z_wait(self, side, d):
        block = self.place(self.w, self.owner_of(side, d))
        pltpu.make_async_copy(block, block, self.z_recv.at[side, d]).wait()

    def m_copy(self, i, side, d):
        block = self.place(self.w, self.owner_of(side, d))
        return pltpu.make_async_remote_copy(
            src_ref=self.x_ref if d == 0 else block,
            dst_ref=block,
            send_sem=self.m_send.at[i, self.slot(side, d)],
            recv_sem=self.m_recv.at[i, self.slot(side, d)],
            device_id=self.to_wide(self.masks[i]),
            device_id_type=MESH,
        )

    def m_wait(self, i, side, d):
        block = self.place(self.w ^ self.masks[i], self.owner_of(side, d))
        pltpu.make_async_copy(block, block, self.m_recv.at[i, self.slot(side, d)]).wait()

    def r_copy(self, part, side, d):
        block = self.place(self.w ^ self.masks[part], self.owner_of(side, d), part)
        return pltpu.make_async_remote_copy(
            src_ref=block,
            dst_ref=block,
            send_sem=self.r_send.at[part, self.slot(side, d)],
            recv_sem=self.r_recv.at[part, self.slot(side, d)],
            device_id=self.to_wide(self.masks[1 - part]),
            device_id_type=MESH,
        )

    def r_wait(self, part, side, d):
        block = self.place(self.w ^ 6, self.owner_of(side, d), part)
        pltpu.make_async_copy(block, block, self.r_recv.at[part, self.slot(side, d)]).wait()

    def c_copy(self, chip, side, d):
        block = self.place(self.w ^ (2 * chip), self.owner_of(side, d))
        return pltpu.make_async_remote_copy(
            src_ref=self.x_ref if d == 0 and chip == 0 else block,
            dst_ref=block,
            send_sem=self.c_send.at[chip, self.slot(side, d)],
            recv_sem=self.c_recv.at[chip, self.slot(side, d)],
            device_id=self.to_wide(1),
            device_id_type=MESH,
        )

    def c_wait(self, chip, side, d):
        block = self.place((self.w ^ 1) ^ (2 * chip), self.owner_of(side, d))
        pltpu.make_async_copy(block, block, self.c_recv.at[chip, self.slot(side, d)]).wait()

    def send_from_here(self, side, d):
        if d > 0:
            self.z_wait(side, d)
        if 0 < d < self.narrow - 1:
            pl.when(self.can_pass(side, d + 1))(lambda: self.z_copy(side, d + 1).start())
        for i in range(len(self.masks)):
            self.m_copy(i, side, d).start()
        self.c_copy(0, side, d).start()

    def send_on(self, side, d):
        for i in range(len(self.masks)):
            self.m_wait(i, side, d)
            if self.relay:
                self.r_copy(i, side, d).start()
            self.c_copy(self.masks[i] // 2, side, d).start()

    def send_last(self, side, d):
        self.r_wait(0, side, d)
        self.r_wait(1, side, d)
        self.c_copy(3, side, d).start()

    def step(self, t):
        if t == 0:
            self.own_copy().start()
            for side in (0, 1):
                pl.when(self.can_pass(side, 1))(lambda side=side: self.z_copy(side, 1).start())
        if 0 <= t < self.narrow:
            self.at_distance(t, self.send_from_here)
        if 0 <= t - 1 < self.narrow:
            self.at_distance(t - 1, self.send_on)
        if self.relay and 0 <= t - 2 < self.narrow:
            self.at_distance(t - 2, self.send_last)

    def finish(self, side, d):
        for i in range(len(self.masks)):
            self.m_copy(i, side, d).wait_send()
            if self.relay:
                self.r_copy(i, side, d).wait_send()
        for chip in range(self.wide // 2):
            self.c_copy(chip, side, d).wait_send()
            self.c_wait(chip, side, d)

    def end(self):
        self.own_copy().wait()
        for side in (0, 1):
            for d in range(1, self.narrow):
                pl.when(self.can_pass(side, d))(
                    lambda side=side, d=d: self.z_copy(side, d).wait_send()
                )
        for d in range(self.narrow):
            self.at_distance(d, self.finish)


class Line:
    def __init__(self, narrow, x_ref, out_ref, sems):
        self.narrow, self.x_ref, self.out_ref = narrow, x_ref, out_ref
        self.w, self.n = lax.axis_index("wide"), lax.axis_index("narrow")
        self.own_sem, self.send, self.recv = sems

    def owner_of(self, side, d):
        return self.n - d if side == 0 else self.n + d

    def valid(self, side, d):
        return self.n - d >= 0 if side == 0 else self.n + d < self.narrow

    def can_pass(self, side, d):
        if side == 0:
            return (self.n - (d - 1) >= 0) & (self.n < self.narrow - 1)
        return (self.n + (d - 1) < self.narrow) & (self.n > 0)

    def own_copy(self):
        return pltpu.make_async_copy(self.x_ref, self.out_ref.at[self.n], self.own_sem)

    def copy(self, side, d):
        block = self.out_ref.at[self.owner_of(side, d - 1)]
        return pltpu.make_async_remote_copy(
            src_ref=self.x_ref if d == 1 else block,
            dst_ref=block,
            send_sem=self.send.at[side, d],
            recv_sem=self.recv.at[side, d],
            device_id={"wide": self.w, "narrow": self.n + 1 if side == 0 else self.n - 1},
            device_id_type=MESH,
        )

    def pass_on(self, side, d):
        arrive(self.out_ref.at[self.owner_of(side, d)], self.recv.at[side, d])
        if d < self.narrow - 1:
            pl.when(self.can_pass(side, d + 1))(lambda: self.copy(side, d + 1).start())

    def step(self, t):
        if t == 0:
            self.own_copy().start()
        for side in (0, 1):
            if t == 0:
                pl.when(self.can_pass(side, 1))(lambda side=side: self.copy(side, 1).start())
            else:
                pl.when(self.valid(side, t))(lambda side=side: self.pass_on(side, t))

    def end(self):
        self.own_copy().wait()
        for side in (0, 1):
            for d in range(1, self.narrow):
                pl.when(self.can_pass(side, d))(lambda side=side, d=d: self.copy(side, d).wait_send())


def flow_sems(wide, narrow):
    slots = 2 * narrow - 1
    masks = 2 if wide == 8 else wide // 2 - 1
    dma = pltpu.SemaphoreType.DMA
    return [
        dma(()),
        dma((2, narrow)),
        dma((2, narrow)),
        dma((masks, slots)),
        dma((masks, slots)),
        dma((2, slots)),
        dma((2, slots)),
        dma((wide // 2, slots)),
        dma((wide // 2, slots)),
    ]


class Reduce:
    def __init__(self, wide, narrow, left, right, dims, out_ref, refs):
        self.wide, self.narrow, self.left, self.right, self.dims = wide, narrow, left, right, dims
        self.out_ref = out_ref
        self.w, self.n = lax.axis_index("wide"), lax.axis_index("narrow")
        self.core, self.chip = lax.rem(self.w, 2), self.w // 2
        self.chips = wide // 2
        self.bits = self.chips.bit_length() - 1
        (self.turned, self.held, self.away, self.core_in, self.chip_in, self.z_in, self.core_send, self.core_recv,
         self.chip_send, self.chip_recv, self.z_send, self.z_recv) = refs
        self.chunks = self.held.shape[0]
        self.rows, self.chunk = self.held.shape[2:]
        self.shard = self.rows // narrow
        self.orders = [list(range(self.bits)), list(range(self.bits))[::-1]]

    def columns_of(self, q):
        return pl.ds(pl.multiple_of(q * self.chunk, self.chunk), self.chunk)

    def arrange(self):
        for k in range(self.chips):
            for core in (0, 1):
                at = (2 * k + core) * self.rows
                if self.dims == NT:
                    tile = self.left[:, at : at + self.rows].T
                else:
                    tile = self.left[at : at + self.rows, :]
                self.turned[core, k * self.rows : (k + 1) * self.rows, :] = tile

    def begin(self, q):
        columns = self.columns_of(q)
        right = self.right[columns, :] if self.dims == NT else self.right[:, columns]
        shape = self.held.shape[1:]
        self.away[q] = dot(self.turned[1 - self.core], right, self.dims, BF16).reshape(shape)
        self.held[q] = dot(self.turned[self.core], right, self.dims, BF16).reshape(shape)
        pltpu.make_async_remote_copy(
            src_ref=self.away.at[q],
            dst_ref=self.core_in.at[q],
            send_sem=self.core_send.at[q],
            recv_sem=self.core_recv.at[q],
            device_id={"wide": self.w ^ 1, "narrow": self.n},
            device_id_type=MESH,
        ).start()

    def add_to(self, target, other):
        def one(r, carry):
            part = pl.ds(pl.multiple_of(r * 16, 16), 16)
            target(part)[...] = (
                target(part)[...].astype(F32) + other(part)[...].astype(F32)
            ).astype(BF16)
            return carry

        lax.fori_loop(0, self.rows // 16, one, 0)

    def tiles_of(self, h, stage):
        order = self.orders[h]
        rest = order[stage + 1 :]
        offset = sum(self.chips >> (i + 1) for i in range(stage))
        fixed = sum(1 << b for b in order[: stage + 1])
        result = []
        for v in range(1 << len(rest)):
            extra = sum(((v >> i) & 1) << b for i, b in enumerate(rest))
            result.append((offset + v, (self.chip & fixed) + extra))
        return result

    def lanes(self, h):
        return pl.ds(h * (self.chunk // 2), self.chunk // 2)

    def chip_copy(self, q, h, stage, slot, kept):
        bit = self.orders[h][stage]
        return pltpu.make_async_remote_copy(
            src_ref=self.held.at[q, kept ^ (1 << bit), :, self.lanes(h)],
            dst_ref=self.chip_in.at[q, h, slot],
            send_sem=self.chip_send.at[q, h, slot],
            recv_sem=self.chip_recv.at[q, h, slot],
            device_id={"wide": self.w ^ (2 << bit), "narrow": self.n},
            device_id_type=MESH,
        )

    def send_stage(self, q, stage):
        for h in (0, 1):
            for slot, kept in self.tiles_of(h, stage):
                self.chip_copy(q, h, stage, slot, kept).start()

    def after_core(self, q):
        arrive(self.core_in.at[q], self.core_recv.at[q])
        for k in range(self.chips):
            self.add_to(
                lambda part, k=k: self.held.at[q, k, part, :],
                lambda part, k=k: self.core_in.at[q, k, part, :],
            )
        self.send_stage(q, 0)

    def z_copy(self, q, step):
        other = lax.rem(self.n + step, self.narrow)
        own = pl.ds(pl.multiple_of(other * self.shard, self.shard), self.shard)
        return pltpu.make_async_remote_copy(
            src_ref=self.held.at[q, self.chip, own, :],
            dst_ref=self.z_in.at[q, step],
            send_sem=self.z_send.at[q, step],
            recv_sem=self.z_recv.at[q, step],
            device_id={"wide": self.w, "narrow": other},
            device_id_type=MESH,
        )

    def after_stage(self, q, stage):
        for h in (0, 1):
            for slot, kept in self.tiles_of(h, stage):
                arrive(self.chip_in.at[q, h, slot], self.chip_recv.at[q, h, slot])
                self.add_to(
                    lambda part, h=h, kept=kept: self.held.at[q, kept, part, self.lanes(h)],
                    lambda part, h=h, slot=slot: self.chip_in.at[q, h, slot, part, :],
                )
        if stage + 1 < self.bits:
            self.send_stage(q, stage + 1)
        else:
            for step in range(1, self.narrow):
                self.z_copy(q, step).start()

    def after_z(self, q):
        for step in range(1, self.narrow):
            arrive(self.z_in.at[q, step], self.z_recv.at[q, step])

        def one(r, carry):
            to = pl.ds(pl.multiple_of(r * 16, 16), 16)
            own = pl.ds(pl.multiple_of(self.n * self.shard + r * 16, 16), 16)
            value = self.held[q, self.chip, own, :].astype(F32)
            for step in range(1, self.narrow):
                value = value + self.z_in[q, step, to, :].astype(F32)
            self.out_ref[to, self.columns_of(q)] = value
            return carry

        lax.fori_loop(0, self.shard // 16, one, 0)

    def after_all(self):
        def one(q, carry):
            self.after_z(q)
            return carry

        lax.fori_loop(0, self.chunks, one, 0)

    def drain(self):
        def one(q, carry):
            arrive(self.core_in.at[q], self.core_send.at[q])
            for stage in range(self.bits):
                for h in (0, 1):
                    for slot, kept in self.tiles_of(h, stage):
                        self.chip_copy(q, h, stage, slot, kept).wait_send()
            for step in range(1, self.narrow):
                self.z_copy(q, step).wait_send()
            return carry

        lax.fori_loop(0, self.chunks, one, 0)


def reduce_scratch(wide, narrow, rows, tokens, columns, chunk):
    chips, rows, chunks = wide // 2, rows // wide, columns // chunk
    dma = pltpu.SemaphoreType.DMA
    return [
        pltpu.VMEM((2, chips * rows, tokens), BF16),
        pltpu.VMEM((chunks, chips, rows, chunk), BF16),
        pltpu.VMEM((chunks, chips, rows, chunk), BF16),
        pltpu.VMEM((chunks, chips, rows, chunk), BF16),
        pltpu.VMEM((chunks, 2, chips - 1, rows, chunk // 2), BF16),
        pltpu.VMEM((chunks, narrow, rows // narrow, chunk), BF16),
        dma((chunks,)),
        dma((chunks,)),
        dma((chunks, 2, chips - 1)),
        dma((chunks, 2, chips - 1)),
        dma((chunks, narrow)),
        dma((chunks, narrow)),
    ]


def greet(wide, narrow):
    w, n = lax.axis_index("wide"), lax.axis_index("narrow")
    barrier = pltpu.get_barrier_semaphore()
    for mask in range(1, wide):
        pl.semaphore_signal(
            barrier, inc=1, device_id={"wide": w ^ mask, "narrow": n}, device_id_type=MESH
        )
    for step in range(1, narrow):
        other = lax.rem(n + step, narrow)
        pl.semaphore_signal(
            barrier, inc=1, device_id={"wide": w, "narrow": other}, device_id_type=MESH
        )
    pl.semaphore_wait(barrier, wide + narrow - 2)


def to_owner(source, target, send_sem, recv_sem, mask):
    w, n = lax.axis_index("wide"), lax.axis_index("narrow")
    return pltpu.make_async_remote_copy(
        src_ref=source,
        dst_ref=target,
        send_sem=send_sem,
        recv_sem=recv_sem,
        device_id={"wide": w ^ mask, "narrow": n},
        device_id_type=MESH,
    )


def to_block(source, target, send_sem, recv_sem, owner):
    n = lax.axis_index("narrow")
    return pltpu.make_async_remote_copy(
        src_ref=source,
        dst_ref=target,
        send_sem=send_sem,
        recv_sem=recv_sem,
        device_id={"wide": owner, "narrow": n},
        device_id_type=MESH,
    )


def arrive(block, sem):
    pltpu.make_async_copy(block, block, sem).wait()


def attend_kernel(
    wide, narrow, groups, start_ref, mine_ref, w_ref, c_ref,
    x_ref, low_ref, full_ref, log_ref, w_all, c_all,
    keys, top, total, acc, done, own_sem, in_send, in_recv, out_send, out_recv,
    line_own, line_send, line_recv, *sems,
):
    me = lax.axis_index("wide")
    blocks, _, rows = x_ref.shape
    width = groups * HEAD_DIM
    own_in = pltpu.make_async_copy(mine_ref.at[me], x_ref.at[me], own_sem.at[0])
    own_in.start()
    greet(wide, narrow)
    for mask in range(1, wide):
        to_owner(
            mine_ref.at[me ^ mask], x_ref.at[me], in_send.at[mask], in_recv.at[me], mask
        ).start()
    flow = Flow(wide, narrow, w_ref, w_all, sems)
    line = Line(narrow, c_ref, c_all, (line_own, line_send, line_recv))
    flow.step(0)
    line.step(0)
    spread = {}
    for t in range(1, flow.last):
        spread.setdefault(min(blocks, blocks // 2 - 1 + t), []).append(functools.partial(flow.step, t))
    for t in range(1, narrow):
        spread.setdefault(min(blocks, blocks // 2 + 2 * t - 1), []).append(functools.partial(line.step, t))
    key_row = lax.broadcasted_iota(jnp.int32, (rows, rows), 0)
    column = lax.broadcasted_iota(jnp.int32, (rows, rows), 1)
    own_in.wait()

    def block(i, carry):
        pl.when(i != me)(lambda: arrive(x_ref.at[i], in_recv.at[i]))
        for at, actions in spread.items():
            if at < blocks:

                @pl.when(i == at)
                def _():
                    for action in actions:
                        action()

        keys[i] = x_ref[i, width : width + HEAD_DIM, :].T
        top[...] = jnp.full_like(top, NEGATIVE)
        total[...] = jnp.zeros_like(total)
        acc[...] = jnp.zeros_like(acc)
        start = start_ref[i]
        query_row = i * rows + column

        def step(j, carry):
            key_index = key_row + j * rows
            allowed = (key_index <= query_row) & (key_index >= start)
            key_block = keys[j]
            value_block = x_ref[j, width + HEAD_DIM :, :]
            for h in range(groups):
                own = pl.ds(h * HEAD_DIM, HEAD_DIM)
                scores = dot(key_block, x_ref[i, own, :], NN)
                scores = jnp.where(allowed, scores, NEGATIVE)
                old = top[h : h + 1, :]
                new = jnp.maximum(old, jnp.max(scores, 0, keepdims=True))
                shrink = jnp.exp(old - new)
                prob = jnp.exp(scores - new)
                top[h : h + 1, :] = new
                total[h : h + 1, :] = total[h : h + 1, :] * shrink + jnp.sum(prob, 0, keepdims=True)
                acc[own, :] = acc[own, :] * shrink + dot(value_block, prob.astype(BF16), NN)
            return carry

        lax.fori_loop(0, i + 1, step, 0)
        log_ref[i] = top[...] + jnp.log(total[...])
        for h in range(groups):
            own = pl.ds(h * HEAD_DIM, HEAD_DIM)
            result = acc[own, :] / total[h : h + 1, :]
            full_ref[i, own, :] = result
            done[i, own, :] = result.astype(BF16)

        @pl.when(i != me)
        def _():
            to_block(done.at[i], low_ref.at[me], out_send.at[i], out_recv.at[me], i).start()

        return carry

    lax.fori_loop(0, blocks, block, 0)
    low_ref[me] = done[me]
    for action in spread.get(blocks, []):
        action()
    flow.end()
    line.end()
    for mask in range(1, wide):
        to_owner(
            mine_ref.at[me ^ mask], x_ref.at[me], in_send.at[mask], in_recv.at[me], mask
        ).wait_send()
        other = me ^ mask
        arrive(low_ref.at[other], out_recv.at[other])
        arrive(done.at[other], out_send.at[other])


def attend(mine, start, w_out, cot, groups):
    wide, narrow = lax.axis_size("wide"), lax.axis_size("narrow")
    blocks, features, rows = mine.shape
    width = groups * HEAD_DIM
    dma = pltpu.SemaphoreType.DMA
    hbm = pl.BlockSpec(memory_space=pl.ANY)
    vmem = pl.BlockSpec(memory_space=pltpu.VMEM)
    return pl.pallas_call(
        functools.partial(attend_kernel, wide, narrow, groups),
        out_shape=(
            jax.ShapeDtypeStruct((blocks, features, rows), BF16),
            jax.ShapeDtypeStruct((blocks, width, rows), BF16),
            jax.ShapeDtypeStruct((blocks, width, rows), F32),
            jax.ShapeDtypeStruct((blocks, groups, rows), F32),
            jax.ShapeDtypeStruct((wide * narrow * w_out.shape[0], w_out.shape[1]), BF16),
            jax.ShapeDtypeStruct((narrow,) + cot.shape, BF16),
        ),
        in_specs=[vmem, vmem, hbm, hbm],
        out_specs=(vmem, vmem, vmem, vmem, hbm, hbm),
        scratch_shapes=[
            pltpu.VMEM((blocks, rows, HEAD_DIM), BF16),
            pltpu.VMEM((groups, rows), F32),
            pltpu.VMEM((groups, rows), F32),
            pltpu.VMEM((width, rows), F32),
            pltpu.VMEM((blocks, width, rows), BF16),
            dma((1,)),
            dma((wide,)),
            dma((wide,)),
            dma((wide,)),
            dma((wide,)),
            dma(()),
            dma((2, narrow)),
            dma((2, narrow)),
        ]
        + flow_sems(wide, narrow),
        compiler_params=pltpu.CompilerParams(
            collective_id=3, has_side_effects=True, vmem_limit_bytes=40 << 20
        ),
        cost_estimate=pl.CostEstimate(
            flops=32 * width * (blocks * rows) ** 2,
            bytes_accessed=64 << 20,
            transcendentals=groups * (blocks * rows) ** 2 // 2,
        ),
    )(start, mine, w_out, cot)


def attend_back_kernel(
    wide, narrow, groups, start_ref, x_ref, mine_ref, full_ref, log_ref, cos_ref, sin_ref, part_ref,
    left_ref, right_ref, out_ref, came_ref, weight_out,
    keys, values, acc, acc_keys, acc_values, grad_ref, done, own_sem, in_send, in_recv,
    q_send, q_recv, k_send, k_recv, p_send, p_recv, *refs,
):
    reduce = Reduce(wide, narrow, left_ref, right_ref, NN, weight_out, refs)
    me, n = lax.axis_index("wide"), lax.axis_index("narrow")

    def part_copy(step):
        other = lax.rem(n + step, narrow)
        return pltpu.make_async_remote_copy(
            src_ref=part_ref.at[other],
            dst_ref=came_ref.at[step],
            send_sem=p_send.at[step],
            recv_sem=p_recv.at[step],
            device_id={"wide": me, "narrow": other},
            device_id_type=MESH,
        )

    own_part = pltpu.make_async_copy(part_ref.at[n], came_ref.at[0], p_send.at[0])
    blocks, _, rows = x_ref.shape
    width = groups * HEAD_DIM
    own_in = pltpu.make_async_copy(mine_ref.at[me], grad_ref.at[me], own_sem.at[0])
    own_in.start()
    for j in range(blocks):
        keys[j] = x_ref[j, width : width + HEAD_DIM, :].T
        values[j] = x_ref[j, width + HEAD_DIM :, :].T
    acc_keys[...] = jnp.zeros_like(acc_keys)
    acc_values[...] = jnp.zeros_like(acc_values)
    greet(wide, narrow)
    for mask in range(1, wide):
        to_owner(
            mine_ref.at[me ^ mask], grad_ref.at[me], in_send.at[mask], in_recv.at[me], mask
        ).start()
    reduce.arrange()
    lax.fori_loop(0, reduce.chunks, lambda q, carry: (reduce.begin(q), carry)[1], 0)
    own_part.start()
    for step in range(1, narrow):
        part_copy(step).start()

    def weight_turn(c):
        chunks = reduce.chunks
        q = jnp.maximum(c - 2, 0) // 2
        ready = (c >= 2) & (lax.rem(c, 2) == 0) & (q < chunks)
        pl.when(ready)(lambda: reduce.after_core(jnp.minimum(q, chunks - 1)))
        actions = [functools.partial(reduce.after_stage, stage=stage) for stage in range(reduce.bits)]
        for index, action in enumerate(actions):
            since = jnp.maximum(c - (2 * chunks + 6 + 6 * index), -1)
            q = jnp.maximum(since, 0) // 5
            ready = (since >= 0) & (lax.rem(jnp.maximum(since, 0), 5) == 0) & (q < chunks)
            pl.when(ready)(functools.partial(action, jnp.minimum(q, chunks - 1)))

    turns = 2 * reduce.chunks + 6 + 6 * (reduce.bits - 1) + 5 * (reduce.chunks - 1) + 1
    key_row = lax.broadcasted_iota(jnp.int32, (rows, rows), 0)
    column = lax.broadcasted_iota(jnp.int32, (rows, rows), 1)
    own_in.wait()
    of_queries, of_keys = pl.ds(0, width), pl.ds(width, 2 * HEAD_DIM)

    def turn_back(block, cos, sin):
        front, back = block[:HALF, :], block[HALF:, :]
        return (front * cos + back * sin).astype(BF16), (back * cos - front * sin).astype(BF16)

    def block(i, carry):
        pl.when(i != me)(lambda: arrive(grad_ref.at[i], in_recv.at[i]))
        acc[...] = jnp.zeros_like(acc)
        start = start_ref[i]
        query_row = i * rows + column
        deltas = [
            jnp.sum(
                grad_ref[i, pl.ds(h * HEAD_DIM, HEAD_DIM), :].astype(F32)
                * full_ref[i, pl.ds(h * HEAD_DIM, HEAD_DIM), :],
                0,
                keepdims=True,
            )
            for h in range(groups)
        ]

        def step(j, carry):
            key_index = key_row + j * rows
            allowed = (key_index <= query_row) & (key_index >= start)
            key_block = keys[j]
            value_block = values[j]
            key_columns = x_ref[j, width : width + HEAD_DIM, :]
            grad_keys = acc_keys[j]
            grad_values = acc_values[j]
            for h in range(groups):
                own = pl.ds(h * HEAD_DIM, HEAD_DIM)
                query = x_ref[i, own, :]
                grad = grad_ref[i, own, :]
                scores = dot(key_block, query, NN)
                scores = jnp.where(allowed, scores, NEGATIVE)
                prob = jnp.exp(scores - log_ref[i, h : h + 1, :])
                grad_prob = dot(value_block, grad, NN)
                grad_scores = (prob * (grad_prob - deltas[h])).astype(BF16)
                acc[own, :] += dot(key_columns, grad_scores, NN)
                grad_keys = grad_keys + dot(query, grad_scores, NT)
                grad_values = grad_values + dot(grad, prob.astype(BF16), NT)
            acc_keys[j] = grad_keys
            acc_values[j] = grad_values
            weight_turn(i * (i + 1) // 2 + j)
            return carry

        lax.fori_loop(0, i + 1, step, 0)
        for h in range(groups):
            at = h * HEAD_DIM
            front, back = turn_back(
                acc[pl.ds(at, HEAD_DIM), :] * SCORE_SCALE, cos_ref[i], sin_ref[i]
            )
            done[i, pl.ds(at, HALF), :] = front
            done[i, pl.ds(at + HALF, HALF), :] = back

        @pl.when(i != me)
        def _():
            to_block(
                done.at[i, of_queries], out_ref.at[me, of_queries], q_send.at[i], q_recv.at[me], i
            ).start()

        return carry

    lax.fori_loop(0, blocks, block, 0)

    def last(j, carry):
        front, back = turn_back(acc_keys[j], cos_ref[j], sin_ref[j])
        done[j, pl.ds(width, HALF), :] = front
        done[j, pl.ds(width + HALF, HALF), :] = back
        done[j, pl.ds(width + HEAD_DIM, HEAD_DIM), :] = acc_values[j].astype(BF16)

        @pl.when(j != me)
        def _():
            to_block(
                done.at[j, of_keys], out_ref.at[me, of_keys], k_send.at[j], k_recv.at[me], j
            ).start()

        return carry

    lax.fori_loop(0, blocks, last, 0)
    out_ref[me] = done[me]

    def left(c, carry):
        weight_turn(c)
        return carry

    lax.fori_loop(blocks * (blocks + 1) // 2, max(turns, blocks * (blocks + 1) // 2), left, 0)

    reduce.after_all()
    reduce.drain()
    for mask in range(1, wide):
        other = me ^ mask
        arrive(mine_ref.at[other], in_send.at[mask])
        arrive(done.at[other, of_queries], q_send.at[other])
        arrive(done.at[other, of_keys], k_send.at[other])
        arrive(out_ref.at[other, of_queries], q_recv.at[other])
        arrive(out_ref.at[other, of_keys], k_recv.at[other])
    own_part.wait()
    for step in range(1, narrow):
        part_copy(step).wait()


def attend_back(x, mine, full, log_total, start, cos, sin, part, left, right, groups):
    wide, narrow = lax.axis_size("wide"), lax.axis_size("narrow")
    blocks, features, rows = x.shape
    width = groups * HEAD_DIM
    dma = pltpu.SemaphoreType.DMA
    hbm = pl.BlockSpec(memory_space=pl.ANY)
    vmem = pl.BlockSpec(memory_space=pltpu.VMEM)
    return pl.pallas_call(
        functools.partial(attend_back_kernel, wide, narrow, groups),
        out_shape=(
            jax.ShapeDtypeStruct(x.shape, BF16),
            jax.ShapeDtypeStruct(part.shape, BF16),
            jax.ShapeDtypeStruct((left.shape[0] // (wide * narrow), right.shape[1]), F32),
        ),
        in_specs=[vmem] * 7 + [hbm, vmem, vmem],
        out_specs=(vmem, hbm, vmem),
        scratch_shapes=[
            pltpu.VMEM((blocks, rows, HEAD_DIM), BF16),
            pltpu.VMEM((blocks, rows, HEAD_DIM), BF16),
            pltpu.VMEM((width, rows), F32),
            pltpu.VMEM((blocks, HEAD_DIM, rows), F32),
            pltpu.VMEM((blocks, HEAD_DIM, rows), F32),
            pltpu.VMEM((blocks, width, rows), BF16),
            pltpu.VMEM((blocks, features, rows), BF16),
            dma((1,)),
        ]
        + [dma((wide,))] * 6
        + [dma((narrow,))] * 2
        + reduce_scratch(wide, narrow, left.shape[0], left.shape[1], right.shape[1], 512),
        compiler_params=pltpu.CompilerParams(
            collective_id=4, has_side_effects=True, vmem_limit_bytes=50 << 20
        ),
        cost_estimate=pl.CostEstimate(
            flops=40 * width * (blocks * rows) ** 2,
            bytes_accessed=4 * x.size * 2,
            transcendentals=groups * (blocks * rows) ** 2 // 2,
        ),
    )(start, x, mine, full, log_total, cos, sin, part, left, right)


def gather(x, axis):
    return lax.all_gather(x, axis, axis=0, tiled=True)


def scatter_sum(x, axis):
    return lax.psum_scatter(x, axis, scatter_dimension=0, tiled=True)


def gather_kernel(wide, narrow, aligned, qkv_ref, cut_ref, qkv_all, cut_all, x_send, x_recv, x_own, *sems):
    w, n = lax.axis_index("wide"), lax.axis_index("narrow")
    greet(wide, narrow)
    flow = Flow(wide, narrow, qkv_ref, qkv_all, sems)
    depth = qkv_ref.shape[0]
    piece = cut_all.shape[1] // (2 * wide)

    def rows_of(owner):
        return cut_all.at[pl.ds(pl.multiple_of(owner * depth, depth), depth), :]

    def pieces(other):
        if not aligned:
            return [(cut_ref.at[other], pl.ds(0, cut_all.shape[1]))]
        return [
            (
                cut_ref.at[:, pl.ds(pl.multiple_of((j * narrow + other) * piece, piece), piece)],
                pl.ds(j * piece, piece),
            )
            for j in range(2 * wide)
        ]

    def target(columns):
        return cut_all.at[pl.ds(pl.multiple_of(n * depth, depth), depth), columns]

    def cut_start(step):
        other = lax.rem(n + step, narrow)
        for source, columns in pieces(other):
            pltpu.make_async_remote_copy(
                src_ref=source,
                dst_ref=target(columns),
                send_sem=x_send.at[step],
                recv_sem=x_recv.at[step],
                device_id={"wide": w, "narrow": other},
                device_id_type=MESH,
            ).start()

    for t in range(flow.last):
        flow.step(t)
        if t == min(1, narrow - 1):
            for source, columns in pieces(n):
                pltpu.make_async_copy(source, target(columns), x_own).start()
            for step in range(1, narrow):
                cut_start(step)
    flow.end()
    own = rows_of(n)
    pltpu.make_async_copy(own, own, x_own).wait()
    for step in range(1, narrow):
        pltpu.make_async_copy(own, own, x_send.at[step]).wait()
        block = rows_of(lax.rem(n + narrow - step, narrow))
        pltpu.make_async_copy(block, block, x_recv.at[step]).wait()


def gather_weights(qkv, gateup):
    wide, narrow = lax.axis_size("wide"), lax.axis_size("narrow")
    dma = pltpu.SemaphoreType.DMA
    hbm = pl.BlockSpec(memory_space=pl.ANY)
    every = wide * narrow
    shard, columns = gateup.shape
    aligned = (columns // (2 * every)) % 128 == 0
    if not aligned:
        gateup = gateup.reshape(shard, 2, wide, narrow, -1).transpose(3, 0, 1, 2, 4)
        gateup = gateup.reshape(narrow, shard, columns // narrow)
    return pl.pallas_call(
        functools.partial(gather_kernel, wide, narrow, aligned),
        out_shape=(
            jax.ShapeDtypeStruct((every * qkv.shape[0], qkv.shape[1]), BF16),
            jax.ShapeDtypeStruct((narrow * shard, columns // narrow), BF16),
        ),
        in_specs=[hbm, hbm],
        out_specs=(hbm, hbm),
        scratch_shapes=[dma((narrow,)), dma((narrow,)), dma(())] + flow_sems(wide, narrow),
        compiler_params=pltpu.CompilerParams(collective_id=0, has_side_effects=True),
        cost_estimate=pl.CostEstimate(flops=0, bytes_accessed=200 << 20, transcendentals=0),
    )(qkv, gateup)


def feed_kernel(
    narrow, x_ref, cot_ref, gate_up_ref, down_ref,
    low_out, grad_x_ref, part_gate_up, part_down,
    group_ref, gate_up, down, cot, hidden, grads, low, came,
    load_sem, x_send, x_recv, out_sem, g_send, g_recv,
):
    w, n = lax.axis_index("wide"), lax.axis_index("narrow")
    rows, width = x_ref.shape
    own = down.shape[0]
    tile = 256
    tiles = own // tile
    wtiles = width // tile

    def to_narrow(other):
        return {"wide": w, "narrow": other}

    loads = [
        pltpu.make_async_copy(gate_up_ref, gate_up, load_sem.at[0]),
        pltpu.make_async_copy(down_ref, down, load_sem.at[1]),
        pltpu.make_async_copy(cot_ref, cot, load_sem.at[2]),
        pltpu.make_async_copy(x_ref, group_ref.at[n], load_sem.at[3]),
    ]
    for load in loads:
        load.start()

    barrier = pltpu.get_barrier_semaphore()
    for step in range(1, narrow):
        pl.semaphore_signal(
            barrier, inc=1, device_id=to_narrow(lax.rem(n + step, narrow)), device_id_type=MESH
        )
    pl.semaphore_wait(barrier, narrow - 1)

    def owner_of(side, d):
        return n - d if side == 0 else n + d

    def valid(side, d):
        return n - d >= 0 if side == 0 else (n + d < narrow) & (d > 0)

    def passes(side, d):
        if side == 0:
            return (n - d >= 0) & (n < narrow - 1)
        return (n + d < narrow) & (n > 0)

    def x_copy(side, d):
        block = group_ref.at[owner_of(side, d)]
        return pltpu.make_async_remote_copy(
            src_ref=block,
            dst_ref=block,
            send_sem=x_send.at[side, d],
            recv_sem=x_recv.at[side, d + 1],
            device_id=to_narrow(n + 1 if side == 0 else n - 1),
            device_id_type=MESH,
        )

    def x_wait(side, d):
        block = group_ref.at[owner_of(side, d)]
        pltpu.make_async_copy(block, block, x_recv.at[side, d]).wait()

    def out_copy(at, block):
        return pltpu.make_async_copy(low.at[at], low_out.at[block], out_sem.at[at])

    def g_copy(block, half):
        columns = pl.ds(half * (width // 4), width // 4)
        return pltpu.make_async_remote_copy(
            src_ref=cot.at[block, :, columns],
            dst_ref=came.at[n, :, columns],
            send_sem=g_send.at[block, half],
            recv_sem=g_recv.at[n, half],
            device_id=to_narrow(block),
            device_id_type=MESH,
        )

    def compute(side, d):
        block = n - d + 2 * d * side
        before = 1 + jnp.minimum(n, d - 1) + jnp.minimum(narrow - 1 - n, d - 1)
        before = jnp.where(d == 0, 0, before + jnp.where((side == 1) & (n - d >= 0), 1, 0))
        at = lax.rem(before, 2)

        pl.when(before >= 2)(lambda: out_copy(at, block).wait())

        def first(f, carry):
            columns = pl.ds(pl.multiple_of(f * tile, tile), tile)
            other = pl.ds(pl.multiple_of(own + f * tile, tile), tile)
            x = group_ref[block]
            gate = dot(x, gate_up[:, columns], NN)
            up = dot(x, gate_up[:, other], NN)
            grad = dot(cot[block], down[columns, :], NT)
            sig = 1.0 / (1.0 + jnp.exp(-gate))
            silu = gate * sig
            hidden[block, :, columns] = (silu * up).astype(BF16)
            grads[block, :, columns] = (grad * up * (sig + silu * (1.0 - sig))).astype(BF16)
            grads[block, :, other] = (grad * silu).astype(BF16)
            return carry

        lax.fori_loop(0, tiles, first, 0)

        def second(f, carry):
            columns = pl.ds(pl.multiple_of(f * tile, tile), tile)
            cot[block, :, columns] = dot(grads[block], gate_up[columns, :], NT, BF16)
            low[at, :, columns] = dot(hidden[block], down[:, columns], NN, BF16)
            return carry

        for half in range(4):
            lax.fori_loop(half * (wtiles // 4), (half + 1) * (wtiles // 4), second, 0)
            pl.when(block != n)(lambda half=half: g_copy(block, half).start())
        out_copy(at, block).start()

    def distance(d, carry):
        for side in (0, 1):

            @pl.when(passes(side, d + 1))
            def _():
                x_wait(side, d + 1)
                x_copy(side, d + 1).start()

            @pl.when(valid(side, d) & (d > 0) & jnp.logical_not(passes(side, d)))
            def _():
                x_wait(side, d)

        @pl.when(d == 0)
        def _():
            for load in loads[:3]:
                load.wait()

        def one(side, carry):
            ok = jnp.where(side == 0, n - d, jnp.where(d > 0, narrow - 1 - n - d, -1)) >= 0
            pl.when(ok)(lambda: compute(side, d))
            return carry

        lax.fori_loop(0, 2, one, 0)
        return carry

    loads[3].wait()
    for side in (0, 1):
        pl.when(passes(side, 0))(lambda side=side: x_copy(side, 0).start())
    lax.fori_loop(0, narrow, distance, 0)

    tokens = narrow * rows
    again = [
        pltpu.make_async_copy(
            cot_ref.at[o], gate_up.at[pl.ds(o * rows, rows), pl.ds(0, width)], load_sem.at[4 + o]
        )
        for o in range(narrow)
    ]
    for load in again:
        load.start()
    for at in range(2):
        out_copy(at, n).wait()

    def flipped(ref, columns):
        return jnp.concatenate([ref[o, :, columns].T for o in range(narrow)], 1)

    def weight_tile(t, left, right, at_row, out_ref, first):
        at = lax.rem(t, 2)
        copy = pltpu.make_async_copy(low.at[at], out_ref, out_sem.at[at])
        pl.when(t >= 2)(lambda: copy.wait())
        turned = flipped(left, pl.ds(pl.multiple_of(at_row, tile), tile))

        def one(c, carry):
            columns = pl.ds(pl.multiple_of(c * 512, 512), 512)
            source = pl.ds(pl.multiple_of(first + c * 512, 512), 512)
            low[at, :, columns] = dot(turned, right(source), NN, BF16)
            return carry

        lax.fori_loop(0, width // 512, one, 0)
        copy.start()

    halves = 2 * own // width

    def gate_up_tile(t, carry):
        row, half = t // halves * tile, lax.rem(t, halves) * width
        row, half = pl.multiple_of(row, tile), pl.multiple_of(half, width)
        weight_tile(
            t, group_ref, lambda source: grads[:, :, source].reshape(tokens, 512), row,
            part_gate_up.at[pl.ds(row, tile), pl.ds(half, width)], half,
        )
        return carry

    def down_tile(t, carry):
        row = pl.multiple_of(t * tile, tile)
        weight_tile(
            t + 2, hidden, lambda source: gate_up[pl.ds(0, tokens), source], row,
            part_down.at[pl.ds(row, tile), :], 0,
        )
        return carry

    lax.fori_loop(0, wtiles * halves, gate_up_tile, 0)
    for load in again:
        load.wait()
    lax.fori_loop(0, tiles, down_tile, 0)
    for at in range(2):
        out_copy(at, n).wait()
    for side in (0, 1):
        for d in range(narrow - 1):
            pl.when(passes(side, d))(lambda side=side, d=d: x_copy(side, d).wait_send())
    for step in range(1, narrow):
        other = lax.rem(n + step, narrow)
        for half in range(4):
            g_copy(other, half).wait_send()
            arrive(came.at[other, :, pl.ds(half * (width // 4), width // 4)], g_recv.at[other, half])

    def add(r, carry):
        part = pl.ds(pl.multiple_of(r * 16, 16), 16)
        total = cot[n, part, :].astype(F32)
        for step in range(1, narrow):
            total = total + came[lax.rem(n + step, narrow), part, :].astype(F32)
        grad_x_ref[part, :] = total
        return carry

    lax.fori_loop(0, rows // 16, add, 0)


def feed(x, cot_group, gate_up, down):
    narrow = lax.axis_size("narrow")
    rows, width = x.shape
    own = down.shape[0]
    dma = pltpu.SemaphoreType.DMA
    hbm = pl.BlockSpec(memory_space=pl.ANY)
    vmem = pl.BlockSpec(memory_space=pltpu.VMEM)
    return pl.pallas_call(
        functools.partial(feed_kernel, narrow),
        out_shape=(
            jax.ShapeDtypeStruct((narrow, rows, width), BF16),
            jax.ShapeDtypeStruct((rows, width), F32),
            jax.ShapeDtypeStruct((width, 2 * own), BF16),
            jax.ShapeDtypeStruct((own, width), BF16),
        ),
        in_specs=[vmem, hbm, hbm, hbm],
        out_specs=(hbm, vmem, hbm, hbm),
        scratch_shapes=[
            pltpu.VMEM((narrow, rows, width), BF16),
            pltpu.VMEM((width, 2 * own), BF16),
            pltpu.VMEM((own, width), BF16),
            pltpu.VMEM((narrow, rows, width), BF16),
            pltpu.VMEM((narrow, rows, own), BF16),
            pltpu.VMEM((narrow, rows, 2 * own), BF16),
            pltpu.VMEM((2, rows, width), BF16),
            pltpu.VMEM((narrow, rows, width), BF16),
            dma((4 + narrow,)),
            dma((2, narrow + 1)),
            dma((2, narrow + 1)),
            dma((2,)),
            dma((narrow, 4)),
            dma((narrow, 4)),
        ],
        compiler_params=pltpu.CompilerParams(
            collective_id=1, has_side_effects=True, vmem_limit_bytes=58 << 20
        ),
        cost_estimate=pl.CostEstimate(
            flops=12 * narrow * rows * width * own, bytes_accessed=300 << 20, transcendentals=0
        ),
    )(x, cot_group.reshape(narrow, rows, width), gate_up, down)


def sum_kernel(
    wide, narrow, left_ref, right_ref, cut_ref, gains_ref, qkv_out, cut_out, gains_out,
    cut_in, gain_w, gain_sum, gain_z, own_sem, cut_send, cut_recv, gw_send, gw_recv, gz_send, gz_recv, *refs,
):
    reduce = Reduce(wide, narrow, left_ref, right_ref, NT, qkv_out, refs)
    w, n = reduce.w, reduce.n
    chunks, bits = reduce.chunks, reduce.bits
    reduce.arrange()
    greet(wide, narrow)

    def to_wide(mask):
        return {"wide": w ^ mask, "narrow": n}

    def to_narrow(step):
        return {"wide": w, "narrow": lax.rem(n + step, narrow)}

    own_cut = pltpu.make_async_copy(cut_ref.at[n], cut_in.at[n], own_sem)

    def cut_copy(step):
        return pltpu.make_async_remote_copy(
            src_ref=cut_ref.at[lax.rem(n + step, narrow)],
            dst_ref=cut_in.at[n],
            send_sem=cut_send.at[step],
            recv_sem=cut_recv.at[step],
            device_id=to_narrow(step),
            device_id_type=MESH,
        )

    def gw_copy(mask):
        return pltpu.make_async_remote_copy(
            src_ref=gains_ref.at[w ^ mask],
            dst_ref=gain_w.at[mask],
            send_sem=gw_send.at[mask],
            recv_sem=gw_recv.at[mask],
            device_id=to_wide(mask),
            device_id_type=MESH,
        )

    def gz_copy(step):
        return pltpu.make_async_remote_copy(
            src_ref=gain_sum.at[lax.rem(n + step, narrow)],
            dst_ref=gain_z.at[step],
            send_sem=gz_send.at[step],
            recv_sem=gz_recv.at[step],
            device_id=to_narrow(step),
            device_id_type=MESH,
        )

    ahead = min(4, chunks)
    lax.fori_loop(0, ahead, lambda q, carry: (reduce.begin(q), carry)[1], 0)
    own_cut.start()
    for step in range(1, narrow):
        cut_copy(step).start()
    for mask in range(1, wide):
        gw_copy(mask).start()

    def turn(t, carry):
        pl.when(t + ahead < chunks)(lambda: reduce.begin(t + ahead))
        pl.when(t < chunks)(lambda: reduce.after_core(t))
        for stage in range(bits):
            q = t - 1 - stage
            pl.when((q >= 0) & (q < chunks))(functools.partial(reduce.after_stage, q, stage))
        return carry

    lax.fori_loop(0, chunks + bits, turn, 0)

    total = gains_ref[w]
    for mask in range(1, wide):
        block = gain_w.at[mask]
        pltpu.make_async_copy(block, block, gw_recv.at[mask]).wait()
        total = total + gain_w[mask]
    gain_sum[...] = total
    for step in range(1, narrow):
        gz_copy(step).start()

    reduce.after_all()
    own_cut.wait()
    for step in range(1, narrow):
        other = lax.rem(n + narrow - step, narrow)
        arrive(cut_in.at[other], cut_recv.at[step])
    piece = cut_in.shape[2] // (2 * wide)
    if cut_out.shape[0] == narrow:
        for other in range(narrow):
            cut_out[other] = cut_in[other].astype(F32)
    else:
        for j in range(2 * wide):
            for other in range(narrow):
                cut_out[:, pl.ds((j * narrow + other) * piece, piece)] = cut_in[
                    other, :, pl.ds(j * piece, piece)
                ].astype(F32)

    total = gain_sum[n]
    for step in range(1, narrow):
        block = gain_z.at[step]
        pltpu.make_async_copy(block, block, gz_recv.at[step]).wait()
        total = total + gain_z[step]
    gains_out[...] = total

    for mask in range(1, wide):
        gw_copy(mask).wait_send()
    for step in range(1, narrow):
        gz_copy(step).wait_send()
        cut_copy(step).wait_send()
    reduce.drain()


def sum_all(left, right, cut, gains):
    wide, narrow = lax.axis_size("wide"), lax.axis_size("narrow")
    shard, cut_width = cut.shape[1:]
    aligned = (cut_width // (2 * wide)) % 128 == 0
    cut_shape = (shard, narrow * cut_width) if aligned else cut.shape
    dma = pltpu.SemaphoreType.DMA
    hbm = pl.BlockSpec(memory_space=pl.ANY)
    vmem = pl.BlockSpec(memory_space=pltpu.VMEM)
    results = pl.pallas_call(
        functools.partial(sum_kernel, wide, narrow),
        out_shape=(
            jax.ShapeDtypeStruct((shard, right.shape[0]), F32),
            jax.ShapeDtypeStruct(cut_shape, F32),
            jax.ShapeDtypeStruct((8, 128), F32),
        ),
        in_specs=[vmem, vmem, hbm, vmem],
        out_specs=(vmem, vmem, vmem),
        scratch_shapes=[
            pltpu.VMEM(cut.shape, BF16),
            pltpu.VMEM((wide, narrow, 8, 128), F32),
            pltpu.VMEM((narrow, 8, 128), F32),
            pltpu.VMEM((narrow, 8, 128), F32),
            dma(()),
            dma((narrow,)),
            dma((narrow,)),
            dma((wide,)),
            dma((wide,)),
            dma((narrow,)),
            dma((narrow,)),
        ]
        + reduce_scratch(wide, narrow, left.shape[1], left.shape[0], right.shape[0], 256),
        compiler_params=pltpu.CompilerParams(
            collective_id=2, has_side_effects=True, vmem_limit_bytes=54 << 20
        ),
        cost_estimate=pl.CostEstimate(flops=0, bytes_accessed=300 << 20, transcendentals=0),
    )(left, right, cut, gains)
    return results, aligned


def per_device(tokens, lengths, gain_attn, w_qkv, w_out, gain_mlp, w_gateup, w_down, cotangent):
    rows, width = tokens.shape[1:]
    wide, narrow = lax.axis_size("wide"), lax.axis_size("narrow")
    pack_rows = rows * wide
    query_width, key_width = HEADS * HEAD_DIM, KV_HEADS * HEAD_DIM
    groups = HEADS // wide
    copies = wide // KV_HEADS
    own_ff = FF // narrow
    first, positions = places(lengths[0], pack_rows)
    cos_all, sin_all = rotary(positions.astype(F32), HALF)
    first_row = lax.axis_index("wide") * rows
    cos = lax.dynamic_slice_in_dim(cos_all, first_row, rows, 1)
    sin = lax.dynamic_slice_in_dim(sin_all, first_row, rows, 1)
    cos_all = cos_all.reshape(HALF, wide, rows).transpose(1, 0, 2)
    sin_all = sin_all.reshape(HALF, wide, rows).transpose(1, 0, 2)
    start = first.reshape(wide, 1, rows)

    gains = jnp.stack([gain_attn, gain_mlp], -1)
    with_gains = jnp.concatenate([w_qkv, jnp.pad(gains, ((0, 0), (0, 126)))], -1)
    shard = w_gateup.shape[0]
    qkv_gained, gateup_rows = gather_weights(with_gains, w_gateup)
    qkv_whole = qkv_gained[:, : w_qkv.shape[1]]
    gain_one = qkv_gained[:, w_qkv.shape[1]].astype(F32)
    gain_two = qkv_gained[:, w_qkv.shape[1] + 1].astype(F32)
    gateup_own = gather(gateup_rows, "wide")
    down_own = gather(w_down, "wide")

    inputs = tokens[0].astype(F32)
    scale_one = lax.rsqrt(jnp.mean(inputs * inputs, -1, keepdims=True) + EPS)
    unit_one = inputs * scale_one
    normed_one = (unit_one * gain_one).astype(BF16)
    projected = dot(qkv_whole, normed_one, (((0,), (1,)), ((), ())))
    turning = projected[: query_width + key_width].reshape(HEADS + KV_HEADS, 2, HALF, rows)
    front, back = turning[:, 0], turning[:, 1]
    turned = jnp.stack([front * cos - back * sin, back * cos + front * sin], 1)
    queries = (turned[:HEADS] * SCORE_SCALE).astype(BF16).reshape(wide, groups * HEAD_DIM, rows)
    keys = turned[HEADS:].astype(BF16).reshape(KV_HEADS, HEAD_DIM, rows)
    values = projected[query_width + key_width :].astype(BF16).reshape(KV_HEADS, HEAD_DIM, rows)
    keys_values = jnp.repeat(jnp.concatenate([keys, values], 1), copies, 0)
    heads, attended_low, attended_full, log_total, out_whole, cot_group = attend(
        jnp.concatenate([queries, keys_values], 1), start, w_out, cotangent[0], groups
    )
    cot_group = cot_group.reshape(-1, width)
    attended_low = attended_low.reshape(query_width, rows)
    middle = inputs + dot(attended_low, out_whole, TN)
    scale_two = lax.rsqrt(jnp.mean(middle * middle, -1, keepdims=True) + EPS)
    unit_two = middle * scale_two
    normed_two = (unit_two * gain_two).astype(BF16)

    low_part, grad_normed_two, part_gateup, part_down = feed(
        normed_two, cot_group, gateup_own, down_own
    )
    grad_gateup = scatter_sum(part_gateup, "wide").reshape(narrow, shard, 2 * own_ff)
    grad_down = scatter_sum(part_down, "wide")
    part_gain_two = jnp.sum(grad_normed_two * unit_two, 0)
    grad_middle = cotangent[0].astype(F32) + norm_back(
        grad_normed_two * gain_two, unit_two, scale_two
    )
    grad_branch = grad_middle.astype(BF16)
    grad_attended = dot(out_whole, grad_branch, NT, BF16).reshape(wide, groups * HEAD_DIM, rows)
    grad_heads, low_came, grad_wout = attend_back(
        heads, grad_attended, attended_full, log_total, start, cos_all, sin_all, low_part,
        attended_low, grad_branch, groups,
    )
    layer_out = (middle + jnp.sum(low_came.astype(F32), 0)).astype(BF16)[None]
    grad_queries = grad_heads[:, : groups * HEAD_DIM].reshape(query_width, rows)
    grad_keys_values = (
        grad_heads[:, groups * HEAD_DIM :]
        .reshape(KV_HEADS, copies, 2, HEAD_DIM, rows)
        .astype(F32)
        .sum(1)
        .astype(BF16)
    )
    grad_projected = jnp.concatenate(
        [
            grad_queries,
            grad_keys_values[:, 0].reshape(key_width, rows),
            grad_keys_values[:, 1].reshape(key_width, rows),
        ],
        0,
    )
    grad_normed_one = dot(grad_projected, qkv_whole, (((0,), (1,)), ((), ())))
    part_gain_one = jnp.sum(grad_normed_one * unit_one, 0)
    part_gains = jnp.stack([part_gain_one, part_gain_two], 0).reshape(2, wide, narrow, shard)
    part_gains = jnp.pad(
        part_gains.transpose(1, 2, 0, 3), ((0, 0), (0, 0), (0, 6), (0, 128 - shard))
    )
    (grad_qkv, grad_gateup, grad_gains), done = sum_all(
        normed_one, grad_projected, grad_gateup, part_gains
    )
    if not done:
        grad_gateup = (
            grad_gateup.reshape(narrow, shard, 2, wide, -1)
            .transpose(1, 2, 3, 0, 4)
            .reshape(shard, 2 * FF)
        )
    grad_down, grad_gains = lax.optimization_barrier((grad_down, grad_gains))
    grad_down = grad_down.astype(F32)
    grad_inputs = grad_middle + norm_back(grad_normed_one * gain_one, unit_one, scale_one)
    grad_tokens = grad_inputs.astype(BF16)[None]
    return (
        layer_out,
        grad_tokens,
        grad_gains[0, :shard],
        grad_qkv,
        grad_wout,
        grad_gains[1, :shard],
        grad_gateup,
        grad_down,
    )


def solution(mesh):
    rows, packs = P("narrow", "wide", None), P("narrow", None)
    weight, gain = P(BOTH, None), P(BOTH)
    return jax.shard_map(
        per_device,
        mesh=mesh,
        in_specs=(rows, packs, gain, weight, weight, gain, weight, weight, rows),
        out_specs=(rows, rows, gain, weight, weight, gain, weight, weight),
        check_vma=False,
    )
```
